32 devices in a mesh: img: 8 (over z, x), lat: 4 (over y, core).
Axes of the slice: x: 2, y: 2, z: 4, core: 2. Of those that a mesh axis runs over, the one named last changes fastest.
Arguments:
- media: bfloat16 [98304, 1024], P(('img', 'lat')), may hold values from -6 to 6
- latents: float32 [192, 64, 1024], P('img', 'lat'), may hold values from -6 to 6
- counts: int32 [8, 24], P('img'), may hold values from 1 to 6, 48 in all within a row
- cotangent: bfloat16 [192, 64, 1024], P('img', 'lat'), may hold values from -6 to 6
- attend_weight: float32 [1024, 1536], P(('img', 'lat')), may hold values from -0.1875 to 0.1875
- output_weight: float32 [512, 1024], P(('img', 'lat')), may hold values from -4 to 4
- expand_weight: float32 [1024, 4096], P(('img', 'lat')), may hold values from -0.1875 to 0.1875
- shrink_weight: float32 [4096, 1024], P(('img', 'lat')), may hold values from -0.09375 to 0.09375
- layer_gains: float32 [1024, 3], P(('img', 'lat')), may hold values from 0.24 to 3.6
- layer_biases: float32 [1024, 3], P(('img', 'lat')), may hold values from -1.2 to 1.2
- attend_momentum: float32 [1024, 1536], P(('img', 'lat')), may hold values from -0.00021362305 to 0.00021362305
- output_momentum: float32 [512, 1024], P(('img', 'lat')), may hold values from -0.00021362305 to 0.00021362305
- expand_momentum: float32 [1024, 4096], P(('img', 'lat')), may hold values from -0.00021362305 to 0.00021362305
- shrink_momentum: float32 [4096, 1024], P(('img', 'lat')), may hold values from -0.00021362305 to 0.00021362305
- gains_momentum: float32 [1024, 3], P(('img', 'lat')), may hold values from -0.0008544922 to 0.0008544922
- biases_momentum: float32 [1024, 3], P(('img', 'lat')), may hold values from -0.0008544922 to 0.0008544922
- attend_average: float32 [1024, 1536], P(('img', 'lat')), may hold values from -0.1875 to 0.1875
- output_average: float32 [512, 1024], P(('img', 'lat')), may hold values from -4 to 4
- expand_average: float32 [1024, 4096], P(('img', 'lat')), may hold values from -0.1875 to 0.1875
- shrink_average: float32 [4096, 1024], P(('img', 'lat')), may hold values from -0.09375 to 0.09375
- gains_average: float32 [1024, 3], P(('img', 'lat')), may hold values from 0.5 to 1.5
- biases_average: float32 [1024, 3], P(('img', 'lat')), may hold values from -1.2 to 1.2
Outputs:
- latents_out: float32 [192, 64, 1024], P('img', 'lat')
- media_grad: bfloat16 [98304, 1024], P(('img', 'lat'))
- latents_grad: float32 [192, 64, 1024], P('img', 'lat')
- grad_norm: float32 [], replicated
- attend_master: float32 [1024, 1536], P(('img', 'lat'))
- output_master: float32 [512, 1024], P(('img', 'lat'))
- expand_master: float32 [1024, 4096], P(('img', 'lat'))
- shrink_master: float32 [4096, 1024], P(('img', 'lat'))
- gains_master: float32 [1024, 3], P(('img', 'lat'))
- biases_master: float32 [1024, 3], P(('img', 'lat'))
- attend_buffer: float32 [1024, 1536], P(('img', 'lat'))
- output_buffer: float32 [512, 1024], P(('img', 'lat'))
- expand_buffer: float32 [1024, 4096], P(('img', 'lat'))
- shrink_buffer: float32 [4096, 1024], P(('img', 'lat'))
- gains_buffer: float32 [1024, 3], P(('img', 'lat'))
- biases_buffer: float32 [1024, 3], P(('img', 'lat'))
- attend_smoothed: float32 [1024, 1536], P(('img', 'lat'))
- output_smoothed: float32 [512, 1024], P(('img', 'lat'))
- expand_smoothed: float32 [1024, 4096], P(('img', 'lat'))
- shrink_smoothed: float32 [4096, 1024], P(('img', 'lat'))
- gains_smoothed: float32 [1024, 3], P(('img', 'lat'))
- biases_smoothed: float32 [1024, 3], P(('img', 'lat'))
The draws below stay inside these ranges and needn't reach their ends.
Inputs may be any that keep to these rules, and one draw needn't show every extreme that they name: Each row of counts holds 24 whole numbers that sum to 48; the largest of a row is exactly 6.
All inputs are finite; a program needn't handle non-finite values.
Results may differ from the reference program's by a relative error of at most 0.017.
The reference program's roundings to bfloat16 on the way count: a program that leaves them out, or rounds other values in their place, can miss the bound.
Values may be sent and summed in bfloat16 or wider, within the bound.
A program may use at most 256 MiB of HBM per device.

```python
import functools
import math
import jax
import jax.numpy as jnp
import numpy as np
from jax import lax

D = 1024
HEADS = 8
HDIM = 64
FF = 4096
LATENTS = 64
PATCH_IMG = 256
MOST_IMG = 6
IMG_DEV = 48
INNER = 512
S_DEV = 24
GROUPS = 8
SAMPLES = 192
PATCHES = 98304


def draw_layer_gains(key, part):
    noise_key = jax.random.fold_in(key, 17)
    position = jnp.arange(D, dtype=jnp.float32) / D
    ramp = 0.45 * jnp.power(2.2 / 0.45, position)
    noise = jax.random.uniform(noise_key, (D, 3), dtype=jnp.float32, minval=0.8, maxval=1.2)
    return (ramp[:, None] * noise).astype(jnp.float32)


def levels(stream_key, shape, shards, smallest, largest):
    def one(dim, blocks):
        draws = jax.random.uniform(jax.random.fold_in(jax.random.fold_in(stream_key, 6), dim), (blocks,), jnp.float32, smallest / len(shards), largest / len(shards))
        return jnp.repeat(jnp.exp(draws), shape[dim] // blocks).reshape((-1,) + (1,) * (len(shape) - dim - 1))

    factor_of = one(*shards[0])
    for cut in shards[1:]:
        factor_of = factor_of * one(*cut)
    return factor_of


def length_profile(number_of, total, bound, slope):
    portions = [(1 << 20) // math.isqrt(grade ** slope) + 1 for grade in range(2, number_of + 1)]
    rest, holding = total - bound - (number_of - 1), [1] * (number_of - 1)
    while rest > 0:
        candidates = [i for i in range(number_of - 1) if holding[i] < bound]
        pool, budget = sum([portions[i] for i in candidates]), rest
        for i in candidates:
            addition = min(bound - holding[i], max(1, budget * portions[i] // pool), rest)
            holding[i] = holding[i] + addition
            rest = rest - addition
    return np.array([bound] + holding)


def uneven_parts(rng, number_of, total, bound, skew):
    if number_of == 2:
        one = jax.random.randint(rng, (), max(1, total - bound), min(bound, total - 1) + 1)
        return jnp.stack([one, total - one])
    tallies = jnp.asarray(length_profile(number_of, total, bound, skew), jnp.int32)
    twos = (number_of - 1) // 2
    giver, taker = tallies[1:1 + 2 * twos:2], tallies[2:2 + 2 * twos:2]
    slack = jnp.minimum(giver - 1, bound - taker)
    shifted = jax.random.randint(jax.random.fold_in(rng, 1), (twos,), 0, 1 << 20) % (slack + 1)
    tallies = tallies.at[1:1 + 2 * twos:2].set(giver - shifted).at[2:2 + 2 * twos:2].set(taker + shifted)
    return tallies[jax.random.permutation(jax.random.fold_in(rng, 2), number_of)]


def centred(own_key, dims, scale, reach, cuts=(), kind=jnp.bfloat16):
    values = scale * jax.random.normal(own_key, dims, jnp.float32)
    if cuts:
        values = values * levels(own_key, dims, cuts, -0.22, 0.18)
    return jnp.clip(values, -reach, reach).astype(kind)


def setup_inputs(seed: int = 0) -> dict:
    key_of = jax.random.split(jax.random.key(seed), 23)
    return {
        "media": centred(key_of[0], (PATCHES, D), 1.0, 6.0, ((0, 32),)),
        "latents": centred(key_of[1], (SAMPLES, LATENTS, D), 1.0, 6.0, ((0, 8), (1, 4)), jnp.float32),
        "counts": jax.vmap(lambda own: uneven_parts(own, S_DEV, IMG_DEV, MOST_IMG, 1))(jax.random.split(key_of[2], GROUPS)).reshape((GROUPS, S_DEV)).astype(jnp.int32),
        "cotangent": centred(key_of[3], (SAMPLES, LATENTS, D), 1.0, 6.0, ((0, 8), (1, 4))),
        "attend_weight": centred(key_of[4], (D, 3 * INNER), D ** -0.5, 0.1875, ((0, 32),), jnp.float32),
        "output_weight": centred(key_of[5], (INNER, D), (max(1, 3 * INNER // (2 * PATCH_IMG + LATENTS))) ** -0.5, 4.0, ((0, 32),), jnp.float32),
        "expand_weight": centred(key_of[6], (D, FF), D ** -0.5, 0.1875, ((0, 32),), jnp.float32),
        "shrink_weight": centred(key_of[7], (FF, D), FF ** -0.5, 0.09375, ((0, 32),), jnp.float32),
        "layer_gains": draw_layer_gains(jax.random.fold_in(key_of[22], 71), 0),
        "layer_biases": centred(key_of[9], (D, 3), 0.2, 1.2, ((0, 32),), jnp.float32),
        "attend_momentum": centred(key_of[10], (D, 3 * INNER), (0.11 * (4 * D * INNER + 2 * D * FF) ** -0.5), 0.00021362305, ((0, 32),), jnp.float32),
        "output_momentum": centred(key_of[11], (INNER, D), (0.11 * (4 * D * INNER + 2 * D * FF) ** -0.5), 0.00021362305, ((0, 32),), jnp.float32),
        "expand_momentum": centred(key_of[12], (D, FF), (0.11 * (4 * D * INNER + 2 * D * FF) ** -0.5), 0.00021362305, ((0, 32),), jnp.float32),
        "shrink_momentum": centred(key_of[13], (FF, D), (0.11 * (4 * D * INNER + 2 * D * FF) ** -0.5), 0.00021362305, ((0, 32),), jnp.float32),
        "gains_momentum": centred(key_of[14], (D, 3), (0.44 * (4 * D * INNER + 2 * D * FF) ** -0.5), 0.0008544922, ((0, 32),), jnp.float32),
        "biases_momentum": centred(key_of[15], (D, 3), (0.44 * (4 * D * INNER + 2 * D * FF) ** -0.5), 0.0008544922, ((0, 32),), jnp.float32),
        "attend_average": centred(key_of[16], (D, 3 * INNER), D ** -0.5, 0.1875, ((0, 32),), jnp.float32),
        "output_average": centred(key_of[17], (INNER, D), (max(1, 3 * INNER // (2 * PATCH_IMG + LATENTS))) ** -0.5, 4.0, ((0, 32),), jnp.float32),
        "expand_average": centred(key_of[18], (D, FF), D ** -0.5, 0.1875, ((0, 32),), jnp.float32),
        "shrink_average": centred(key_of[19], (FF, D), FF ** -0.5, 0.09375, ((0, 32),), jnp.float32),
        "gains_average": jnp.clip(1.0 + 0.1 * jax.random.normal(key_of[20], (D, 3), jnp.float32), 0.5, 1.5),
        "biases_average": centred(key_of[21], (D, 3), 0.2, 1.2, ((0, 32),), jnp.float32),
    }


EPS = 1e-05
MOMENTUM = 0.9
DECAY = 0.0001
AVERAGING = 0.6
CLIP_NORM = 1.0
MASKED = -1e+30
RATE_SCALES = (1.0, 100.0, 1.0, 1.0, 15.0, 1.0)

@jax.custom_vjp
def low(v):
    return lax.optimization_barrier(v.astype(jnp.bfloat16)).astype(jnp.float32)

@jax.custom_vjp
def low_back(v):
    return v

def low_keep(v):
    return (low(v), None)

def low_pass(kept, grad):
    return (grad,)

def back_keep(v):
    return (v, None)

def back_low(kept, grad):
    return (low(grad),)
low.defvjp(low_keep, low_pass)
low_back.defvjp(back_keep, back_low)

def matmul(first_op, second_op):
    return jnp.dot(first_op, second_op, precision=lax.Precision.HIGHEST, preferred_element_type=jnp.float32)

def layer_norm(values, norm_gain, norm_bias):
    centered = values - lax.optimization_barrier(jnp.mean(values, axis=-1, keepdims=True))
    row_spread = lax.optimization_barrier(jnp.mean(centered * centered, axis=-1, keepdims=True))
    return centered * lax.rsqrt(row_spread + EPS) * norm_gain + norm_bias

def step_size():
    return 0.37 * math.sqrt((4 * D * INNER + 2 * D * FF) / D)

def heads_first(matrix):
    return matrix.reshape(matrix.shape[0], HEADS, HDIM).transpose(1, 0, 2)

def head_attention(query_rows, key_rows, value_rows, query_ids, key_ids):
    scores = low_back(matmul(query_rows, key_rows.T) * HDIM ** (-0.5))
    scores = jnp.where(query_ids[:, None] == key_ids[None, :], scores, MASKED)
    row_top = lax.optimization_barrier(jnp.max(scores, axis=-1, keepdims=True))
    log_total = row_top + jnp.log(lax.optimization_barrier(jnp.sum(jnp.exp(scores - row_top), axis=-1, keepdims=True)))
    attn_probs = low(jnp.exp(scores - log_total))
    return matmul(attn_probs, value_rows)

def group_forward(weights, media_rows, latent_rows, count_row):
    attend_w, output_w, expand_w, shrink_w, gain_cols, bias_cols = weights
    sample_ends = jnp.cumsum(count_row).astype(jnp.int32)
    image_ids = lax.optimization_barrier(jnp.sum((jnp.arange(IMG_DEV, dtype=jnp.int32)[:, None] >= sample_ends[None, :]).astype(jnp.int32), axis=1)).astype(jnp.int32)
    patch_ids = jnp.repeat(image_ids, PATCH_IMG)
    latent_ids = jnp.repeat(jnp.arange(S_DEV, dtype=jnp.int32), LATENTS)
    normed_media = low(layer_norm(media_rows, gain_cols[:, 0], bias_cols[:, 0]))
    normed_latents = low(layer_norm(latent_rows, gain_cols[:, 1], bias_cols[:, 1]))
    query_rows = low_back(low(matmul(normed_latents, attend_w[:, :INNER])))
    source_rows = jnp.concatenate([normed_media, normed_latents], axis=0)
    key_rows = low_back(low(matmul(source_rows, attend_w[:, INNER:2 * INNER])))
    value_rows = low_back(low(matmul(source_rows, attend_w[:, 2 * INNER:])))
    key_ids = jnp.concatenate([patch_ids, latent_ids])

    def one_head(head_item):
        return head_attention(head_item[0], head_item[1], head_item[2], latent_ids, key_ids)
    context = lax.map(jax.checkpoint(one_head), (heads_first(query_rows), heads_first(key_rows), heads_first(value_rows)))
    context = low_back(low(context.transpose(1, 0, 2).reshape(S_DEV * LATENTS, INNER)))
    mixed_rows = latent_rows + low_back(matmul(context, output_w))
    normed_mixed = low(layer_norm(mixed_rows, gain_cols[:, 2], bias_cols[:, 2]))
    hidden_rows = low(jax.nn.gelu(low_back(matmul(normed_mixed, expand_w)), approximate=False))
    return mixed_rows + low_back(matmul(hidden_rows, shrink_w))

def forward(attend_weight, output_weight, expand_weight, shrink_weight, layer_gains, layer_biases, media_rows, latent_rows, counts):
    weights = (low(attend_weight), low(output_weight), low(expand_weight), low(shrink_weight), low(layer_gains), low(layer_biases))

    def one_group(group_item):
        return group_forward(weights, group_item[0], group_item[1], group_item[2])
    result = lax.map(jax.checkpoint(one_group), (media_rows.reshape(GROUPS, IMG_DEV * PATCH_IMG, D), latent_rows.reshape(GROUPS, S_DEV * LATENTS, D), counts))
    return result.reshape(SAMPLES, LATENTS, D)

def reference(media, latents, counts, cotangent, attend_weight, output_weight, expand_weight, shrink_weight, layer_gains, layer_biases, attend_momentum, output_momentum, expand_momentum, shrink_momentum, gains_momentum, biases_momentum, attend_average, output_average, expand_average, shrink_average, gains_average, biases_average):
    latents_out, pullback = jax.vjp(functools.partial(forward, counts=counts), attend_weight, output_weight, expand_weight, shrink_weight, layer_gains, layer_biases, media.astype(jnp.float32), latents)
    gradients = pullback(cotangent.astype(jnp.float32))
    media_grad = gradients[6].astype(jnp.bfloat16)
    latents_grad = gradients[7]
    squares = sum((jnp.sum(piece * piece) for piece in gradients[:6]))
    grad_norm = jnp.sqrt(squares)
    factor = jnp.minimum(1.0, CLIP_NORM / (grad_norm + 1e-06))
    masters = (attend_weight, output_weight, expand_weight, shrink_weight, layer_gains, layer_biases)
    moments = (attend_momentum, output_momentum, expand_momentum, shrink_momentum, gains_momentum, biases_momentum)
    averages = (attend_average, output_average, expand_average, shrink_average, gains_average, biases_average)
    decay_rates = (DECAY, DECAY, DECAY, DECAY, 0.0, 0.0)
    step_rate = step_size()
    new_masters = []
    new_buffers = []
    new_smoothed = []
    for master, moment, average, gradient, decay_rate, rate_scale in zip(masters, moments, averages, gradients[:6], decay_rates, RATE_SCALES):
        step_grad = factor * gradient + decay_rate * master
        buffer = MOMENTUM * moment + step_grad
        master_new = master - step_rate * rate_scale * (step_grad + MOMENTUM * buffer)
        new_masters.append(master_new)
        new_buffers.append(buffer)
        new_smoothed.append(AVERAGING * average + (1.0 - AVERAGING) * master_new)
    return (latents_out, media_grad, latents_grad, grad_norm, new_masters[0], new_masters[1], new_masters[2], new_masters[3], new_masters[4], new_masters[5], new_buffers[0], new_buffers[1], new_buffers[2], new_buffers[3], new_buffers[4], new_buffers[5], new_smoothed[0], new_smoothed[1], new_smoothed[2], new_smoothed[3], new_smoothed[4], new_smoothed[5])
```

```python
import functools
import math

import jax
import jax.numpy as jnp
from jax import lax
from jax.experimental import pallas as pl
from jax.experimental.pallas import tpu as pltpu
from jax.sharding import PartitionSpec as P

HEADS = 8
HDIM = 64
PATCH_IMG = 256
GROUP = 4
EPS = 1e-05
MOMENTUM = 0.9
DECAY = 0.0001
AVERAGING = 0.6
CLIP_NORM = 1.0
RATE_SCALES = (1.0, 100.0, 1.0, 1.0, 15.0, 1.0)
AXES = ("img", "lat")
LANES = 128
BLOCKS = 32
SCALE = HDIM ** (-0.5)
F32 = jnp.float32
BF16 = jnp.bfloat16
MESH = pl.DeviceIdType.MESH
VMEM_LIMIT = 60 * 1024 * 1024


def mm(a, b):
    return jnp.dot(a, b, preferred_element_type=F32)


def mm_tn(a, b):
    return lax.dot_general(a, b, (((0,), (0,)), ((), ())), preferred_element_type=F32)


def mm_nt(a, b):
    return lax.dot_general(a, b, (((1,), (1,)), ((), ())), preferred_element_type=F32)


def any_spec():
    return pl.BlockSpec(memory_space=pl.ANY)


def vmem_spec():
    return pl.BlockSpec(memory_space=pltpu.VMEM)


def params(**more):
    return pltpu.CompilerParams(vmem_limit_bytes=VMEM_LIMIT, **more)


def place():
    img = lax.axis_index("img")
    lat = lax.axis_index("lat")
    return img // 2, img % 2, lat // 2, lat % 2


def flat(a, b, e, c):
    return ((a * 2 + b) * 2 + e) * 2 + c


def device(a, b, e, c):
    return (a * 2 + b, e * 2 + c)


def first_partner(a, b, e, c):
    return a, (b + 1 - c) % 2, (e + c) % 2, c


def second_partner(a, b, e, c):
    return a, (b + c) % 2, (e + 1 - c) % 2, c


def z_order(depth):
    order = [0]
    for k in range(1, depth // 2 + 1):
        order.append(k)
        if depth - k != k:
            order.append(depth - k)
    return order


def greet(depth, a, b, e, c):
    barrier = pltpu.get_barrier_semaphore()
    friends = [device((a + k) % depth, b, e, c) for k in range(1, depth)]
    friends += [
        device(*first_partner(a, b, e, c)),
        device(*second_partner(a, b, e, c)),
        device(a, b, e, 1 - c),
    ]
    for friend in friends:
        pl.semaphore_signal(barrier, inc=1, device_id=friend, device_id_type=MESH)
    pl.semaphore_wait(barrier, len(friends))


def gather_kernel(depth, x_ref, o_ref, local_sem, send_sem, recv_sem):
    a, b, e, c = place()
    me = flat(a, b, e, c)
    greet(depth, a, b, e, c)
    own = pltpu.make_async_copy(x_ref, o_ref.at[me], local_sem)
    own.start()
    one = first_partner(a, b, e, c)
    two = second_partner(a, b, e, c)
    both = second_partner(*one)
    homes = [(a, b, e, c), one, two, both]
    twin = device(a, b, e, 1 - c)
    sends = []

    def source(k, j):
        _, hb, he, hc = homes[j % 4]
        return flat((a - k) % depth, hb, he, hc if j < 4 else 1 - c)

    def send(k, j, src, row, target):
        slot = k * 8 + j
        copy = pltpu.make_async_remote_copy(
            src_ref=src,
            dst_ref=o_ref.at[row],
            send_sem=send_sem.at[slot],
            recv_sem=recv_sem.at[slot],
            device_id=target,
            device_id_type=MESH,
        )
        copy.start()
        sends.append(copy)

    def arrive(k, j):
        slot = k * 8 + j
        pltpu.make_async_remote_copy(
            src_ref=x_ref,
            dst_ref=o_ref.at[source(k, j)],
            send_sem=send_sem.at[slot],
            recv_sem=recv_sem.at[slot],
            device_id=twin,
            device_id_type=MESH,
        ).wait_recv()

    def block(k, j):
        return x_ref if (k, j) == (0, 0) else o_ref.at[source(k, j)]

    def stage_one(k):
        if k:
            arrive(k, 0)
        row = source(k, 0)
        send(k, 1, block(k, 0), row, device(*one))
        send(k, 2, block(k, 0), row, device(*two))
        send(k, 4, block(k, 0), row, twin)

    def stage_two(k):
        arrive(k, 1)
        send(k, 3, block(k, 1), source(k, 1), device(*two))
        send(k, 5, block(k, 1), source(k, 1), twin)
        arrive(k, 2)
        send(k, 6, block(k, 2), source(k, 2), twin)

    def stage_three(k):
        arrive(k, 3)
        send(k, 7, block(k, 3), source(k, 3), twin)

    order = z_order(depth)
    for k in order[1:]:
        send(k, 0, x_ref, me, device((a + k) % depth, b, e, c))
    for n in range(depth + 2):
        if n < depth:
            stage_one(order[n])
        if 1 <= n < depth + 1:
            stage_two(order[n - 1])
        if n >= 2:
            stage_three(order[n - 2])
    for k in range(depth):
        for j in range(4, 8):
            arrive(k, j)
    for copy in sends:
        copy.wait_send()
    own.wait()


def gather_fast(shard, depth, collective_id):
    count = depth * 8
    return pl.pallas_call(
        functools.partial(gather_kernel, depth),
        out_shape=jax.ShapeDtypeStruct((count,) + shard.shape, shard.dtype),
        in_specs=[any_spec()],
        out_specs=any_spec(),
        scratch_shapes=[
            pltpu.SemaphoreType.DMA,
            pltpu.SemaphoreType.DMA((count,)),
            pltpu.SemaphoreType.DMA((count,)),
        ],
        compiler_params=pltpu.CompilerParams(collective_id=collective_id, has_side_effects=True),
        name=f"gather{collective_id}",
    )(shard)


def add_into(target, first, second, rows, chunk):
    @pl.loop(0, rows // chunk)
    def _(step):
        part = pl.ds(step * chunk, chunk)
        total = first[part, :].astype(F32) + second[part, :].astype(F32)
        target[part, :] = total.astype(target.dtype)


def scatter_kernel(
    depth, chunk, g_ref, o_ref, own, from_c, from_two, from_one, from_z, load_sem, send_sem, recv_sem
):
    a, b, e, c = place()
    rows = o_ref.shape[0]
    one = first_partner(a, b, e, c)
    two = second_partner(a, b, e, c)
    both = second_partner(*one)
    homes = [(a, b, e, c), one, two, both]
    twin = device(a, b, e, 1 - c)
    order = z_order(depth)
    order = order[1:] + order[:1]
    sends = []

    def target_row(k, j, core):
        _, hb, he, _ = homes[j]
        return flat((a + k) % depth, hb, he, core)

    def remote(slot, src, dst, target):
        return pltpu.make_async_remote_copy(
            src_ref=src,
            dst_ref=dst,
            send_sem=send_sem.at[slot],
            recv_sem=recv_sem.at[slot],
            device_id=target,
            device_id_type=MESH,
        )

    def send(slot, src, dst, target):
        copy = remote(slot, src, dst, target)
        copy.start()
        sends.append(copy)

    loads = {}
    for k in order:
        for j in (3, 2, 1, 0):
            copy = pltpu.make_async_copy(
                g_ref.at[target_row(k, j, c)], own.at[k * 4 + j], load_sem.at[k * 4 + j]
            )
            copy.start()
            loads[k, j] = copy
    greet(depth, a, b, e, c)
    for k in order:
        for j in (3, 2, 1, 0):
            there = (0, 2, 1, 3)[j]
            send(k * 8 + j, g_ref.at[target_row(k, there, 1 - c)], from_c.at[k * 4 + j], twin)

    def stage_c(k):
        for j in (3, 2, 1, 0):
            loads[k, j].wait()
            remote(k * 8 + j, own.at[k * 4 + j], from_c.at[k * 4 + j], twin).wait_recv()
            add_into(own.at[k * 4 + j], own.at[k * 4 + j], from_c.at[k * 4 + j], rows, chunk)
            if j >= 2:
                send(k * 8 + 2 + j, own.at[k * 4 + j], from_two.at[k * 2 + j - 2], device(*two))

    def stage_two(k):
        for j in (3, 2):
            spot = from_two.at[k * 2 + j - 2]
            remote(k * 8 + 2 + j, own.at[k * 4 + j], spot, device(*two)).wait_recv()
            add_into(own.at[k * 4 + j - 2], own.at[k * 4 + j - 2], spot, rows, chunk)
            if j == 3:
                send(k * 8 + 6, own.at[k * 4 + 1], from_one.at[k], device(*one))

    def stage_one(k):
        spot = from_one.at[k]
        remote(k * 8 + 6, own.at[k * 4 + 1], spot, device(*one)).wait_recv()
        if k:
            add_into(own.at[k * 4], own.at[k * 4], spot, rows, chunk)
            send(k * 8 + 7, own.at[k * 4], from_z.at[k - 1], device((a + k) % depth, b, e, c))

    for n in range(depth + 2):
        if n < depth:
            stage_c(order[n])
        if 1 <= n < depth + 1:
            stage_two(order[n - 1])
        if n >= 2:
            stage_one(order[n - 2])
    for k in range(1, depth):
        remote(k * 8 + 7, own.at[k * 4], from_z.at[k - 1], twin).wait_recv()

    @pl.loop(0, rows // chunk)
    def _(step):
        part = pl.ds(step * chunk, chunk)
        total = own[0, part, :].astype(F32) + from_one[0, part, :].astype(F32)
        for k in range(1, depth):
            total = total + from_z[k - 1, part, :].astype(F32)
        o_ref[part, :] = total

    for copy in sends:
        copy.wait_send()


def scatter_fast(parts, depth, collective_id, chunk):
    _, rows, cols = parts.shape
    count = depth * 8

    def slots(n):
        return pltpu.VMEM((n, rows, cols), parts.dtype)

    return pl.pallas_call(
        functools.partial(scatter_kernel, depth, chunk),
        out_shape=jax.ShapeDtypeStruct((rows, cols), F32),
        in_specs=[any_spec()],
        out_specs=vmem_spec(),
        scratch_shapes=[
            slots(depth * 4),
            slots(depth * 4),
            slots(depth * 2),
            slots(depth),
            slots(depth - 1),
            pltpu.SemaphoreType.DMA((depth * 4,)),
            pltpu.SemaphoreType.DMA((count,)),
            pltpu.SemaphoreType.DMA((count,)),
        ],
        compiler_params=params(collective_id=collective_id, has_side_effects=True),
        name=f"scatter{collective_id}",
    )(parts)


def total_kernel(images, lats, x_ref, o_ref, slots, send_sem, recv_sem):
    img = lax.axis_index("img")
    lat = lax.axis_index("lat")
    count = images * lats
    me = img * lats + lat
    barrier = pltpu.get_barrier_semaphore()
    for k in range(1, count):
        there = (me + k) % count
        pl.semaphore_signal(
            barrier, inc=1, device_id=(there // lats, there % lats), device_id_type=MESH
        )
    pl.semaphore_wait(barrier, count - 1)
    slots[me] = x_ref[...]
    copies = []
    for k in range(1, count):
        there = (me + k) % count
        copy = pltpu.make_async_remote_copy(
            src_ref=x_ref,
            dst_ref=slots.at[me],
            send_sem=send_sem.at[k],
            recv_sem=recv_sem.at[k],
            device_id=(there // lats, there % lats),
            device_id_type=MESH,
        )
        copy.start()
        copies.append(copy)
    for k in range(1, count):
        pltpu.make_async_remote_copy(
            src_ref=x_ref,
            dst_ref=slots.at[(me - k) % count],
            send_sem=send_sem.at[k],
            recv_sem=recv_sem.at[k],
            device_id=(img, lat),
            device_id_type=MESH,
        ).wait_recv()
    o_ref[...] = jnp.sum(slots[...], axis=0)
    for copy in copies:
        copy.wait_send()


def total_fast(tile, images, lats, collective_id):
    count = images * lats
    return pl.pallas_call(
        functools.partial(total_kernel, images, lats),
        out_shape=jax.ShapeDtypeStruct(tile.shape, tile.dtype),
        in_specs=[vmem_spec()],
        out_specs=vmem_spec(),
        scratch_shapes=[
            pltpu.VMEM((count,) + tile.shape, tile.dtype),
            pltpu.SemaphoreType.DMA((count,)),
            pltpu.SemaphoreType.DMA((count,)),
        ],
        compiler_params=pltpu.CompilerParams(collective_id=collective_id, has_side_effects=True),
        name=f"total{collective_id}",
    )(tile)


def normalise(values):
    center = values - jnp.mean(values, axis=-1, keepdims=True)
    spread = jnp.mean(center * center, axis=-1, keepdims=True)
    scale = lax.rsqrt(spread + EPS)
    return center * scale, scale


def norm_back(grad, hat, scale, gain):
    inner = grad * gain
    first = jnp.mean(inner, axis=-1, keepdims=True)
    second = jnp.mean(inner * hat, axis=-1, keepdims=True)
    return scale * (inner - first - hat * second)


def media_kernel(m_ref, gb_ref, wk_ref, wv_ref, k_ref, v_ref):
    hat, _ = normalise(m_ref[...].astype(F32))
    normed = (hat * gb_ref[0:1, :] + gb_ref[3:4, :]).astype(BF16)
    k_ref[...] = mm(normed, wk_ref[...]).astype(BF16)
    v_ref[...] = mm(normed, wv_ref[...]).astype(BF16)


def media_project(media, gains, attend, inner):
    rows, width = media.shape
    out = jax.ShapeDtypeStruct((rows, inner), BF16)
    block = pl.BlockSpec((PATCH_IMG, inner), lambda i: (i, 0))
    return pl.pallas_call(
        media_kernel,
        grid=(rows // PATCH_IMG,),
        out_shape=(out, out),
        in_specs=[
            pl.BlockSpec((PATCH_IMG, width), lambda i: (i, 0)),
            pl.BlockSpec(gains.shape, lambda i: (0, 0)),
            pl.BlockSpec((width, inner), lambda i: (0, 1)),
            pl.BlockSpec((width, inner), lambda i: (0, 2)),
        ],
        out_specs=(block, block),
        compiler_params=params(),
        cost_estimate=pl.CostEstimate(
            flops=4 * rows * width * inner, bytes_accessed=4 * rows * width, transcendentals=0
        ),
        name="media_project",
    )(media, gains, attend, attend)


def latent_kernel(l_ref, gb_ref, w_ref, q_ref, k_ref, v_ref):
    inner = q_ref.shape[1]
    hat, _ = normalise(l_ref[...])
    normed = (hat * gb_ref[1:2, :] + gb_ref[4:5, :]).astype(BF16)
    q_ref[...] = mm(normed, w_ref[:, :inner]).astype(BF16)
    k_ref[...] = mm(normed, w_ref[:, inner : 2 * inner]).astype(BF16)
    v_ref[...] = mm(normed, w_ref[:, 2 * inner : 3 * inner]).astype(BF16)


def latent_project(latents, gains, attend, inner):
    out = jax.ShapeDtypeStruct((latents.shape[0], inner), BF16)
    return pl.pallas_call(
        latent_kernel,
        out_shape=(out, out, out),
        in_specs=[vmem_spec()] * 3,
        out_specs=(vmem_spec(),) * 3,
        compiler_params=params(),
        name="latent_project",
    )(latents, gains, attend)


def head_mask(kind):
    rows = lax.broadcasted_iota(jnp.int32, (GROUP * HDIM, GROUP * HDIM), 0) // HDIM
    cols = lax.broadcasted_iota(jnp.int32, (GROUP * HDIM, GROUP * HDIM), 1) // HDIM
    return (rows == cols).astype(F32).astype(kind)


def spread_heads(queries, group, mask):
    width = GROUP * HDIM
    part = queries[:, group * width : (group + 1) * width]
    return jnp.concatenate([part] * GROUP, axis=0) * mask


def take_heads(full, mask):
    total = None
    for h in range(GROUP):
        part = slice(h * HDIM, (h + 1) * HDIM)
        term = full[part, :] * mask[part, :]
        total = term if total is None else total + term
    return total


def pack_columns(columns, first=0):
    rows = columns[0].shape[0]
    lane = lax.broadcasted_iota(jnp.int32, (rows, LANES), 1)
    tile = jnp.zeros((rows, LANES), F32)
    for h, column in enumerate(columns):
        tile = jnp.where(lane == first + h, column, tile)
    return tile


def expand_columns(tile, width):
    rows = tile.shape[0]
    head = lax.broadcasted_iota(jnp.int32, (rows, width), 1) // HDIM
    out = jnp.zeros((rows, width), F32)
    for h in range(width // HDIM):
        out = jnp.where(head == h, tile[:, h : h + 1], out)
    return out


def forward_kernel(
    ids, q0, q1, q2, q3, k_ref, v_ref, kl_ref, vl_ref, keep, send, keep_st, send_st, acc, tops, sums
):
    step = pl.program_id(0)
    clips = acc.shape[0]
    inner = acc.shape[2]
    groups = inner // (GROUP * HDIM)
    width = GROUP * HDIM
    mask = head_mask(F32)
    mask_half = mask.astype(BF16)

    def clip_queries(clip):
        parts = [q[clip] for q in (q0, q1, q2, q3)]
        return jnp.concatenate(parts, axis=0) * BF16(SCALE)

    def attend(clip, keys, values, fresh):
        queries = clip_queries(clip)
        new_tops, new_sums = [], []
        for g in range(groups):
            cols = slice(g * width, (g + 1) * width)
            scores = mm_nt(spread_heads(queries, g, mask_half), keys[:, cols])
            top = jnp.max(scores, axis=-1, keepdims=True)
            if not fresh:
                old_tile = tops[clip]
                old_top = jnp.concatenate(
                    [old_tile[:, g * GROUP + h : g * GROUP + h + 1] for h in range(GROUP)], axis=0
                )
                top = jnp.maximum(top, old_top)
            probs = jnp.exp(scores - top)
            total = jnp.sum(probs, axis=-1, keepdims=True)
            part = take_heads(mm(probs.astype(BF16), values[:, cols]), mask)
            if not fresh:
                old_tile = sums[clip]
                old_sum = jnp.concatenate(
                    [old_tile[:, g * GROUP + h : g * GROUP + h + 1] for h in range(GROUP)], axis=0
                )
                shrink = jnp.exp(old_top - top)
                total = total + old_sum * shrink
                part = part + acc[clip, :, cols] * take_heads(shrink, mask)
            acc[clip, :, cols] = part
            for h in range(GROUP):
                new_tops.append(top[h * HDIM : (h + 1) * HDIM])
                new_sums.append(total[h * HDIM : (h + 1) * HDIM])
        tops[clip] = pack_columns(new_tops)
        sums[clip] = pack_columns(new_sums)

    @pl.when(step == 0)
    def _():
        @pl.loop(0, clips)
        def _(clip):
            attend(clip, kl_ref[clip], vl_ref[clip], True)

    attend(ids[step], k_ref[...], v_ref[...], False)

    @pl.when(step == pl.num_programs(0) - 1)
    def _():
        rows = keep.shape[2]
        lane = lax.broadcasted_iota(jnp.int32, (HDIM, LANES), 1)

        @pl.loop(0, clips)
        def _(clip):
            total = jnp.where(lane < HEADS, sums[clip], 1.0)
            stat = tops[clip] + jnp.log(total)
            out = (acc[clip] / expand_columns(total, inner)).astype(BF16)
            for r in range(4):
                part = slice(r * rows, (r + 1) * rows)
                where_o, where_s = (send, send_st) if r % 2 else (keep, keep_st)
                where_o[r // 2, clip] = out[part]
                where_s[r // 2, clip] = stat[part]


def attention_forward(ids, queries, keys, values, latent_keys, latent_values):
    clips, rows, inner = queries[0].shape
    frames = keys.shape[0] // PATCH_IMG
    out = jax.ShapeDtypeStruct((2, clips, rows, inner), BF16)
    stat = jax.ShapeDtypeStruct((2, clips, rows, LANES), F32)
    block = pl.BlockSpec((PATCH_IMG, inner), lambda i, ids: (i, 0))

    def whole(shape):
        return pl.BlockSpec(shape, lambda i, ids: (0,) * len(shape))

    return pl.pallas_call(
        forward_kernel,
        grid_spec=pltpu.PrefetchScalarGridSpec(
            num_scalar_prefetch=1,
            grid=(frames,),
            in_specs=[whole((clips, rows, inner))] * 4
            + [block, block]
            + [whole((clips, rows, inner))] * 2,
            out_specs=(whole(out.shape), whole(out.shape), whole(stat.shape), whole(stat.shape)),
            scratch_shapes=[
                pltpu.VMEM((clips, 4 * rows, inner), F32),
                pltpu.VMEM((clips, 4 * rows, LANES), F32),
                pltpu.VMEM((clips, 4 * rows, LANES), F32),
            ],
        ),
        out_shape=(out, out, stat, stat),
        compiler_params=params(),
        name="attention_forward",
    )(ids, *queries, keys, values, latent_keys, latent_values)


def join_partials(first, first_stat, second, second_stat):
    width = first.shape[-1]
    top = jnp.maximum(first_stat, second_stat)
    total = jnp.exp(first_stat - top) + jnp.exp(second_stat - top)
    stat = top + jnp.log(total)
    out = first.astype(F32) * expand_columns(jnp.exp(first_stat - stat), width)
    out = out + second.astype(F32) * expand_columns(jnp.exp(second_stat - stat), width)
    return out, stat


def join_kernel(keep, keep_st, got, got_st, own, own_st, away, away_st):
    out, stat = join_partials(keep[0], keep_st[0], got[0], got_st[0])
    own[...] = out
    own_st[...] = stat
    out, stat = join_partials(keep[1], keep_st[1], got[1], got_st[1])
    away[...] = out.astype(BF16)
    away_st[...] = stat


def join_cores(keep, keep_st, got, got_st):
    _, rows, inner = keep.shape
    stat = jax.ShapeDtypeStruct((rows, LANES), F32)
    return pl.pallas_call(
        join_kernel,
        out_shape=(
            jax.ShapeDtypeStruct((rows, inner), F32),
            stat,
            jax.ShapeDtypeStruct((rows, inner), BF16),
            stat,
        ),
        in_specs=[vmem_spec()] * 4,
        out_specs=(vmem_spec(),) * 4,
        compiler_params=params(),
        name="join_cores",
    )(keep, keep_st, got, got_st)


def feed_kernel(
    own,
    own_st,
    got,
    got_st,
    lat_ref,
    cot_ref,
    gb_ref,
    w_ref,
    out_ref,
    mixed_grad,
    context_grad,
    tile_ref,
    gain_ref,
    gw_ref,
    expand_v,
    shrink_v,
    output_v,
    grad_e,
    grad_s,
    grad_o,
    normed_v,
    normed_t,
    hat_v,
    acc_g,
    load_sem,
    store_sem,
):
    groups = expand_v.shape[0]
    width = expand_v.shape[3]
    blocks = expand_v.shape[1]
    shrink_rows = shrink_v.shape[1]
    per_group = blocks // groups
    expand_rows = expand_v.shape[2]
    shrink_at = groups * expand_rows
    output_at = shrink_at + shrink_rows
    output_rows = output_v.shape[1]
    half = width // 2
    inner = own.shape[1]

    def load_expand(g):
        return pltpu.make_async_copy(
            w_ref.at[:, pl.ds(g * expand_rows, expand_rows), :], expand_v.at[g], load_sem.at[g]
        )

    def load_shrink(g):
        part = pl.ds(g * per_group, per_group)
        return pltpu.make_async_copy(
            w_ref.at[part, pl.ds(shrink_at, shrink_rows), :],
            shrink_v.at[part],
            load_sem.at[groups + g],
        )

    load_output = pltpu.make_async_copy(
        w_ref.at[:, pl.ds(output_at, output_rows), :], output_v, load_sem.at[2 * groups]
    )
    load_output.start()
    for g in range(groups):
        load_expand(g).start()
        load_shrink(g).start()

    context, stat = join_partials(own[...], own_st[...], got[...], got_st[...])
    context_half = context.astype(BF16)
    load_output.wait()
    weight_o = output_v[...].reshape(inner, width)
    mixed = lat_ref[...] + mm(context_half, weight_o)
    hat, scale = normalise(mixed)
    hat_v[...] = hat
    normed = (hat * gb_ref[2:3, :] + gb_ref[5:6, :]).astype(BF16)
    normed_v[...] = normed
    normed_t[...] = normed.astype(F32).T.astype(BF16)
    out_ref[...] = mixed
    acc_g[...] = jnp.zeros_like(acc_g)

    def store_e(s, slot):
        return pltpu.make_async_copy(
            grad_e.at[slot],
            gw_ref.at[:, pl.ds((s // 2) * expand_rows, expand_rows), pl.ds((s % 2) * half, half)],
            store_sem.at[slot],
        )

    def store_s(s, slot):
        rows = half // shrink_rows
        return pltpu.make_async_copy(
            grad_s.at[slot],
            gw_ref.at[pl.ds(s * rows, rows), pl.ds(shrink_at, shrink_rows), :],
            store_sem.at[2 + slot],
        )

    cot = cot_ref[...]
    steps = 2 * groups
    for s in range(steps):
        g, slot = s // 2, s % 2
        if slot == 0:
            load_expand(g).wait()
            load_shrink(g).wait()
        cols = slice(slot * half, (slot + 1) * half)
        w_e = expand_v[g, :, :, cols].reshape(blocks * expand_rows, half)
        first = s * half // shrink_rows
        w_s = shrink_v[first : first + half // shrink_rows].reshape(half, width)
        pre = mm(normed_v[...], w_e)
        cdf = 0.5 * (1.0 + lax.erf(pre * (0.5**0.5)))
        hidden = (pre * cdf).astype(BF16)
        out_ref[...] += mm(hidden, w_s)
        grad_hidden = mm_nt(cot, w_s)
        pdf = jnp.exp(-0.5 * pre * pre) * (1.0 / math.sqrt(2.0 * math.pi))
        grad_pre = (grad_hidden * (cdf + pre * pdf)).astype(BF16)
        if s >= 2:
            store_e(s - 2, slot).wait()
            store_s(s - 2, slot).wait()
        grad_s[slot] = mm_tn(hidden, cot).astype(BF16).reshape(half // shrink_rows, shrink_rows, width)
        grad_e[slot] = (
            mm(normed_t[...], grad_pre).astype(BF16).reshape(blocks, expand_rows, half)
        )
        store_e(s, slot).start()
        store_s(s, slot).start()
        acc_g[...] += mm_nt(grad_pre, w_e)

    grad_normed = acc_g[...]
    hat = hat_v[...]
    rows = gain_ref.shape[0]
    gain_ref[...] = jnp.concatenate(
        [
            jnp.sum(grad_normed * hat, axis=0, keepdims=True),
            jnp.sum(grad_normed, axis=0, keepdims=True),
            jnp.zeros((rows - 2, width), F32),
        ],
        axis=0,
    )
    total = cot.astype(F32) + norm_back(grad_normed, hat, scale, gb_ref[2:3, :])
    mixed_grad[...] = total
    attended = total.astype(BF16)
    grad_o[...] = mm_tn(context_half, attended).astype(BF16).reshape(grad_o.shape)
    store_o = pltpu.make_async_copy(
        grad_o, gw_ref.at[:, pl.ds(output_at, output_rows), :], store_sem.at[4]
    )
    store_o.start()
    grad_c = mm_nt(attended, weight_o).astype(BF16)
    context_grad[...] = grad_c
    product = grad_c.astype(F32) * context
    head = lax.broadcasted_iota(jnp.int32, product.shape, 1) // HDIM
    deltas = [
        jnp.sum(jnp.where(head == h, product, 0.0), axis=-1, keepdims=True) for h in range(HEADS)
    ]
    lane = lax.broadcasted_iota(jnp.int32, stat.shape, 1)
    tile_ref[...] = jnp.where(lane < HEADS, stat, pack_columns(deltas, HEADS))
    for s in range(steps - 2, steps):
        store_e(s, s % 2).wait()
        store_s(s, s % 2).wait()
    store_o.wait()


def feed_forward(own, own_st, got, got_st, latents, cotangent, gains, weights):
    rows, width = latents.shape
    inner = own.shape[1]
    blocks = weights.shape[0]
    ff = 4 * width
    groups = ff // width
    expand_rows = width // blocks
    shrink_rows = ff // blocks
    output_rows = inner // blocks
    half = width // 2
    flops = 2 * rows * (6 * width * ff + 3 * width * inner)
    return pl.pallas_call(
        feed_kernel,
        out_shape=(
            jax.ShapeDtypeStruct((rows, width), F32),
            jax.ShapeDtypeStruct((rows, width), F32),
            jax.ShapeDtypeStruct((rows, inner), BF16),
            jax.ShapeDtypeStruct((rows, LANES), F32),
            jax.ShapeDtypeStruct((8, width), F32),
            jax.ShapeDtypeStruct(weights.shape, BF16),
        ),
        in_specs=[vmem_spec()] * 7 + [any_spec()],
        out_specs=(vmem_spec(),) * 5 + (any_spec(),),
        scratch_shapes=[
            pltpu.VMEM((groups, blocks, expand_rows, width), BF16),
            pltpu.VMEM((blocks, shrink_rows, width), BF16),
            pltpu.VMEM((blocks, output_rows, width), BF16),
            pltpu.VMEM((2, blocks, expand_rows, half), BF16),
            pltpu.VMEM((2, half // shrink_rows, shrink_rows, width), BF16),
            pltpu.VMEM((blocks, output_rows, width), BF16),
            pltpu.VMEM((rows, width), BF16),
            pltpu.VMEM((width, rows), BF16),
            pltpu.VMEM((rows, width), F32),
            pltpu.VMEM((rows, width), F32),
            pltpu.SemaphoreType.DMA((2 * groups + 1,)),
            pltpu.SemaphoreType.DMA((5,)),
        ],
        compiler_params=params(),
        cost_estimate=pl.CostEstimate(
            flops=flops, bytes_accessed=4 * weights.size, transcendentals=2 * rows * ff
        ),
        name="feed_forward",
    )(own, own_st, got, got_st, latents, cotangent, gains, weights)


def backward_kernel(
    ids,
    q0,
    q1,
    q2,
    q3,
    g0,
    g1,
    g2,
    g3,
    t0,
    t1,
    t2,
    t3,
    k_ref,
    v_ref,
    kl_ref,
    vl_ref,
    m_ref,
    gb_ref,
    wk_ref,
    wv_ref,
    media_grad,
    latent_kv,
    keep,
    send,
    weight_grad,
    gain_ref,
    acc,
):
    step = pl.program_id(0)
    clips = acc.shape[0]
    inner = acc.shape[2]
    groups = inner // (GROUP * HDIM)
    width = GROUP * HDIM
    mask = head_mask(F32)
    mask_half = mask.astype(BF16)

    def attend(clip, keys, values, fresh):
        queries = jnp.concatenate([q[clip] for q in (q0, q1, q2, q3)], axis=0) * BF16(SCALE)
        grads = jnp.concatenate([g[clip] for g in (g0, g1, g2, g3)], axis=0)
        stats = jnp.concatenate([t[clip] for t in (t0, t1, t2, t3)], axis=0).T
        key_parts, value_parts = [], []
        for g in range(groups):
            cols = slice(g * width, (g + 1) * width)

            def line(first):
                at = first + g * GROUP
                return jnp.concatenate([stats[at + h : at + h + 1, :] for h in range(GROUP)], axis=1)

            wide_q = spread_heads(queries, g, mask_half)
            wide_g = spread_heads(grads, g, mask_half)
            probs = jnp.exp(mm_nt(keys[:, cols], wide_q) - line(0))
            grad_probs = mm_nt(values[:, cols], wide_g)
            grad_scores = (probs * (grad_probs - line(HEADS))).astype(BF16)
            key_parts.append(mm(grad_scores, wide_q))
            value_parts.append(mm(probs.astype(BF16), wide_g))
            part = take_heads(mm_tn(grad_scores, keys[:, cols]), mask)
            if fresh:
                acc[clip, :, cols] = part
            else:
                acc[clip, :, cols] += part
        return jnp.concatenate(key_parts + value_parts, axis=1).astype(BF16)

    @pl.when(step == 0)
    def _():
        gain_ref[...] = jnp.zeros_like(gain_ref)
        weight_grad[...] = jnp.zeros_like(weight_grad)

        @pl.loop(0, clips)
        def _(clip):
            latent_kv[clip] = attend(clip, kl_ref[clip], vl_ref[clip], True)

    grad_kv = attend(ids[step], k_ref[...], v_ref[...], False)
    hat, scale = normalise(m_ref[...].astype(F32))
    gain = gb_ref[0:1, :]
    normed = (hat * gain + gb_ref[3:4, :]).astype(BF16)
    weight_grad[...] += mm_tn(normed, grad_kv)
    grad = mm_nt(grad_kv[:, :inner], wk_ref[...]) + mm_nt(grad_kv[:, inner:], wv_ref[...])
    gain_ref[0:1, :] += jnp.sum(grad * hat, axis=0, keepdims=True)
    gain_ref[1:2, :] += jnp.sum(grad, axis=0, keepdims=True)
    media_grad[...] = norm_back(grad, hat, scale, gain).astype(BF16)

    @pl.when(step == pl.num_programs(0) - 1)
    def _():
        rows = keep.shape[2]

        @pl.loop(0, clips)
        def _(clip):
            out = (acc[clip] * SCALE).astype(BF16)
            for r in range(4):
                part = slice(r * rows, (r + 1) * rows)
                where_o = send if r % 2 else keep
                where_o[r // 2, clip] = out[part]


def attention_backward(
    ids, queries, grads, tiles, keys, values, latent_keys, latent_values, media, gains, attend
):
    clips, rows, inner = queries[0].shape
    width = media.shape[1]
    frames = keys.shape[0] // PATCH_IMG
    block = pl.BlockSpec((PATCH_IMG, inner), lambda i, ids: (i, 0))
    wide = pl.BlockSpec((PATCH_IMG, width), lambda i, ids: (i, 0))

    def whole(shape):
        return pl.BlockSpec(shape, lambda i, ids: (0,) * len(shape))

    def column(n):
        return pl.BlockSpec((width, inner), lambda i, ids: (0, n))

    query = whole((clips, rows, inner))
    pair = (2, clips, rows, inner)
    return pl.pallas_call(
        backward_kernel,
        grid_spec=pltpu.PrefetchScalarGridSpec(
            num_scalar_prefetch=1,
            grid=(frames,),
            in_specs=[query] * 8
            + [whole((clips, rows, LANES))] * 4
            + [block, block, query, query, wide, whole(gains.shape), column(1), column(2)],
            out_specs=(
                wide,
                whole((clips, rows, 2 * inner)),
                whole(pair),
                whole(pair),
                whole((width, 2 * inner)),
                whole((8, width)),
            ),
            scratch_shapes=[pltpu.VMEM((clips, 4 * rows, inner), F32)],
        ),
        out_shape=(
            jax.ShapeDtypeStruct(media.shape, BF16),
            jax.ShapeDtypeStruct((clips, rows, 2 * inner), BF16),
            jax.ShapeDtypeStruct(pair, BF16),
            jax.ShapeDtypeStruct(pair, BF16),
            jax.ShapeDtypeStruct((width, 2 * inner), F32),
            jax.ShapeDtypeStruct((8, width), F32),
        ),
        compiler_params=params(),
        name="attention_backward",
    )(
        ids,
        *queries,
        *grads,
        *tiles,
        keys,
        values,
        latent_keys,
        latent_values,
        media,
        gains,
        attend,
        attend,
    )


def last_kernel(
    lat_ref, mixed_grad, first, second, kv_ref, gb_ref, w_ref, gw_ref, gm_ref, gf_ref, out_ref, pack_ref
):
    inner = first.shape[1]
    width = lat_ref.shape[1]
    hat, scale = normalise(lat_ref[...])
    gain = gb_ref[1:2, :]
    normed = (hat * gain + gb_ref[4:5, :]).astype(BF16)
    grad_q = (first[...].astype(F32) + second[...].astype(F32)).astype(BF16)
    grad_kv = kv_ref[...]
    grad = mm_nt(grad_q, w_ref[:, :inner]) + mm_nt(grad_kv, w_ref[:, inner : 3 * inner])
    pack_ref[:, :inner] = mm_tn(normed, grad_q).astype(BF16)
    pack_ref[:, inner : 3 * inner] = (gw_ref[...] + mm_tn(normed, grad_kv)).astype(BF16)
    lines = jnp.concatenate(
        [
            gm_ref[0:1, :],
            jnp.sum(grad * hat, axis=0, keepdims=True),
            gf_ref[0:1, :],
            gm_ref[1:2, :],
            jnp.sum(grad, axis=0, keepdims=True),
            gf_ref[1:2, :],
            jnp.zeros((LANES - 6, width), F32),
        ],
        axis=0,
    )
    pack_ref[:, 3 * inner :] = lines.T.astype(BF16)
    out_ref[...] = mixed_grad[...] + norm_back(grad, hat, scale, gain)


def latent_backward(latents, mixed_grad, first, second, grad_kv, gains, attend, grad_w, gain_m, gain_f):
    return pl.pallas_call(
        last_kernel,
        out_shape=(
            jax.ShapeDtypeStruct(latents.shape, F32),
            jax.ShapeDtypeStruct(attend.shape, BF16),
        ),
        in_specs=[vmem_spec()] * 10,
        out_specs=(vmem_spec(), vmem_spec()),
        compiler_params=params(),
        name="latent_backward",
    )(latents, mixed_grad, first, second, grad_kv, gains, attend, grad_w, gain_m, gain_f)


def pack_feed(expand, shrink, output):
    width = shrink.shape[-1]
    groups = expand.shape[-1] // width
    lead = expand.shape[:-2]
    rows = expand.shape[-2]
    cut = expand.reshape(lead + (rows, groups, width))
    cut = jnp.moveaxis(cut, -2, -3).reshape(lead + (groups * rows, width))
    return jnp.concatenate([cut, shrink, output], axis=-2)


def unpack_feed(packed, rows, shrink_rows):
    width = packed.shape[-1]
    lead = packed.shape[:-2]
    groups = (packed.shape[-2] - shrink_rows) // rows
    split = groups * rows
    cut = packed[..., :split, :].reshape(lead + (groups, rows, width))
    expand = jnp.moveaxis(cut, -3, -2).reshape(lead + (rows, groups * width))
    return (
        expand,
        packed[..., split : split + shrink_rows, :],
        packed[..., split + shrink_rows :, :],
    )


def step_size(width, inner, ff):
    return 0.37 * math.sqrt((4 * width * inner + 2 * width * ff) / width)


def lat_pairs(count, along_core):
    pairs = []
    for lat in range(count):
        e, c = lat // 2, lat % 2
        pairs.append((lat, e * 2 + 1 - c if along_core else (1 - e) * 2 + c))
    return pairs


def shards(
    images,
    lats,
    media,
    latents,
    counts,
    cotangent,
    attend_weight,
    output_weight,
    expand_weight,
    shrink_weight,
    layer_gains,
    layer_biases,
    attend_momentum,
    output_momentum,
    expand_momentum,
    shrink_momentum,
    gains_momentum,
    biases_momentum,
    attend_average,
    output_average,
    expand_average,
    shrink_average,
    gains_average,
    biases_average,
):
    devices = images * lats
    depth = images // 2
    fast = devices == BLOCKS and lats == 4 and images % 2 == 0
    samples, lat_dev, width = latents.shape
    rows = samples * lat_dev
    ff = expand_weight.shape[1]
    inner = attend_weight.shape[1] // 3
    patch_dev = media.shape[0]
    frames = patch_dev // PATCH_IMG
    over_core = functools.partial(lax.ppermute, axis_name="lat", perm=lat_pairs(lats, True))
    over_y = functools.partial(lax.ppermute, axis_name="lat", perm=lat_pairs(lats, False))

    attend_rows = attend_weight.shape[0]
    small = jnp.concatenate([layer_gains, layer_biases], axis=1)
    small = jnp.pad(small, ((0, 0), (0, LANES - small.shape[1])))
    attend_shard = jnp.concatenate([attend_weight, small], axis=1).astype(BF16)
    if fast:
        feed_shard = pack_feed(
            expand_weight.astype(BF16), shrink_weight.astype(BF16), output_weight.astype(BF16)
        )
        attend = gather_fast(attend_shard, depth, 1).reshape(width, attend_shard.shape[1])
        attend, feed_shard = lax.optimization_barrier((attend, feed_shard))
        feed = gather_fast(feed_shard, depth, 2)
    else:

        def everywhere(x):
            return lax.all_gather(x.astype(BF16), AXES, axis=0, tiled=True)

        attend = everywhere(attend_shard)
        feed = pack_feed(
            everywhere(expand_weight).reshape(BLOCKS, width // BLOCKS, ff),
            everywhere(shrink_weight).reshape(BLOCKS, ff // BLOCKS, width),
            everywhere(output_weight).reshape(BLOCKS, inner // BLOCKS, width),
        )
    gains = attend[:, 3 * inner : 3 * inner + 8].astype(F32).T

    sample_ends = jnp.cumsum(counts[0])
    first_frame = lax.axis_index("lat") * frames
    frame_ids = first_frame + jnp.arange(frames, dtype=jnp.int32)
    ids = jnp.sum((frame_ids[:, None] >= sample_ends[None, :]).astype(jnp.int32), axis=1)
    ids = jnp.clip(ids, 0, samples - 1)

    latent_flat = latents.reshape(rows, width)
    query, latent_key, latent_value = latent_project(latent_flat, gains, attend, inner)
    cut = (samples, lat_dev, inner)
    latent_key = latent_key.reshape(cut)
    latent_value = latent_value.reshape(cut)

    def to_group(own):
        other = over_y(own)
        return [own, over_core(own), other, over_core(other)]

    queries = to_group(query.reshape(cut))
    keys, values = media_project(media, gains, attend, inner)
    keep, send, keep_st, send_st = attention_forward(
        ids, queries, keys, values, latent_key, latent_value
    )
    got, got_st = over_core(send), over_core(send_st)
    flat_o, flat_s = (2, rows, inner), (2, rows, LANES)
    own, own_st, away, away_st = join_cores(
        keep.reshape(flat_o), keep_st.reshape(flat_s), got.reshape(flat_o), got_st.reshape(flat_s)
    )
    got, got_st = over_y(away), over_y(away_st)
    cot_flat = cotangent.reshape(rows, width)
    out_rows, mixed_grad, context_grad, tile, gain_f, grad_feed = feed_forward(
        own, own_st, got, got_st, latent_flat, cot_flat, gains, feed
    )
    grads = to_group(context_grad.reshape(cut))
    tiles = to_group(tile.reshape(samples, lat_dev, LANES))
    grad_media, latent_kv, keep, send, grad_kv, gain_m = attention_backward(
        ids,
        queries,
        grads,
        tiles,
        keys,
        values,
        latent_key,
        latent_value,
        media,
        gains,
        attend,
    )
    got = over_core(send)
    pair = keep.astype(F32) + got.astype(F32)
    got = over_y(pair[1].astype(BF16))
    latents_grad, grad_attend = latent_backward(
        latent_flat,
        mixed_grad,
        pair[0].reshape(rows, inner),
        got.reshape(rows, inner),
        latent_kv.reshape(rows, 2 * inner),
        gains,
        attend,
        grad_kv,
        gain_m,
        gain_f,
    )
    if fast:
        mine = scatter_fast(
            grad_attend.reshape(BLOCKS, attend_rows, grad_attend.shape[1]), depth, 3, 16
        )
        mine_feed = scatter_fast(grad_feed, depth, 4, 16)
        own_expand, own_shrink, own_output = unpack_feed(
            mine_feed, attend_rows, shrink_weight.shape[0]
        )
    else:

        def owners(x):
            return lax.psum_scatter(x.astype(F32), AXES, scatter_dimension=0, tiled=True)

        mine = owners(grad_attend)
        own_expand, own_shrink, own_output = unpack_feed(grad_feed, width // BLOCKS, ff // BLOCKS)
        own_expand = owners(own_expand.reshape(width, ff))
        own_shrink = owners(own_shrink.reshape(ff, width))
        own_output = owners(own_output.reshape(inner, width))
    small = mine[:, 3 * inner :]
    owned = (
        mine[:, : 3 * inner],
        own_output,
        own_expand,
        own_shrink,
        small[:, 0:3],
        small[:, 3:6],
    )
    squares = sum(jnp.sum(piece * piece) for piece in owned)
    if fast:
        squares = total_fast(jnp.full((8, LANES), squares, F32), images, lats, 5)[0, 0]
    else:
        squares = lax.psum(squares, AXES)
    grad_norm = jnp.sqrt(squares)
    factor = jnp.minimum(1.0, CLIP_NORM / (grad_norm + 1e-06))
    masters = (
        attend_weight,
        output_weight,
        expand_weight,
        shrink_weight,
        layer_gains,
        layer_biases,
    )
    moments = (
        attend_momentum,
        output_momentum,
        expand_momentum,
        shrink_momentum,
        gains_momentum,
        biases_momentum,
    )
    averages = (
        attend_average,
        output_average,
        expand_average,
        shrink_average,
        gains_average,
        biases_average,
    )
    decay_rates = (DECAY, DECAY, DECAY, DECAY, 0.0, 0.0)
    step_rate = step_size(width, inner, ff)
    new_masters = []
    new_buffers = []
    new_smoothed = []
    for master, moment, average, reduced, decay_rate, rate_scale in zip(
        masters, moments, averages, owned, decay_rates, RATE_SCALES
    ):
        step_grad = factor * reduced + decay_rate * master
        buffer = MOMENTUM * moment + step_grad
        master_new = master - step_rate * rate_scale * (step_grad + MOMENTUM * buffer)
        new_masters.append(master_new)
        new_buffers.append(buffer)
        new_smoothed.append(AVERAGING * average + (1.0 - AVERAGING) * master_new)
    return (
        out_rows.reshape(latents.shape),
        grad_media,
        latents_grad.reshape(latents.shape),
        grad_norm,
        *new_masters,
        *new_buffers,
        *new_smoothed,
    )


def solution(mesh):
    rows = P(AXES, None)
    split = P("img", "lat", None)
    return jax.shard_map(
        functools.partial(shards, mesh.shape["img"], mesh.shape["lat"]),
        mesh=mesh,
        in_specs=(rows, split, P("img", None), split) + (rows,) * 18,
        out_specs=(split, rows, split, P()) + (rows,) * 18,
        check_vma=False,
    )
```

```python
import functools
import math

import jax
import jax.numpy as jnp
from jax import lax
from jax.experimental import pallas as pl
from jax.experimental.pallas import tpu as pltpu
from jax.sharding import PartitionSpec as P

HEADS = 8
HDIM = 64
PATCH_IMG = 256
GROUP = 4
EPS = 1e-05
MOMENTUM = 0.9
DECAY = 0.0001
AVERAGING = 0.6
CLIP_NORM = 1.0
RATE_SCALES = (1.0, 100.0, 1.0, 1.0, 15.0, 1.0)
AXES = ("img", "lat")
LANES = 128
BLOCKS = 32
SCALE = HDIM ** (-0.5)
MASKED = -1e30
F32 = jnp.float32
BF16 = jnp.bfloat16
MESH = pl.DeviceIdType.MESH
FRONT_PLAN = (
    (6, "a1 z2 b0"),
    (14, "z3"),
    (16, "c0 b1 a2"),
    (22, "c1 b2 a3"),
    (24, "c2 b3 c3"),
)
BACK_PLAN = (
    (0, "a0"),
    (1, "a1"),
    (2, "a2"),
    (3, "a3"),
    (5, "b0"),
    (7, "c0 b1"),
    (10, "c1 b2"),
    (12, "c2"),
    (13, "b3 c3"),
)
VMEM_LIMIT = 60 * 1024 * 1024


def mm(a, b):
    return jnp.dot(a, b, preferred_element_type=F32)


def mm_tn(a, b):
    return lax.dot_general(a, b, (((0,), (0,)), ((), ())), preferred_element_type=F32)


def mm_nt(a, b):
    return lax.dot_general(a, b, (((1,), (1,)), ((), ())), preferred_element_type=F32)


def any_spec():
    return pl.BlockSpec(memory_space=pl.ANY)


def vmem_spec():
    return pl.BlockSpec(memory_space=pltpu.VMEM)


def params(**more):
    return pltpu.CompilerParams(vmem_limit_bytes=VMEM_LIMIT, **more)


def place():
    img = lax.axis_index("img")
    lat = lax.axis_index("lat")
    return img // 2, img % 2, lat // 2, lat % 2


def flat(a, b, e, c):
    return ((a * 2 + b) * 2 + e) * 2 + c


def device(a, b, e, c):
    return (a * 2 + b, e * 2 + c)


def first_partner(a, b, e, c):
    return a, (b + 1 - c) % 2, (e + c) % 2, c


def second_partner(a, b, e, c):
    return a, (b + c) % 2, (e + 1 - c) % 2, c


def z_order(depth):
    order = [0]
    for k in range(1, depth // 2 + 1):
        order.append(k)
        if depth - k != k:
            order.append(depth - k)
    return order


def greet(depth, a, b, e, c):
    barrier = pltpu.get_barrier_semaphore()
    friends = [device((a + k) % depth, b, e, c) for k in range(1, depth)]
    friends += [
        device(*first_partner(a, b, e, c)),
        device(*second_partner(a, b, e, c)),
        device(a, b, e, 1 - c),
    ]
    for friend in friends:
        pl.semaphore_signal(barrier, inc=1, device_id=friend, device_id_type=MESH)
    pl.semaphore_wait(barrier, len(friends))


def gather_kernel(depth, x_ref, o_ref, local_sem, send_sem, recv_sem):
    a, b, e, c = place()
    me = flat(a, b, e, c)
    greet(depth, a, b, e, c)
    own = pltpu.make_async_copy(x_ref, o_ref.at[me], local_sem)
    own.start()
    one = first_partner(a, b, e, c)
    two = second_partner(a, b, e, c)
    both = second_partner(*one)
    homes = [(a, b, e, c), one, two, both]
    twin = device(a, b, e, 1 - c)
    sends = []

    def source(k, j):
        _, hb, he, hc = homes[j % 4]
        return flat((a - k) % depth, hb, he, hc if j < 4 else 1 - c)

    def send(k, j, src, row, target):
        slot = k * 8 + j
        copy = pltpu.make_async_remote_copy(
            src_ref=src,
            dst_ref=o_ref.at[row],
            send_sem=send_sem.at[slot],
            recv_sem=recv_sem.at[slot],
            device_id=target,
            device_id_type=MESH,
        )
        copy.start()
        sends.append(copy)

    def arrive(k, j):
        slot = k * 8 + j
        pltpu.make_async_remote_copy(
            src_ref=x_ref,
            dst_ref=o_ref.at[source(k, j)],
            send_sem=send_sem.at[slot],
            recv_sem=recv_sem.at[slot],
            device_id=twin,
            device_id_type=MESH,
        ).wait_recv()

    def block(k, j):
        return x_ref if (k, j) == (0, 0) else o_ref.at[source(k, j)]

    def stage_one(k):
        if k:
            arrive(k, 0)
        row = source(k, 0)
        send(k, 1, block(k, 0), row, device(*one))
        send(k, 2, block(k, 0), row, device(*two))
        send(k, 4, block(k, 0), row, twin)

    def stage_two(k):
        arrive(k, 1)
        send(k, 3, block(k, 1), source(k, 1), device(*two))
        send(k, 5, block(k, 1), source(k, 1), twin)
        arrive(k, 2)
        send(k, 6, block(k, 2), source(k, 2), twin)

    def stage_three(k):
        arrive(k, 3)
        send(k, 7, block(k, 3), source(k, 3), twin)

    order = z_order(depth)
    for k in order[1:]:
        send(k, 0, x_ref, me, device((a + k) % depth, b, e, c))
    for n in range(depth + 2):
        if n < depth:
            stage_one(order[n])
        if 1 <= n < depth + 1:
            stage_two(order[n - 1])
        if n >= 2:
            stage_three(order[n - 2])
    for k in range(depth):
        for j in range(4, 8):
            arrive(k, j)
    for copy in sends:
        copy.wait_send()
    own.wait()


def gather_fast(shard, depth, collective_id):
    count = depth * 8
    return pl.pallas_call(
        functools.partial(gather_kernel, depth),
        out_shape=jax.ShapeDtypeStruct((count,) + shard.shape, shard.dtype),
        in_specs=[any_spec()],
        out_specs=any_spec(),
        scratch_shapes=[
            pltpu.SemaphoreType.DMA,
            pltpu.SemaphoreType.DMA((count,)),
            pltpu.SemaphoreType.DMA((count,)),
        ],
        compiler_params=pltpu.CompilerParams(collective_id=collective_id, has_side_effects=True),
        name=f"gather{collective_id}",
    )(shard)


def add_into(target, first, second, rows, chunk):
    @pl.loop(0, rows // chunk)
    def _(step):
        part = pl.ds(step * chunk, chunk)
        total = first[part, :].astype(F32) + second[part, :].astype(F32)
        target[part, :] = total.astype(target.dtype)


def scatter_kernel(
    depth, chunk, g_ref, o_ref, own, from_c, from_two, from_one, from_z, load_sem, send_sem, recv_sem
):
    a, b, e, c = place()
    rows = o_ref.shape[0]
    one = first_partner(a, b, e, c)
    two = second_partner(a, b, e, c)
    both = second_partner(*one)
    homes = [(a, b, e, c), one, two, both]
    twin = device(a, b, e, 1 - c)
    order = z_order(depth)
    order = order[1:] + order[:1]
    sends = []

    def target_row(k, j, core):
        _, hb, he, _ = homes[j]
        return flat((a + k) % depth, hb, he, core)

    def remote(slot, src, dst, target):
        return pltpu.make_async_remote_copy(
            src_ref=src,
            dst_ref=dst,
            send_sem=send_sem.at[slot],
            recv_sem=recv_sem.at[slot],
            device_id=target,
            device_id_type=MESH,
        )

    def send(slot, src, dst, target):
        copy = remote(slot, src, dst, target)
        copy.start()
        sends.append(copy)

    loads = {}
    for k in order:
        for j in (3, 2, 1, 0):
            copy = pltpu.make_async_copy(
                g_ref.at[target_row(k, j, c)], own.at[k * 4 + j], load_sem.at[k * 4 + j]
            )
            copy.start()
            loads[k, j] = copy
    greet(depth, a, b, e, c)
    for k in order:
        for j in (3, 2, 1, 0):
            there = (0, 2, 1, 3)[j]
            send(k * 8 + j, g_ref.at[target_row(k, there, 1 - c)], from_c.at[k * 4 + j], twin)

    def stage_c(k):
        for j in (3, 2, 1, 0):
            loads[k, j].wait()
            remote(k * 8 + j, own.at[k * 4 + j], from_c.at[k * 4 + j], twin).wait_recv()
            add_into(own.at[k * 4 + j], own.at[k * 4 + j], from_c.at[k * 4 + j], rows, chunk)
            if j >= 2:
                send(k * 8 + 2 + j, own.at[k * 4 + j], from_two.at[k * 2 + j - 2], device(*two))

    def stage_two(k):
        for j in (3, 2):
            spot = from_two.at[k * 2 + j - 2]
            remote(k * 8 + 2 + j, own.at[k * 4 + j], spot, device(*two)).wait_recv()
            add_into(own.at[k * 4 + j - 2], own.at[k * 4 + j - 2], spot, rows, chunk)
            if j == 3:
                send(k * 8 + 6, own.at[k * 4 + 1], from_one.at[k], device(*one))

    def stage_one(k):
        spot = from_one.at[k]
        remote(k * 8 + 6, own.at[k * 4 + 1], spot, device(*one)).wait_recv()
        if k:
            add_into(own.at[k * 4], own.at[k * 4], spot, rows, chunk)
            send(k * 8 + 7, own.at[k * 4], from_z.at[k - 1], device((a + k) % depth, b, e, c))

    for n in range(depth + 2):
        if n < depth:
            stage_c(order[n])
        if 1 <= n < depth + 1:
            stage_two(order[n - 1])
        if n >= 2:
            stage_one(order[n - 2])
    for k in range(1, depth):
        remote(k * 8 + 7, own.at[k * 4], from_z.at[k - 1], twin).wait_recv()

    @pl.loop(0, rows // chunk)
    def _(step):
        part = pl.ds(step * chunk, chunk)
        total = own[0, part, :].astype(F32) + from_one[0, part, :].astype(F32)
        for k in range(1, depth):
            total = total + from_z[k - 1, part, :].astype(F32)
        o_ref[part, :] = total

    for copy in sends:
        copy.wait_send()


def scatter_fast(parts, depth, collective_id, chunk):
    _, rows, cols = parts.shape
    count = depth * 8

    def slots(n):
        return pltpu.VMEM((n, rows, cols), parts.dtype)

    return pl.pallas_call(
        functools.partial(scatter_kernel, depth, chunk),
        out_shape=jax.ShapeDtypeStruct((rows, cols), F32),
        in_specs=[any_spec()],
        out_specs=vmem_spec(),
        scratch_shapes=[
            slots(depth * 4),
            slots(depth * 4),
            slots(depth * 2),
            slots(depth),
            slots(depth - 1),
            pltpu.SemaphoreType.DMA((depth * 4,)),
            pltpu.SemaphoreType.DMA((count,)),
            pltpu.SemaphoreType.DMA((count,)),
        ],
        compiler_params=params(collective_id=collective_id, has_side_effects=True),
        name=f"scatter{collective_id}",
    )(parts)


def total_kernel(images, lats, x_ref, o_ref, slots, send_sem, recv_sem):
    img = lax.axis_index("img")
    lat = lax.axis_index("lat")
    count = images * lats
    me = img * lats + lat
    barrier = pltpu.get_barrier_semaphore()
    for k in range(1, count):
        there = (me + k) % count
        pl.semaphore_signal(
            barrier, inc=1, device_id=(there // lats, there % lats), device_id_type=MESH
        )
    pl.semaphore_wait(barrier, count - 1)
    slots[me] = x_ref[...]
    copies = []
    for k in range(1, count):
        there = (me + k) % count
        copy = pltpu.make_async_remote_copy(
            src_ref=x_ref,
            dst_ref=slots.at[me],
            send_sem=send_sem.at[k],
            recv_sem=recv_sem.at[k],
            device_id=(there // lats, there % lats),
            device_id_type=MESH,
        )
        copy.start()
        copies.append(copy)
    for k in range(1, count):
        pltpu.make_async_remote_copy(
            src_ref=x_ref,
            dst_ref=slots.at[(me - k) % count],
            send_sem=send_sem.at[k],
            recv_sem=recv_sem.at[k],
            device_id=(img, lat),
            device_id_type=MESH,
        ).wait_recv()
    o_ref[...] = jnp.sum(slots[...], axis=0)
    for copy in copies:
        copy.wait_send()


def total_fast(tile, images, lats, collective_id):
    count = images * lats
    return pl.pallas_call(
        functools.partial(total_kernel, images, lats),
        out_shape=jax.ShapeDtypeStruct(tile.shape, tile.dtype),
        in_specs=[vmem_spec()],
        out_specs=vmem_spec(),
        scratch_shapes=[
            pltpu.VMEM((count,) + tile.shape, tile.dtype),
            pltpu.SemaphoreType.DMA((count,)),
            pltpu.SemaphoreType.DMA((count,)),
        ],
        compiler_params=pltpu.CompilerParams(collective_id=collective_id, has_side_effects=True),
        name=f"total{collective_id}",
    )(tile)


def normalise(values):
    center = values - jnp.mean(values, axis=-1, keepdims=True)
    spread = jnp.mean(center * center, axis=-1, keepdims=True)
    scale = lax.rsqrt(spread + EPS)
    return center * scale, scale


def norm_back(grad, hat, scale, gain):
    inner = grad * gain
    first = jnp.mean(inner, axis=-1, keepdims=True)
    second = jnp.mean(inner * hat, axis=-1, keepdims=True)
    return scale * (inner - first - hat * second)


def media_kernel(m_ref, gb_ref, wk_ref, wv_ref, k_ref, v_ref):
    hat, _ = normalise(m_ref[...].astype(F32))
    normed = (hat * gb_ref[0:1, :] + gb_ref[3:4, :]).astype(BF16)
    k_ref[...] = mm(normed, wk_ref[...]).astype(BF16)
    v_ref[...] = mm(normed, wv_ref[...]).astype(BF16)


def media_project(media, gains, attend, inner):
    rows, width = media.shape
    out = jax.ShapeDtypeStruct((rows, inner), BF16)
    block = pl.BlockSpec((PATCH_IMG, inner), lambda i: (i, 0))
    return pl.pallas_call(
        media_kernel,
        grid=(rows // PATCH_IMG,),
        out_shape=(out, out),
        in_specs=[
            pl.BlockSpec((PATCH_IMG, width), lambda i: (i, 0)),
            pl.BlockSpec(gains.shape, lambda i: (0, 0)),
            pl.BlockSpec((width, inner), lambda i: (0, 1)),
            pl.BlockSpec((width, inner), lambda i: (0, 2)),
        ],
        out_specs=(block, block),
        compiler_params=params(),
        cost_estimate=pl.CostEstimate(
            flops=4 * rows * width * inner, bytes_accessed=4 * rows * width, transcendentals=0
        ),
        name="media_project",
    )(media, gains, attend, attend)


def latent_kernel(l_ref, gb_ref, w_ref, q_ref, k_ref, v_ref):
    inner = q_ref.shape[1]
    hat, _ = normalise(l_ref[...])
    normed = (hat * gb_ref[1:2, :] + gb_ref[4:5, :]).astype(BF16)
    q_ref[...] = mm(normed, w_ref[:, :inner]).astype(BF16)
    k_ref[...] = mm(normed, w_ref[:, inner : 2 * inner]).astype(BF16)
    v_ref[...] = mm(normed, w_ref[:, 2 * inner : 3 * inner]).astype(BF16)


def latent_project(latents, gains, attend, inner):
    out = jax.ShapeDtypeStruct((latents.shape[0], inner), BF16)
    return pl.pallas_call(
        latent_kernel,
        out_shape=(out, out, out),
        in_specs=[vmem_spec()] * 3,
        out_specs=(vmem_spec(),) * 3,
        compiler_params=params(),
        name="latent_project",
    )(latents, gains, attend)


def head_mask(kind):
    rows = lax.broadcasted_iota(jnp.int32, (GROUP * HDIM, GROUP * HDIM), 0) // HDIM
    cols = lax.broadcasted_iota(jnp.int32, (GROUP * HDIM, GROUP * HDIM), 1) // HDIM
    return (rows == cols).astype(F32).astype(kind)


def spread_heads(queries, group, mask):
    width = GROUP * HDIM
    part = queries[:, group * width : (group + 1) * width]
    return jnp.concatenate([part] * GROUP, axis=0) * mask


def take_heads(full, mask):
    total = None
    for h in range(GROUP):
        part = slice(h * HDIM, (h + 1) * HDIM)
        term = full[part, :] * mask[part, :]
        total = term if total is None else total + term
    return total


def pack_columns(columns, first=0):
    rows = columns[0].shape[0]
    lane = lax.broadcasted_iota(jnp.int32, (rows, LANES), 1)
    tile = jnp.zeros((rows, LANES), F32)
    for h, column in enumerate(columns):
        tile = jnp.where(lane == first + h, column, tile)
    return tile


def expand_columns(tile, width):
    rows = tile.shape[0]
    head = lax.broadcasted_iota(jnp.int32, (rows, width), 1) // HDIM
    out = jnp.zeros((rows, width), F32)
    for h in range(width // HDIM):
        out = jnp.where(head == h, tile[:, h : h + 1], out)
    return out


def forward_kernel(
    ids, q0, q1, q2, q3, k_ref, v_ref, kl_ref, vl_ref, keep, send, keep_st, send_st, acc, tops, sums
):
    step = pl.program_id(0)
    clips = acc.shape[0]
    inner = acc.shape[2]
    groups = inner // (GROUP * HDIM)
    width = GROUP * HDIM
    mask = head_mask(F32)
    mask_half = mask.astype(BF16)

    def clip_queries(clip):
        parts = [q[clip] for q in (q0, q1, q2, q3)]
        return jnp.concatenate(parts, axis=0) * BF16(SCALE)

    def attend(clip, keys, values, fresh):
        queries = clip_queries(clip)
        new_tops, new_sums = [], []
        for g in range(groups):
            cols = slice(g * width, (g + 1) * width)
            scores = mm_nt(spread_heads(queries, g, mask_half), keys[:, cols])
            top = jnp.max(scores, axis=-1, keepdims=True)
            if not fresh:
                old_tile = tops[clip]
                old_top = jnp.concatenate(
                    [old_tile[:, g * GROUP + h : g * GROUP + h + 1] for h in range(GROUP)], axis=0
                )
                top = jnp.maximum(top, old_top)
            probs = jnp.exp(scores - top)
            total = jnp.sum(probs, axis=-1, keepdims=True)
            part = take_heads(mm(probs.astype(BF16), values[:, cols]), mask)
            if not fresh:
                old_tile = sums[clip]
                old_sum = jnp.concatenate(
                    [old_tile[:, g * GROUP + h : g * GROUP + h + 1] for h in range(GROUP)], axis=0
                )
                shrink = jnp.exp(old_top - top)
                total = total + old_sum * shrink
                part = part + acc[clip, :, cols] * take_heads(shrink, mask)
            acc[clip, :, cols] = part
            for h in range(GROUP):
                new_tops.append(top[h * HDIM : (h + 1) * HDIM])
                new_sums.append(total[h * HDIM : (h + 1) * HDIM])
        tops[clip] = pack_columns(new_tops)
        sums[clip] = pack_columns(new_sums)

    @pl.when(step == 0)
    def _():
        @pl.loop(0, clips)
        def _(clip):
            attend(clip, kl_ref[clip], vl_ref[clip], True)

    attend(ids[step], k_ref[...], v_ref[...], False)

    @pl.when(step == pl.num_programs(0) - 1)
    def _():
        rows = keep.shape[2]
        lane = lax.broadcasted_iota(jnp.int32, (HDIM, LANES), 1)

        @pl.loop(0, clips)
        def _(clip):
            total = jnp.where(lane < HEADS, sums[clip], 1.0)
            stat = tops[clip] + jnp.log(total)
            out = (acc[clip] / expand_columns(total, inner)).astype(BF16)
            for r in range(4):
                part = slice(r * rows, (r + 1) * rows)
                where_o, where_s = (send, send_st) if r % 2 else (keep, keep_st)
                where_o[r // 2, clip] = out[part]
                where_s[r // 2, clip] = stat[part]


def attention_forward(ids, queries, keys, values, latent_keys, latent_values):
    clips, rows, inner = queries[0].shape
    frames = keys.shape[0] // PATCH_IMG
    out = jax.ShapeDtypeStruct((2, clips, rows, inner), BF16)
    stat = jax.ShapeDtypeStruct((2, clips, rows, LANES), F32)
    block = pl.BlockSpec((PATCH_IMG, inner), lambda i, ids: (i, 0))

    def whole(shape):
        return pl.BlockSpec(shape, lambda i, ids: (0,) * len(shape))

    return pl.pallas_call(
        forward_kernel,
        grid_spec=pltpu.PrefetchScalarGridSpec(
            num_scalar_prefetch=1,
            grid=(frames,),
            in_specs=[whole((clips, rows, inner))] * 4
            + [block, block]
            + [whole((clips, rows, inner))] * 2,
            out_specs=(whole(out.shape), whole(out.shape), whole(stat.shape), whole(stat.shape)),
            scratch_shapes=[
                pltpu.VMEM((clips, 4 * rows, inner), F32),
                pltpu.VMEM((clips, 4 * rows, LANES), F32),
                pltpu.VMEM((clips, 4 * rows, LANES), F32),
            ],
        ),
        out_shape=(out, out, stat, stat),
        compiler_params=params(),
        name="attention_forward",
    )(ids, *queries, keys, values, latent_keys, latent_values)


def join_partials(first, first_stat, second, second_stat):
    width = first.shape[-1]
    top = jnp.maximum(first_stat, second_stat)
    total = jnp.exp(first_stat - top) + jnp.exp(second_stat - top)
    stat = top + jnp.log(total)
    out = first.astype(F32) * expand_columns(jnp.exp(first_stat - stat), width)
    out = out + second.astype(F32) * expand_columns(jnp.exp(second_stat - stat), width)
    return out, stat


def join_kernel(keep, keep_st, got, got_st, own, own_st, away, away_st):
    out, stat = join_partials(keep[0], keep_st[0], got[0], got_st[0])
    own[...] = out
    own_st[...] = stat
    out, stat = join_partials(keep[1], keep_st[1], got[1], got_st[1])
    away[...] = out.astype(BF16)
    away_st[...] = stat


def join_cores(keep, keep_st, got, got_st):
    _, rows, inner = keep.shape
    stat = jax.ShapeDtypeStruct((rows, LANES), F32)
    return pl.pallas_call(
        join_kernel,
        out_shape=(
            jax.ShapeDtypeStruct((rows, inner), F32),
            stat,
            jax.ShapeDtypeStruct((rows, inner), BF16),
            stat,
        ),
        in_specs=[vmem_spec()] * 4,
        out_specs=(vmem_spec(),) * 4,
        compiler_params=params(),
        name="join_cores",
    )(keep, keep_st, got, got_st)


class Gather:
    def __init__(self, depth, x_ref, o_ref, local_sem, send_sem, recv_sem):
        self.depth = depth
        self.refs = x_ref, o_ref
        self.sems = local_sem, send_sem, recv_sem
        self.at = place()
        one = first_partner(*self.at)
        two = second_partner(*self.at)
        self.homes = [self.at, one, two, second_partner(*one)]
        self.order = z_order(depth)

    def row(self, k, j):
        a, _, _, c = self.at
        _, b, e, _ = self.homes[j % 4]
        return flat((a - k) % self.depth, b, e, c if j < 4 else 1 - c)

    def copy(self, k, j):
        x_ref, o_ref = self.refs
        a, b, e, c = self.at
        base = {1: 0, 2: 0, 3: 1}.get(j, j - 4)
        if j == 0:
            target, row, src = ((a + k) % self.depth, b, e, c), flat(a, b, e, c), x_ref
        else:
            target = self.homes[1] if j == 1 else self.homes[2] if j < 4 else (a, b, e, 1 - c)
            row = self.row(k, base)
            src = x_ref if (k, base) == (0, 0) else o_ref.at[row]
        slot = k * 8 + j
        return pltpu.make_async_remote_copy(
            src_ref=src,
            dst_ref=o_ref.at[row],
            send_sem=self.sems[1].at[slot],
            recv_sem=self.sems[2].at[slot],
            device_id=device(*target),
            device_id_type=MESH,
        )

    def arrive(self, k, j):
        x_ref, o_ref = self.refs
        a, b, e, c = self.at
        slot = k * 8 + j
        pltpu.make_async_remote_copy(
            src_ref=x_ref,
            dst_ref=o_ref.at[self.row(k, j)],
            send_sem=self.sems[1].at[slot],
            recv_sem=self.sems[2].at[slot],
            device_id=device(a, b, e, 1 - c),
            device_id_type=MESH,
        ).wait_recv()

    def own(self):
        x_ref, o_ref = self.refs
        return pltpu.make_async_copy(x_ref, o_ref.at[flat(*self.at)], self.sems[0])

    def far(self, k):
        self.copy(k, 0).start()

    def begin(self):
        self.own().start()
        self.far(self.order[1])
        self.first(0)

    def first(self, k):
        if k:
            self.arrive(k, 0)
        for j in (1, 2, 4):
            self.copy(k, j).start()

    def second(self, k):
        self.arrive(k, 1)
        self.copy(k, 3).start()
        self.copy(k, 5).start()
        self.arrive(k, 2)
        self.copy(k, 6).start()

    def third(self, k):
        self.arrive(k, 3)
        self.copy(k, 7).start()

    def run(self, names):
        acts = {"z": self.far, "a": self.first, "b": self.second, "c": self.third}
        for name in names.split():
            acts[name[0]](self.order[int(name[1:])])

    def finish(self):
        for k in range(self.depth):
            for j in range(4, 8):
                self.arrive(k, j)
        for k in range(self.depth):
            for j in range(8):
                if k or j:
                    self.copy(k, j).wait_send()
        self.own().wait()


def latent_mask(rows, inner):
    row = lax.broadcasted_iota(jnp.int32, (HEADS * rows, inner), 0) // rows
    col = lax.broadcasted_iota(jnp.int32, (HEADS * rows, inner), 1) // HDIM
    return (row == col).astype(F32)


def latent_attention(queries, keys, values, mask):
    rows = keys.shape[0]
    count = queries.shape[0]
    half = mask.astype(BF16)
    wide_k = jnp.concatenate([keys] * HEADS, axis=0) * half
    wide_v = jnp.concatenate([values] * HEADS, axis=0) * half
    scores = mm_nt(wide_k, queries).reshape(HEADS, rows, count)
    top = jnp.max(scores, axis=1, keepdims=True)
    probs = jnp.exp(scores - top)
    total = jnp.sum(probs, axis=1)
    out = mm_tn(probs.reshape(HEADS * rows, count).astype(BF16), wide_v)
    zeros = jnp.zeros((LANES - HEADS, count), F32)

    def tile(x):
        return jnp.concatenate([x, zeros], axis=0).T

    return out, tile(top.reshape(HEADS, count)), tile(total)


def remote_copy(src, dst, sems, slot, target):
    return pltpu.make_async_remote_copy(
        src_ref=src,
        dst_ref=dst,
        send_sem=sems[0].at[slot],
        recv_sem=sems[1].at[slot],
        device_id=device(*target),
        device_id_type=MESH,
    )


def front_kernel(
    depth,
    frames,
    plan,
    ids,
    last,
    has,
    same,
    shard_ref,
    m_ref,
    lat_ref,
    gb_ref,
    wq_ref,
    feed_ref,
    k_ref,
    v_ref,
    q_ref,
    kl_ref,
    vl_ref,
    own,
    own_st,
    got,
    got_st,
    all_k,
    all_v,
    all_q,
    outs,
    tops,
    sums,
    keep,
    keep_st,
    send,
    send_st,
    core_o,
    core_st,
    away,
    away_st,
    y_o,
    y_st,
    local_sem,
    send_sem,
    recv_sem,
    link_send,
    link_recv,
    out_sem,
):
    step = pl.program_id(0)
    a, b, e, c = place()
    twin, other = (a, b, e, 1 - c), (a, b, 1 - e, c)
    links = link_send, link_recv
    gather = Gather(depth, shard_ref, feed_ref, local_sem, send_sem, recv_sem)
    clips, rows, inner = kl_ref.shape
    groups = inner // (GROUP * HDIM)
    width = GROUP * HDIM
    mask = head_mask(F32)
    mask_half = mask.astype(BF16)
    query_copies = [
        remote_copy(all_q.at[0], all_q.at[2], links, 0, other),
        remote_copy(all_q.at[0], all_q.at[1], links, 1, twin),
        remote_copy(all_q.at[2], all_q.at[3], links, 2, twin),
    ]
    core_copies = [
        remote_copy(send, core_o, links, 3, twin),
        remote_copy(send_st, core_st, links, 4, twin),
    ]
    y_copies = [
        remote_copy(away, y_o, links, 5, other),
        remote_copy(away_st, y_st, links, 6, other),
    ]
    keep_queries = pltpu.make_async_copy(all_q, q_ref, out_sem)

    def clip_queries(clip):
        return jnp.concatenate([all_q[r, clip] for r in range(4)], axis=0) * BF16(SCALE)

    @pl.when(step == 0)
    def _():
        greet(depth, a, b, e, c)
        hat, _ = normalise(lat_ref[...])
        normed = (hat * gb_ref[1:2, :] + gb_ref[4:5, :]).astype(BF16)
        all_q[0] = mm(normed, wq_ref[:, :inner]).astype(BF16).reshape(clips, rows, inner)
        query_copies[0].start()
        query_copies[1].start()
        gather.begin()
        kl_ref[...] = (
            mm(normed, wq_ref[:, inner : 2 * inner]).astype(BF16).reshape(clips, rows, inner)
        )
        vl_ref[...] = (
            mm(normed, wq_ref[:, 2 * inner : 3 * inner]).astype(BF16).reshape(clips, rows, inner)
        )
        outs[0] = jnp.zeros_like(outs[0])
        tops[0] = jnp.zeros_like(tops[0])
        sums[0] = jnp.zeros_like(sums[0])

    @pl.when(step < frames)
    def _():
        hat, _ = normalise(m_ref[...].astype(F32))
        normed = (hat * gb_ref[0:1, :] + gb_ref[3:4, :]).astype(BF16)
        new_k = mm(normed, wq_ref[:, inner : 2 * inner]).astype(BF16)
        new_v = mm(normed, wq_ref[:, 2 * inner : 3 * inner]).astype(BF16)
        k_ref[...] = new_k
        v_ref[...] = new_v
        all_k[step] = new_k
        all_v[step] = new_v

    for when, names in plan[:-1]:

        @pl.when(step == when)
        def _(names=names):
            gather.run(names)

    @pl.when(step == frames // 2)
    def _():
        query_copies[0].wait()
        query_copies[2].start()

    @pl.when(step == frames)
    def _():
        query_copies[1].wait()
        query_copies[2].wait()
        keep_queries.start()

    @pl.when((step >= frames) & (step < 2 * frames))
    def _():
        frame = step - frames
        before = jnp.maximum(frame - 1, 0)
        queries = clip_queries(ids[frame])
        joined = same[frame] == 1
        old_tops = jnp.where(joined, tops[before], MASKED)
        old_sums = jnp.where(joined, sums[before], 0.0)
        new_tops, new_sums = [], []
        for g in range(groups):
            cols = slice(g * width, (g + 1) * width)

            def column(tile):
                at = g * GROUP
                return jnp.concatenate([tile[:, at + h : at + h + 1] for h in range(GROUP)], axis=0)

            scores = mm_nt(spread_heads(queries, g, mask_half), all_k[frame, :, cols])
            old_top = column(old_tops)
            top = jnp.maximum(jnp.max(scores, axis=-1, keepdims=True), old_top)
            probs = jnp.exp(scores - top)
            shrink = jnp.exp(old_top - top)
            total = jnp.sum(probs, axis=-1, keepdims=True) + column(old_sums) * shrink
            part = take_heads(mm(probs.astype(BF16), all_v[frame, :, cols]), mask)
            old = jnp.where(joined, outs[before, :, cols], 0.0)
            outs[frame, :, cols] = part + old * take_heads(shrink, mask)
            for h in range(GROUP):
                new_tops.append(top[h * HDIM : (h + 1) * HDIM])
                new_sums.append(total[h * HDIM : (h + 1) * HDIM])
        tops[frame] = pack_columns(new_tops)
        sums[frame] = pack_columns(new_sums)

    @pl.when(step == 2 * frames)
    def _():
        wide = latent_mask(rows, inner)
        lane = lax.broadcasted_iota(jnp.int32, (4 * rows, LANES), 1)

        @pl.loop(0, clips)
        def _(clip):
            out, top, total = latent_attention(clip_queries(clip), kl_ref[clip], vl_ref[clip], wide)
            at = last[clip]
            there = has[clip] == 1
            far_top = jnp.where(there, tops[at], MASKED)
            far_sum = jnp.where(there, sums[at], 0.0)
            far_out = jnp.where(there, outs[at], 0.0)
            both = jnp.maximum(top, far_top)
            near, far = jnp.exp(top - both), jnp.exp(far_top - both)
            total = jnp.where(lane < HEADS, total * near + far_sum * far, 1.0)
            stat = both + jnp.log(total)
            out = out * expand_columns(near / total, inner)
            out = out + far_out * expand_columns(far / total, inner)
            for r in range(4):
                part = slice(r * rows, (r + 1) * rows)
                if r % 2:
                    send[r // 2, clip] = out[part].astype(BF16)
                    send_st[r // 2, clip] = stat[part]
                else:
                    keep[r // 2, clip] = out[part]
                    keep_st[r // 2, clip] = stat[part]

        for copy in core_copies:
            copy.start()
        for copy in core_copies:
            copy.wait()

        def flat_o(ref, n):
            return ref[n].reshape(clips * rows, inner)

        def flat_s(ref, n):
            return ref[n].reshape(clips * rows, LANES)

        out, stat = join_partials(
            flat_o(keep, 1), flat_s(keep_st, 1), flat_o(core_o, 1), flat_s(core_st, 1)
        )
        away[...] = out.astype(BF16)
        away_st[...] = stat
        for copy in y_copies:
            copy.start()
        out, stat = join_partials(
            flat_o(keep, 0), flat_s(keep_st, 0), flat_o(core_o, 0), flat_s(core_st, 0)
        )
        own[...] = out
        own_st[...] = stat
        gather.run(plan[-1][1])
        for copy in y_copies:
            copy.wait()
        got[...] = y_o[...]
        got_st[...] = y_st[...]
        keep_queries.wait()
        gather.finish()


def front(ids, last, has, same, shard, media, latents, gains, attend, clips, inner, depth, plan):
    rows = latents.shape[0] // clips
    frames = media.shape[0] // PATCH_IMG
    width = media.shape[1]
    total = clips * rows
    cut = (clips, rows, inner)

    def whole(shape):
        return pl.BlockSpec(shape, lambda i: (0,) * len(shape))

    def block(columns):
        return pl.BlockSpec((PATCH_IMG, columns), lambda i: (jnp.minimum(i, frames - 1), 0))

    smem = pl.BlockSpec(memory_space=pltpu.SMEM)
    kv = jax.ShapeDtypeStruct((media.shape[0], inner), BF16)
    small = jax.ShapeDtypeStruct(cut, BF16)
    stat = jax.ShapeDtypeStruct((total, LANES), F32)
    count = depth * 8
    return pl.pallas_call(
        functools.partial(front_kernel, depth, frames, plan),
        grid=(2 * frames + 1,),
        out_shape=(
            jax.ShapeDtypeStruct((count,) + shard.shape, BF16),
            kv,
            kv,
            jax.ShapeDtypeStruct((4,) + cut, BF16),
            small,
            small,
            jax.ShapeDtypeStruct((total, inner), F32),
            stat,
            jax.ShapeDtypeStruct((total, inner), BF16),
            stat,
        ),
        in_specs=[smem] * 4
        + [any_spec(), block(width), whole(latents.shape), whole(gains.shape), whole(attend.shape)],
        out_specs=(
            any_spec(),
            block(inner),
            block(inner),
            any_spec(),
            whole(cut),
            whole(cut),
            whole((total, inner)),
            whole(stat.shape),
            whole((total, inner)),
            whole(stat.shape),
        ),
        scratch_shapes=[
            pltpu.VMEM((frames, PATCH_IMG, inner), BF16),
            pltpu.VMEM((frames, PATCH_IMG, inner), BF16),
            pltpu.VMEM((4,) + cut, BF16),
            pltpu.VMEM((frames, 4 * rows, inner), F32),
            pltpu.VMEM((frames, 4 * rows, LANES), F32),
            pltpu.VMEM((frames, 4 * rows, LANES), F32),
            pltpu.VMEM((2,) + cut, F32),
            pltpu.VMEM((2, clips, rows, LANES), F32),
            pltpu.VMEM((2,) + cut, BF16),
            pltpu.VMEM((2, clips, rows, LANES), F32),
            pltpu.VMEM((2,) + cut, BF16),
            pltpu.VMEM((2, clips, rows, LANES), F32),
            pltpu.VMEM((total, inner), BF16),
            pltpu.VMEM((total, LANES), F32),
            pltpu.VMEM((total, inner), BF16),
            pltpu.VMEM((total, LANES), F32),
            pltpu.SemaphoreType.DMA,
            pltpu.SemaphoreType.DMA((count,)),
            pltpu.SemaphoreType.DMA((count,)),
            pltpu.SemaphoreType.DMA((7,)),
            pltpu.SemaphoreType.DMA((7,)),
            pltpu.SemaphoreType.DMA,
        ],
        compiler_params=params(collective_id=2, has_side_effects=True),
        name="front",
    )(ids, last, has, same, shard, media, latents, gains, attend)


def feed_kernel(
    own,
    own_st,
    got,
    got_st,
    lat_ref,
    cot_ref,
    gb_ref,
    w_ref,
    out_ref,
    mixed_grad,
    context_grad,
    tile_ref,
    gain_ref,
    gw_ref,
    expand_v,
    shrink_v,
    output_v,
    grad_e,
    grad_s,
    grad_o,
    normed_v,
    normed_t,
    hat_v,
    acc_g,
    load_sem,
    store_sem,
):
    groups = expand_v.shape[0]
    width = expand_v.shape[3]
    blocks = expand_v.shape[1]
    shrink_rows = shrink_v.shape[1]
    per_group = blocks // groups
    expand_rows = expand_v.shape[2]
    shrink_at = groups * expand_rows
    output_at = shrink_at + shrink_rows
    output_rows = output_v.shape[1]
    half = width // 2
    inner = own.shape[1]

    def load_expand(g):
        return pltpu.make_async_copy(
            w_ref.at[:, pl.ds(g * expand_rows, expand_rows), :], expand_v.at[g], load_sem.at[g]
        )

    def load_shrink(g):
        part = pl.ds(g * per_group, per_group)
        return pltpu.make_async_copy(
            w_ref.at[part, pl.ds(shrink_at, shrink_rows), :],
            shrink_v.at[part],
            load_sem.at[groups + g],
        )

    load_output = pltpu.make_async_copy(
        w_ref.at[:, pl.ds(output_at, output_rows), :], output_v, load_sem.at[2 * groups]
    )
    load_output.start()
    for g in range(groups):
        load_expand(g).start()
        load_shrink(g).start()

    context, stat = join_partials(own[...], own_st[...], got[...], got_st[...])
    context_half = context.astype(BF16)
    load_output.wait()
    weight_o = output_v[...].reshape(inner, width)
    mixed = lat_ref[...] + mm(context_half, weight_o)
    hat, scale = normalise(mixed)
    hat_v[...] = hat
    normed = (hat * gb_ref[2:3, :] + gb_ref[5:6, :]).astype(BF16)
    normed_v[...] = normed
    normed_t[...] = normed.astype(F32).T.astype(BF16)
    out_ref[...] = mixed
    acc_g[...] = jnp.zeros_like(acc_g)

    def store_e(s, slot):
        return pltpu.make_async_copy(
            grad_e.at[slot],
            gw_ref.at[:, pl.ds((s // 2) * expand_rows, expand_rows), pl.ds((s % 2) * half, half)],
            store_sem.at[slot],
        )

    def store_s(s, slot):
        rows = half // shrink_rows
        return pltpu.make_async_copy(
            grad_s.at[slot],
            gw_ref.at[pl.ds(s * rows, rows), pl.ds(shrink_at, shrink_rows), :],
            store_sem.at[2 + slot],
        )

    cot = cot_ref[...]
    steps = 2 * groups
    for s in range(steps):
        g, slot = s // 2, s % 2
        if slot == 0:
            load_expand(g).wait()
            load_shrink(g).wait()
        cols = slice(slot * half, (slot + 1) * half)
        w_e = expand_v[g, :, :, cols].reshape(blocks * expand_rows, half)
        first = s * half // shrink_rows
        w_s = shrink_v[first : first + half // shrink_rows].reshape(half, width)
        pre = mm(normed_v[...], w_e)
        cdf = 0.5 * (1.0 + lax.erf(pre * (0.5**0.5)))
        hidden = (pre * cdf).astype(BF16)
        out_ref[...] += mm(hidden, w_s)
        grad_hidden = mm_nt(cot, w_s)
        pdf = jnp.exp(-0.5 * pre * pre) * (1.0 / math.sqrt(2.0 * math.pi))
        grad_pre = (grad_hidden * (cdf + pre * pdf)).astype(BF16)
        if s >= 2:
            store_e(s - 2, slot).wait()
            store_s(s - 2, slot).wait()
        grad_s[slot] = mm_tn(hidden, cot).astype(BF16).reshape(half // shrink_rows, shrink_rows, width)
        grad_e[slot] = (
            mm(normed_t[...], grad_pre).astype(BF16).reshape(blocks, expand_rows, half)
        )
        store_e(s, slot).start()
        store_s(s, slot).start()
        acc_g[...] += mm_nt(grad_pre, w_e)

    grad_normed = acc_g[...]
    hat = hat_v[...]
    rows = gain_ref.shape[0]
    gain_ref[...] = jnp.concatenate(
        [
            jnp.sum(grad_normed * hat, axis=0, keepdims=True),
            jnp.sum(grad_normed, axis=0, keepdims=True),
            jnp.zeros((rows - 2, width), F32),
        ],
        axis=0,
    )
    total = cot.astype(F32) + norm_back(grad_normed, hat, scale, gb_ref[2:3, :])
    mixed_grad[...] = total
    attended = total.astype(BF16)
    grad_o[...] = mm_tn(context_half, attended).astype(BF16).reshape(grad_o.shape)
    store_o = pltpu.make_async_copy(
        grad_o, gw_ref.at[:, pl.ds(output_at, output_rows), :], store_sem.at[4]
    )
    store_o.start()
    grad_c = mm_nt(attended, weight_o).astype(BF16)
    context_grad[...] = grad_c
    product = grad_c.astype(F32) * context
    head = lax.broadcasted_iota(jnp.int32, product.shape, 1) // HDIM
    deltas = [
        jnp.sum(jnp.where(head == h, product, 0.0), axis=-1, keepdims=True) for h in range(HEADS)
    ]
    lane = lax.broadcasted_iota(jnp.int32, stat.shape, 1)
    tile_ref[...] = jnp.where(lane < HEADS, stat, pack_columns(deltas, HEADS))
    for s in range(steps - 2, steps):
        store_e(s, s % 2).wait()
        store_s(s, s % 2).wait()
    store_o.wait()


def feed_forward(own, own_st, got, got_st, latents, cotangent, gains, weights):
    rows, width = latents.shape
    inner = own.shape[1]
    blocks = weights.shape[0]
    ff = 4 * width
    groups = ff // width
    expand_rows = width // blocks
    shrink_rows = ff // blocks
    output_rows = inner // blocks
    half = width // 2
    flops = 2 * rows * (6 * width * ff + 3 * width * inner)
    return pl.pallas_call(
        feed_kernel,
        out_shape=(
            jax.ShapeDtypeStruct((rows, width), F32),
            jax.ShapeDtypeStruct((rows, width), F32),
            jax.ShapeDtypeStruct((rows, inner), BF16),
            jax.ShapeDtypeStruct((rows, LANES), F32),
            jax.ShapeDtypeStruct((8, width), F32),
            jax.ShapeDtypeStruct(weights.shape, BF16),
        ),
        in_specs=[vmem_spec()] * 7 + [any_spec()],
        out_specs=(vmem_spec(),) * 5 + (any_spec(),),
        scratch_shapes=[
            pltpu.VMEM((groups, blocks, expand_rows, width), BF16),
            pltpu.VMEM((blocks, shrink_rows, width), BF16),
            pltpu.VMEM((blocks, output_rows, width), BF16),
            pltpu.VMEM((2, blocks, expand_rows, half), BF16),
            pltpu.VMEM((2, half // shrink_rows, shrink_rows, width), BF16),
            pltpu.VMEM((blocks, output_rows, width), BF16),
            pltpu.VMEM((rows, width), BF16),
            pltpu.VMEM((width, rows), BF16),
            pltpu.VMEM((rows, width), F32),
            pltpu.VMEM((rows, width), F32),
            pltpu.SemaphoreType.DMA((2 * groups + 1,)),
            pltpu.SemaphoreType.DMA((5,)),
        ],
        compiler_params=params(),
        cost_estimate=pl.CostEstimate(
            flops=flops, bytes_accessed=4 * weights.size, transcendentals=2 * rows * ff
        ),
        name="feed_forward",
    )(own, own_st, got, got_st, latents, cotangent, gains, weights)


def backward_kernel(
    ids,
    q0,
    q1,
    q2,
    q3,
    g0,
    g1,
    g2,
    g3,
    t0,
    t1,
    t2,
    t3,
    k_ref,
    v_ref,
    kl_ref,
    vl_ref,
    m_ref,
    gb_ref,
    wk_ref,
    wv_ref,
    media_grad,
    latent_kv,
    keep,
    send,
    weight_grad,
    gain_ref,
    acc,
):
    step = pl.program_id(0)
    clips = acc.shape[0]
    inner = acc.shape[2]
    groups = inner // (GROUP * HDIM)
    width = GROUP * HDIM
    mask = head_mask(F32)
    mask_half = mask.astype(BF16)

    def attend(clip, keys, values, fresh):
        queries = jnp.concatenate([q[clip] for q in (q0, q1, q2, q3)], axis=0) * BF16(SCALE)
        grads = jnp.concatenate([g[clip] for g in (g0, g1, g2, g3)], axis=0)
        stats = jnp.concatenate([t[clip] for t in (t0, t1, t2, t3)], axis=0).T
        key_parts, value_parts = [], []
        for g in range(groups):
            cols = slice(g * width, (g + 1) * width)

            def line(first):
                at = first + g * GROUP
                return jnp.concatenate([stats[at + h : at + h + 1, :] for h in range(GROUP)], axis=1)

            wide_q = spread_heads(queries, g, mask_half)
            wide_g = spread_heads(grads, g, mask_half)
            probs = jnp.exp(mm_nt(keys[:, cols], wide_q) - line(0))
            grad_probs = mm_nt(values[:, cols], wide_g)
            grad_scores = (probs * (grad_probs - line(HEADS))).astype(BF16)
            key_parts.append(mm(grad_scores, wide_q))
            value_parts.append(mm(probs.astype(BF16), wide_g))
            part = take_heads(mm_tn(grad_scores, keys[:, cols]), mask)
            if fresh:
                acc[clip, :, cols] = part
            else:
                acc[clip, :, cols] += part
        return jnp.concatenate(key_parts + value_parts, axis=1).astype(BF16)

    @pl.when(step == 0)
    def _():
        gain_ref[...] = jnp.zeros_like(gain_ref)
        weight_grad[...] = jnp.zeros_like(weight_grad)

        @pl.loop(0, clips)
        def _(clip):
            latent_kv[clip] = attend(clip, kl_ref[clip], vl_ref[clip], True)

    grad_kv = attend(ids[step], k_ref[...], v_ref[...], False)
    hat, scale = normalise(m_ref[...].astype(F32))
    gain = gb_ref[0:1, :]
    normed = (hat * gain + gb_ref[3:4, :]).astype(BF16)
    weight_grad[...] += mm_tn(normed, grad_kv)
    grad = mm_nt(grad_kv[:, :inner], wk_ref[...]) + mm_nt(grad_kv[:, inner:], wv_ref[...])
    gain_ref[0:1, :] += jnp.sum(grad * hat, axis=0, keepdims=True)
    gain_ref[1:2, :] += jnp.sum(grad, axis=0, keepdims=True)
    media_grad[...] = norm_back(grad, hat, scale, gain).astype(BF16)

    @pl.when(step == pl.num_programs(0) - 1)
    def _():
        rows = keep.shape[2]

        @pl.loop(0, clips)
        def _(clip):
            out = (acc[clip] * SCALE).astype(BF16)
            for r in range(4):
                part = slice(r * rows, (r + 1) * rows)
                where_o = send if r % 2 else keep
                where_o[r // 2, clip] = out[part]


def attention_backward(
    ids, queries, grads, tiles, keys, values, latent_keys, latent_values, media, gains, attend
):
    clips, rows, inner = queries[0].shape
    width = media.shape[1]
    frames = keys.shape[0] // PATCH_IMG
    block = pl.BlockSpec((PATCH_IMG, inner), lambda i, ids: (i, 0))
    wide = pl.BlockSpec((PATCH_IMG, width), lambda i, ids: (i, 0))

    def whole(shape):
        return pl.BlockSpec(shape, lambda i, ids: (0,) * len(shape))

    def column(n):
        return pl.BlockSpec((width, inner), lambda i, ids: (0, n))

    query = whole((clips, rows, inner))
    pair = (2, clips, rows, inner)
    return pl.pallas_call(
        backward_kernel,
        grid_spec=pltpu.PrefetchScalarGridSpec(
            num_scalar_prefetch=1,
            grid=(frames,),
            in_specs=[query] * 8
            + [whole((clips, rows, LANES))] * 4
            + [block, block, query, query, wide, whole(gains.shape), column(1), column(2)],
            out_specs=(
                wide,
                whole((clips, rows, 2 * inner)),
                whole(pair),
                whole(pair),
                whole((width, 2 * inner)),
                whole((8, width)),
            ),
            scratch_shapes=[pltpu.VMEM((clips, 4 * rows, inner), F32)],
        ),
        out_shape=(
            jax.ShapeDtypeStruct(media.shape, BF16),
            jax.ShapeDtypeStruct((clips, rows, 2 * inner), BF16),
            jax.ShapeDtypeStruct(pair, BF16),
            jax.ShapeDtypeStruct(pair, BF16),
            jax.ShapeDtypeStruct((width, 2 * inner), F32),
            jax.ShapeDtypeStruct((8, width), F32),
        ),
        compiler_params=params(),
        name="attention_backward",
    )(
        ids,
        *queries,
        *grads,
        *tiles,
        keys,
        values,
        latent_keys,
        latent_values,
        media,
        gains,
        attend,
        attend,
    )


def last_kernel(
    lat_ref, mixed_grad, first, second, kv_ref, gb_ref, w_ref, gw_ref, gm_ref, gf_ref, out_ref, pack_ref
):
    inner = first.shape[1]
    width = lat_ref.shape[1]
    hat, scale = normalise(lat_ref[...])
    gain = gb_ref[1:2, :]
    normed = (hat * gain + gb_ref[4:5, :]).astype(BF16)
    grad_q = (first[...].astype(F32) + second[...].astype(F32)).astype(BF16)
    grad_kv = kv_ref[...]
    grad = mm_nt(grad_q, w_ref[:, :inner]) + mm_nt(grad_kv, w_ref[:, inner : 3 * inner])
    pack_ref[:, :inner] = mm_tn(normed, grad_q).astype(BF16)
    pack_ref[:, inner : 3 * inner] = (gw_ref[...] + mm_tn(normed, grad_kv)).astype(BF16)
    lines = jnp.concatenate(
        [
            gm_ref[0:1, :],
            jnp.sum(grad * hat, axis=0, keepdims=True),
            gf_ref[0:1, :],
            gm_ref[1:2, :],
            jnp.sum(grad, axis=0, keepdims=True),
            gf_ref[1:2, :],
            jnp.zeros((LANES - 6, width), F32),
        ],
        axis=0,
    )
    pack_ref[:, 3 * inner :] = lines.T.astype(BF16)
    out_ref[...] = mixed_grad[...] + norm_back(grad, hat, scale, gain)


def latent_backward(latents, mixed_grad, first, second, grad_kv, gains, attend, grad_w, gain_m, gain_f):
    return pl.pallas_call(
        last_kernel,
        out_shape=(
            jax.ShapeDtypeStruct(latents.shape, F32),
            jax.ShapeDtypeStruct(attend.shape, BF16),
        ),
        in_specs=[vmem_spec()] * 10,
        out_specs=(vmem_spec(), vmem_spec()),
        compiler_params=params(),
        name="latent_backward",
    )(latents, mixed_grad, first, second, grad_kv, gains, attend, grad_w, gain_m, gain_f)


class Scatter:
    def __init__(self, depth, chunk, g_ref, buffers, load_sem, sems):
        self.depth = depth
        self.chunk = chunk
        self.g_ref = g_ref
        self.own, self.from_c, self.from_two, self.from_one, self.from_z = buffers
        self.load_sem = load_sem
        self.sems = sems
        self.at = place()
        self.one = first_partner(*self.at)
        self.two = second_partner(*self.at)
        self.homes = [self.at, self.one, self.two, second_partner(*self.one)]
        a, b, e, c = self.at
        self.twin = (a, b, e, 1 - c)
        order = z_order(depth)
        self.order = order[1:] + order[:1]
        self.rows = self.own.shape[1]

    def row(self, k, j, core):
        _, b, e, _ = self.homes[j]
        return flat((self.at[0] + k) % self.depth, b, e, core)

    def load(self, k, j):
        slot = k * 4 + j
        src = self.g_ref.at[self.row(k, j, self.at[3])]
        return pltpu.make_async_copy(src, self.own.at[slot], self.load_sem.at[slot])

    def to_twin(self, k, j):
        src = self.g_ref.at[self.row(k, (0, 2, 1, 3)[j], 1 - self.at[3])]
        return remote_copy(src, self.from_c.at[k * 4 + j], self.sems, k * 8 + j, self.twin)

    def to_two(self, k, j):
        spot = self.from_two.at[k * 2 + j - 2]
        return remote_copy(self.own.at[k * 4 + j], spot, self.sems, k * 8 + 2 + j, self.two)

    def to_one(self, k):
        return remote_copy(
            self.own.at[k * 4 + 1], self.from_one.at[k], self.sems, k * 8 + 6, self.one
        )

    def to_far(self, k):
        a, b, e, c = self.at
        target = ((a + k) % self.depth, b, e, c)
        return remote_copy(
            self.own.at[k * 4], self.from_z.at[k - 1], self.sems, k * 8 + 7, target
        )

    def add(self, slot, spot):
        mine = self.own.at[slot]
        add_into(mine, mine, spot, self.rows, self.chunk)

    def begin(self):
        for k in self.order:
            for j in (3, 2, 1, 0):
                self.load(k, j).start()
                self.to_twin(k, j).start()

    def first(self, k):
        for j in (3, 2, 1, 0):
            self.load(k, j).wait()
            self.to_twin(k, j).wait_recv()
            self.add(k * 4 + j, self.from_c.at[k * 4 + j])
            if j >= 2:
                self.to_two(k, j).start()

    def second(self, k):
        for j in (3, 2):
            self.to_two(k, j).wait_recv()
            self.add(k * 4 + j - 2, self.from_two.at[k * 2 + j - 2])
            if j == 3:
                self.to_one(k).start()

    def third(self, k):
        self.to_one(k).wait_recv()
        self.add(k * 4, self.from_one.at[k])
        if k:
            self.to_far(k).start()

    def run(self, names):
        acts = {"a": self.first, "b": self.second, "c": self.third}
        for name in names.split():
            acts[name[0]](self.order[int(name[1:])])

    def finish(self, o_ref):
        for k in range(1, self.depth):
            self.to_far(k).wait_recv()

        @pl.loop(0, self.rows // self.chunk)
        def _(step):
            part = pl.ds(step * self.chunk, self.chunk)
            total = self.own[0, part, :].astype(F32)
            for k in range(1, self.depth):
                total = total + self.from_z[k - 1, part, :].astype(F32)
            o_ref[part, :] = total

        for k in range(self.depth):
            for j in range(4):
                self.to_twin(k, j).wait_send()
            self.to_two(k, 3).wait_send()
            self.to_two(k, 2).wait_send()
            self.to_one(k).wait_send()
            if k:
                self.to_far(k).wait_send()


def scatter_buffers(depth, rows, cols):
    def slots(n):
        return pltpu.VMEM((n, rows, cols), BF16)

    return [slots(depth * 4), slots(depth * 4), slots(depth * 2), slots(depth), slots(depth - 1)]


def scatter_sems(depth):
    return [
        pltpu.SemaphoreType.DMA((depth * 4,)),
        pltpu.SemaphoreType.DMA((depth * 8,)),
        pltpu.SemaphoreType.DMA((depth * 8,)),
    ]


def latent_attention_back(queries, grads, stats, keys, values, mask):
    rows = keys.shape[0]
    count = queries.shape[0]
    half = mask.astype(BF16)
    wide_k = jnp.concatenate([keys] * HEADS, axis=0) * half
    wide_v = jnp.concatenate([values] * HEADS, axis=0) * half
    cut = (HEADS, rows, count)
    scores = mm_nt(wide_k, queries).reshape(cut)
    probs = jnp.exp(scores - stats[:HEADS][:, None, :])
    grad_probs = mm_nt(wide_v, grads).reshape(cut)
    grad_scores = probs * (grad_probs - stats[HEADS : 2 * HEADS][:, None, :])
    grad_scores = grad_scores.reshape(HEADS * rows, count).astype(BF16)
    probs = probs.reshape(HEADS * rows, count).astype(BF16)

    def fold(full):
        full = full * mask
        total = full[:rows]
        for h in range(1, HEADS):
            total = total + full[h * rows : (h + 1) * rows]
        return total

    grad_kv = [fold(mm(grad_scores, queries)), fold(mm(probs, grads))]
    return mm_tn(grad_scores, wide_k), jnp.concatenate(grad_kv, axis=1).astype(BF16)


def to_lines(tile):
    return tile.T[: 2 * HEADS]


def from_lines(lines):
    zeros = jnp.zeros((LANES - lines.shape[0], lines.shape[1]), F32)
    return jnp.concatenate([lines, zeros], axis=0).T


def back_kernel(
    depth,
    frames,
    chunk,
    plan,
    ids,
    last,
    has,
    same,
    g_ref,
    q_ref,
    context_grad,
    tile_ref,
    k_ref,
    v_ref,
    m_ref,
    kl_ref,
    vl_ref,
    gb_ref,
    w_ref,
    lat_ref,
    mixed_ref,
    gain_f,
    media_grad,
    latents_grad,
    pack_ref,
    mine_ref,
    own,
    from_c,
    from_two,
    from_one,
    from_z,
    load_sem,
    send_sem,
    recv_sem,
    all_g,
    lines,
    tiles,
    weight_acc,
    gain_acc,
    outs,
    latent_kv,
    keep,
    send,
    core_q,
    away,
    y_q,
    link_send,
    link_recv,
    mixed_sem,
):
    step = pl.program_id(0)
    a, b, e, c = place()
    twin, other = (a, b, e, 1 - c), (a, b, 1 - e, c)
    links = link_send, link_recv
    scatter = Scatter(
        depth, chunk, g_ref, (own, from_c, from_two, from_one, from_z), load_sem, (send_sem, recv_sem)
    )
    clips, rows, inner = kl_ref.shape
    total_rows = clips * rows
    groups = inner // (GROUP * HDIM)
    width = GROUP * HDIM
    mask = head_mask(F32)
    mask_half = mask.astype(BF16)
    grad_copies = [
        remote_copy(all_g.at[0], all_g.at[2], links, 0, other),
        remote_copy(all_g.at[0], all_g.at[1], links, 1, twin),
        remote_copy(all_g.at[2], all_g.at[3], links, 2, twin),
    ]
    line_copies = [
        remote_copy(lines.at[0], lines.at[2], links, 3, other),
        remote_copy(lines.at[0], lines.at[1], links, 4, twin),
        remote_copy(lines.at[2], lines.at[3], links, 5, twin),
    ]
    core_copy = remote_copy(send, core_q, links, 6, twin)
    y_copy = remote_copy(away, y_q, links, 7, other)

    def clip_queries(clip):
        return jnp.concatenate([q_ref[r, clip] for r in range(4)], axis=0) * BF16(SCALE)

    def clip_grads(clip):
        return jnp.concatenate([all_g[r, clip] for r in range(4)], axis=0)

    def clip_stats(clip):
        return jnp.concatenate([tiles[r, clip] for r in range(4)], axis=0).T

    @pl.when(step == 0)
    def _():
        all_g[0] = context_grad[...]
        lines[0] = to_lines(tile_ref[...])
        greet(depth, a, b, e, c)
        for copies in (grad_copies, line_copies):
            copies[0].start()
            copies[1].start()
        scatter.begin()
        gain_acc[...] = jnp.zeros_like(gain_acc)
        weight_acc[...] = jnp.zeros_like(weight_acc)
        outs[0] = jnp.zeros_like(outs[0])

    for when, names in plan[:-1]:

        @pl.when(step == when)
        def _(names=names):
            scatter.run(names)

    @pl.when(step == 0)
    def _():
        for copies in (grad_copies, line_copies):
            copies[0].wait()
            copies[2].start()
        for copies in (grad_copies, line_copies):
            copies[1].wait()
            copies[2].wait()
        for r in range(4):
            tiles[r] = from_lines(lines[r]).reshape(clips, rows, LANES)

    @pl.when((step >= 1) & (step <= frames))
    def _():
        frame = step - 1
        before = jnp.maximum(frame - 1, 0)
        clip = ids[frame]
        joined = same[frame] == 1
        queries, grads, stats = clip_queries(clip), clip_grads(clip), clip_stats(clip)
        key_parts, value_parts = [], []
        for g in range(groups):
            cols = slice(g * width, (g + 1) * width)

            def line(first):
                at = first + g * GROUP
                return jnp.concatenate([stats[at + h : at + h + 1, :] for h in range(GROUP)], axis=1)

            wide_q = spread_heads(queries, g, mask_half)
            wide_g = spread_heads(grads, g, mask_half)
            keys = k_ref[:, cols]
            probs = jnp.exp(mm_nt(keys, wide_q) - line(0))
            grad_probs = mm_nt(v_ref[:, cols], wide_g)
            grad_scores = (probs * (grad_probs - line(HEADS))).astype(BF16)
            key_parts.append(mm(grad_scores, wide_q))
            value_parts.append(mm(probs.astype(BF16), wide_g))
            part = take_heads(mm_tn(grad_scores, keys), mask)
            outs[frame, :, cols] = part + jnp.where(joined, outs[before, :, cols], 0.0)
        grad_kv = jnp.concatenate(key_parts + value_parts, axis=1).astype(BF16)
        hat, scale = normalise(m_ref[...].astype(F32))
        gain = gb_ref[0:1, :]
        normed = (hat * gain + gb_ref[3:4, :]).astype(BF16)
        weight_acc[...] += mm_tn(normed, grad_kv)
        grad = mm_nt(grad_kv, w_ref[:, inner : 3 * inner])
        gain_acc[0:1, :] += jnp.sum(grad * hat, axis=0, keepdims=True)
        gain_acc[1:2, :] += jnp.sum(grad, axis=0, keepdims=True)
        media_grad[...] = norm_back(grad, hat, scale, gain).astype(BF16)

    @pl.when(step == frames + 1)
    def _():
        wide = latent_mask(rows, inner)

        @pl.loop(0, clips)
        def _(clip):
            out, grad_kv = latent_attention_back(
                clip_queries(clip),
                clip_grads(clip),
                clip_stats(clip),
                kl_ref[clip],
                vl_ref[clip],
                wide,
            )
            latent_kv[clip] = grad_kv
            out = (out + jnp.where(has[clip] == 1, outs[last[clip]], 0.0)) * SCALE
            for r in range(4):
                part = slice(r * rows, (r + 1) * rows)
                if r % 2:
                    send[r // 2, clip] = out[part].astype(BF16)
                else:
                    keep[r // 2, clip] = out[part]

        core_copy.start()
        hat, scale = normalise(lat_ref[...])
        gain = gb_ref[1:2, :]
        normed = (hat * gain + gb_ref[4:5, :]).astype(BF16)
        core_copy.wait()
        away[...] = (keep[1] + core_q[1].astype(F32)).astype(BF16)
        y_copy.start()
        grad_kv = latent_kv[...].reshape(total_rows, 2 * inner)
        pack_ref[:, inner : 3 * inner] = (weight_acc[...] + mm_tn(normed, grad_kv)).astype(BF16)
        grad = mm_nt(grad_kv, w_ref[:, inner : 3 * inner])
        mixed = weight_acc.at[:total_rows]
        load_mixed = pltpu.make_async_copy(mixed_ref, mixed, mixed_sem)
        load_mixed.start()
        scatter.run(plan[-1][1])
        y_copy.wait()
        grad_q = (keep[0] + core_q[0].astype(F32) + y_q[...].astype(F32)).astype(BF16)
        grad_q = grad_q.reshape(total_rows, inner)
        grad = grad + mm_nt(grad_q, w_ref[:, :inner])
        pack_ref[:, :inner] = mm_tn(normed, grad_q).astype(BF16)
        table = jnp.concatenate(
            [
                gain_acc[0:1, :],
                jnp.sum(grad * hat, axis=0, keepdims=True),
                gain_f[0:1, :],
                gain_acc[1:2, :],
                jnp.sum(grad, axis=0, keepdims=True),
                gain_f[1:2, :],
                jnp.zeros((LANES - 6, grad.shape[1]), F32),
            ],
            axis=0,
        )
        pack_ref[:, 3 * inner :] = table.T.astype(BF16)
        load_mixed.wait()
        latents_grad[...] = mixed[...] + norm_back(grad, hat, scale, gain)
        scatter.finish(mine_ref)


def back(
    ids,
    last,
    has,
    same,
    grad_feed,
    query_all,
    context_grad,
    tile,
    keys,
    values,
    media,
    latent_key,
    latent_value,
    gains,
    attend,
    latents,
    mixed_grad,
    gain_f,
    depth,
    chunk,
    plan,
):
    clips, rows, inner = latent_key.shape
    frames = media.shape[0] // PATCH_IMG
    width = media.shape[1]
    total = clips * rows
    cut = (clips, rows, inner)
    _, feed_rows, feed_cols = grad_feed.shape
    once = pl.Buffered(buffer_count=1)

    def whole(x):
        return pl.BlockSpec(x.shape, lambda i: (0,) * len(x.shape), pipeline_mode=once)

    def block(columns):
        return pl.BlockSpec((PATCH_IMG, columns), lambda i: (jnp.clip(i - 1, 0, frames - 1), 0))

    smem = pl.BlockSpec(memory_space=pltpu.SMEM)
    outs = (
        jax.ShapeDtypeStruct(media.shape, BF16),
        jax.ShapeDtypeStruct(latents.shape, F32),
        jax.ShapeDtypeStruct(attend.shape, BF16),
        jax.ShapeDtypeStruct((feed_rows, feed_cols), F32),
    )
    return pl.pallas_call(
        functools.partial(back_kernel, depth, frames, chunk, plan),
        grid=(frames + 2,),
        out_shape=outs,
        in_specs=[smem] * 4
        + [any_spec(), whole(query_all), whole(context_grad), whole(tile)]
        + [block(inner), block(inner), block(width)]
        + [whole(x) for x in (latent_key, latent_value, gains, attend, latents)]
        + [any_spec(), whole(gain_f)],
        out_specs=(block(width),) + tuple(whole(x) for x in outs[1:]),
        scratch_shapes=scatter_buffers(depth, feed_rows, feed_cols)
        + scatter_sems(depth)
        + [
            pltpu.VMEM((4,) + cut, BF16),
            pltpu.VMEM((4, 2 * HEADS, total), F32),
            pltpu.VMEM((4, clips, rows, LANES), F32),
            pltpu.VMEM((width, 2 * inner), F32),
            pltpu.VMEM((8, width), F32),
            pltpu.VMEM((frames, 4 * rows, inner), F32),
            pltpu.VMEM((clips, rows, 2 * inner), BF16),
            pltpu.VMEM((2,) + cut, F32),
            pltpu.VMEM((2,) + cut, BF16),
            pltpu.VMEM((2,) + cut, BF16),
            pltpu.VMEM(cut, BF16),
            pltpu.VMEM(cut, BF16),
            pltpu.SemaphoreType.DMA((8,)),
            pltpu.SemaphoreType.DMA((8,)),
            pltpu.SemaphoreType.DMA,
        ],
        compiler_params=params(collective_id=4, has_side_effects=True),
        name="back",
    )(
        ids,
        last,
        has,
        same,
        grad_feed,
        query_all,
        context_grad,
        tile,
        keys,
        values,
        media,
        latent_key,
        latent_value,
        gains,
        attend,
        latents,
        mixed_grad,
        gain_f,
    )


def pack_feed(expand, shrink, output):
    width = shrink.shape[-1]
    groups = expand.shape[-1] // width
    lead = expand.shape[:-2]
    rows = expand.shape[-2]
    cut = expand.reshape(lead + (rows, groups, width))
    cut = jnp.moveaxis(cut, -2, -3).reshape(lead + (groups * rows, width))
    return jnp.concatenate([cut, shrink, output], axis=-2)


def unpack_feed(packed, rows, shrink_rows):
    width = packed.shape[-1]
    lead = packed.shape[:-2]
    groups = (packed.shape[-2] - shrink_rows) // rows
    split = groups * rows
    cut = packed[..., :split, :].reshape(lead + (groups, rows, width))
    expand = jnp.moveaxis(cut, -3, -2).reshape(lead + (rows, groups * width))
    return (
        expand,
        packed[..., split : split + shrink_rows, :],
        packed[..., split + shrink_rows :, :],
    )


def step_size(width, inner, ff):
    return 0.37 * math.sqrt((4 * width * inner + 2 * width * ff) / width)


def lat_pairs(count, along_core):
    pairs = []
    for lat in range(count):
        e, c = lat // 2, lat % 2
        pairs.append((lat, e * 2 + 1 - c if along_core else (1 - e) * 2 + c))
    return pairs


def shards(
    images,
    lats,
    media,
    latents,
    counts,
    cotangent,
    attend_weight,
    output_weight,
    expand_weight,
    shrink_weight,
    layer_gains,
    layer_biases,
    attend_momentum,
    output_momentum,
    expand_momentum,
    shrink_momentum,
    gains_momentum,
    biases_momentum,
    attend_average,
    output_average,
    expand_average,
    shrink_average,
    gains_average,
    biases_average,
):
    devices = images * lats
    depth = images // 2
    fast = devices == BLOCKS and lats == 4 and images % 2 == 0
    samples, lat_dev, width = latents.shape
    rows = samples * lat_dev
    ff = expand_weight.shape[1]
    inner = attend_weight.shape[1] // 3
    patch_dev = media.shape[0]
    frames = patch_dev // PATCH_IMG
    over_core = functools.partial(lax.ppermute, axis_name="lat", perm=lat_pairs(lats, True))
    over_y = functools.partial(lax.ppermute, axis_name="lat", perm=lat_pairs(lats, False))

    attend_rows = attend_weight.shape[0]
    small = jnp.concatenate([layer_gains, layer_biases], axis=1)
    small = jnp.pad(small, ((0, 0), (0, LANES - small.shape[1])))
    attend_shard = jnp.concatenate([attend_weight, small], axis=1).astype(BF16)
    if fast:
        feed_shard = pack_feed(
            expand_weight.astype(BF16), shrink_weight.astype(BF16), output_weight.astype(BF16)
        )
        attend = gather_fast(attend_shard, depth, 1).reshape(width, attend_shard.shape[1])
    else:

        def everywhere(x):
            return lax.all_gather(x.astype(BF16), AXES, axis=0, tiled=True)

        attend = everywhere(attend_shard)
        feed = pack_feed(
            everywhere(expand_weight).reshape(BLOCKS, width // BLOCKS, ff),
            everywhere(shrink_weight).reshape(BLOCKS, ff // BLOCKS, width),
            everywhere(output_weight).reshape(BLOCKS, inner // BLOCKS, width),
        )
    gains = attend[:, 3 * inner : 3 * inner + 8].astype(F32).T

    sample_ends = jnp.cumsum(counts[0])
    first_frame = lax.axis_index("lat") * frames
    frame_ids = first_frame + jnp.arange(frames, dtype=jnp.int32)
    ids = jnp.sum((frame_ids[:, None] >= sample_ends[None, :]).astype(jnp.int32), axis=1)
    ids = jnp.clip(ids, 0, samples - 1)

    latent_flat = latents.reshape(rows, width)
    cut = (samples, lat_dev, inner)

    def to_group(own):
        other = over_y(own)
        return [own, over_core(own), other, over_core(other)]

    if fast:
        clip = jnp.arange(samples, dtype=jnp.int32)
        here = ids[None, :] == clip[:, None]
        has = jnp.any(here, axis=1).astype(jnp.int32)
        last = jnp.max(jnp.where(here, jnp.arange(frames, dtype=jnp.int32)[None, :], 0), axis=1)
        same = jnp.concatenate([jnp.zeros((1,), jnp.int32), (ids[1:] == ids[:-1]).astype(jnp.int32)])
        feed, keys, values, query_all, latent_key, latent_value, own, own_st, got, got_st = front(
            ids,
            last,
            has,
            same,
            feed_shard,
            media,
            latent_flat,
            gains,
            attend,
            samples,
            inner,
            depth,
            FRONT_PLAN,
        )
    else:
        query, latent_key, latent_value = latent_project(latent_flat, gains, attend, inner)
        latent_key = latent_key.reshape(cut)
        latent_value = latent_value.reshape(cut)
        queries = to_group(query.reshape(cut))
        keys, values = media_project(media, gains, attend, inner)
        keep, send, keep_st, send_st = attention_forward(
            ids, queries, keys, values, latent_key, latent_value
        )
        got, got_st = over_core(send), over_core(send_st)
        flat_o, flat_s = (2, rows, inner), (2, rows, LANES)
        own, own_st, away, away_st = join_cores(
            keep.reshape(flat_o),
            keep_st.reshape(flat_s),
            got.reshape(flat_o),
            got_st.reshape(flat_s),
        )
        got, got_st = over_y(away), over_y(away_st)
    cot_flat = cotangent.reshape(rows, width)
    out_rows, mixed_grad, context_grad, tile, gain_f, grad_feed = feed_forward(
        own, own_st, got, got_st, latent_flat, cot_flat, gains, feed
    )
    if fast:
        grad_media, latents_grad, grad_attend, mine_feed = back(
            ids,
            last,
            has,
            same,
            grad_feed,
            query_all,
            context_grad.reshape(cut),
            tile,
            keys,
            values,
            media,
            latent_key,
            latent_value,
            gains,
            attend,
            latent_flat,
            mixed_grad,
            gain_f,
            depth,
            16,
            BACK_PLAN,
        )
        mine = scatter_fast(
            grad_attend.reshape(BLOCKS, attend_rows, grad_attend.shape[1]), depth, 3, 16
        )
        own_expand, own_shrink, own_output = unpack_feed(
            mine_feed, attend_rows, shrink_weight.shape[0]
        )
    else:
        grads = to_group(context_grad.reshape(cut))
        tiles = to_group(tile.reshape(samples, lat_dev, LANES))
        grad_media, latent_kv, keep, send, grad_kv, gain_m = attention_backward(
            ids,
            queries,
            grads,
            tiles,
            keys,
            values,
            latent_key,
            latent_value,
            media,
            gains,
            attend,
        )
        got = over_core(send)
        pair = keep.astype(F32) + got.astype(F32)
        got = over_y(pair[1].astype(BF16))
        latents_grad, grad_attend = latent_backward(
            latent_flat,
            mixed_grad,
            pair[0].reshape(rows, inner),
            got.reshape(rows, inner),
            latent_kv.reshape(rows, 2 * inner),
            gains,
            attend,
            grad_kv,
            gain_m,
            gain_f,
        )

        def owners(x):
            return lax.psum_scatter(x.astype(F32), AXES, scatter_dimension=0, tiled=True)

        mine = owners(grad_attend)
        own_expand, own_shrink, own_output = unpack_feed(grad_feed, width // BLOCKS, ff // BLOCKS)
        own_expand = owners(own_expand.reshape(width, ff))
        own_shrink = owners(own_shrink.reshape(ff, width))
        own_output = owners(own_output.reshape(inner, width))
    small = mine[:, 3 * inner :]
    owned = (
        mine[:, : 3 * inner],
        own_output,
        own_expand,
        own_shrink,
        small[:, 0:3],
        small[:, 3:6],
    )
    squares = sum(jnp.sum(piece * piece) for piece in owned)
    if fast:
        squares = total_fast(jnp.full((8, LANES), squares, F32), images, lats, 5)[0, 0]
    else:
        squares = lax.psum(squares, AXES)
    grad_norm = jnp.sqrt(squares)
    factor = jnp.minimum(1.0, CLIP_NORM / (grad_norm + 1e-06))
    masters = (
        attend_weight,
        output_weight,
        expand_weight,
        shrink_weight,
        layer_gains,
        layer_biases,
    )
    moments = (
        attend_momentum,
        output_momentum,
        expand_momentum,
        shrink_momentum,
        gains_momentum,
        biases_momentum,
    )
    averages = (
        attend_average,
        output_average,
        expand_average,
        shrink_average,
        gains_average,
        biases_average,
    )
    decay_rates = (DECAY, DECAY, DECAY, DECAY, 0.0, 0.0)
    step_rate = step_size(width, inner, ff)
    new_masters = []
    new_buffers = []
    new_smoothed = []
    for master, moment, average, reduced, decay_rate, rate_scale in zip(
        masters, moments, averages, owned, decay_rates, RATE_SCALES
    ):
        step_grad = factor * reduced + decay_rate * master
        buffer = MOMENTUM * moment + step_grad
        master_new = master - step_rate * rate_scale * (step_grad + MOMENTUM * buffer)
        new_masters.append(master_new)
        new_buffers.append(buffer)
        new_smoothed.append(AVERAGING * average + (1.0 - AVERAGING) * master_new)
    return (
        out_rows.reshape(latents.shape),
        grad_media,
        latents_grad.reshape(latents.shape),
        grad_norm,
        *new_masters,
        *new_buffers,
        *new_smoothed,
    )


def solution(mesh):
    rows = P(AXES, None)
    split = P("img", "lat", None)
    return jax.shard_map(
        functools.partial(shards, mesh.shape["img"], mesh.shape["lat"]),
        mesh=mesh,
        in_specs=(rows, split, P("img", None), split) + (rows,) * 18,
        out_specs=(split, rows, split, P()) + (rows,) * 18,
        check_vma=False,
    )
```

```python
import functools
import math

import jax
import jax.numpy as jnp
from jax import lax
from jax.experimental import pallas as pl
from jax.experimental.pallas import tpu as pltpu
from jax.sharding import PartitionSpec as P

HEADS = 8
HDIM = 64
PATCH_IMG = 256
GROUP = 4
EPS = 1e-05
MOMENTUM = 0.9
DECAY = 0.0001
AVERAGING = 0.6
CLIP_NORM = 1.0
RATE_SCALES = (1.0, 100.0, 1.0, 1.0, 15.0, 1.0)
AXES = ("img", "lat")
LANES = 128
BLOCKS = 32
SCALE = HDIM ** (-0.5)
MASKED = -1e30
F32 = jnp.float32
BF16 = jnp.bfloat16
MESH = pl.DeviceIdType.MESH
HEAD_PLAN = (
    (3, "ea1 ez2 eb0"),
    (10, "ez3"),
    (12, "eb1 ea2"),
    (17, "ec0 eb2 ea3 sz1"),
    (23, "ec1 eb3 sa0"),
    (26, "ec2 ec3 sa1 sz2 sb0"),
)
HEAD_LATE = ("sz3", "sc0 sb1 sa2", "", "", "sc1 sb2 sa3", "sc2 sb3", "sc3")
BACK_PLAN = (
    (0, "a0"),
    (1, "a1"),
    (2, "a2"),
    (3, "a3"),
    (5, "b0"),
    (7, "c0 b1"),
    (10, "c1 b2"),
    (12, "c2"),
    (13, "b3 c3"),
)
VMEM_LIMIT = 60 * 1024 * 1024


def mm(a, b):
    return jnp.dot(a, b, preferred_element_type=F32)


def mm_tn(a, b):
    return lax.dot_general(a, b, (((0,), (0,)), ((), ())), preferred_element_type=F32)


def mm_nt(a, b):
    return lax.dot_general(a, b, (((1,), (1,)), ((), ())), preferred_element_type=F32)


def any_spec():
    return pl.BlockSpec(memory_space=pl.ANY)


def vmem_spec():
    return pl.BlockSpec(memory_space=pltpu.VMEM)


def params(**more):
    return pltpu.CompilerParams(vmem_limit_bytes=VMEM_LIMIT, **more)


def place():
    img = lax.axis_index("img")
    lat = lax.axis_index("lat")
    return img // 2, img % 2, lat // 2, lat % 2


def flat(a, b, e, c):
    return ((a * 2 + b) * 2 + e) * 2 + c


def device(a, b, e, c):
    return (a * 2 + b, e * 2 + c)


def first_partner(a, b, e, c):
    return a, (b + 1 - c) % 2, (e + c) % 2, c


def second_partner(a, b, e, c):
    return a, (b + c) % 2, (e + 1 - c) % 2, c


def z_order(depth):
    order = [0]
    for k in range(1, depth // 2 + 1):
        order.append(k)
        if depth - k != k:
            order.append(depth - k)
    return order


def greet(depth, a, b, e, c):
    barrier = pltpu.get_barrier_semaphore()
    friends = [device((a + k) % depth, b, e, c) for k in range(1, depth)]
    friends += [
        device(*first_partner(a, b, e, c)),
        device(*second_partner(a, b, e, c)),
        device(a, b, e, 1 - c),
    ]
    for friend in friends:
        pl.semaphore_signal(barrier, inc=1, device_id=friend, device_id_type=MESH)
    pl.semaphore_wait(barrier, len(friends))


def add_into(target, first, second, rows, chunk):
    @pl.loop(0, rows // chunk)
    def _(step):
        part = pl.ds(step * chunk, chunk)
        total = first[part, :].astype(F32) + second[part, :].astype(F32)
        target[part, :] = total.astype(target.dtype)


def normalise(values):
    center = values - jnp.mean(values, axis=-1, keepdims=True)
    spread = jnp.mean(center * center, axis=-1, keepdims=True)
    scale = lax.rsqrt(spread + EPS)
    return center * scale, scale


def norm_back(grad, hat, scale, gain):
    inner = grad * gain
    first = jnp.mean(inner, axis=-1, keepdims=True)
    second = jnp.mean(inner * hat, axis=-1, keepdims=True)
    return scale * (inner - first - hat * second)


def media_kernel(m_ref, gb_ref, wk_ref, wv_ref, k_ref, v_ref):
    hat, _ = normalise(m_ref[...].astype(F32))
    normed = (hat * gb_ref[0:1, :] + gb_ref[3:4, :]).astype(BF16)
    k_ref[...] = mm(normed, wk_ref[...]).astype(BF16)
    v_ref[...] = mm(normed, wv_ref[...]).astype(BF16)


def media_project(media, gains, attend, inner):
    rows, width = media.shape
    out = jax.ShapeDtypeStruct((rows, inner), BF16)
    block = pl.BlockSpec((PATCH_IMG, inner), lambda i: (i, 0))
    return pl.pallas_call(
        media_kernel,
        grid=(rows // PATCH_IMG,),
        out_shape=(out, out),
        in_specs=[
            pl.BlockSpec((PATCH_IMG, width), lambda i: (i, 0)),
            pl.BlockSpec(gains.shape, lambda i: (0, 0)),
            pl.BlockSpec((width, inner), lambda i: (0, 1)),
            pl.BlockSpec((width, inner), lambda i: (0, 2)),
        ],
        out_specs=(block, block),
        compiler_params=params(),
        cost_estimate=pl.CostEstimate(
            flops=4 * rows * width * inner, bytes_accessed=4 * rows * width, transcendentals=0
        ),
        name="media_project",
    )(media, gains, attend, attend)


def latent_kernel(l_ref, gb_ref, w_ref, q_ref, k_ref, v_ref):
    inner = q_ref.shape[1]
    hat, _ = normalise(l_ref[...])
    normed = (hat * gb_ref[1:2, :] + gb_ref[4:5, :]).astype(BF16)
    q_ref[...] = mm(normed, w_ref[:, :inner]).astype(BF16)
    k_ref[...] = mm(normed, w_ref[:, inner : 2 * inner]).astype(BF16)
    v_ref[...] = mm(normed, w_ref[:, 2 * inner : 3 * inner]).astype(BF16)


def latent_project(latents, gains, attend, inner):
    out = jax.ShapeDtypeStruct((latents.shape[0], inner), BF16)
    return pl.pallas_call(
        latent_kernel,
        out_shape=(out, out, out),
        in_specs=[vmem_spec()] * 3,
        out_specs=(vmem_spec(),) * 3,
        compiler_params=params(),
        name="latent_project",
    )(latents, gains, attend)


def head_mask(kind):
    rows = lax.broadcasted_iota(jnp.int32, (GROUP * HDIM, GROUP * HDIM), 0) // HDIM
    cols = lax.broadcasted_iota(jnp.int32, (GROUP * HDIM, GROUP * HDIM), 1) // HDIM
    return (rows == cols).astype(F32).astype(kind)


def spread_heads(queries, group, mask):
    width = GROUP * HDIM
    part = queries[:, group * width : (group + 1) * width]
    return jnp.concatenate([part] * GROUP, axis=0) * mask


def take_heads(full, mask):
    total = None
    for h in range(GROUP):
        part = slice(h * HDIM, (h + 1) * HDIM)
        term = full[part, :] * mask[part, :]
        total = term if total is None else total + term
    return total


def pack_columns(columns, first=0):
    rows = columns[0].shape[0]
    lane = lax.broadcasted_iota(jnp.int32, (rows, LANES), 1)
    tile = jnp.zeros((rows, LANES), F32)
    for h, column in enumerate(columns):
        tile = jnp.where(lane == first + h, column, tile)
    return tile


def expand_columns(tile, width):
    rows = tile.shape[0]
    head = lax.broadcasted_iota(jnp.int32, (rows, width), 1) // HDIM
    out = jnp.zeros((rows, width), F32)
    for h in range(width // HDIM):
        out = jnp.where(head == h, tile[:, h : h + 1], out)
    return out


def forward_kernel(
    ids, q0, q1, q2, q3, k_ref, v_ref, kl_ref, vl_ref, keep, send, keep_st, send_st, acc, tops, sums
):
    step = pl.program_id(0)
    clips = acc.shape[0]
    inner = acc.shape[2]
    groups = inner // (GROUP * HDIM)
    width = GROUP * HDIM
    mask = head_mask(F32)
    mask_half = mask.astype(BF16)

    def clip_queries(clip):
        parts = [q[clip] for q in (q0, q1, q2, q3)]
        return jnp.concatenate(parts, axis=0) * BF16(SCALE)

    def attend(clip, keys, values, fresh):
        queries = clip_queries(clip)
        new_tops, new_sums = [], []
        for g in range(groups):
            cols = slice(g * width, (g + 1) * width)
            scores = mm_nt(spread_heads(queries, g, mask_half), keys[:, cols])
            top = jnp.max(scores, axis=-1, keepdims=True)
            if not fresh:
                old_tile = tops[clip]
                old_top = jnp.concatenate(
                    [old_tile[:, g * GROUP + h : g * GROUP + h + 1] for h in range(GROUP)], axis=0
                )
                top = jnp.maximum(top, old_top)
            probs = jnp.exp(scores - top)
            total = jnp.sum(probs, axis=-1, keepdims=True)
            part = take_heads(mm(probs.astype(BF16), values[:, cols]), mask)
            if not fresh:
                old_tile = sums[clip]
                old_sum = jnp.concatenate(
                    [old_tile[:, g * GROUP + h : g * GROUP + h + 1] for h in range(GROUP)], axis=0
                )
                shrink = jnp.exp(old_top - top)
                total = total + old_sum * shrink
                part = part + acc[clip, :, cols] * take_heads(shrink, mask)
            acc[clip, :, cols] = part
            for h in range(GROUP):
                new_tops.append(top[h * HDIM : (h + 1) * HDIM])
                new_sums.append(total[h * HDIM : (h + 1) * HDIM])
        tops[clip] = pack_columns(new_tops)
        sums[clip] = pack_columns(new_sums)

    @pl.when(step == 0)
    def _():
        @pl.loop(0, clips)
        def _(clip):
            attend(clip, kl_ref[clip], vl_ref[clip], True)

    attend(ids[step], k_ref[...], v_ref[...], False)

    @pl.when(step == pl.num_programs(0) - 1)
    def _():
        rows = keep.shape[2]
        lane = lax.broadcasted_iota(jnp.int32, (HDIM, LANES), 1)

        @pl.loop(0, clips)
        def _(clip):
            total = jnp.where(lane < HEADS, sums[clip], 1.0)
            stat = tops[clip] + jnp.log(total)
            out = (acc[clip] / expand_columns(total, inner)).astype(BF16)
            for r in range(4):
                part = slice(r * rows, (r + 1) * rows)
                where_o, where_s = (send, send_st) if r % 2 else (keep, keep_st)
                where_o[r // 2, clip] = out[part]
                where_s[r // 2, clip] = stat[part]


def attention_forward(ids, queries, keys, values, latent_keys, latent_values):
    clips, rows, inner = queries[0].shape
    frames = keys.shape[0] // PATCH_IMG
    out = jax.ShapeDtypeStruct((2, clips, rows, inner), BF16)
    stat = jax.ShapeDtypeStruct((2, clips, rows, LANES), F32)
    block = pl.BlockSpec((PATCH_IMG, inner), lambda i, ids: (i, 0))

    def whole(shape):
        return pl.BlockSpec(shape, lambda i, ids: (0,) * len(shape))

    return pl.pallas_call(
        forward_kernel,
        grid_spec=pltpu.PrefetchScalarGridSpec(
            num_scalar_prefetch=1,
            grid=(frames,),
            in_specs=[whole((clips, rows, inner))] * 4
            + [block, block]
            + [whole((clips, rows, inner))] * 2,
            out_specs=(whole(out.shape), whole(out.shape), whole(stat.shape), whole(stat.shape)),
            scratch_shapes=[
                pltpu.VMEM((clips, 4 * rows, inner), F32),
                pltpu.VMEM((clips, 4 * rows, LANES), F32),
                pltpu.VMEM((clips, 4 * rows, LANES), F32),
            ],
        ),
        out_shape=(out, out, stat, stat),
        compiler_params=params(),
        name="attention_forward",
    )(ids, *queries, keys, values, latent_keys, latent_values)


def join_partials(first, first_stat, second, second_stat):
    width = first.shape[-1]
    top = jnp.maximum(first_stat, second_stat)
    total = jnp.exp(first_stat - top) + jnp.exp(second_stat - top)
    stat = top + jnp.log(total)
    out = first.astype(F32) * expand_columns(jnp.exp(first_stat - stat), width)
    out = out + second.astype(F32) * expand_columns(jnp.exp(second_stat - stat), width)
    return out, stat


def join_kernel(keep, keep_st, got, got_st, own, own_st, away, away_st):
    out, stat = join_partials(keep[0], keep_st[0], got[0], got_st[0])
    own[...] = out
    own_st[...] = stat
    out, stat = join_partials(keep[1], keep_st[1], got[1], got_st[1])
    away[...] = out.astype(BF16)
    away_st[...] = stat


def join_cores(keep, keep_st, got, got_st):
    _, rows, inner = keep.shape
    stat = jax.ShapeDtypeStruct((rows, LANES), F32)
    return pl.pallas_call(
        join_kernel,
        out_shape=(
            jax.ShapeDtypeStruct((rows, inner), F32),
            stat,
            jax.ShapeDtypeStruct((rows, inner), BF16),
            stat,
        ),
        in_specs=[vmem_spec()] * 4,
        out_specs=(vmem_spec(),) * 4,
        compiler_params=params(),
        name="join_cores",
    )(keep, keep_st, got, got_st)


class Gather:
    def __init__(self, depth, x_ref, o_ref, local_sem, send_sem, recv_sem):
        self.depth = depth
        self.refs = x_ref, o_ref
        self.sems = local_sem, send_sem, recv_sem
        self.at = place()
        one = first_partner(*self.at)
        two = second_partner(*self.at)
        self.homes = [self.at, one, two, second_partner(*one)]
        self.order = z_order(depth)

    def row(self, k, j):
        a, _, _, c = self.at
        _, b, e, _ = self.homes[j % 4]
        return flat((a - k) % self.depth, b, e, c if j < 4 else 1 - c)

    def copy(self, k, j):
        x_ref, o_ref = self.refs
        a, b, e, c = self.at
        base = {1: 0, 2: 0, 3: 1}.get(j, j - 4)
        if j == 0:
            target, row, src = ((a + k) % self.depth, b, e, c), flat(a, b, e, c), x_ref
        else:
            target = self.homes[1] if j == 1 else self.homes[2] if j < 4 else (a, b, e, 1 - c)
            row = self.row(k, base)
            src = x_ref if (k, base) == (0, 0) else o_ref.at[row]
        slot = k * 8 + j
        return pltpu.make_async_remote_copy(
            src_ref=src,
            dst_ref=o_ref.at[row],
            send_sem=self.sems[1].at[slot],
            recv_sem=self.sems[2].at[slot],
            device_id=device(*target),
            device_id_type=MESH,
        )

    def arrive(self, k, j):
        x_ref, o_ref = self.refs
        a, b, e, c = self.at
        slot = k * 8 + j
        pltpu.make_async_remote_copy(
            src_ref=x_ref,
            dst_ref=o_ref.at[self.row(k, j)],
            send_sem=self.sems[1].at[slot],
            recv_sem=self.sems[2].at[slot],
            device_id=device(a, b, e, 1 - c),
            device_id_type=MESH,
        ).wait_recv()

    def own(self):
        x_ref, o_ref = self.refs
        return pltpu.make_async_copy(x_ref, o_ref.at[flat(*self.at)], self.sems[0])

    def far(self, k):
        self.copy(k, 0).start()

    def begin(self):
        self.far(self.order[1])
        self.first(0)

    def settle(self, k=None):
        for k in self.order if k is None else [k]:
            for j in range(4, 8):
                self.arrive(k, j)
            if k == 0:
                self.own().wait()

    def first(self, k):
        if k:
            self.arrive(k, 0)
        for j in (1, 2, 4):
            self.copy(k, j).start()

    def second(self, k):
        self.arrive(k, 1)
        self.copy(k, 3).start()
        self.copy(k, 5).start()
        self.arrive(k, 2)
        self.copy(k, 6).start()

    def third(self, k):
        self.arrive(k, 3)
        self.copy(k, 7).start()

    def run(self, names):
        acts = {"z": self.far, "a": self.first, "b": self.second, "c": self.third}
        for name in names.split():
            acts[name[0]](self.order[int(name[1:])])

    def finish(self):
        for k in range(self.depth):
            for j in range(8):
                if k or j:
                    self.copy(k, j).wait_send()


def start_kernel(
    depth,
    w_ref,
    g_ref,
    b_ref,
    expand_ref,
    shrink_ref,
    output_ref,
    all_ref,
    shard_e,
    shard_s,
    gains_ref,
    shard,
    small,
    local_sem,
    send_sem,
    recv_sem,
    small_sem,
):
    rows, cols = w_ref.shape
    gather = Gather(depth, shard, all_ref, local_sem, send_sem, recv_sem)
    shard[:, :cols] = w_ref[...].astype(BF16)
    zeros = jnp.zeros((LANES - 6, rows), F32)
    lines = jnp.concatenate([g_ref[...], b_ref[...], zeros], axis=0)
    shard[:, cols:] = lines.T.astype(BF16)
    greet(depth, *gather.at)
    gather.own().start()
    gather.begin()
    gather.run("z2 z3")
    width = output_ref.shape[1]
    groups = expand_ref.shape[1] // width
    for n in range(groups):
        shard_e[n * rows : (n + 1) * rows, :] = expand_ref[:, n * width : (n + 1) * width].astype(BF16)
    shard_e[groups * rows :, :] = output_ref[...].astype(BF16)
    shard_s[...] = shrink_ref[...].astype(BF16)
    gather.run("b0 a1 c0 b1 a2 c1 b2 a3 c2 b3 c3")
    gather.settle()
    load = pltpu.make_async_copy(all_ref.at[:, :, pl.ds(cols, LANES)], small, small_sem)
    load.start()
    load.wait()
    lines = small[...].reshape(depth * 8 * rows, LANES).astype(F32).T
    gains_ref[...] = lines[:8]
    gather.finish()


def start(weight, gains, biases, expand, shrink, output, depth):
    rows, cols = weight.shape
    count = depth * 8
    width = output.shape[1]
    rows_e = expand.shape[1] // width * rows + output.shape[0]
    return pl.pallas_call(
        functools.partial(start_kernel, depth),
        out_shape=(
            jax.ShapeDtypeStruct((count, rows, cols + LANES), BF16),
            jax.ShapeDtypeStruct((rows_e, width), BF16),
            jax.ShapeDtypeStruct(shrink.shape, BF16),
            jax.ShapeDtypeStruct((8, count * rows), F32),
        ),
        in_specs=[vmem_spec()] * 6,
        out_specs=(any_spec(), vmem_spec(), vmem_spec(), vmem_spec()),
        scratch_shapes=[
            pltpu.VMEM((rows, cols + LANES), BF16),
            pltpu.VMEM((count, rows, LANES), BF16),
            pltpu.SemaphoreType.DMA,
            pltpu.SemaphoreType.DMA((count,)),
            pltpu.SemaphoreType.DMA((count,)),
            pltpu.SemaphoreType.DMA,
        ],
        compiler_params=params(collective_id=1, has_side_effects=True),
        name="start",
    )(weight, gains, biases, expand, shrink, output)


def latent_mask(rows, inner):
    row = lax.broadcasted_iota(jnp.int32, (HEADS * rows, inner), 0) // rows
    col = lax.broadcasted_iota(jnp.int32, (HEADS * rows, inner), 1) // HDIM
    return (row == col).astype(F32)


def latent_attention(queries, keys, values, mask):
    rows = keys.shape[0]
    count = queries.shape[0]
    half = mask.astype(BF16)
    wide_k = jnp.concatenate([keys] * HEADS, axis=0) * half
    wide_v = jnp.concatenate([values] * HEADS, axis=0) * half
    scores = mm_nt(wide_k, queries).reshape(HEADS, rows, count)
    top = jnp.max(scores, axis=1, keepdims=True)
    probs = jnp.exp(scores - top)
    total = jnp.sum(probs, axis=1)
    out = mm_tn(probs.reshape(HEADS * rows, count).astype(BF16), wide_v)
    zeros = jnp.zeros((LANES - HEADS, count), F32)

    def tile(x):
        return jnp.concatenate([x, zeros], axis=0).T

    return out, tile(top.reshape(HEADS, count)), tile(total)


def remote_copy(src, dst, sems, slot, target):
    return pltpu.make_async_remote_copy(
        src_ref=src,
        dst_ref=dst,
        send_sem=sems[0].at[slot],
        recv_sem=sems[1].at[slot],
        device_id=device(*target),
        device_id_type=MESH,
    )


def feed_kernel(
    own,
    own_st,
    got,
    got_st,
    lat_ref,
    cot_ref,
    gb_ref,
    w_ref,
    out_ref,
    mixed_grad,
    context_grad,
    tile_ref,
    gain_ref,
    gw_ref,
    expand_v,
    shrink_v,
    output_v,
    grad_e,
    grad_s,
    grad_o,
    normed_v,
    normed_t,
    hat_v,
    acc_g,
    load_sem,
    store_sem,
):
    groups = expand_v.shape[0]
    width = expand_v.shape[3]
    blocks = expand_v.shape[1]
    shrink_rows = shrink_v.shape[1]
    per_group = blocks // groups
    expand_rows = expand_v.shape[2]
    shrink_at = groups * expand_rows
    output_at = shrink_at + shrink_rows
    output_rows = output_v.shape[1]
    half = width // 2
    inner = own.shape[1]

    def load_expand(g):
        return pltpu.make_async_copy(
            w_ref.at[:, pl.ds(g * expand_rows, expand_rows), :], expand_v.at[g], load_sem.at[g]
        )

    def load_shrink(g):
        part = pl.ds(g * per_group, per_group)
        return pltpu.make_async_copy(
            w_ref.at[part, pl.ds(shrink_at, shrink_rows), :],
            shrink_v.at[part],
            load_sem.at[groups + g],
        )

    load_output = pltpu.make_async_copy(
        w_ref.at[:, pl.ds(output_at, output_rows), :], output_v, load_sem.at[2 * groups]
    )
    load_output.start()
    for g in range(groups):
        load_expand(g).start()
        load_shrink(g).start()

    context, stat = join_partials(own[...], own_st[...], got[...], got_st[...])
    context_half = context.astype(BF16)
    load_output.wait()
    weight_o = output_v[...].reshape(inner, width)
    mixed = lat_ref[...] + mm(context_half, weight_o)
    hat, scale = normalise(mixed)
    hat_v[...] = hat
    normed = (hat * gb_ref[2:3, :] + gb_ref[5:6, :]).astype(BF16)
    normed_v[...] = normed
    normed_t[...] = normed.astype(F32).T.astype(BF16)
    out_ref[...] = mixed
    acc_g[...] = jnp.zeros_like(acc_g)

    def store_e(s, slot):
        return pltpu.make_async_copy(
            grad_e.at[slot],
            gw_ref.at[:, pl.ds((s // 2) * expand_rows, expand_rows), pl.ds((s % 2) * half, half)],
            store_sem.at[slot],
        )

    def store_s(s, slot):
        rows = half // shrink_rows
        return pltpu.make_async_copy(
            grad_s.at[slot],
            gw_ref.at[pl.ds(s * rows, rows), pl.ds(shrink_at, shrink_rows), :],
            store_sem.at[2 + slot],
        )

    cot = cot_ref[...]
    steps = 2 * groups
    for s in range(steps):
        g, slot = s // 2, s % 2
        if slot == 0:
            load_expand(g).wait()
            load_shrink(g).wait()
        cols = slice(slot * half, (slot + 1) * half)
        w_e = expand_v[g, :, :, cols].reshape(blocks * expand_rows, half)
        first = s * half // shrink_rows
        w_s = shrink_v[first : first + half // shrink_rows].reshape(half, width)
        pre = mm(normed_v[...], w_e)
        cdf = 0.5 * (1.0 + lax.erf(pre * (0.5**0.5)))
        hidden = (pre * cdf).astype(BF16)
        out_ref[...] += mm(hidden, w_s)
        grad_hidden = mm_nt(cot, w_s)
        pdf = jnp.exp(-0.5 * pre * pre) * (1.0 / math.sqrt(2.0 * math.pi))
        grad_pre = (grad_hidden * (cdf + pre * pdf)).astype(BF16)
        if s >= 2:
            store_e(s - 2, slot).wait()
            store_s(s - 2, slot).wait()
        grad_s[slot] = mm_tn(hidden, cot).astype(BF16).reshape(half // shrink_rows, shrink_rows, width)
        grad_e[slot] = (
            mm(normed_t[...], grad_pre).astype(BF16).reshape(blocks, expand_rows, half)
        )
        store_e(s, slot).start()
        store_s(s, slot).start()
        acc_g[...] += mm_nt(grad_pre, w_e)

    grad_normed = acc_g[...]
    hat = hat_v[...]
    rows = gain_ref.shape[0]
    gain_ref[...] = jnp.concatenate(
        [
            jnp.sum(grad_normed * hat, axis=0, keepdims=True),
            jnp.sum(grad_normed, axis=0, keepdims=True),
            jnp.zeros((rows - 2, width), F32),
        ],
        axis=0,
    )
    total = cot.astype(F32) + norm_back(grad_normed, hat, scale, gb_ref[2:3, :])
    mixed_grad[...] = total
    attended = total.astype(BF16)
    grad_o[...] = mm_tn(context_half, attended).astype(BF16).reshape(grad_o.shape)
    store_o = pltpu.make_async_copy(
        grad_o, gw_ref.at[:, pl.ds(output_at, output_rows), :], store_sem.at[4]
    )
    store_o.start()
    grad_c = mm_nt(attended, weight_o).astype(BF16)
    context_grad[...] = grad_c
    product = grad_c.astype(F32) * context
    head = lax.broadcasted_iota(jnp.int32, product.shape, 1) // HDIM
    deltas = [
        jnp.sum(jnp.where(head == h, product, 0.0), axis=-1, keepdims=True) for h in range(HEADS)
    ]
    lane = lax.broadcasted_iota(jnp.int32, stat.shape, 1)
    tile_ref[...] = jnp.where(lane < HEADS, stat, pack_columns(deltas, HEADS))
    for s in range(steps - 2, steps):
        store_e(s, s % 2).wait()
        store_s(s, s % 2).wait()
    store_o.wait()


def feed_forward(own, own_st, got, got_st, latents, cotangent, gains, weights):
    rows, width = latents.shape
    inner = own.shape[1]
    blocks = weights.shape[0]
    ff = 4 * width
    groups = ff // width
    expand_rows = width // blocks
    shrink_rows = ff // blocks
    output_rows = inner // blocks
    half = width // 2
    flops = 2 * rows * (6 * width * ff + 3 * width * inner)
    return pl.pallas_call(
        feed_kernel,
        out_shape=(
            jax.ShapeDtypeStruct((rows, width), F32),
            jax.ShapeDtypeStruct((rows, width), F32),
            jax.ShapeDtypeStruct((rows, inner), BF16),
            jax.ShapeDtypeStruct((rows, LANES), F32),
            jax.ShapeDtypeStruct((8, width), F32),
            jax.ShapeDtypeStruct(weights.shape, BF16),
        ),
        in_specs=[vmem_spec()] * 7 + [any_spec()],
        out_specs=(vmem_spec(),) * 5 + (any_spec(),),
        scratch_shapes=[
            pltpu.VMEM((groups, blocks, expand_rows, width), BF16),
            pltpu.VMEM((blocks, shrink_rows, width), BF16),
            pltpu.VMEM((blocks, output_rows, width), BF16),
            pltpu.VMEM((2, blocks, expand_rows, half), BF16),
            pltpu.VMEM((2, half // shrink_rows, shrink_rows, width), BF16),
            pltpu.VMEM((blocks, output_rows, width), BF16),
            pltpu.VMEM((rows, width), BF16),
            pltpu.VMEM((width, rows), BF16),
            pltpu.VMEM((rows, width), F32),
            pltpu.VMEM((rows, width), F32),
            pltpu.SemaphoreType.DMA((2 * groups + 1,)),
            pltpu.SemaphoreType.DMA((5,)),
        ],
        compiler_params=params(),
        cost_estimate=pl.CostEstimate(
            flops=flops, bytes_accessed=4 * weights.size, transcendentals=2 * rows * ff
        ),
        name="feed_forward",
    )(own, own_st, got, got_st, latents, cotangent, gains, weights)


def backward_kernel(
    ids,
    q0,
    q1,
    q2,
    q3,
    g0,
    g1,
    g2,
    g3,
    t0,
    t1,
    t2,
    t3,
    k_ref,
    v_ref,
    kl_ref,
    vl_ref,
    m_ref,
    gb_ref,
    wk_ref,
    wv_ref,
    media_grad,
    latent_kv,
    keep,
    send,
    weight_grad,
    gain_ref,
    acc,
):
    step = pl.program_id(0)
    clips = acc.shape[0]
    inner = acc.shape[2]
    groups = inner // (GROUP * HDIM)
    width = GROUP * HDIM
    mask = head_mask(F32)
    mask_half = mask.astype(BF16)

    def attend(clip, keys, values, fresh):
        queries = jnp.concatenate([q[clip] for q in (q0, q1, q2, q3)], axis=0) * BF16(SCALE)
        grads = jnp.concatenate([g[clip] for g in (g0, g1, g2, g3)], axis=0)
        stats = jnp.concatenate([t[clip] for t in (t0, t1, t2, t3)], axis=0).T
        key_parts, value_parts = [], []
        for g in range(groups):
            cols = slice(g * width, (g + 1) * width)

            def line(first):
                at = first + g * GROUP
                return jnp.concatenate([stats[at + h : at + h + 1, :] for h in range(GROUP)], axis=1)

            wide_q = spread_heads(queries, g, mask_half)
            wide_g = spread_heads(grads, g, mask_half)
            probs = jnp.exp(mm_nt(keys[:, cols], wide_q) - line(0))
            grad_probs = mm_nt(values[:, cols], wide_g)
            grad_scores = (probs * (grad_probs - line(HEADS))).astype(BF16)
            key_parts.append(mm(grad_scores, wide_q))
            value_parts.append(mm(probs.astype(BF16), wide_g))
            part = take_heads(mm_tn(grad_scores, keys[:, cols]), mask)
            if fresh:
                acc[clip, :, cols] = part
            else:
                acc[clip, :, cols] += part
        return jnp.concatenate(key_parts + value_parts, axis=1).astype(BF16)

    @pl.when(step == 0)
    def _():
        gain_ref[...] = jnp.zeros_like(gain_ref)
        weight_grad[...] = jnp.zeros_like(weight_grad)

        @pl.loop(0, clips)
        def _(clip):
            latent_kv[clip] = attend(clip, kl_ref[clip], vl_ref[clip], True)

    grad_kv = attend(ids[step], k_ref[...], v_ref[...], False)
    hat, scale = normalise(m_ref[...].astype(F32))
    gain = gb_ref[0:1, :]
    normed = (hat * gain + gb_ref[3:4, :]).astype(BF16)
    weight_grad[...] += mm_tn(normed, grad_kv)
    grad = mm_nt(grad_kv[:, :inner], wk_ref[...]) + mm_nt(grad_kv[:, inner:], wv_ref[...])
    gain_ref[0:1, :] += jnp.sum(grad * hat, axis=0, keepdims=True)
    gain_ref[1:2, :] += jnp.sum(grad, axis=0, keepdims=True)
    media_grad[...] = norm_back(grad, hat, scale, gain).astype(BF16)

    @pl.when(step == pl.num_programs(0) - 1)
    def _():
        rows = keep.shape[2]

        @pl.loop(0, clips)
        def _(clip):
            out = (acc[clip] * SCALE).astype(BF16)
            for r in range(4):
                part = slice(r * rows, (r + 1) * rows)
                where_o = send if r % 2 else keep
                where_o[r // 2, clip] = out[part]


def attention_backward(
    ids, queries, grads, tiles, keys, values, latent_keys, latent_values, media, gains, attend
):
    clips, rows, inner = queries[0].shape
    width = media.shape[1]
    frames = keys.shape[0] // PATCH_IMG
    block = pl.BlockSpec((PATCH_IMG, inner), lambda i, ids: (i, 0))
    wide = pl.BlockSpec((PATCH_IMG, width), lambda i, ids: (i, 0))

    def whole(shape):
        return pl.BlockSpec(shape, lambda i, ids: (0,) * len(shape))

    def column(n):
        return pl.BlockSpec((width, inner), lambda i, ids: (0, n))

    query = whole((clips, rows, inner))
    pair = (2, clips, rows, inner)
    return pl.pallas_call(
        backward_kernel,
        grid_spec=pltpu.PrefetchScalarGridSpec(
            num_scalar_prefetch=1,
            grid=(frames,),
            in_specs=[query] * 8
            + [whole((clips, rows, LANES))] * 4
            + [block, block, query, query, wide, whole(gains.shape), column(1), column(2)],
            out_specs=(
                wide,
                whole((clips, rows, 2 * inner)),
                whole(pair),
                whole(pair),
                whole((width, 2 * inner)),
                whole((8, width)),
            ),
            scratch_shapes=[pltpu.VMEM((clips, 4 * rows, inner), F32)],
        ),
        out_shape=(
            jax.ShapeDtypeStruct(media.shape, BF16),
            jax.ShapeDtypeStruct((clips, rows, 2 * inner), BF16),
            jax.ShapeDtypeStruct(pair, BF16),
            jax.ShapeDtypeStruct(pair, BF16),
            jax.ShapeDtypeStruct((width, 2 * inner), F32),
            jax.ShapeDtypeStruct((8, width), F32),
        ),
        compiler_params=params(),
        name="attention_backward",
    )(
        ids,
        *queries,
        *grads,
        *tiles,
        keys,
        values,
        latent_keys,
        latent_values,
        media,
        gains,
        attend,
        attend,
    )


def last_kernel(
    lat_ref, mixed_grad, first, second, kv_ref, gb_ref, w_ref, gw_ref, gm_ref, gf_ref, out_ref, pack_ref
):
    inner = first.shape[1]
    width = lat_ref.shape[1]
    hat, scale = normalise(lat_ref[...])
    gain = gb_ref[1:2, :]
    normed = (hat * gain + gb_ref[4:5, :]).astype(BF16)
    grad_q = (first[...].astype(F32) + second[...].astype(F32)).astype(BF16)
    grad_kv = kv_ref[...]
    grad = mm_nt(grad_q, w_ref[:, :inner]) + mm_nt(grad_kv, w_ref[:, inner : 3 * inner])
    pack_ref[:, :inner] = mm_tn(normed, grad_q).astype(BF16)
    pack_ref[:, inner : 3 * inner] = (gw_ref[...] + mm_tn(normed, grad_kv)).astype(BF16)
    lines = jnp.concatenate(
        [
            gm_ref[0:1, :],
            jnp.sum(grad * hat, axis=0, keepdims=True),
            gf_ref[0:1, :],
            gm_ref[1:2, :],
            jnp.sum(grad, axis=0, keepdims=True),
            gf_ref[1:2, :],
            jnp.zeros((LANES - 6, width), F32),
        ],
        axis=0,
    )
    pack_ref[:, 3 * inner :] = lines.T.astype(BF16)
    out_ref[...] = mixed_grad[...] + norm_back(grad, hat, scale, gain)


def latent_backward(latents, mixed_grad, first, second, grad_kv, gains, attend, grad_w, gain_m, gain_f):
    return pl.pallas_call(
        last_kernel,
        out_shape=(
            jax.ShapeDtypeStruct(latents.shape, F32),
            jax.ShapeDtypeStruct(attend.shape, BF16),
        ),
        in_specs=[vmem_spec()] * 10,
        out_specs=(vmem_spec(), vmem_spec()),
        compiler_params=params(),
        name="latent_backward",
    )(latents, mixed_grad, first, second, grad_kv, gains, attend, grad_w, gain_m, gain_f)


class Scatter:
    def __init__(self, depth, chunk, g_ref, buffers, load_sem, sems):
        self.depth = depth
        self.chunk = chunk
        self.g_ref = g_ref
        self.own, self.from_c, self.from_two, self.from_one, self.from_z = buffers
        self.load_sem = load_sem
        self.sems = sems
        self.at = place()
        self.one = first_partner(*self.at)
        self.two = second_partner(*self.at)
        self.homes = [self.at, self.one, self.two, second_partner(*self.one)]
        a, b, e, c = self.at
        self.twin = (a, b, e, 1 - c)
        order = z_order(depth)
        self.order = order[1:] + order[:1]
        self.rows = self.own.shape[1]

    def row(self, k, j, core):
        _, b, e, _ = self.homes[j]
        return flat((self.at[0] + k) % self.depth, b, e, core)

    def load(self, k, j):
        slot = k * 4 + j
        src = self.g_ref.at[self.row(k, j, self.at[3])]
        return pltpu.make_async_copy(src, self.own.at[slot], self.load_sem.at[slot])

    def to_twin(self, k, j):
        src = self.g_ref.at[self.row(k, (0, 2, 1, 3)[j], 1 - self.at[3])]
        return remote_copy(src, self.from_c.at[k * 4 + j], self.sems, k * 8 + j, self.twin)

    def to_two(self, k, j):
        spot = self.from_two.at[k * 2 + j - 2]
        return remote_copy(self.own.at[k * 4 + j], spot, self.sems, k * 8 + 2 + j, self.two)

    def to_one(self, k):
        return remote_copy(
            self.own.at[k * 4 + 1], self.from_one.at[k], self.sems, k * 8 + 6, self.one
        )

    def to_far(self, k):
        a, b, e, c = self.at
        target = ((a + k) % self.depth, b, e, c)
        return remote_copy(
            self.own.at[k * 4], self.from_z.at[k - 1], self.sems, k * 8 + 7, target
        )

    def add(self, slot, spot):
        mine = self.own.at[slot]
        add_into(mine, mine, spot, self.rows, self.chunk)

    def begin(self):
        for k in self.order:
            for j in (3, 2, 1, 0):
                self.load(k, j).start()
                self.to_twin(k, j).start()

    def first(self, k):
        for j in (3, 2, 1, 0):
            self.load(k, j).wait()
            self.to_twin(k, j).wait_recv()
            self.add(k * 4 + j, self.from_c.at[k * 4 + j])
            if j >= 2:
                self.to_two(k, j).start()

    def second(self, k):
        for j in (3, 2):
            self.to_two(k, j).wait_recv()
            self.add(k * 4 + j - 2, self.from_two.at[k * 2 + j - 2])
            if j == 3:
                self.to_one(k).start()

    def third(self, k):
        self.to_one(k).wait_recv()
        self.add(k * 4, self.from_one.at[k])
        if k:
            self.to_far(k).start()

    def run(self, names):
        acts = {"a": self.first, "b": self.second, "c": self.third}
        for name in names.split():
            acts[name[0]](self.order[int(name[1:])])

    def finish(self, o_ref):
        for k in range(1, self.depth):
            self.to_far(k).wait_recv()

        @pl.loop(0, self.rows // self.chunk)
        def _(step):
            part = pl.ds(step * self.chunk, self.chunk)
            total = self.own[0, part, :].astype(F32)
            for k in range(1, self.depth):
                total = total + self.from_z[k - 1, part, :].astype(F32)
            o_ref[part, :] = total

        for k in range(self.depth):
            for j in range(4):
                self.to_twin(k, j).wait_send()
            self.to_two(k, 3).wait_send()
            self.to_two(k, 2).wait_send()
            self.to_one(k).wait_send()
            if k:
                self.to_far(k).wait_send()


def scatter_buffers(depth, rows, cols):
    def slots(n):
        return pltpu.VMEM((n, rows, cols), BF16)

    return [slots(depth * 4), slots(depth * 4), slots(depth * 2), slots(depth), slots(depth - 1)]


def scatter_sems(depth):
    return [
        pltpu.SemaphoreType.DMA((depth * 4,)),
        pltpu.SemaphoreType.DMA((depth * 8,)),
        pltpu.SemaphoreType.DMA((depth * 8,)),
    ]


def latent_attention_back(queries, grads, stats, keys, values, mask):
    rows = keys.shape[0]
    count = queries.shape[0]
    half = mask.astype(BF16)
    wide_k = jnp.concatenate([keys] * HEADS, axis=0) * half
    wide_v = jnp.concatenate([values] * HEADS, axis=0) * half
    cut = (HEADS, rows, count)
    scores = mm_nt(wide_k, queries).reshape(cut)
    probs = jnp.exp(scores - stats[:HEADS][:, None, :])
    grad_probs = mm_nt(wide_v, grads).reshape(cut)
    grad_scores = probs * (grad_probs - stats[HEADS : 2 * HEADS][:, None, :])
    grad_scores = grad_scores.reshape(HEADS * rows, count).astype(BF16)
    probs = probs.reshape(HEADS * rows, count).astype(BF16)

    def fold(full):
        full = full * mask
        total = full[:rows]
        for h in range(1, HEADS):
            total = total + full[h * rows : (h + 1) * rows]
        return total

    grad_kv = [fold(mm(grad_scores, queries)), fold(mm(probs, grads))]
    return mm_tn(grad_scores, wide_k), jnp.concatenate(grad_kv, axis=1).astype(BF16)


def to_lines(tile):
    return tile.T[: 2 * HEADS]


def from_lines(lines):
    zeros = jnp.zeros((LANES - lines.shape[0], lines.shape[1]), F32)
    return jnp.concatenate([lines, zeros], axis=0).T


def back_kernel(
    depth,
    frames,
    chunk,
    plan,
    ids,
    last,
    has,
    same,
    g_ref,
    q_ref,
    context_grad,
    tile_ref,
    k_ref,
    v_ref,
    m_ref,
    kl_ref,
    vl_ref,
    gb_ref,
    w_ref,
    lat_ref,
    mixed_ref,
    gain_f,
    media_grad,
    latents_grad,
    pack_ref,
    mine_ref,
    own,
    from_c,
    from_two,
    from_one,
    from_z,
    load_sem,
    send_sem,
    recv_sem,
    all_g,
    lines,
    tiles,
    weight_acc,
    gain_acc,
    outs,
    latent_kv,
    keep,
    send,
    core_q,
    away,
    y_q,
    link_send,
    link_recv,
    mixed_sem,
):
    step = pl.program_id(0)
    a, b, e, c = place()
    twin, other = (a, b, e, 1 - c), (a, b, 1 - e, c)
    links = link_send, link_recv
    scatter = Scatter(
        depth, chunk, g_ref, (own, from_c, from_two, from_one, from_z), load_sem, (send_sem, recv_sem)
    )
    clips, rows, inner = kl_ref.shape
    total_rows = clips * rows
    groups = inner // (GROUP * HDIM)
    width = GROUP * HDIM
    mask = head_mask(F32)
    mask_half = mask.astype(BF16)
    grad_copies = [
        remote_copy(all_g.at[0], all_g.at[2], links, 0, other),
        remote_copy(all_g.at[0], all_g.at[1], links, 1, twin),
        remote_copy(all_g.at[2], all_g.at[3], links, 2, twin),
    ]
    line_copies = [
        remote_copy(lines.at[0], lines.at[2], links, 3, other),
        remote_copy(lines.at[0], lines.at[1], links, 4, twin),
        remote_copy(lines.at[2], lines.at[3], links, 5, twin),
    ]
    core_copy = remote_copy(send, core_q, links, 6, twin)
    y_copy = remote_copy(away, y_q, links, 7, other)

    def clip_queries(clip):
        return jnp.concatenate([q_ref[r, clip] for r in range(4)], axis=0) * BF16(SCALE)

    def clip_grads(clip):
        return jnp.concatenate([all_g[r, clip] for r in range(4)], axis=0)

    def clip_stats(clip):
        return jnp.concatenate([tiles[r, clip] for r in range(4)], axis=0).T

    @pl.when(step == 0)
    def _():
        all_g[0] = context_grad[...]
        lines[0] = to_lines(tile_ref[...])
        greet(depth, a, b, e, c)
        for copies in (grad_copies, line_copies):
            copies[0].start()
            copies[1].start()
        scatter.begin()
        gain_acc[...] = jnp.zeros_like(gain_acc)
        weight_acc[...] = jnp.zeros_like(weight_acc)
        outs[0] = jnp.zeros_like(outs[0])

    for when, names in plan[:-1]:

        @pl.when(step == when)
        def _(names=names):
            scatter.run(names)

    @pl.when(step == 0)
    def _():
        for copies in (grad_copies, line_copies):
            copies[0].wait()
            copies[2].start()
        for copies in (grad_copies, line_copies):
            copies[1].wait()
            copies[2].wait()
        for r in range(4):
            tiles[r] = from_lines(lines[r]).reshape(clips, rows, LANES)

    @pl.when((step >= 1) & (step <= frames))
    def _():
        frame = step - 1
        before = jnp.maximum(frame - 1, 0)
        clip = ids[frame]
        joined = same[frame] == 1
        queries, grads, stats = clip_queries(clip), clip_grads(clip), clip_stats(clip)
        key_parts, value_parts = [], []
        for g in range(groups):
            cols = slice(g * width, (g + 1) * width)

            def line(first):
                at = first + g * GROUP
                return jnp.concatenate([stats[at + h : at + h + 1, :] for h in range(GROUP)], axis=1)

            wide_q = spread_heads(queries, g, mask_half)
            wide_g = spread_heads(grads, g, mask_half)
            keys = k_ref[:, cols]
            probs = jnp.exp(mm_nt(keys, wide_q) - line(0))
            grad_probs = mm_nt(v_ref[:, cols], wide_g)
            grad_scores = (probs * (grad_probs - line(HEADS))).astype(BF16)
            key_parts.append(mm(grad_scores, wide_q))
            value_parts.append(mm(probs.astype(BF16), wide_g))
            part = take_heads(mm_tn(grad_scores, keys), mask)
            outs[frame, :, cols] = part + jnp.where(joined, outs[before, :, cols], 0.0)
        grad_kv = jnp.concatenate(key_parts + value_parts, axis=1).astype(BF16)
        hat, scale = normalise(m_ref[...].astype(F32))
        gain = gb_ref[0:1, :]
        normed = (hat * gain + gb_ref[3:4, :]).astype(BF16)
        weight_acc[...] += mm_tn(normed, grad_kv)
        grad = mm_nt(grad_kv, w_ref[:, inner : 3 * inner])
        gain_acc[0:1, :] += jnp.sum(grad * hat, axis=0, keepdims=True)
        gain_acc[1:2, :] += jnp.sum(grad, axis=0, keepdims=True)
        media_grad[...] = norm_back(grad, hat, scale, gain).astype(BF16)

    @pl.when(step == frames + 1)
    def _():
        wide = latent_mask(rows, inner)

        @pl.loop(0, clips)
        def _(clip):
            out, grad_kv = latent_attention_back(
                clip_queries(clip),
                clip_grads(clip),
                clip_stats(clip),
                kl_ref[clip],
                vl_ref[clip],
                wide,
            )
            latent_kv[clip] = grad_kv
            out = (out + jnp.where(has[clip] == 1, outs[last[clip]], 0.0)) * SCALE
            for r in range(4):
                part = slice(r * rows, (r + 1) * rows)
                if r % 2:
                    send[r // 2, clip] = out[part].astype(BF16)
                else:
                    keep[r // 2, clip] = out[part]

        core_copy.start()
        hat, scale = normalise(lat_ref[...])
        gain = gb_ref[1:2, :]
        normed = (hat * gain + gb_ref[4:5, :]).astype(BF16)
        core_copy.wait()
        away[...] = (keep[1] + core_q[1].astype(F32)).astype(BF16)
        y_copy.start()
        grad_kv = latent_kv[...].reshape(total_rows, 2 * inner)
        pack_ref[:, inner : 3 * inner] = (weight_acc[...] + mm_tn(normed, grad_kv)).astype(BF16)
        grad = mm_nt(grad_kv, w_ref[:, inner : 3 * inner])
        mixed = weight_acc.at[:total_rows]
        load_mixed = pltpu.make_async_copy(mixed_ref, mixed, mixed_sem)
        load_mixed.start()
        scatter.run(plan[-1][1])
        y_copy.wait()
        grad_q = (keep[0] + core_q[0].astype(F32) + y_q[...].astype(F32)).astype(BF16)
        grad_q = grad_q.reshape(total_rows, inner)
        grad = grad + mm_nt(grad_q, w_ref[:, :inner])
        pack_ref[:, :inner] = mm_tn(normed, grad_q).astype(BF16)
        table = jnp.concatenate(
            [
                gain_acc[0:1, :],
                jnp.sum(grad * hat, axis=0, keepdims=True),
                gain_f[0:1, :],
                gain_acc[1:2, :],
                jnp.sum(grad, axis=0, keepdims=True),
                gain_f[1:2, :],
                jnp.zeros((LANES - 6, grad.shape[1]), F32),
            ],
            axis=0,
        )
        pack_ref[:, 3 * inner :] = table.T.astype(BF16)
        load_mixed.wait()
        latents_grad[...] = mixed[...] + norm_back(grad, hat, scale, gain)
        scatter.finish(mine_ref)


def back(
    ids,
    last,
    has,
    same,
    grad_feed,
    query_all,
    context_grad,
    tile,
    keys,
    values,
    media,
    latent_key,
    latent_value,
    gains,
    attend,
    latents,
    mixed_grad,
    gain_f,
    depth,
    chunk,
    plan,
):
    clips, rows, inner = latent_key.shape
    frames = media.shape[0] // PATCH_IMG
    width = media.shape[1]
    total = clips * rows
    cut = (clips, rows, inner)
    _, feed_rows, feed_cols = grad_feed.shape
    once = pl.Buffered(buffer_count=1)

    def whole(x):
        return pl.BlockSpec(x.shape, lambda i: (0,) * len(x.shape), pipeline_mode=once)

    def block(columns):
        return pl.BlockSpec((PATCH_IMG, columns), lambda i: (jnp.clip(i - 1, 0, frames - 1), 0))

    smem = pl.BlockSpec(memory_space=pltpu.SMEM)
    outs = (
        jax.ShapeDtypeStruct(media.shape, BF16),
        jax.ShapeDtypeStruct(latents.shape, F32),
        jax.ShapeDtypeStruct(attend.shape, BF16),
        jax.ShapeDtypeStruct((feed_rows, feed_cols), F32),
    )
    return pl.pallas_call(
        functools.partial(back_kernel, depth, frames, chunk, plan),
        grid=(frames + 2,),
        out_shape=outs,
        in_specs=[smem] * 4
        + [any_spec(), whole(query_all), whole(context_grad), whole(tile)]
        + [block(inner), block(inner), block(width)]
        + [whole(x) for x in (latent_key, latent_value, gains, attend, latents)]
        + [any_spec(), whole(gain_f)],
        out_specs=(block(width),) + tuple(whole(x) for x in outs[1:]),
        scratch_shapes=scatter_buffers(depth, feed_rows, feed_cols)
        + scatter_sems(depth)
        + [
            pltpu.VMEM((4,) + cut, BF16),
            pltpu.VMEM((4, 2 * HEADS, total), F32),
            pltpu.VMEM((4, clips, rows, LANES), F32),
            pltpu.VMEM((width, 2 * inner), F32),
            pltpu.VMEM((8, width), F32),
            pltpu.VMEM((frames, 4 * rows, inner), F32),
            pltpu.VMEM((clips, rows, 2 * inner), BF16),
            pltpu.VMEM((2,) + cut, F32),
            pltpu.VMEM((2,) + cut, BF16),
            pltpu.VMEM((2,) + cut, BF16),
            pltpu.VMEM(cut, BF16),
            pltpu.VMEM(cut, BF16),
            pltpu.SemaphoreType.DMA((8,)),
            pltpu.SemaphoreType.DMA((8,)),
            pltpu.SemaphoreType.DMA,
        ],
        compiler_params=params(collective_id=4, has_side_effects=True),
        name="back",
    )(
        ids,
        last,
        has,
        same,
        grad_feed,
        query_all,
        context_grad,
        tile,
        keys,
        values,
        media,
        latent_key,
        latent_value,
        gains,
        attend,
        latents,
        mixed_grad,
        gain_f,
    )


def head_kernel(
    depth,
    frames,
    parts,
    plan,
    late,
    ids,
    last,
    has,
    same,
    shard_e,
    shard_s,
    m_ref,
    lat_ref,
    cot_ref,
    gb_ref,
    wq_ref,
    k_ref,
    v_ref,
    q_ref,
    kl_ref,
    vl_ref,
    out_ref,
    mixed_grad,
    context_grad,
    tile_ref,
    gain_ref,
    gw_ref,
    all_k,
    all_v,
    all_q,
    outs,
    tops,
    sums,
    keep,
    keep_st,
    send,
    send_st,
    core_o,
    send_li,
    core_li,
    away,
    y_o,
    away_li,
    y_li,
    weights_e,
    weights_s,
    grad_s,
    grad_o,
    normed_v,
    normed_t,
    hat_v,
    local_sem,
    send_e,
    recv_e,
    send_s,
    recv_s,
    link_send,
    link_recv,
    out_sem,
    store_sem,
):
    step = pl.program_id(0)
    a, b, e, c = place()
    twin, other = (a, b, e, 1 - c), (a, b, 1 - e, c)
    links = link_send, link_recv
    gather_e = Gather(depth, shard_e, weights_e, local_sem.at[0], send_e, recv_e)
    gather_s = Gather(depth, shard_s, weights_s, local_sem.at[1], send_s, recv_s)
    clips, rows, inner = kl_ref.shape
    total_rows = clips * rows
    groups = inner // (GROUP * HDIM)
    width = GROUP * HDIM
    slabs = PATCH_IMG // all_k.shape[1]
    mask = head_mask(F32)
    mask_half = mask.astype(BF16)
    query_copies = [
        remote_copy(all_q.at[0], all_q.at[2], links, 0, other),
        remote_copy(all_q.at[0], all_q.at[1], links, 1, twin),
        remote_copy(all_q.at[2], all_q.at[3], links, 2, twin),
    ]
    core_copies = [
        remote_copy(send, core_o, links, 3, twin),
        remote_copy(send_li, core_li, links, 4, twin),
    ]
    y_copies = [
        remote_copy(away, y_o, links, 5, other),
        remote_copy(away_li, y_li, links, 6, other),
    ]
    keep_queries = pltpu.make_async_copy(all_q, q_ref, out_sem)

    def run(names):
        for name in names.split():
            (gather_e if name[0] == "e" else gather_s).run(name[1:])

    def clip_queries(clip):
        return jnp.concatenate([all_q[r, clip] for r in range(4)], axis=0) * BF16(SCALE)

    @pl.when(step == 0)
    def _():
        greet(depth, a, b, e, c)
        hat, _ = normalise(lat_ref[...])
        normed = (hat * gb_ref[1:2, :] + gb_ref[4:5, :]).astype(BF16)
        all_q[0] = mm(normed, wq_ref[:, :inner]).astype(BF16).reshape(clips, rows, inner)
        query_copies[0].start()
        query_copies[1].start()
        gather_s.own().start()
        gather_e.own().start()
        gather_e.begin()
        kl_ref[...] = (
            mm(normed, wq_ref[:, inner : 2 * inner]).astype(BF16).reshape(clips, rows, inner)
        )
        vl_ref[...] = (
            mm(normed, wq_ref[:, 2 * inner : 3 * inner]).astype(BF16).reshape(clips, rows, inner)
        )
        outs[0] = jnp.zeros_like(outs[0])
        tops[0] = jnp.zeros_like(tops[0])
        sums[0] = jnp.zeros_like(sums[0])

    @pl.when(step < frames)
    def _():
        hat, _ = normalise(m_ref[...].astype(F32))
        normed = (hat * gb_ref[0:1, :] + gb_ref[3:4, :]).astype(BF16)
        new_k = mm(normed, wq_ref[:, inner : 2 * inner]).astype(BF16)
        new_v = mm(normed, wq_ref[:, 2 * inner : 3 * inner]).astype(BF16)
        k_ref[...] = new_k
        v_ref[...] = new_v
        at = pl.ds(step * slabs, slabs)
        all_k[at] = new_k.reshape(slabs, PATCH_IMG // slabs, inner)
        all_v[at] = new_v.reshape(slabs, PATCH_IMG // slabs, inner)

    for when, names in plan:

        @pl.when(step == when)
        def _(names=names):
            run(names)

    @pl.when(step == frames // 2)
    def _():
        query_copies[0].wait()
        query_copies[2].start()

    @pl.when(step == frames)
    def _():
        query_copies[1].wait()
        query_copies[2].wait()
        keep_queries.start()

    @pl.when((step >= frames) & (step < 2 * frames))
    def _():
        frame = step - frames
        before = jnp.maximum(frame - 1, 0)
        queries = clip_queries(ids[frame])
        joined = same[frame] == 1
        old_tops = jnp.where(joined, tops[before], MASKED)
        old_sums = jnp.where(joined, sums[before], 0.0)
        at = pl.ds(frame * slabs, slabs)
        new_tops, new_sums = [], []
        for g in range(groups):
            cols = slice(g * width, (g + 1) * width)

            def column(tile):
                first = g * GROUP
                return jnp.concatenate(
                    [tile[:, first + h : first + h + 1] for h in range(GROUP)], axis=0
                )

            keys = all_k[at, :, cols].reshape(PATCH_IMG, width)
            values = all_v[at, :, cols].reshape(PATCH_IMG, width)
            scores = mm_nt(spread_heads(queries, g, mask_half), keys)
            old_top = column(old_tops)
            top = jnp.maximum(jnp.max(scores, axis=-1, keepdims=True), old_top)
            probs = jnp.exp(scores - top)
            shrink = jnp.exp(old_top - top)
            total = jnp.sum(probs, axis=-1, keepdims=True) + column(old_sums) * shrink
            part = take_heads(mm(probs.astype(BF16), values), mask)
            old = jnp.where(joined, outs[before, :, cols], 0.0)
            outs[frame, :, cols] = part + old * take_heads(shrink, mask)
            for h in range(GROUP):
                new_tops.append(top[h * HDIM : (h + 1) * HDIM])
                new_sums.append(total[h * HDIM : (h + 1) * HDIM])
        tops[frame] = pack_columns(new_tops)
        sums[frame] = pack_columns(new_sums)

    @pl.when((step >= 2 * frames) & (step < 2 * frames + parts))
    def _():
        wide = latent_mask(rows, inner)
        lane = lax.broadcasted_iota(jnp.int32, (4 * rows, LANES), 1)
        first = (step - 2 * frames) * (clips // parts)

        @pl.loop(0, clips // parts)
        def _(index):
            clip = first + index
            out, top, total = latent_attention(clip_queries(clip), kl_ref[clip], vl_ref[clip], wide)
            at = last[clip]
            there = has[clip] == 1
            far_top = jnp.where(there, tops[at], MASKED)
            far_sum = jnp.where(there, sums[at], 0.0)
            far_out = jnp.where(there, outs[at], 0.0)
            both = jnp.maximum(top, far_top)
            near, far = jnp.exp(top - both), jnp.exp(far_top - both)
            total = jnp.where(lane < HEADS, total * near + far_sum * far, 1.0)
            stat = both + jnp.log(total)
            out = out * expand_columns(near / total, inner)
            out = out + far_out * expand_columns(far / total, inner)
            for r in range(4):
                part = slice(r * rows, (r + 1) * rows)
                if r % 2:
                    send[r // 2, clip] = out[part].astype(BF16)
                    send_st[r // 2, clip] = stat[part]
                else:
                    keep[r // 2, clip] = out[part]
                    keep_st[r // 2, clip] = stat[part]

    @pl.when(step == 2 * frames + parts)
    def _():
        for n in range(2):
            send_li[n] = to_lines(send_st[n].reshape(total_rows, LANES))
        for copy in core_copies:
            copy.start()
        run(late[0])
        for copy in core_copies:
            copy.wait()

        def core_part(n):
            return join_partials(
                keep[n].reshape(total_rows, inner),
                keep_st[n].reshape(total_rows, LANES),
                core_o[n].reshape(total_rows, inner),
                from_lines(core_li[n]),
            )

        out, stat = core_part(1)
        away[...] = out.astype(BF16)
        away_li[...] = to_lines(stat)
        for copy in y_copies:
            copy.start()
        out, stat = core_part(0)
        run(late[1])
        gather_e.settle()
        run(late[2])
        for copy in y_copies:
            copy.wait()
        context, stat = join_partials(out, stat, y_o[...], from_lines(y_li[...]))
        feed_part(
            functools.partial(run_late, run, late[3:], gather_s),
            context,
            stat,
            depth,
            a,
            gather_s.order,
            lat_ref,
            cot_ref,
            gb_ref,
            weights_e,
            weights_s,
            out_ref,
            mixed_grad,
            context_grad,
            tile_ref,
            gain_ref,
            gw_ref,
            all_k,
            grad_s,
            grad_o,
            normed_v,
            normed_t,
            hat_v,
            store_sem,
        )
        keep_queries.wait()
        gather_e.finish()
        gather_s.finish()


def run_late(run, late, gather, n):
    run(late[n])
    gather.settle(gather.order[n])


def feed_part(
    ready,
    context,
    stat,
    depth,
    plane,
    order,
    lat_ref,
    cot_ref,
    gb_ref,
    weights_e,
    weights_s,
    out_ref,
    mixed_grad,
    context_grad,
    tile_ref,
    gain_ref,
    gw_ref,
    grad_e,
    grad_s,
    grad_o,
    normed_v,
    normed_t,
    hat_v,
    store_sem,
):
    blocks, shrink_rows, width = weights_s.shape
    per_plane = blocks // depth
    inner = context.shape[1]
    output_rows = inner // blocks
    expand_rows = (weights_e.shape[1] - output_rows) // depth
    shrink_at = depth * expand_rows
    output_at = shrink_at + shrink_rows
    half = width // 2
    half_rows = half // shrink_rows
    context_half = context.astype(BF16)

    def weight_o():
        return weights_e[:, shrink_at : shrink_at + output_rows, :].reshape(inner, width)

    mixed = lat_ref[...] + mm(context_half, weight_o())
    hat, scale = normalise(mixed)
    hat_v[...] = hat
    normed = (hat * gb_ref[2:3, :] + gb_ref[5:6, :]).astype(BF16)
    normed_v[...] = normed
    normed_t[...] = normed.astype(F32).T.astype(BF16)
    out_ref[...] = mixed
    mixed_grad[...] = jnp.zeros_like(mixed_grad)
    cot = cot_ref[...]
    stores = []
    for n, k in enumerate(order):
        ready(n)
        plane_k = (plane - k) % depth
        e_rows = pl.ds(pl.multiple_of(plane_k * expand_rows, expand_rows), expand_rows)
        for slot in range(2):
            cols = slice(slot * half, (slot + 1) * half)
            w_e = weights_e[:, e_rows, cols].reshape(blocks * expand_rows, half)
            s_rows = pl.ds(plane_k * per_plane + slot * half_rows, half_rows)
            w_s = weights_s[s_rows].reshape(half, width)
            pre = mm(normed_v[...], w_e)
            cdf = 0.5 * (1.0 + lax.erf(pre * (0.5**0.5)))
            hidden = (pre * cdf).astype(BF16)
            out_ref[...] += mm(hidden, w_s)
            grad_hidden = mm_nt(cot, w_s)
            pdf = jnp.exp(-0.5 * pre * pre) * (1.0 / math.sqrt(2.0 * math.pi))
            grad_pre = (grad_hidden * (cdf + pre * pdf)).astype(BF16)
            if n:
                for copy in stores[2 * (2 * n + slot) - 4 : 2 * (2 * n + slot) - 2]:
                    copy.wait()
            grad_s[slot] = mm_tn(hidden, cot).astype(BF16).reshape(half_rows, shrink_rows, width)
            e_spot = grad_e.at[pl.ds(slot * blocks, blocks)]
            e_spot[...] = (
                mm(normed_t[...], grad_pre).astype(BF16).reshape(blocks, expand_rows, half)
            )
            stores += [
                pltpu.make_async_copy(
                    e_spot, gw_ref.at[:, e_rows, pl.ds(slot * half, half)], store_sem.at[slot]
                ),
                pltpu.make_async_copy(
                    grad_s.at[slot],
                    gw_ref.at[s_rows, pl.ds(shrink_at, shrink_rows), :],
                    store_sem.at[2 + slot],
                ),
            ]
            stores[-1].start()
            stores[-2].start()
            mixed_grad[...] += mm_nt(grad_pre, w_e)

    grad_normed = mixed_grad[...]
    hat = hat_v[...]
    rows = gain_ref.shape[0]
    gain_ref[...] = jnp.concatenate(
        [
            jnp.sum(grad_normed * hat, axis=0, keepdims=True),
            jnp.sum(grad_normed, axis=0, keepdims=True),
            jnp.zeros((rows - 2, width), F32),
        ],
        axis=0,
    )
    total = cot.astype(F32) + norm_back(grad_normed, hat, scale, gb_ref[2:3, :])
    mixed_grad[...] = total
    attended = total.astype(BF16)
    grad_o[...] = mm_tn(context_half, attended).astype(BF16).reshape(grad_o.shape)
    store_o = pltpu.make_async_copy(
        grad_o, gw_ref.at[:, pl.ds(output_at, output_rows), :], store_sem.at[4]
    )
    store_o.start()
    grad_c = mm_nt(attended, weight_o()).astype(BF16)
    context_grad[...] = grad_c
    product = grad_c.astype(F32) * context
    head = lax.broadcasted_iota(jnp.int32, product.shape, 1) // HDIM
    deltas = [
        jnp.sum(jnp.where(head == h, product, 0.0), axis=-1, keepdims=True) for h in range(HEADS)
    ]
    lane = lax.broadcasted_iota(jnp.int32, stat.shape, 1)
    tile_ref[...] = jnp.where(lane < HEADS, stat, pack_columns(deltas, HEADS))
    for copy in stores[-4:]:
        copy.wait()
    store_o.wait()


def head(
    ids,
    last,
    has,
    same,
    shard_e,
    shard_s,
    media,
    latents,
    cotangent,
    gains,
    attend,
    clips,
    inner,
    depth,
    parts,
    plan,
    late,
):
    rows = latents.shape[0] // clips
    frames = media.shape[0] // PATCH_IMG
    width = media.shape[1]
    total = clips * rows
    cut = (clips, rows, inner)
    count = depth * 8
    expand_rows = (shard_e.shape[0] - inner // count) // depth
    feed_rows = shard_e.shape[0] + shard_s.shape[0]
    slabs = PATCH_IMG // expand_rows * frames
    half_rows = width // 2 // shard_s.shape[0]
    once = pl.Buffered(buffer_count=1)

    def whole(x):
        return pl.BlockSpec(x.shape, lambda i: (0,) * len(x.shape), pipeline_mode=once)

    def block(columns):
        return pl.BlockSpec((PATCH_IMG, columns), lambda i: (jnp.minimum(i, frames - 1), 0))

    smem = pl.BlockSpec(memory_space=pltpu.SMEM)
    kv = jax.ShapeDtypeStruct((media.shape[0], inner), BF16)
    small = jax.ShapeDtypeStruct(cut, BF16)
    outs = (
        small,
        small,
        jax.ShapeDtypeStruct((total, width), F32),
        jax.ShapeDtypeStruct((total, width), F32),
        jax.ShapeDtypeStruct((total, inner), BF16),
        jax.ShapeDtypeStruct((total, LANES), F32),
        jax.ShapeDtypeStruct((8, width), F32),
    )
    lines = (2 * HEADS, total)
    dma = pltpu.SemaphoreType.DMA
    return pl.pallas_call(
        functools.partial(head_kernel, depth, frames, parts, plan, late),
        grid=(2 * frames + parts + 1,),
        out_shape=(kv, kv, jax.ShapeDtypeStruct((4,) + cut, BF16))
        + outs
        + (jax.ShapeDtypeStruct((count, feed_rows, width), BF16),),
        in_specs=[smem] * 4
        + [any_spec(), any_spec(), block(width)]
        + [whole(x) for x in (latents, cotangent, gains, attend)],
        out_specs=(block(inner), block(inner), any_spec())
        + tuple(whole(x) for x in outs)
        + (any_spec(),),
        scratch_shapes=[
            pltpu.VMEM((slabs, expand_rows, inner), BF16),
            pltpu.VMEM((slabs, expand_rows, inner), BF16),
            pltpu.VMEM((4,) + cut, BF16),
            pltpu.VMEM((frames, 4 * rows, inner), F32),
            pltpu.VMEM((frames, 4 * rows, LANES), F32),
            pltpu.VMEM((frames, 4 * rows, LANES), F32),
            pltpu.VMEM((2,) + cut, F32),
            pltpu.VMEM((2, clips, rows, LANES), F32),
            pltpu.VMEM((2,) + cut, BF16),
            pltpu.VMEM((2, clips, rows, LANES), F32),
            pltpu.VMEM((2,) + cut, BF16),
            pltpu.VMEM((2,) + lines, F32),
            pltpu.VMEM((2,) + lines, F32),
            pltpu.VMEM((total, inner), BF16),
            pltpu.VMEM((total, inner), BF16),
            pltpu.VMEM(lines, F32),
            pltpu.VMEM(lines, F32),
            pltpu.VMEM((count,) + shard_e.shape, BF16),
            pltpu.VMEM((count,) + shard_s.shape, BF16),
            pltpu.VMEM((2, half_rows) + shard_s.shape, BF16),
            pltpu.VMEM((count, inner // count, width), BF16),
            pltpu.VMEM((total, width), BF16),
            pltpu.VMEM((width, total), BF16),
            pltpu.VMEM((total, width), F32),
            dma((2,)),
            dma((count,)),
            dma((count,)),
            dma((count,)),
            dma((count,)),
            dma((7,)),
            dma((7,)),
            dma,
            dma((5,)),
        ],
        compiler_params=params(collective_id=2, has_side_effects=True),
        name="head",
    )(ids, last, has, same, shard_e, shard_s, media, latents, cotangent, gains, attend)


def norm_kernel(depth, images, lats, chunk, pack_ref, feed_ref, norm_ref, mine_ref, *refs):
    buffers, refs = refs[:5], refs[5:]
    load_sem, send_sem, recv_sem, tile, slots, tile_send, tile_recv = refs
    count = images * lats
    img = lax.axis_index("img")
    lat = lax.axis_index("lat")
    me = img * lats + lat
    scatter = Scatter(depth, chunk, pack_ref, buffers, load_sem, (send_sem, recv_sem))
    barrier = pltpu.get_barrier_semaphore()

    def other(k):
        there = (me + k) % count
        return there // lats, there % lats

    for k in range(1, count):
        pl.semaphore_signal(barrier, inc=1, device_id=other(k), device_id_type=MESH)
    pl.semaphore_wait(barrier, count - 1)
    scatter.begin()
    feed_rows = feed_ref.shape[0]
    squares = jnp.zeros((8, feed_ref.shape[1]), F32)
    for n in range(feed_rows // 8):
        part = feed_ref[n * 8 : (n + 1) * 8, :]
        squares = squares + part * part
    squares = jnp.sum(squares)
    scatter.run("a0 a1 b0 a2 b1 c0 a3 b2 c1 b3 c2 c3")
    scatter.finish(mine_ref)
    own = mine_ref[...]
    tile[...] = jnp.full(tile.shape, squares + jnp.sum(own * own), F32)
    slots[me] = tile[...]

    def exchange(k, spot):
        return pltpu.make_async_remote_copy(
            src_ref=tile,
            dst_ref=slots.at[spot],
            send_sem=tile_send.at[k],
            recv_sem=tile_recv.at[k],
            device_id=other(k),
            device_id_type=MESH,
        )

    for k in range(1, count):
        exchange(k, me).start()
    for k in range(1, count):
        exchange(k, (me - k) % count).wait_recv()
    norm_ref[...] = jnp.sqrt(jnp.sum(slots[...], axis=0))
    for k in range(1, count):
        exchange(k, me).wait_send()


def norm_and_sum(grad_attend, mine_feed, images, lats):
    count = images * lats
    depth = images // 2
    rows = grad_attend.shape[0] // count
    cols = grad_attend.shape[1]
    tile = (8, LANES)
    return pl.pallas_call(
        functools.partial(norm_kernel, depth, images, lats, 16),
        out_shape=(jax.ShapeDtypeStruct(tile, F32), jax.ShapeDtypeStruct((rows, cols), F32)),
        in_specs=[any_spec(), vmem_spec()],
        out_specs=(vmem_spec(), vmem_spec()),
        scratch_shapes=scatter_buffers(depth, rows, cols)
        + scatter_sems(depth)
        + [
            pltpu.VMEM(tile, F32),
            pltpu.VMEM((count,) + tile, F32),
            pltpu.SemaphoreType.DMA((count,)),
            pltpu.SemaphoreType.DMA((count,)),
        ],
        compiler_params=params(collective_id=3, has_side_effects=True),
        name="norm",
    )(grad_attend.reshape(count, rows, cols), mine_feed)


def update_kernel(rates, inner, count, norm_ref, mine, feed_ref, *refs):
    states, refs = refs[:18], refs[18:]
    olds, refs = refs[:count], refs[count:]
    norm_out, news, moved = refs[0], refs[1:19], refs[19:]
    for old, new in zip(olds, moved):
        new[...] = old[...]

    @pl.when(pl.program_id(0) == 0)
    def _():
        update_states(rates, inner, norm_ref, mine, feed_ref, states, norm_out, news)


def update_states(rates, inner, norm_ref, mine, feed_ref, states, norm_out, news):
    norm = norm_ref[...]
    norm_out[...] = norm
    factor = jnp.minimum(1.0, CLIP_NORM / (norm + 1e-06))[0:1, 0:1]

    def update(n, grad, rows, cols, decay):
        at = (rows, cols)
        master = states[n][at]
        step_grad = factor * grad
        if decay:
            step_grad = step_grad + decay * master
        buffer = MOMENTUM * states[6 + n][at] + step_grad
        new = master - rates[n] * (step_grad + MOMENTUM * buffer)
        news[n][at] = new
        news[6 + n][at] = buffer
        news[12 + n][at] = AVERAGING * states[12 + n][at] + (1.0 - AVERAGING) * new

    every = slice(None)
    width = feed_ref.shape[1]
    expand_rows, expand_cols = states[2].shape
    shrink_rows = states[3].shape[0]
    at = expand_cols // width * expand_rows
    update(0, mine[:, : 3 * inner], every, every, DECAY)
    update(1, feed_ref[at + shrink_rows :, :], every, every, DECAY)
    for g in range(expand_cols // width):
        grad = feed_ref[g * expand_rows : (g + 1) * expand_rows, :]
        update(2, grad, every, slice(g * width, (g + 1) * width), DECAY)
    update(3, feed_ref[at : at + shrink_rows, :], every, every, DECAY)
    small = mine[:, 3 * inner :].T
    update(4, small[0:3], every, every, 0.0)
    update(5, small[3:6], every, every, 0.0)


def update_all(norm, mine, mine_feed, states, rates, inner, moved, steps):
    def like(x):
        return jax.ShapeDtypeStruct(x.shape, x.dtype)

    def whole(x):
        return pl.BlockSpec(x.shape, lambda i: (0, 0), pipeline_mode=pl.Buffered(buffer_count=1))

    def block(x):
        return pl.BlockSpec((x.shape[0] // steps, x.shape[1]), lambda i: (i, 0))

    blocks = [block(x) for x in moved]
    kept = [whole(x) for x in states]
    return pl.pallas_call(
        functools.partial(update_kernel, rates, inner, len(moved)),
        grid=(steps,),
        out_shape=(like(norm),) + tuple(like(x) for x in states) + tuple(like(x) for x in moved),
        in_specs=[whole(norm), whole(mine), whole(mine_feed)] + kept + blocks,
        out_specs=tuple([whole(norm)] + kept + blocks),
        compiler_params=params(),
        name="update",
    )(norm, mine, mine_feed, *states, *moved)


def pack_feed(expand, shrink, output):
    width = shrink.shape[-1]
    groups = expand.shape[-1] // width
    lead = expand.shape[:-2]
    rows = expand.shape[-2]
    cut = expand.reshape(lead + (rows, groups, width))
    cut = jnp.moveaxis(cut, -2, -3).reshape(lead + (groups * rows, width))
    return jnp.concatenate([cut, shrink, output], axis=-2)


def unpack_feed(packed, rows, shrink_rows):
    width = packed.shape[-1]
    lead = packed.shape[:-2]
    groups = (packed.shape[-2] - shrink_rows) // rows
    split = groups * rows
    cut = packed[..., :split, :].reshape(lead + (groups, rows, width))
    expand = jnp.moveaxis(cut, -3, -2).reshape(lead + (rows, groups * width))
    return (
        expand,
        packed[..., split : split + shrink_rows, :],
        packed[..., split + shrink_rows :, :],
    )


def step_size(width, inner, ff):
    return 0.37 * math.sqrt((4 * width * inner + 2 * width * ff) / width)


def lat_pairs(count, along_core):
    pairs = []
    for lat in range(count):
        e, c = lat // 2, lat % 2
        pairs.append((lat, e * 2 + 1 - c if along_core else (1 - e) * 2 + c))
    return pairs


def shards(
    images,
    lats,
    media,
    latents,
    counts,
    cotangent,
    attend_weight,
    output_weight,
    expand_weight,
    shrink_weight,
    layer_gains,
    layer_biases,
    attend_momentum,
    output_momentum,
    expand_momentum,
    shrink_momentum,
    gains_momentum,
    biases_momentum,
    attend_average,
    output_average,
    expand_average,
    shrink_average,
    gains_average,
    biases_average,
):
    devices = images * lats
    depth = images // 2
    fast = devices == BLOCKS and lats == 4 and images % 2 == 0
    samples, lat_dev, width = latents.shape
    rows = samples * lat_dev
    ff = expand_weight.shape[1]
    inner = attend_weight.shape[1] // 3
    patch_dev = media.shape[0]
    frames = patch_dev // PATCH_IMG
    over_core = functools.partial(lax.ppermute, axis_name="lat", perm=lat_pairs(lats, True))
    over_y = functools.partial(lax.ppermute, axis_name="lat", perm=lat_pairs(lats, False))

    attend_rows = attend_weight.shape[0]
    if fast:
        attend, shard_e, shard_s, gains = start(
            attend_weight,
            layer_gains.T,
            layer_biases.T,
            expand_weight,
            shrink_weight,
            output_weight,
            depth,
        )
        attend = attend.reshape(width, attend.shape[2])
    else:

        def everywhere(x):
            return lax.all_gather(x.astype(BF16), AXES, axis=0, tiled=True)

        small = jnp.concatenate([layer_gains, layer_biases], axis=1)
        small = jnp.pad(small, ((0, 0), (0, LANES - small.shape[1])))
        attend = everywhere(jnp.concatenate([attend_weight, small], axis=1))
        feed = pack_feed(
            everywhere(expand_weight).reshape(BLOCKS, width // BLOCKS, ff),
            everywhere(shrink_weight).reshape(BLOCKS, ff // BLOCKS, width),
            everywhere(output_weight).reshape(BLOCKS, inner // BLOCKS, width),
        )
        gains = attend[:, 3 * inner : 3 * inner + 8].astype(F32).T

    sample_ends = jnp.cumsum(counts[0])
    first_frame = lax.axis_index("lat") * frames
    frame_ids = first_frame + jnp.arange(frames, dtype=jnp.int32)
    ids = jnp.sum((frame_ids[:, None] >= sample_ends[None, :]).astype(jnp.int32), axis=1)
    ids = jnp.clip(ids, 0, samples - 1)

    latent_flat = latents.reshape(rows, width)
    cot_flat = cotangent.reshape(rows, width)
    cut = (samples, lat_dev, inner)

    def to_group(own):
        other = over_y(own)
        return [own, over_core(own), other, over_core(other)]

    if fast:
        clip = jnp.arange(samples, dtype=jnp.int32)
        here = ids[None, :] == clip[:, None]
        has = jnp.any(here, axis=1).astype(jnp.int32)
        last = jnp.max(jnp.where(here, jnp.arange(frames, dtype=jnp.int32)[None, :], 0), axis=1)
        same = jnp.concatenate([jnp.zeros((1,), jnp.int32), (ids[1:] == ids[:-1]).astype(jnp.int32)])
        (
            keys,
            values,
            query_all,
            latent_key,
            latent_value,
            out_rows,
            mixed_grad,
            context_grad,
            tile,
            gain_f,
            grad_feed,
        ) = head(
            ids,
            last,
            has,
            same,
            shard_e,
            shard_s,
            media,
            latent_flat,
            cot_flat,
            gains,
            attend,
            samples,
            inner,
            depth,
            4,
            HEAD_PLAN,
            HEAD_LATE,
        )
    else:
        query, latent_key, latent_value = latent_project(latent_flat, gains, attend, inner)
        latent_key = latent_key.reshape(cut)
        latent_value = latent_value.reshape(cut)
        queries = to_group(query.reshape(cut))
        keys, values = media_project(media, gains, attend, inner)
        keep, send, keep_st, send_st = attention_forward(
            ids, queries, keys, values, latent_key, latent_value
        )
        got, got_st = over_core(send), over_core(send_st)
        flat_o, flat_s = (2, rows, inner), (2, rows, LANES)
        own, own_st, away, away_st = join_cores(
            keep.reshape(flat_o),
            keep_st.reshape(flat_s),
            got.reshape(flat_o),
            got_st.reshape(flat_s),
        )
        got, got_st = over_y(away), over_y(away_st)
        out_rows, mixed_grad, context_grad, tile, gain_f, grad_feed = feed_forward(
            own, own_st, got, got_st, latent_flat, cot_flat, gains, feed
        )
    if fast:
        grad_media, latents_grad, grad_attend, mine_feed = back(
            ids,
            last,
            has,
            same,
            grad_feed,
            query_all,
            context_grad.reshape(cut),
            tile,
            keys,
            values,
            media,
            latent_key,
            latent_value,
            gains,
            attend,
            latent_flat,
            mixed_grad,
            gain_f,
            depth,
            16,
            BACK_PLAN,
        )
    else:
        grads = to_group(context_grad.reshape(cut))
        tiles = to_group(tile.reshape(samples, lat_dev, LANES))
        grad_media, latent_kv, keep, send, grad_kv, gain_m = attention_backward(
            ids,
            queries,
            grads,
            tiles,
            keys,
            values,
            latent_key,
            latent_value,
            media,
            gains,
            attend,
        )
        got = over_core(send)
        pair = keep.astype(F32) + got.astype(F32)
        got = over_y(pair[1].astype(BF16))
        latents_grad, grad_attend = latent_backward(
            latent_flat,
            mixed_grad,
            pair[0].reshape(rows, inner),
            got.reshape(rows, inner),
            latent_kv.reshape(rows, 2 * inner),
            gains,
            attend,
            grad_kv,
            gain_m,
            gain_f,
        )

        def owners(x):
            return lax.psum_scatter(x.astype(F32), AXES, scatter_dimension=0, tiled=True)

        mine = owners(grad_attend)
        own_expand, own_shrink, own_output = unpack_feed(grad_feed, width // BLOCKS, ff // BLOCKS)
        own_expand = owners(own_expand.reshape(width, ff))
        own_shrink = owners(own_shrink.reshape(ff, width))
        own_output = owners(own_output.reshape(inner, width))
    masters = (
        attend_weight,
        output_weight,
        expand_weight,
        shrink_weight,
        layer_gains,
        layer_biases,
    )
    moments = (
        attend_momentum,
        output_momentum,
        expand_momentum,
        shrink_momentum,
        gains_momentum,
        biases_momentum,
    )
    averages = (
        attend_average,
        output_average,
        expand_average,
        shrink_average,
        gains_average,
        biases_average,
    )
    step_rate = step_size(width, inner, ff)
    if fast:
        rates = tuple(step_rate * scale for scale in RATE_SCALES)
        states = masters + moments + averages
        states = tuple(x.T if x.shape[1] == 3 else x for x in states)
        norm, mine = norm_and_sum(grad_attend, mine_feed, images, lats)
        norm, *news = update_all(
            norm,
            mine,
            mine_feed,
            states,
            rates,
            inner,
            (out_rows, latents_grad, grad_media),
            6,
        )
        out_rows, latents_grad, grad_media = news[18:]
        news = [x.T if x.shape[0] == 3 else x for x in news[:18]]
        grad_norm = norm[0, 0]
        new_masters, new_buffers, new_smoothed = news[:6], news[6:12], news[12:]
    else:
        small = mine[:, 3 * inner :]
        owned = (
            mine[:, : 3 * inner],
            own_output,
            own_expand,
            own_shrink,
            small[:, 0:3],
            small[:, 3:6],
        )
        squares = sum(jnp.sum(piece * piece) for piece in owned)
        squares = lax.psum(squares, AXES)
        grad_norm = jnp.sqrt(squares)
        factor = jnp.minimum(1.0, CLIP_NORM / (grad_norm + 1e-06))
        decay_rates = (DECAY, DECAY, DECAY, DECAY, 0.0, 0.0)
        new_masters = []
        new_buffers = []
        new_smoothed = []
        for master, moment, average, reduced, decay_rate, rate_scale in zip(
            masters, moments, averages, owned, decay_rates, RATE_SCALES
        ):
            step_grad = factor * reduced + decay_rate * master
            buffer = MOMENTUM * moment + step_grad
            master_new = master - step_rate * rate_scale * (step_grad + MOMENTUM * buffer)
            new_masters.append(master_new)
            new_buffers.append(buffer)
            new_smoothed.append(AVERAGING * average + (1.0 - AVERAGING) * master_new)
    return (
        out_rows.reshape(latents.shape),
        grad_media,
        latents_grad.reshape(latents.shape),
        grad_norm,
        *new_masters,
        *new_buffers,
        *new_smoothed,
    )


def solution(mesh):
    rows = P(AXES, None)
    split = P("img", "lat", None)
    return jax.shard_map(
        functools.partial(shards, mesh.shape["img"], mesh.shape["lat"]),
        mesh=mesh,
        in_specs=(rows, split, P("img", None), split) + (rows,) * 18,
        out_specs=(split, rows, split, P()) + (rows,) * 18,
        check_vma=False,
    )
```

```python
import functools
import math

import jax
import jax.numpy as jnp
from jax import lax
from jax.experimental import pallas as pl
from jax.experimental.pallas import tpu as pltpu
from jax.sharding import PartitionSpec as P

HEADS = 8
HDIM = 64
PATCH_IMG = 256
GROUP = 4
TOGETHER = 2
EPS = 1e-05
MOMENTUM = 0.9
DECAY = 0.0001
AVERAGING = 0.6
CLIP_NORM = 1.0
RATE_SCALES = (1.0, 100.0, 1.0, 1.0, 15.0, 1.0)
AXES = ("img", "lat")
LANES = 128
BLOCKS = 32
SCALE = HDIM ** (-0.5)
MASKED = -1e30
F32 = jnp.float32
BF16 = jnp.bfloat16
MESH = pl.DeviceIdType.MESH
START_PLAN = ("b0", "a1", "c0", "b1", "a2", "c1", "b2", "a3", "c2", "b3", "c3")
HEAD_FLIPS = (0,)
BACK_FLIPS = ()
HEAD_PLAN = ((2, ('ea1', 'ez2', 'eb0')), (9, ('ez3',)), (12, ('eb1', 'ea2')), (19, ('ec0', 'eb2', 'ea3', 'sz1')), (24, ('ec1', 'eb3', 'sa0')), (26, ('ec2', 'ec3', 'sa1', 'sz2', 'sb0')))
HEAD_LATE = (
    ("sz3",),
    ("sc0", "sb1", "sa2"),
    (),
    (),
    ("sc1", "sb2", "sa3"),
    ("sc2", "sb3"),
    ("sc3",),
)
BACK_PLAN = ((0, ('a0',)), (1, ('a1',)), (3, ('b0',)), (4, ('a2',)), (7, ('c0', 'b1')), (8, ('a3',)), (11, ('c1', 'b2')), (13, ('c2', 'b3')), (13, ('c3',)))
NORM_PLAN = ("a0", "a1", "b0", "a2", "b1", "c0", "a3", "b2", "c1", "b3", "c2", "c3")
VMEM_LIMIT = 60 * 1024 * 1024


def mm(a, b):
    return jnp.dot(a, b, preferred_element_type=F32)


def mm_tn(a, b):
    return lax.dot_general(a, b, (((0,), (0,)), ((), ())), preferred_element_type=F32)


def mm_nt(a, b):
    return lax.dot_general(a, b, (((1,), (1,)), ((), ())), preferred_element_type=F32)


def any_spec():
    return pl.BlockSpec(memory_space=pl.ANY)


def vmem_spec():
    return pl.BlockSpec(memory_space=pltpu.VMEM)


def params(**more):
    return pltpu.CompilerParams(vmem_limit_bytes=VMEM_LIMIT, **more)


def place():
    img = lax.axis_index("img")
    lat = lax.axis_index("lat")
    return img // 2, img % 2, lat // 2, lat % 2


def flat(a, b, e, c):
    return ((a * 2 + b) * 2 + e) * 2 + c


def device(a, b, e, c):
    return (a * 2 + b, e * 2 + c)


def neighbours(a, b, e, c, colour):
    one = (a, (b + 1 - colour) % 2, (e + colour) % 2, c)
    two = (a, (b + colour) % 2, (e + 1 - colour) % 2, c)
    return [(a, b, e, c), one, two, (a, 1 - b, 1 - e, c)]


def z_order(depth):
    order = [0]
    for k in range(1, depth // 2 + 1):
        order.append(k)
        if depth - k != k:
            order.append(depth - k)
    return order


def greet(depth, a, b, e, c):
    barrier = pltpu.get_barrier_semaphore()
    friends = [device((a + k) % depth, b, e, c) for k in range(1, depth)]
    friends += [device(a, 1 - b, e, c), device(a, b, 1 - e, c), device(a, b, e, 1 - c)]
    for friend in friends:
        pl.semaphore_signal(barrier, inc=1, device_id=friend, device_id_type=MESH)
    pl.semaphore_wait(barrier, len(friends))


def add_into(target, first, second, chunk):
    @pl.loop(0, target.shape[1] // chunk)
    def _(step):
        part = pl.ds(pl.multiple_of(step * chunk, chunk), chunk)
        target[:, part] = first[:, part] + second[:, part]


def normalise(values):
    center = values - jnp.mean(values, axis=-1, keepdims=True)
    spread = jnp.mean(center * center, axis=-1, keepdims=True)
    scale = lax.rsqrt(spread + EPS)
    return center * scale, scale


def norm_back(grad, hat, scale, gain):
    inner = grad * gain
    first = jnp.mean(inner, axis=-1, keepdims=True)
    second = jnp.mean(inner * hat, axis=-1, keepdims=True)
    return scale * (inner - first - hat * second)


def media_kernel(m_ref, gb_ref, wk_ref, wv_ref, k_ref, v_ref):
    hat, _ = normalise(m_ref[...].astype(F32))
    normed = (hat * gb_ref[0:1, :] + gb_ref[3:4, :]).astype(BF16)
    k_ref[...] = mm(normed, wk_ref[...]).astype(BF16)
    v_ref[...] = mm(normed, wv_ref[...]).astype(BF16)


def media_project(media, gains, attend, inner):
    rows, width = media.shape
    out = jax.ShapeDtypeStruct((rows, inner), BF16)
    block = pl.BlockSpec((PATCH_IMG, inner), lambda i: (i, 0))
    return pl.pallas_call(
        media_kernel,
        grid=(rows // PATCH_IMG,),
        out_shape=(out, out),
        in_specs=[
            pl.BlockSpec((PATCH_IMG, width), lambda i: (i, 0)),
            pl.BlockSpec(gains.shape, lambda i: (0, 0)),
            pl.BlockSpec((width, inner), lambda i: (0, 1)),
            pl.BlockSpec((width, inner), lambda i: (0, 2)),
        ],
        out_specs=(block, block),
        compiler_params=params(),
        cost_estimate=pl.CostEstimate(
            flops=4 * rows * width * inner, bytes_accessed=4 * rows * width, transcendentals=0
        ),
        name="media_project",
    )(media, gains, attend, attend)


def latent_kernel(l_ref, gb_ref, w_ref, q_ref, k_ref, v_ref):
    inner = q_ref.shape[1]
    hat, _ = normalise(l_ref[...])
    normed = (hat * gb_ref[1:2, :] + gb_ref[4:5, :]).astype(BF16)
    q_ref[...] = mm(normed, w_ref[:, :inner]).astype(BF16)
    k_ref[...] = mm(normed, w_ref[:, inner : 2 * inner]).astype(BF16)
    v_ref[...] = mm(normed, w_ref[:, 2 * inner : 3 * inner]).astype(BF16)


def latent_project(latents, gains, attend, inner):
    out = jax.ShapeDtypeStruct((latents.shape[0], inner), BF16)
    return pl.pallas_call(
        latent_kernel,
        out_shape=(out, out, out),
        in_specs=[vmem_spec()] * 3,
        out_specs=(vmem_spec(),) * 3,
        compiler_params=params(),
        name="latent_project",
    )(latents, gains, attend)


def head_mask(kind):
    rows = lax.broadcasted_iota(jnp.int32, (GROUP * HDIM, GROUP * HDIM), 0) // HDIM
    cols = lax.broadcasted_iota(jnp.int32, (GROUP * HDIM, GROUP * HDIM), 1) // HDIM
    return (rows == cols).astype(F32).astype(kind)


def spread_heads(queries, group, mask):
    width = GROUP * HDIM
    part = queries[:, group * width : (group + 1) * width]
    return jnp.concatenate([part] * GROUP, axis=0) * mask


def take_heads(full, mask):
    total = None
    for h in range(GROUP):
        part = slice(h * HDIM, (h + 1) * HDIM)
        term = full[part, :] * mask[part, :]
        total = term if total is None else total + term
    return total


def pack_columns(columns, first=0):
    rows = columns[0].shape[0]
    lane = lax.broadcasted_iota(jnp.int32, (rows, LANES), 1)
    tile = jnp.zeros((rows, LANES), F32)
    for h, column in enumerate(columns):
        tile = jnp.where(lane == first + h, column, tile)
    return tile


def expand_columns(tile, width):
    rows = tile.shape[0]
    head = lax.broadcasted_iota(jnp.int32, (rows, width), 1) // HDIM
    out = jnp.zeros((rows, width), F32)
    for h in range(width // HDIM):
        out = jnp.where(head == h, tile[:, h : h + 1], out)
    return out


def forward_kernel(
    ids, q0, q1, q2, q3, k_ref, v_ref, kl_ref, vl_ref, keep, send, keep_st, send_st, acc, tops, sums
):
    step = pl.program_id(0)
    clips = acc.shape[0]
    inner = acc.shape[2]
    groups = inner // (GROUP * HDIM)
    width = GROUP * HDIM
    mask = head_mask(F32)
    mask_half = mask.astype(BF16)

    def clip_queries(clip):
        parts = [q[clip] for q in (q0, q1, q2, q3)]
        return jnp.concatenate(parts, axis=0) * BF16(SCALE)

    def attend(clip, keys, values, fresh):
        queries = clip_queries(clip)
        new_tops, new_sums = [], []
        for g in range(groups):
            cols = slice(g * width, (g + 1) * width)
            scores = mm_nt(spread_heads(queries, g, mask_half), keys[:, cols])
            top = jnp.max(scores, axis=-1, keepdims=True)
            if not fresh:
                old_tile = tops[clip]
                old_top = jnp.concatenate(
                    [old_tile[:, g * GROUP + h : g * GROUP + h + 1] for h in range(GROUP)], axis=0
                )
                top = jnp.maximum(top, old_top)
            probs = jnp.exp(scores - top)
            total = jnp.sum(probs, axis=-1, keepdims=True)
            part = take_heads(mm(probs.astype(BF16), values[:, cols]), mask)
            if not fresh:
                old_tile = sums[clip]
                old_sum = jnp.concatenate(
                    [old_tile[:, g * GROUP + h : g * GROUP + h + 1] for h in range(GROUP)], axis=0
                )
                shrink = jnp.exp(old_top - top)
                total = total + old_sum * shrink
                part = part + acc[clip, :, cols] * take_heads(shrink, mask)
            acc[clip, :, cols] = part
            for h in range(GROUP):
                new_tops.append(top[h * HDIM : (h + 1) * HDIM])
                new_sums.append(total[h * HDIM : (h + 1) * HDIM])
        tops[clip] = pack_columns(new_tops)
        sums[clip] = pack_columns(new_sums)

    @pl.when(step == 0)
    def _():
        @pl.loop(0, clips)
        def _(clip):
            attend(clip, kl_ref[clip], vl_ref[clip], True)

    attend(ids[step], k_ref[...], v_ref[...], False)

    @pl.when(step == pl.num_programs(0) - 1)
    def _():
        rows = keep.shape[2]
        lane = lax.broadcasted_iota(jnp.int32, (HDIM, LANES), 1)

        @pl.loop(0, clips)
        def _(clip):
            total = jnp.where(lane < HEADS, sums[clip], 1.0)
            stat = tops[clip] + jnp.log(total)
            out = (acc[clip] / expand_columns(total, inner)).astype(BF16)
            for r in range(4):
                part = slice(r * rows, (r + 1) * rows)
                where_o, where_s = (send, send_st) if r % 2 else (keep, keep_st)
                where_o[r // 2, clip] = out[part]
                where_s[r // 2, clip] = stat[part]


def attention_forward(ids, queries, keys, values, latent_keys, latent_values):
    clips, rows, inner = queries[0].shape
    frames = keys.shape[0] // PATCH_IMG
    out = jax.ShapeDtypeStruct((2, clips, rows, inner), BF16)
    stat = jax.ShapeDtypeStruct((2, clips, rows, LANES), F32)
    block = pl.BlockSpec((PATCH_IMG, inner), lambda i, ids: (i, 0))

    def whole(shape):
        return pl.BlockSpec(shape, lambda i, ids: (0,) * len(shape))

    return pl.pallas_call(
        forward_kernel,
        grid_spec=pltpu.PrefetchScalarGridSpec(
            num_scalar_prefetch=1,
            grid=(frames,),
            in_specs=[whole((clips, rows, inner))] * 4
            + [block, block]
            + [whole((clips, rows, inner))] * 2,
            out_specs=(whole(out.shape), whole(out.shape), whole(stat.shape), whole(stat.shape)),
            scratch_shapes=[
                pltpu.VMEM((clips, 4 * rows, inner), F32),
                pltpu.VMEM((clips, 4 * rows, LANES), F32),
                pltpu.VMEM((clips, 4 * rows, LANES), F32),
            ],
        ),
        out_shape=(out, out, stat, stat),
        compiler_params=params(),
        name="attention_forward",
    )(ids, *queries, keys, values, latent_keys, latent_values)


def join_partials(first, first_stat, second, second_stat):
    width = first.shape[-1]
    top = jnp.maximum(first_stat, second_stat)
    total = jnp.exp(first_stat - top) + jnp.exp(second_stat - top)
    stat = top + jnp.log(total)
    out = first.astype(F32) * expand_columns(jnp.exp(first_stat - stat), width)
    out = out + second.astype(F32) * expand_columns(jnp.exp(second_stat - stat), width)
    return out, stat


def join_kernel(keep, keep_st, got, got_st, own, own_st, away, away_st):
    out, stat = join_partials(keep[0], keep_st[0], got[0], got_st[0])
    own[...] = out
    own_st[...] = stat
    out, stat = join_partials(keep[1], keep_st[1], got[1], got_st[1])
    away[...] = out.astype(BF16)
    away_st[...] = stat


def join_cores(keep, keep_st, got, got_st):
    _, rows, inner = keep.shape
    stat = jax.ShapeDtypeStruct((rows, LANES), F32)
    return pl.pallas_call(
        join_kernel,
        out_shape=(
            jax.ShapeDtypeStruct((rows, inner), F32),
            stat,
            jax.ShapeDtypeStruct((rows, inner), BF16),
            stat,
        ),
        in_specs=[vmem_spec()] * 4,
        out_specs=(vmem_spec(),) * 4,
        compiler_params=params(),
        name="join_cores",
    )(keep, keep_st, got, got_st)


class Gather:
    def __init__(self, depth, x_ref, o_ref, local_sem, send_sem, recv_sem, flips=()):
        self.depth = depth
        self.refs = x_ref, o_ref
        self.sems = local_sem, send_sem, recv_sem
        self.at = place()
        c = self.at[3]
        self.homes = [neighbours(*self.at, 1 if k in flips else c) for k in range(depth)]
        self.order = z_order(depth)

    def row(self, k, j):
        a, _, _, c = self.at
        _, b, e, _ = self.homes[k][j % 4]
        return flat((a - k) % self.depth, b, e, c if j < 4 else 1 - c)

    def copy(self, k, j):
        x_ref, o_ref = self.refs
        a, b, e, c = self.at
        base = {1: 0, 2: 0, 3: 1}.get(j, j - 4)
        if j == 0:
            target, row, src = ((a + k) % self.depth, b, e, c), flat(a, b, e, c), x_ref
        else:
            target = self.homes[k][min(j, 2)] if j < 4 else (a, b, e, 1 - c)
            row = self.row(k, base)
            src = x_ref if (k, base) == (0, 0) else o_ref.at[row]
        slot = k * 8 + j
        return pltpu.make_async_remote_copy(
            src_ref=src,
            dst_ref=o_ref.at[row],
            send_sem=self.sems[1].at[slot],
            recv_sem=self.sems[2].at[slot],
            device_id=device(*target),
            device_id_type=MESH,
        )

    def arrive(self, k, j):
        x_ref, o_ref = self.refs
        a, b, e, c = self.at
        slot = k * 8 + j
        pltpu.make_async_remote_copy(
            src_ref=x_ref,
            dst_ref=o_ref.at[self.row(k, j)],
            send_sem=self.sems[1].at[slot],
            recv_sem=self.sems[2].at[slot],
            device_id=device(a, b, e, 1 - c),
            device_id_type=MESH,
        ).wait_recv()

    def own(self):
        x_ref, o_ref = self.refs
        return pltpu.make_async_copy(x_ref, o_ref.at[flat(*self.at)], self.sems[0])

    def far(self, k):
        self.copy(k, 0).start()

    def begin(self):
        self.far(self.order[1])
        self.first(0)

    def settle(self, k=None):
        for k in self.order if k is None else [k]:
            for j in range(4, 8):
                self.arrive(k, j)
            if k == 0:
                self.own().wait()

    def first(self, k):
        if k:
            self.arrive(k, 0)
        for j in (1, 2, 4):
            self.copy(k, j).start()

    def second(self, k):
        self.arrive(k, 1)
        self.copy(k, 3).start()
        self.copy(k, 5).start()
        self.arrive(k, 2)
        self.copy(k, 6).start()

    def third(self, k):
        self.arrive(k, 3)
        self.copy(k, 7).start()

    def run(self, names):
        acts = {"z": self.far, "a": self.first, "b": self.second, "c": self.third}
        for name in names:
            acts[name[0]](self.order[int(name[1:])])

    def finish(self):
        for k in range(self.depth):
            for j in range(8):
                if k or j:
                    self.copy(k, j).wait_send()


def start_kernel(
    depth,
    w_ref,
    g_ref,
    b_ref,
    expand_ref,
    shrink_ref,
    output_ref,
    all_ref,
    shard_e,
    shard_s,
    gains_ref,
    shard,
    small,
    local_sem,
    send_sem,
    recv_sem,
    small_sem,
):
    rows, cols = w_ref.shape
    gather = Gather(depth, shard, all_ref, local_sem, send_sem, recv_sem)
    shard[:, :cols] = w_ref[...].astype(BF16)
    zeros = jnp.zeros((LANES - 6, rows), F32)
    lines = jnp.concatenate([g_ref[...], b_ref[...], zeros], axis=0)
    shard[:, cols:] = lines.T.astype(BF16)
    greet(depth, *gather.at)
    gather.own().start()
    gather.begin()
    gather.run(("z2", "z3"))
    width = output_ref.shape[1]
    groups = expand_ref.shape[1] // width
    for n in range(groups):
        shard_e[n * rows : (n + 1) * rows, :] = expand_ref[:, n * width : (n + 1) * width].astype(BF16)
    shard_e[groups * rows :, :] = output_ref[...].astype(BF16)
    shard_s[...] = shrink_ref[...].astype(BF16)
    gather.run(START_PLAN)
    gather.settle()
    load = pltpu.make_async_copy(all_ref.at[:, :, pl.ds(cols, LANES)], small, small_sem)
    load.start()
    load.wait()
    lines = small[...].reshape(depth * 8 * rows, LANES).astype(F32).T
    gains_ref[...] = lines[:8]
    gather.finish()


def start(weight, gains, biases, expand, shrink, output, depth):
    rows, cols = weight.shape
    count = depth * 8
    width = output.shape[1]
    rows_e = expand.shape[1] // width * rows + output.shape[0]
    return pl.pallas_call(
        functools.partial(start_kernel, depth),
        out_shape=(
            jax.ShapeDtypeStruct((count, rows, cols + LANES), BF16),
            jax.ShapeDtypeStruct((rows_e, width), BF16),
            jax.ShapeDtypeStruct(shrink.shape, BF16),
            jax.ShapeDtypeStruct((8, count * rows), F32),
        ),
        in_specs=[vmem_spec()] * 6,
        out_specs=(any_spec(), vmem_spec(), vmem_spec(), vmem_spec()),
        scratch_shapes=[
            pltpu.VMEM((rows, cols + LANES), BF16),
            pltpu.VMEM((count, rows, LANES), BF16),
            pltpu.SemaphoreType.DMA,
            pltpu.SemaphoreType.DMA((count,)),
            pltpu.SemaphoreType.DMA((count,)),
            pltpu.SemaphoreType.DMA,
        ],
        compiler_params=params(collective_id=1, has_side_effects=True),
        name="start",
    )(weight, gains, biases, expand, shrink, output)


def latent_mask(rows, inner):
    row = lax.broadcasted_iota(jnp.int32, (HEADS * rows, inner), 0) // rows
    col = lax.broadcasted_iota(jnp.int32, (HEADS * rows, inner), 1) // HDIM
    return (row == col).astype(F32)


def latent_attention(queries, keys, values, mask):
    rows = keys.shape[0]
    count = queries.shape[0]
    half = mask.astype(BF16)
    wide_k = jnp.concatenate([keys] * HEADS, axis=0) * half
    wide_v = jnp.concatenate([values] * HEADS, axis=0) * half
    scores = mm_nt(wide_k, queries).reshape(HEADS, rows, count)
    top = jnp.max(scores, axis=1, keepdims=True)
    probs = jnp.exp(scores - top)
    total = jnp.sum(probs, axis=1)
    out = mm_tn(probs.reshape(HEADS * rows, count).astype(BF16), wide_v)
    zeros = jnp.zeros((LANES - HEADS, count), F32)

    def tile(x):
        return jnp.concatenate([x, zeros], axis=0).T

    return out, tile(top.reshape(HEADS, count)), tile(total)


def remote_copy(src, dst, sems, slot, target):
    return pltpu.make_async_remote_copy(
        src_ref=src,
        dst_ref=dst,
        send_sem=sems[0].at[slot],
        recv_sem=sems[1].at[slot],
        device_id=device(*target),
        device_id_type=MESH,
    )


def feed_kernel(
    own,
    own_st,
    got,
    got_st,
    lat_ref,
    cot_ref,
    gb_ref,
    w_ref,
    out_ref,
    mixed_grad,
    context_grad,
    tile_ref,
    gain_ref,
    gw_ref,
    expand_v,
    shrink_v,
    output_v,
    grad_e,
    grad_s,
    grad_o,
    normed_v,
    normed_t,
    hat_v,
    acc_g,
    load_sem,
    store_sem,
):
    groups = expand_v.shape[0]
    width = expand_v.shape[3]
    blocks = expand_v.shape[1]
    shrink_rows = shrink_v.shape[1]
    per_group = blocks // groups
    expand_rows = expand_v.shape[2]
    shrink_at = groups * expand_rows
    output_at = shrink_at + shrink_rows
    output_rows = output_v.shape[1]
    half = width // 2
    inner = own.shape[1]

    def load_expand(g):
        return pltpu.make_async_copy(
            w_ref.at[:, pl.ds(g * expand_rows, expand_rows), :], expand_v.at[g], load_sem.at[g]
        )

    def load_shrink(g):
        part = pl.ds(g * per_group, per_group)
        return pltpu.make_async_copy(
            w_ref.at[part, pl.ds(shrink_at, shrink_rows), :],
            shrink_v.at[part],
            load_sem.at[groups + g],
        )

    load_output = pltpu.make_async_copy(
        w_ref.at[:, pl.ds(output_at, output_rows), :], output_v, load_sem.at[2 * groups]
    )
    load_output.start()
    for g in range(groups):
        load_expand(g).start()
        load_shrink(g).start()

    context, stat = join_partials(own[...], own_st[...], got[...], got_st[...])
    context_half = context.astype(BF16)
    load_output.wait()
    weight_o = output_v[...].reshape(inner, width)
    mixed = lat_ref[...] + mm(context_half, weight_o)
    hat, scale = normalise(mixed)
    hat_v[...] = hat
    normed = (hat * gb_ref[2:3, :] + gb_ref[5:6, :]).astype(BF16)
    normed_v[...] = normed
    normed_t[...] = normed.astype(F32).T.astype(BF16)
    out_ref[...] = mixed
    acc_g[...] = jnp.zeros_like(acc_g)

    def store_e(s, slot):
        return pltpu.make_async_copy(
            grad_e.at[slot],
            gw_ref.at[:, pl.ds((s // 2) * expand_rows, expand_rows), pl.ds((s % 2) * half, half)],
            store_sem.at[slot],
        )

    def store_s(s, slot):
        rows = half // shrink_rows
        return pltpu.make_async_copy(
            grad_s.at[slot],
            gw_ref.at[pl.ds(s * rows, rows), pl.ds(shrink_at, shrink_rows), :],
            store_sem.at[2 + slot],
        )

    cot = cot_ref[...]
    steps = 2 * groups
    for s in range(steps):
        g, slot = s // 2, s % 2
        if slot == 0:
            load_expand(g).wait()
            load_shrink(g).wait()
        cols = slice(slot * half, (slot + 1) * half)
        w_e = expand_v[g, :, :, cols].reshape(blocks * expand_rows, half)
        first = s * half // shrink_rows
        w_s = shrink_v[first : first + half // shrink_rows].reshape(half, width)
        pre = mm(normed_v[...], w_e)
        cdf = 0.5 * (1.0 + lax.erf(pre * (0.5**0.5)))
        hidden = (pre * cdf).astype(BF16)
        out_ref[...] += mm(hidden, w_s)
        grad_hidden = mm_nt(cot, w_s)
        pdf = jnp.exp(-0.5 * pre * pre) * (1.0 / math.sqrt(2.0 * math.pi))
        grad_pre = (grad_hidden * (cdf + pre * pdf)).astype(BF16)
        if s >= 2:
            store_e(s - 2, slot).wait()
            store_s(s - 2, slot).wait()
        grad_s[slot] = mm_tn(hidden, cot).astype(BF16).reshape(half // shrink_rows, shrink_rows, width)
        grad_e[slot] = (
            mm(normed_t[...], grad_pre).astype(BF16).reshape(blocks, expand_rows, half)
        )
        store_e(s, slot).start()
        store_s(s, slot).start()
        acc_g[...] += mm_nt(grad_pre, w_e)

    grad_normed = acc_g[...]
    hat = hat_v[...]
    rows = gain_ref.shape[0]
    gain_ref[...] = jnp.concatenate(
        [
            jnp.sum(grad_normed * hat, axis=0, keepdims=True),
            jnp.sum(grad_normed, axis=0, keepdims=True),
            jnp.zeros((rows - 2, width), F32),
        ],
        axis=0,
    )
    total = cot.astype(F32) + norm_back(grad_normed, hat, scale, gb_ref[2:3, :])
    mixed_grad[...] = total
    attended = total.astype(BF16)
    grad_o[...] = mm_tn(context_half, attended).astype(BF16).reshape(grad_o.shape)
    store_o = pltpu.make_async_copy(
        grad_o, gw_ref.at[:, pl.ds(output_at, output_rows), :], store_sem.at[4]
    )
    store_o.start()
    grad_c = mm_nt(attended, weight_o).astype(BF16)
    context_grad[...] = grad_c
    product = grad_c.astype(F32) * context
    head = lax.broadcasted_iota(jnp.int32, product.shape, 1) // HDIM
    deltas = [
        jnp.sum(jnp.where(head == h, product, 0.0), axis=-1, keepdims=True) for h in range(HEADS)
    ]
    lane = lax.broadcasted_iota(jnp.int32, stat.shape, 1)
    tile_ref[...] = jnp.where(lane < HEADS, stat, pack_columns(deltas, HEADS))
    for s in range(steps - 2, steps):
        store_e(s, s % 2).wait()
        store_s(s, s % 2).wait()
    store_o.wait()


def feed_forward(own, own_st, got, got_st, latents, cotangent, gains, weights):
    rows, width = latents.shape
    inner = own.shape[1]
    blocks = weights.shape[0]
    ff = 4 * width
    groups = ff // width
    expand_rows = width // blocks
    shrink_rows = ff // blocks
    output_rows = inner // blocks
    half = width // 2
    flops = 2 * rows * (6 * width * ff + 3 * width * inner)
    return pl.pallas_call(
        feed_kernel,
        out_shape=(
            jax.ShapeDtypeStruct((rows, width), F32),
            jax.ShapeDtypeStruct((rows, width), F32),
            jax.ShapeDtypeStruct((rows, inner), BF16),
            jax.ShapeDtypeStruct((rows, LANES), F32),
            jax.ShapeDtypeStruct((8, width), F32),
            jax.ShapeDtypeStruct(weights.shape, BF16),
        ),
        in_specs=[vmem_spec()] * 7 + [any_spec()],
        out_specs=(vmem_spec(),) * 5 + (any_spec(),),
        scratch_shapes=[
            pltpu.VMEM((groups, blocks, expand_rows, width), BF16),
            pltpu.VMEM((blocks, shrink_rows, width), BF16),
            pltpu.VMEM((blocks, output_rows, width), BF16),
            pltpu.VMEM((2, blocks, expand_rows, half), BF16),
            pltpu.VMEM((2, half // shrink_rows, shrink_rows, width), BF16),
            pltpu.VMEM((blocks, output_rows, width), BF16),
            pltpu.VMEM((rows, width), BF16),
            pltpu.VMEM((width, rows), BF16),
            pltpu.VMEM((rows, width), F32),
            pltpu.VMEM((rows, width), F32),
            pltpu.SemaphoreType.DMA((2 * groups + 1,)),
            pltpu.SemaphoreType.DMA((5,)),
        ],
        compiler_params=params(),
        cost_estimate=pl.CostEstimate(
            flops=flops, bytes_accessed=4 * weights.size, transcendentals=2 * rows * ff
        ),
        name="feed_forward",
    )(own, own_st, got, got_st, latents, cotangent, gains, weights)


def backward_kernel(
    ids,
    q0,
    q1,
    q2,
    q3,
    g0,
    g1,
    g2,
    g3,
    t0,
    t1,
    t2,
    t3,
    k_ref,
    v_ref,
    kl_ref,
    vl_ref,
    m_ref,
    gb_ref,
    wk_ref,
    wv_ref,
    media_grad,
    latent_kv,
    keep,
    send,
    weight_grad,
    gain_ref,
    acc,
):
    step = pl.program_id(0)
    clips = acc.shape[0]
    inner = acc.shape[2]
    groups = inner // (GROUP * HDIM)
    width = GROUP * HDIM
    mask = head_mask(F32)
    mask_half = mask.astype(BF16)

    def attend(clip, keys, values, fresh):
        queries = jnp.concatenate([q[clip] for q in (q0, q1, q2, q3)], axis=0) * BF16(SCALE)
        grads = jnp.concatenate([g[clip] for g in (g0, g1, g2, g3)], axis=0)
        stats = jnp.concatenate([t[clip] for t in (t0, t1, t2, t3)], axis=0).T
        key_parts, value_parts = [], []
        for g in range(groups):
            cols = slice(g * width, (g + 1) * width)

            def line(first):
                at = first + g * GROUP
                return jnp.concatenate([stats[at + h : at + h + 1, :] for h in range(GROUP)], axis=1)

            wide_q = spread_heads(queries, g, mask_half)
            wide_g = spread_heads(grads, g, mask_half)
            probs = jnp.exp(mm_nt(keys[:, cols], wide_q) - line(0))
            grad_probs = mm_nt(values[:, cols], wide_g)
            grad_scores = (probs * (grad_probs - line(HEADS))).astype(BF16)
            key_parts.append(mm(grad_scores, wide_q))
            value_parts.append(mm(probs.astype(BF16), wide_g))
            part = take_heads(mm_tn(grad_scores, keys[:, cols]), mask)
            if fresh:
                acc[clip, :, cols] = part
            else:
                acc[clip, :, cols] += part
        return jnp.concatenate(key_parts + value_parts, axis=1).astype(BF16)

    @pl.when(step == 0)
    def _():
        gain_ref[...] = jnp.zeros_like(gain_ref)
        weight_grad[...] = jnp.zeros_like(weight_grad)

        @pl.loop(0, clips)
        def _(clip):
            latent_kv[clip] = attend(clip, kl_ref[clip], vl_ref[clip], True)

    grad_kv = attend(ids[step], k_ref[...], v_ref[...], False)
    hat, scale = normalise(m_ref[...].astype(F32))
    gain = gb_ref[0:1, :]
    normed = (hat * gain + gb_ref[3:4, :]).astype(BF16)
    weight_grad[...] += mm_tn(normed, grad_kv)
    grad = mm_nt(grad_kv[:, :inner], wk_ref[...]) + mm_nt(grad_kv[:, inner:], wv_ref[...])
    gain_ref[0:1, :] += jnp.sum(grad * hat, axis=0, keepdims=True)
    gain_ref[1:2, :] += jnp.sum(grad, axis=0, keepdims=True)
    media_grad[...] = norm_back(grad, hat, scale, gain).astype(BF16)

    @pl.when(step == pl.num_programs(0) - 1)
    def _():
        rows = keep.shape[2]

        @pl.loop(0, clips)
        def _(clip):
            out = (acc[clip] * SCALE).astype(BF16)
            for r in range(4):
                part = slice(r * rows, (r + 1) * rows)
                where_o = send if r % 2 else keep
                where_o[r // 2, clip] = out[part]


def attention_backward(
    ids, queries, grads, tiles, keys, values, latent_keys, latent_values, media, gains, attend
):
    clips, rows, inner = queries[0].shape
    width = media.shape[1]
    frames = keys.shape[0] // PATCH_IMG
    block = pl.BlockSpec((PATCH_IMG, inner), lambda i, ids: (i, 0))
    wide = pl.BlockSpec((PATCH_IMG, width), lambda i, ids: (i, 0))

    def whole(shape):
        return pl.BlockSpec(shape, lambda i, ids: (0,) * len(shape))

    def column(n):
        return pl.BlockSpec((width, inner), lambda i, ids: (0, n))

    query = whole((clips, rows, inner))
    pair = (2, clips, rows, inner)
    return pl.pallas_call(
        backward_kernel,
        grid_spec=pltpu.PrefetchScalarGridSpec(
            num_scalar_prefetch=1,
            grid=(frames,),
            in_specs=[query] * 8
            + [whole((clips, rows, LANES))] * 4
            + [block, block, query, query, wide, whole(gains.shape), column(1), column(2)],
            out_specs=(
                wide,
                whole((clips, rows, 2 * inner)),
                whole(pair),
                whole(pair),
                whole((width, 2 * inner)),
                whole((8, width)),
            ),
            scratch_shapes=[pltpu.VMEM((clips, 4 * rows, inner), F32)],
        ),
        out_shape=(
            jax.ShapeDtypeStruct(media.shape, BF16),
            jax.ShapeDtypeStruct((clips, rows, 2 * inner), BF16),
            jax.ShapeDtypeStruct(pair, BF16),
            jax.ShapeDtypeStruct(pair, BF16),
            jax.ShapeDtypeStruct((width, 2 * inner), F32),
            jax.ShapeDtypeStruct((8, width), F32),
        ),
        compiler_params=params(),
        name="attention_backward",
    )(
        ids,
        *queries,
        *grads,
        *tiles,
        keys,
        values,
        latent_keys,
        latent_values,
        media,
        gains,
        attend,
        attend,
    )


def last_kernel(
    lat_ref, mixed_grad, first, second, kv_ref, gb_ref, w_ref, gw_ref, gm_ref, gf_ref, out_ref, pack_ref
):
    inner = first.shape[1]
    width = lat_ref.shape[1]
    hat, scale = normalise(lat_ref[...])
    gain = gb_ref[1:2, :]
    normed = (hat * gain + gb_ref[4:5, :]).astype(BF16)
    grad_q = (first[...].astype(F32) + second[...].astype(F32)).astype(BF16)
    grad_kv = kv_ref[...]
    grad = mm_nt(grad_q, w_ref[:, :inner]) + mm_nt(grad_kv, w_ref[:, inner : 3 * inner])
    pack_ref[:, :inner] = mm_tn(normed, grad_q).astype(BF16)
    pack_ref[:, inner : 3 * inner] = (gw_ref[...] + mm_tn(normed, grad_kv)).astype(BF16)
    lines = jnp.concatenate(
        [
            gm_ref[0:1, :],
            jnp.sum(grad * hat, axis=0, keepdims=True),
            gf_ref[0:1, :],
            gm_ref[1:2, :],
            jnp.sum(grad, axis=0, keepdims=True),
            gf_ref[1:2, :],
            jnp.zeros((LANES - 6, width), F32),
        ],
        axis=0,
    )
    pack_ref[:, 3 * inner :] = lines.T.astype(BF16)
    out_ref[...] = mixed_grad[...] + norm_back(grad, hat, scale, gain)


def latent_backward(latents, mixed_grad, first, second, grad_kv, gains, attend, grad_w, gain_m, gain_f):
    return pl.pallas_call(
        last_kernel,
        out_shape=(
            jax.ShapeDtypeStruct(latents.shape, F32),
            jax.ShapeDtypeStruct(attend.shape, BF16),
        ),
        in_specs=[vmem_spec()] * 10,
        out_specs=(vmem_spec(), vmem_spec()),
        compiler_params=params(),
        name="latent_backward",
    )(latents, mixed_grad, first, second, grad_kv, gains, attend, grad_w, gain_m, gain_f)


class Scatter:
    def __init__(self, depth, chunk, g_ref, buffers, load_sem, sems, flips=()):
        self.depth = depth
        self.chunk = chunk
        self.g_ref = g_ref
        self.own, self.from_c, self.from_two, self.from_one, self.from_z = buffers
        self.load_sem = load_sem
        self.sems = sems
        self.at = place()
        a, b, e, c = self.at
        self.flips = flips
        self.homes = [neighbours(*self.at, 1 if k in flips else c) for k in range(depth)]
        self.twin = (a, b, e, 1 - c)
        self.order = z_order(depth)[::-1]

    def row(self, k, j, core):
        _, b, e, _ = self.homes[k][j]
        return flat((self.at[0] + k) % self.depth, b, e, core)

    def load(self, k, j):
        slot = k * 4 + j
        src = self.g_ref.at[self.row(k, j, self.at[3])]
        return pltpu.make_async_copy(src, self.own.at[slot], self.load_sem.at[slot])

    def to_twin(self, k, j):
        there = j if k in self.flips else (0, 2, 1, 3)[j]
        src = self.g_ref.at[self.row(k, there, 1 - self.at[3])]
        return remote_copy(src, self.from_c.at[k * 4 + j], self.sems, k * 8 + j, self.twin)

    def to_two(self, k, j):
        spot = self.from_two.at[k * 2 + j - 2]
        return remote_copy(self.own.at[k * 4 + j], spot, self.sems, k * 8 + 2 + j, self.homes[k][2])

    def to_one(self, k):
        return remote_copy(
            self.own.at[k * 4 + 1], self.from_one.at[k], self.sems, k * 8 + 6, self.homes[k][1]
        )

    def to_far(self, k):
        a, b, e, c = self.at
        target = ((a + k) % self.depth, b, e, c)
        return remote_copy(
            self.own.at[k * 4], self.from_z.at[k - 1], self.sems, k * 8 + 7, target
        )

    def add(self, slot, spot):
        mine = self.own.at[slot]
        add_into(mine, mine, spot, self.chunk)

    def begin(self):
        for k in self.order:
            for j in (3, 2, 1, 0):
                self.load(k, j).start()
                self.to_twin(k, j).start()

    def first(self, k):
        for j in (3, 2, 1, 0):
            self.load(k, j).wait()
            self.to_twin(k, j).wait_recv()
            self.add(k * 4 + j, self.from_c.at[k * 4 + j])
            if j >= 2:
                self.to_two(k, j).start()

    def second(self, k):
        for j in (3, 2):
            self.to_two(k, j).wait_recv()
            self.add(k * 4 + j - 2, self.from_two.at[k * 2 + j - 2])
            if j == 3:
                self.to_one(k).start()

    def third(self, k):
        self.to_one(k).wait_recv()
        self.add(k * 4, self.from_one.at[k])
        if k:
            self.to_far(k).start()

    def run(self, names):
        acts = {"a": self.first, "b": self.second, "c": self.third}
        for name in names:
            acts[name[0]](self.order[int(name[1:])])

    def finish(self, o_ref):
        for k in range(1, self.depth):
            self.to_far(k).wait_recv()

        @pl.loop(0, o_ref.shape[1] // self.chunk)
        def _(step):
            part = pl.ds(pl.multiple_of(step * self.chunk, self.chunk), self.chunk)
            total = self.own[0, :, part].astype(F32)
            for k in range(1, self.depth):
                total = total + self.from_z[k - 1, :, part].astype(F32)
            o_ref[:, part] = total

        for k in range(self.depth):
            for j in range(4):
                self.to_twin(k, j).wait_send()
            self.to_two(k, 3).wait_send()
            self.to_two(k, 2).wait_send()
            self.to_one(k).wait_send()
            if k:
                self.to_far(k).wait_send()


def scatter_buffers(depth, rows, cols):
    def slots(n):
        return pltpu.VMEM((n, rows, cols), BF16)

    return [slots(depth * 4), slots(depth * 4), slots(depth * 2), slots(depth), slots(depth - 1)]


def scatter_sems(depth):
    return [
        pltpu.SemaphoreType.DMA((depth * 4,)),
        pltpu.SemaphoreType.DMA((depth * 8,)),
        pltpu.SemaphoreType.DMA((depth * 8,)),
    ]


def latent_attention_back(queries, grads, stats, keys, values, mask):
    rows = keys.shape[0]
    count = queries.shape[0]
    half = mask.astype(BF16)
    wide_k = jnp.concatenate([keys] * HEADS, axis=0) * half
    wide_v = jnp.concatenate([values] * HEADS, axis=0) * half
    cut = (HEADS, rows, count)
    scores = mm_nt(wide_k, queries).reshape(cut)
    probs = jnp.exp(scores - stats[:HEADS][:, None, :])
    grad_probs = mm_nt(wide_v, grads).reshape(cut)
    grad_scores = probs * (grad_probs - stats[HEADS : 2 * HEADS][:, None, :])
    grad_scores = grad_scores.reshape(HEADS * rows, count).astype(BF16)
    probs = probs.reshape(HEADS * rows, count).astype(BF16)

    def fold(full):
        full = full * mask
        total = full[:rows]
        for h in range(1, HEADS):
            total = total + full[h * rows : (h + 1) * rows]
        return total

    grad_kv = [fold(mm(grad_scores, queries)), fold(mm(probs, grads))]
    return mm_tn(grad_scores, wide_k), jnp.concatenate(grad_kv, axis=1).astype(BF16)


def to_lines(tile):
    return tile.T[: 2 * HEADS]


def from_lines(lines):
    zeros = jnp.zeros((LANES - lines.shape[0], lines.shape[1]), F32)
    return jnp.concatenate([lines, zeros], axis=0).T


def back_kernel(
    depth,
    frames,
    chunk,
    plan,
    ids,
    last,
    has,
    same,
    g_ref,
    q_ref,
    context_grad,
    tile_ref,
    k_ref,
    v_ref,
    m_ref,
    kl_ref,
    vl_ref,
    gb_ref,
    w_ref,
    lat_ref,
    mixed_ref,
    gain_f,
    media_grad,
    latents_grad,
    pack_ref,
    mine_ref,
    own,
    from_c,
    from_two,
    from_one,
    from_z,
    load_sem,
    send_sem,
    recv_sem,
    all_g,
    lines,
    tiles,
    weight_acc,
    gain_acc,
    outs,
    latent_kv,
    keep,
    send,
    core_q,
    away,
    y_q,
    link_send,
    link_recv,
    mixed_sem,
):
    step = pl.program_id(0)
    a, b, e, c = place()
    twin, other = (a, b, e, 1 - c), (a, b, 1 - e, c)
    links = link_send, link_recv
    buffers = own, from_c, from_two, from_one, from_z
    scatter = Scatter(depth, chunk, g_ref, buffers, load_sem, (send_sem, recv_sem), BACK_FLIPS)
    clips, rows, inner = kl_ref.shape
    total_rows = clips * rows
    groups = inner // (GROUP * HDIM)
    width = GROUP * HDIM
    mask = head_mask(F32)
    mask_half = mask.astype(BF16)
    grad_copies = [
        remote_copy(all_g.at[0], all_g.at[2], links, 0, other),
        remote_copy(all_g.at[0], all_g.at[1], links, 1, twin),
        remote_copy(all_g.at[2], all_g.at[3], links, 2, twin),
    ]
    line_copies = [
        remote_copy(lines.at[0], lines.at[2], links, 3, other),
        remote_copy(lines.at[0], lines.at[1], links, 4, twin),
        remote_copy(lines.at[2], lines.at[3], links, 5, twin),
    ]
    core_copy = remote_copy(send, core_q, links, 6, twin)
    y_copy = remote_copy(away, y_q, links, 7, other)

    def clip_queries(clip):
        return jnp.concatenate([q_ref[r, clip] for r in range(4)], axis=0) * BF16(SCALE)

    def clip_grads(clip):
        return jnp.concatenate([all_g[r, clip] for r in range(4)], axis=0)

    def clip_stats(clip):
        return jnp.concatenate([tiles[r, clip] for r in range(4)], axis=0).T

    @pl.when(step == 0)
    def _():
        all_g[0] = context_grad[...]
        lines[0] = to_lines(tile_ref[...])
        greet(depth, a, b, e, c)
        for copies in (grad_copies, line_copies):
            copies[0].start()
            copies[1].start()
        scatter.begin()
        gain_acc[...] = jnp.zeros_like(gain_acc)
        weight_acc[...] = jnp.zeros_like(weight_acc)
        outs[0] = jnp.zeros_like(outs[0])

    for when, names in plan[:-2]:

        @pl.when(step == when)
        def _(names=names):
            scatter.run(names)

    @pl.when(step == 0)
    def _():
        for copies in (grad_copies, line_copies):
            copies[0].wait()
            copies[2].start()
        for copies in (grad_copies, line_copies):
            copies[1].wait()
            copies[2].wait()
        for r in range(4):
            tiles[r] = from_lines(lines[r]).reshape(clips, rows, LANES)

    @pl.when((step >= 1) & (step <= frames))
    def _():
        frame = step - 1
        before = jnp.maximum(frame - 1, 0)
        clip = ids[frame]
        joined = same[frame] == 1
        queries, grads, stats = clip_queries(clip), clip_grads(clip), clip_stats(clip)
        key_parts, value_parts = [], []
        for g in range(groups):
            cols = slice(g * width, (g + 1) * width)

            def line(first):
                at = first + g * GROUP
                return jnp.concatenate([stats[at + h : at + h + 1, :] for h in range(GROUP)], axis=1)

            wide_q = spread_heads(queries, g, mask_half)
            wide_g = spread_heads(grads, g, mask_half)
            keys = k_ref[:, cols]
            probs = jnp.exp(mm_nt(keys, wide_q) - line(0))
            grad_probs = mm_nt(v_ref[:, cols], wide_g)
            grad_scores = (probs * (grad_probs - line(HEADS))).astype(BF16)
            key_parts.append(mm(grad_scores, wide_q))
            value_parts.append(mm(probs.astype(BF16), wide_g))
            part = take_heads(mm_tn(grad_scores, keys), mask)
            outs[frame, :, cols] = part + jnp.where(joined, outs[before, :, cols], 0.0)
        grad_kv = jnp.concatenate(key_parts + value_parts, axis=1).astype(BF16)
        hat, scale = normalise(m_ref[...].astype(F32))
        gain = gb_ref[0:1, :]
        normed = (hat * gain + gb_ref[3:4, :]).astype(BF16)
        weight_acc[...] += mm_tn(normed, grad_kv)
        grad = mm_nt(grad_kv, w_ref[:, inner : 3 * inner])
        gain_acc[0:1, :] += jnp.sum(grad * hat, axis=0, keepdims=True)
        gain_acc[1:2, :] += jnp.sum(grad, axis=0, keepdims=True)
        media_grad[...] = norm_back(grad, hat, scale, gain).astype(BF16)

    @pl.when(step == frames + 1)
    def _():
        wide = latent_mask(rows, inner)

        def one_clip(clip):
            out, grad_kv = latent_attention_back(
                clip_queries(clip),
                clip_grads(clip),
                clip_stats(clip),
                kl_ref[clip],
                vl_ref[clip],
                wide,
            )
            out = (out + jnp.where(has[clip] == 1, outs[last[clip]], 0.0)) * SCALE
            return out, grad_kv

        @pl.loop(0, clips // TOGETHER)
        def _(index):
            some = [index * TOGETHER + n for n in range(TOGETHER)]
            results = [one_clip(clip) for clip in some]
            for clip, (out, grad_kv) in zip(some, results):
                latent_kv[clip] = grad_kv
                for r in range(4):
                    part = slice(r * rows, (r + 1) * rows)
                    if r % 2:
                        send[r // 2, clip] = out[part].astype(BF16)
                    else:
                        keep[r // 2, clip] = out[part]

        core_copy.start()
        hat, scale = normalise(lat_ref[...])
        gain = gb_ref[1:2, :]
        normed = (hat * gain + gb_ref[4:5, :]).astype(BF16)
        core_copy.wait()
        away[...] = (keep[1] + core_q[1].astype(F32)).astype(BF16)
        y_copy.start()
        grad_kv = latent_kv[...].reshape(total_rows, 2 * inner)
        pack_ref[:, inner : 3 * inner] = (weight_acc[...] + mm_tn(normed, grad_kv)).astype(BF16)
        grad = mm_nt(grad_kv, w_ref[:, inner : 3 * inner])
        mixed = weight_acc.at[:total_rows]
        load_mixed = pltpu.make_async_copy(mixed_ref, mixed, mixed_sem)
        load_mixed.start()
        scatter.run(plan[-2][1])
        y_copy.wait()
        grad_q = (keep[0] + core_q[0].astype(F32) + y_q[...].astype(F32)).astype(BF16)
        grad_q = grad_q.reshape(total_rows, inner)
        grad = grad + mm_nt(grad_q, w_ref[:, :inner])
        pack_ref[:, :inner] = mm_tn(normed, grad_q).astype(BF16)
        table = jnp.concatenate(
            [
                gain_acc[0:1, :],
                jnp.sum(grad * hat, axis=0, keepdims=True),
                gain_f[0:1, :],
                gain_acc[1:2, :],
                jnp.sum(grad, axis=0, keepdims=True),
                gain_f[1:2, :],
                jnp.zeros((LANES - 6, grad.shape[1]), F32),
            ],
            axis=0,
        )
        pack_ref[:, 3 * inner :] = table.T.astype(BF16)
        load_mixed.wait()
        latents_grad[...] = mixed[...] + norm_back(grad, hat, scale, gain)
        scatter.run(plan[-1][1])
        scatter.finish(mine_ref)


def back(
    ids,
    last,
    has,
    same,
    grad_feed,
    query_all,
    context_grad,
    tile,
    keys,
    values,
    media,
    latent_key,
    latent_value,
    gains,
    attend,
    latents,
    mixed_grad,
    gain_f,
    depth,
    chunk,
    plan,
):
    clips, rows, inner = latent_key.shape
    frames = media.shape[0] // PATCH_IMG
    width = media.shape[1]
    total = clips * rows
    cut = (clips, rows, inner)
    _, feed_rows, feed_cols = grad_feed.shape
    once = pl.Buffered(buffer_count=1)

    def whole(x):
        return pl.BlockSpec(x.shape, lambda i: (0,) * len(x.shape), pipeline_mode=once)

    def block(columns):
        return pl.BlockSpec((PATCH_IMG, columns), lambda i: (jnp.clip(i - 1, 0, frames - 1), 0))

    smem = pl.BlockSpec(memory_space=pltpu.SMEM)
    outs = (
        jax.ShapeDtypeStruct(media.shape, BF16),
        jax.ShapeDtypeStruct(latents.shape, F32),
        jax.ShapeDtypeStruct(attend.shape, BF16),
        jax.ShapeDtypeStruct((feed_rows, feed_cols), F32),
    )
    return pl.pallas_call(
        functools.partial(back_kernel, depth, frames, chunk, plan),
        grid=(frames + 2,),
        out_shape=outs,
        in_specs=[smem] * 4
        + [any_spec(), whole(query_all), whole(context_grad), whole(tile)]
        + [block(inner), block(inner), block(width)]
        + [whole(x) for x in (latent_key, latent_value, gains, attend, latents)]
        + [any_spec(), whole(gain_f)],
        out_specs=(block(width),) + tuple(whole(x) for x in outs[1:]),
        scratch_shapes=scatter_buffers(depth, feed_rows, feed_cols)
        + scatter_sems(depth)
        + [
            pltpu.VMEM((4,) + cut, BF16),
            pltpu.VMEM((4, 2 * HEADS, total), F32),
            pltpu.VMEM((4, clips, rows, LANES), F32),
            pltpu.VMEM((width, 2 * inner), F32),
            pltpu.VMEM((8, width), F32),
            pltpu.VMEM((frames, 4 * rows, inner), F32),
            pltpu.VMEM((clips, rows, 2 * inner), BF16),
            pltpu.VMEM((2,) + cut, F32),
            pltpu.VMEM((2,) + cut, BF16),
            pltpu.VMEM((2,) + cut, BF16),
            pltpu.VMEM(cut, BF16),
            pltpu.VMEM(cut, BF16),
            pltpu.SemaphoreType.DMA((8,)),
            pltpu.SemaphoreType.DMA((8,)),
            pltpu.SemaphoreType.DMA,
        ],
        compiler_params=params(collective_id=4, has_side_effects=True),
        name="back",
    )(
        ids,
        last,
        has,
        same,
        grad_feed,
        query_all,
        context_grad,
        tile,
        keys,
        values,
        media,
        latent_key,
        latent_value,
        gains,
        attend,
        latents,
        mixed_grad,
        gain_f,
    )


def head_kernel(
    depth,
    frames,
    parts,
    plan,
    late,
    ids,
    last,
    has,
    same,
    shard_e,
    shard_s,
    m_ref,
    lat_ref,
    cot_ref,
    gb_ref,
    wq_ref,
    k_ref,
    v_ref,
    q_ref,
    kl_ref,
    vl_ref,
    out_ref,
    mixed_grad,
    context_grad,
    tile_ref,
    gain_ref,
    gw_ref,
    all_k,
    all_v,
    all_q,
    outs,
    tops,
    sums,
    keep,
    keep_st,
    send,
    send_st,
    core_o,
    send_li,
    core_li,
    away,
    y_o,
    away_li,
    y_li,
    weights_e,
    weights_s,
    grad_s,
    grad_o,
    normed_v,
    normed_t,
    hat_v,
    local_sem,
    send_e,
    recv_e,
    send_s,
    recv_s,
    link_send,
    link_recv,
    out_sem,
    store_sem,
):
    step = pl.program_id(0)
    a, b, e, c = place()
    twin, other = (a, b, e, 1 - c), (a, b, 1 - e, c)
    links = link_send, link_recv
    gather_e = Gather(depth, shard_e, weights_e, local_sem.at[0], send_e, recv_e, HEAD_FLIPS)
    gather_s = Gather(depth, shard_s, weights_s, local_sem.at[1], send_s, recv_s, HEAD_FLIPS)
    clips, rows, inner = kl_ref.shape
    total_rows = clips * rows
    groups = inner // (GROUP * HDIM)
    width = GROUP * HDIM
    slabs = PATCH_IMG // all_k.shape[1]
    mask = head_mask(F32)
    mask_half = mask.astype(BF16)
    query_copies = [
        remote_copy(all_q.at[0], all_q.at[2], links, 0, other),
        remote_copy(all_q.at[0], all_q.at[1], links, 1, twin),
        remote_copy(all_q.at[2], all_q.at[3], links, 2, twin),
    ]
    share = clips // parts
    lot = share * rows

    def core_copies(p):
        some = pl.ds(p * share, share)
        return [
            remote_copy(send.at[:, some], core_o.at[:, some], links, 3 + 4 * p, twin),
            remote_copy(send_li.at[p], core_li.at[p], links, 4 + 4 * p, twin),
        ]

    def y_copies(p):
        some = pl.ds(p * lot, lot)
        return [
            remote_copy(away.at[some], y_o.at[some], links, 5 + 4 * p, other),
            remote_copy(away_li.at[p], y_li.at[p], links, 6 + 4 * p, other),
        ]

    def join_part(p):
        some = slice(p * share, (p + 1) * share)
        for copy in core_copies(p):
            copy.wait()
        for n in (1, 0):
            out, stat = join_partials(
                keep[n, some].reshape(lot, inner),
                keep_st[n, some].reshape(lot, LANES),
                core_o[n, some].reshape(lot, inner),
                from_lines(core_li[p, n]),
            )
            if n:
                away[p * lot : (p + 1) * lot] = out.astype(BF16)
                away_li[p] = to_lines(stat)
                for copy in y_copies(p):
                    copy.start()
            else:
                keep[0, some] = out.reshape(share, rows, inner)
                keep_st[0, some] = stat.reshape(share, rows, LANES)

    keep_queries = pltpu.make_async_copy(all_q, q_ref, out_sem)

    def run(names):
        for name in names:
            (gather_e if name[0] == "e" else gather_s).run((name[1:],))

    def clip_queries(clip):
        return jnp.concatenate([all_q[r, clip] for r in range(4)], axis=0) * BF16(SCALE)

    @pl.when(step == 0)
    def _():
        greet(depth, a, b, e, c)
        hat, _ = normalise(lat_ref[...])
        normed = (hat * gb_ref[1:2, :] + gb_ref[4:5, :]).astype(BF16)
        all_q[0] = mm(normed, wq_ref[:, :inner]).astype(BF16).reshape(clips, rows, inner)
        query_copies[0].start()
        query_copies[1].start()
        gather_s.own().start()
        gather_e.own().start()
        gather_e.begin()
        kl_ref[...] = (
            mm(normed, wq_ref[:, inner : 2 * inner]).astype(BF16).reshape(clips, rows, inner)
        )
        vl_ref[...] = (
            mm(normed, wq_ref[:, 2 * inner : 3 * inner]).astype(BF16).reshape(clips, rows, inner)
        )
        outs[0] = jnp.zeros_like(outs[0])
        tops[0] = jnp.zeros_like(tops[0])
        sums[0] = jnp.zeros_like(sums[0])

    @pl.when(step < frames)
    def _():
        hat, _ = normalise(m_ref[...].astype(F32))
        normed = (hat * gb_ref[0:1, :] + gb_ref[3:4, :]).astype(BF16)
        new_k = mm(normed, wq_ref[:, inner : 2 * inner]).astype(BF16)
        new_v = mm(normed, wq_ref[:, 2 * inner : 3 * inner]).astype(BF16)
        k_ref[...] = new_k
        v_ref[...] = new_v
        at = pl.ds(step * slabs, slabs)
        all_k[at] = new_k.reshape(slabs, PATCH_IMG // slabs, inner)
        all_v[at] = new_v.reshape(slabs, PATCH_IMG // slabs, inner)

    for when, names in plan:

        @pl.when(step == when)
        def _(names=names):
            run(names)

    @pl.when(step == frames // 2)
    def _():
        query_copies[0].wait()
        query_copies[2].start()

    @pl.when(step == frames)
    def _():
        query_copies[1].wait()
        query_copies[2].wait()
        keep_queries.start()

    @pl.when((step >= frames) & (step < 2 * frames))
    def _():
        frame = step - frames
        before = jnp.maximum(frame - 1, 0)
        queries = clip_queries(ids[frame])
        joined = same[frame] == 1
        old_tops = jnp.where(joined, tops[before], MASKED)
        old_sums = jnp.where(joined, sums[before], 0.0)
        at = pl.ds(frame * slabs, slabs)
        new_tops, new_sums = [], []
        for g in range(groups):
            cols = slice(g * width, (g + 1) * width)

            def column(tile):
                first = g * GROUP
                return jnp.concatenate(
                    [tile[:, first + h : first + h + 1] for h in range(GROUP)], axis=0
                )

            keys = all_k[at, :, cols].reshape(PATCH_IMG, width)
            values = all_v[at, :, cols].reshape(PATCH_IMG, width)
            scores = mm_nt(spread_heads(queries, g, mask_half), keys)
            old_top = column(old_tops)
            top = jnp.maximum(jnp.max(scores, axis=-1, keepdims=True), old_top)
            probs = jnp.exp(scores - top)
            shrink = jnp.exp(old_top - top)
            total = jnp.sum(probs, axis=-1, keepdims=True) + column(old_sums) * shrink
            part = take_heads(mm(probs.astype(BF16), values), mask)
            old = jnp.where(joined, outs[before, :, cols], 0.0)
            outs[frame, :, cols] = part + old * take_heads(shrink, mask)
            for h in range(GROUP):
                new_tops.append(top[h * HDIM : (h + 1) * HDIM])
                new_sums.append(total[h * HDIM : (h + 1) * HDIM])
        tops[frame] = pack_columns(new_tops)
        sums[frame] = pack_columns(new_sums)

    @pl.when((step >= 2 * frames) & (step < 2 * frames + parts))
    def _():
        wide = latent_mask(rows, inner)
        lane = lax.broadcasted_iota(jnp.int32, (4 * rows, LANES), 1)
        first = (step - 2 * frames) * share

        def one_clip(clip):
            out, top, total = latent_attention(clip_queries(clip), kl_ref[clip], vl_ref[clip], wide)
            at = last[clip]
            there = has[clip] == 1
            far_top = jnp.where(there, tops[at], MASKED)
            far_sum = jnp.where(there, sums[at], 0.0)
            far_out = jnp.where(there, outs[at], 0.0)
            both = jnp.maximum(top, far_top)
            near, far = jnp.exp(top - both), jnp.exp(far_top - both)
            total = jnp.where(lane < HEADS, total * near + far_sum * far, 1.0)
            stat = both + jnp.log(total)
            out = out * expand_columns(near / total, inner)
            return out + far_out * expand_columns(far / total, inner), stat

        @pl.loop(0, share // TOGETHER)
        def _(index):
            some = [first + index * TOGETHER + n for n in range(TOGETHER)]
            results = [one_clip(clip) for clip in some]
            for clip, (out, stat) in zip(some, results):
                for r in range(4):
                    part = slice(r * rows, (r + 1) * rows)
                    if r % 2:
                        send[r // 2, clip] = out[part].astype(BF16)
                        send_st[r // 2, clip] = stat[part]
                    else:
                        keep[r // 2, clip] = out[part]
                        keep_st[r // 2, clip] = stat[part]

    for p in range(parts):

        @pl.when(step == 2 * frames + p)
        def _(p=p):
            for n in range(2):
                some = slice(p * share, (p + 1) * share)
                send_li[p, n] = to_lines(send_st[n, some].reshape(lot, LANES))
            for copy in core_copies(p):
                copy.start()
            if p:
                join_part(p - 1)

    @pl.when(step == 2 * frames + parts)
    def _():
        run(late[0])
        join_part(parts - 1)
        run(late[1])
        gather_e.settle()
        run(late[2])
        for p in range(parts):
            for copy in y_copies(p):
                copy.wait()
        stat_y = jnp.concatenate([from_lines(y_li[p]) for p in range(parts)], axis=0)
        context, stat = join_partials(
            keep[0].reshape(total_rows, inner),
            keep_st[0].reshape(total_rows, LANES),
            y_o[...],
            stat_y,
        )
        feed_part(
            functools.partial(run_late, run, late[3:], gather_s),
            context,
            stat,
            depth,
            a,
            gather_s.order,
            lat_ref,
            cot_ref,
            gb_ref,
            weights_e,
            weights_s,
            out_ref,
            mixed_grad,
            context_grad,
            tile_ref,
            gain_ref,
            gw_ref,
            all_k,
            grad_s,
            grad_o,
            normed_v,
            normed_t,
            hat_v,
            store_sem,
        )
        keep_queries.wait()
        gather_e.finish()
        gather_s.finish()


def run_late(run, late, gather, n):
    run(late[n])
    gather.settle(gather.order[n])


def feed_part(
    ready,
    context,
    stat,
    depth,
    plane,
    order,
    lat_ref,
    cot_ref,
    gb_ref,
    weights_e,
    weights_s,
    out_ref,
    mixed_grad,
    context_grad,
    tile_ref,
    gain_ref,
    gw_ref,
    grad_e,
    grad_s,
    grad_o,
    normed_v,
    normed_t,
    hat_v,
    store_sem,
):
    blocks, shrink_rows, width = weights_s.shape
    per_plane = blocks // depth
    inner = context.shape[1]
    output_rows = inner // blocks
    expand_rows = (weights_e.shape[1] - output_rows) // depth
    shrink_at = depth * expand_rows
    output_at = shrink_at + shrink_rows
    half = width // 2
    half_rows = half // shrink_rows
    context_half = context.astype(BF16)

    def weight_o():
        return weights_e[:, shrink_at : shrink_at + output_rows, :].reshape(inner, width)

    mixed = lat_ref[...] + mm(context_half, weight_o())
    hat, scale = normalise(mixed)
    hat_v[...] = hat
    normed = (hat * gb_ref[2:3, :] + gb_ref[5:6, :]).astype(BF16)
    normed_v[...] = normed
    normed_t[...] = normed.astype(F32).T.astype(BF16)
    out_ref[...] = mixed
    mixed_grad[...] = jnp.zeros_like(mixed_grad)
    cot = cot_ref[...]
    stores = []
    for n, k in enumerate(order):
        ready(n)
        plane_k = (plane - k) % depth
        e_rows = pl.ds(pl.multiple_of(plane_k * expand_rows, expand_rows), expand_rows)
        for slot in range(2):
            cols = slice(slot * half, (slot + 1) * half)
            w_e = weights_e[:, e_rows, cols].reshape(blocks * expand_rows, half)
            s_rows = pl.ds(plane_k * per_plane + slot * half_rows, half_rows)
            w_s = weights_s[s_rows].reshape(half, width)
            pre = mm(normed_v[...], w_e)
            cdf = 0.5 * (1.0 + lax.erf(pre * (0.5**0.5)))
            hidden = (pre * cdf).astype(BF16)
            out_ref[...] += mm(hidden, w_s)
            grad_hidden = mm_nt(cot, w_s)
            pdf = jnp.exp(-0.5 * pre * pre) * (1.0 / math.sqrt(2.0 * math.pi))
            grad_pre = (grad_hidden * (cdf + pre * pdf)).astype(BF16)
            if n:
                for copy in stores[2 * (2 * n + slot) - 4 : 2 * (2 * n + slot) - 2]:
                    copy.wait()
            grad_s[slot] = mm_tn(hidden, cot).astype(BF16).reshape(half_rows, shrink_rows, width)
            e_spot = grad_e.at[pl.ds(slot * blocks, blocks)]
            e_spot[...] = (
                mm(normed_t[...], grad_pre).astype(BF16).reshape(blocks, expand_rows, half)
            )
            stores += [
                pltpu.make_async_copy(
                    e_spot, gw_ref.at[:, e_rows, pl.ds(slot * half, half)], store_sem.at[slot]
                ),
                pltpu.make_async_copy(
                    grad_s.at[slot],
                    gw_ref.at[s_rows, pl.ds(shrink_at, shrink_rows), :],
                    store_sem.at[2 + slot],
                ),
            ]
            stores[-1].start()
            stores[-2].start()
            mixed_grad[...] += mm_nt(grad_pre, w_e)

    grad_normed = mixed_grad[...]
    hat = hat_v[...]
    rows = gain_ref.shape[0]
    gain_ref[...] = jnp.concatenate(
        [
            jnp.sum(grad_normed * hat, axis=0, keepdims=True),
            jnp.sum(grad_normed, axis=0, keepdims=True),
            jnp.zeros((rows - 2, width), F32),
        ],
        axis=0,
    )
    total = cot.astype(F32) + norm_back(grad_normed, hat, scale, gb_ref[2:3, :])
    mixed_grad[...] = total
    attended = total.astype(BF16)
    grad_o[...] = mm_tn(context_half, attended).astype(BF16).reshape(grad_o.shape)
    store_o = pltpu.make_async_copy(
        grad_o, gw_ref.at[:, pl.ds(output_at, output_rows), :], store_sem.at[4]
    )
    store_o.start()
    grad_c = mm_nt(attended, weight_o()).astype(BF16)
    context_grad[...] = grad_c
    product = grad_c.astype(F32) * context
    head = lax.broadcasted_iota(jnp.int32, product.shape, 1) // HDIM
    deltas = [
        jnp.sum(jnp.where(head == h, product, 0.0), axis=-1, keepdims=True) for h in range(HEADS)
    ]
    lane = lax.broadcasted_iota(jnp.int32, stat.shape, 1)
    tile_ref[...] = jnp.where(lane < HEADS, stat, pack_columns(deltas, HEADS))
    for copy in stores[-4:]:
        copy.wait()
    store_o.wait()


def head(
    ids,
    last,
    has,
    same,
    shard_e,
    shard_s,
    media,
    latents,
    cotangent,
    gains,
    attend,
    clips,
    inner,
    depth,
    parts,
    plan,
    late,
):
    rows = latents.shape[0] // clips
    frames = media.shape[0] // PATCH_IMG
    width = media.shape[1]
    total = clips * rows
    cut = (clips, rows, inner)
    count = depth * 8
    expand_rows = (shard_e.shape[0] - inner // count) // depth
    feed_rows = shard_e.shape[0] + shard_s.shape[0]
    slabs = PATCH_IMG // expand_rows * frames
    half_rows = width // 2 // shard_s.shape[0]
    once = pl.Buffered(buffer_count=1)

    def whole(x):
        return pl.BlockSpec(x.shape, lambda i: (0,) * len(x.shape), pipeline_mode=once)

    def block(columns):
        return pl.BlockSpec((PATCH_IMG, columns), lambda i: (jnp.minimum(i, frames - 1), 0))

    smem = pl.BlockSpec(memory_space=pltpu.SMEM)
    kv = jax.ShapeDtypeStruct((media.shape[0], inner), BF16)
    small = jax.ShapeDtypeStruct(cut, BF16)
    outs = (
        small,
        small,
        jax.ShapeDtypeStruct((total, width), F32),
        jax.ShapeDtypeStruct((total, width), F32),
        jax.ShapeDtypeStruct((total, inner), BF16),
        jax.ShapeDtypeStruct((total, LANES), F32),
        jax.ShapeDtypeStruct((8, width), F32),
    )
    lines = (2 * HEADS, total // parts)
    dma = pltpu.SemaphoreType.DMA
    return pl.pallas_call(
        functools.partial(head_kernel, depth, frames, parts, plan, late),
        grid=(2 * frames + parts + 1,),
        out_shape=(kv, kv, jax.ShapeDtypeStruct((4,) + cut, BF16))
        + outs
        + (jax.ShapeDtypeStruct((count, feed_rows, width), BF16),),
        in_specs=[smem] * 4
        + [any_spec(), any_spec(), block(width)]
        + [whole(x) for x in (latents, cotangent, gains, attend)],
        out_specs=(block(inner), block(inner), any_spec())
        + tuple(whole(x) for x in outs)
        + (any_spec(),),
        scratch_shapes=[
            pltpu.VMEM((slabs, expand_rows, inner), BF16),
            pltpu.VMEM((slabs, expand_rows, inner), BF16),
            pltpu.VMEM((4,) + cut, BF16),
            pltpu.VMEM((frames, 4 * rows, inner), F32),
            pltpu.VMEM((frames, 4 * rows, LANES), F32),
            pltpu.VMEM((frames, 4 * rows, LANES), F32),
            pltpu.VMEM((2,) + cut, F32),
            pltpu.VMEM((2, clips, rows, LANES), F32),
            pltpu.VMEM((2,) + cut, BF16),
            pltpu.VMEM((2, clips, rows, LANES), F32),
            pltpu.VMEM((2,) + cut, BF16),
            pltpu.VMEM((parts, 2) + lines, F32),
            pltpu.VMEM((parts, 2) + lines, F32),
            pltpu.VMEM((total, inner), BF16),
            pltpu.VMEM((total, inner), BF16),
            pltpu.VMEM((parts,) + lines, F32),
            pltpu.VMEM((parts,) + lines, F32),
            pltpu.VMEM((count,) + shard_e.shape, BF16),
            pltpu.VMEM((count,) + shard_s.shape, BF16),
            pltpu.VMEM((2, half_rows) + shard_s.shape, BF16),
            pltpu.VMEM((count, inner // count, width), BF16),
            pltpu.VMEM((total, width), BF16),
            pltpu.VMEM((width, total), BF16),
            pltpu.VMEM((total, width), F32),
            dma((2,)),
            dma((count,)),
            dma((count,)),
            dma((count,)),
            dma((count,)),
            dma((3 + 4 * parts,)),
            dma((3 + 4 * parts,)),
            dma,
            dma((5,)),
        ],
        compiler_params=params(collective_id=2, has_side_effects=True),
        name="head",
    )(ids, last, has, same, shard_e, shard_s, media, latents, cotangent, gains, attend)


def norm_kernel(depth, images, lats, chunk, pack_ref, feed_ref, norm_ref, mine_ref, *refs):
    buffers, refs = refs[:5], refs[5:]
    load_sem, send_sem, recv_sem, tile, slots, tile_send, tile_recv = refs
    count = images * lats
    img = lax.axis_index("img")
    lat = lax.axis_index("lat")
    me = img * lats + lat
    scatter = Scatter(depth, chunk, pack_ref, buffers, load_sem, (send_sem, recv_sem))
    barrier = pltpu.get_barrier_semaphore()

    def other(k):
        there = (me + k) % count
        return there // lats, there % lats

    for k in range(1, count):
        pl.semaphore_signal(barrier, inc=1, device_id=other(k), device_id_type=MESH)
    pl.semaphore_wait(barrier, count - 1)
    scatter.begin()
    feed_rows = feed_ref.shape[0]
    squares = jnp.zeros((8, feed_ref.shape[1]), F32)
    for n in range(feed_rows // 8):
        part = feed_ref[n * 8 : (n + 1) * 8, :]
        squares = squares + part * part
    squares = jnp.sum(squares)
    scatter.run(NORM_PLAN)
    scatter.finish(mine_ref)
    own = mine_ref[...]
    tile[...] = jnp.full(tile.shape, squares + jnp.sum(own * own), F32)
    slots[me] = tile[...]

    def exchange(k, spot):
        return pltpu.make_async_remote_copy(
            src_ref=tile,
            dst_ref=slots.at[spot],
            send_sem=tile_send.at[k],
            recv_sem=tile_recv.at[k],
            device_id=other(k),
            device_id_type=MESH,
        )

    for k in range(1, count):
        exchange(k, me).start()
    for k in range(1, count):
        exchange(k, (me - k) % count).wait_recv()
    norm_ref[...] = jnp.sqrt(jnp.sum(slots[...], axis=0))
    for k in range(1, count):
        exchange(k, me).wait_send()


def norm_and_sum(grad_attend, mine_feed, images, lats):
    count = images * lats
    depth = images // 2
    rows = grad_attend.shape[0] // count
    cols = grad_attend.shape[1]
    tile = (8, LANES)
    return pl.pallas_call(
        functools.partial(norm_kernel, depth, images, lats, cols),
        out_shape=(jax.ShapeDtypeStruct(tile, F32), jax.ShapeDtypeStruct((rows, cols), F32)),
        in_specs=[any_spec(), vmem_spec()],
        out_specs=(vmem_spec(), vmem_spec()),
        scratch_shapes=scatter_buffers(depth, rows, cols)
        + scatter_sems(depth)
        + [
            pltpu.VMEM(tile, F32),
            pltpu.VMEM((count,) + tile, F32),
            pltpu.SemaphoreType.DMA((count,)),
            pltpu.SemaphoreType.DMA((count,)),
        ],
        compiler_params=params(collective_id=3, has_side_effects=True),
        name="norm",
    )(grad_attend.reshape(count, rows, cols), mine_feed)


def update_kernel(rates, inner, count, norm_ref, mine, feed_ref, *refs):
    states, refs = refs[:18], refs[18:]
    olds, refs = refs[:count], refs[count:]
    norm_out, news, moved = refs[0], refs[1:19], refs[19:]
    for old, new in zip(olds, moved):
        new[...] = old[...]

    @pl.when(pl.program_id(0) == 0)
    def _():
        update_states(rates, inner, norm_ref, mine, feed_ref, states, norm_out, news)


def update_states(rates, inner, norm_ref, mine, feed_ref, states, norm_out, news):
    norm = norm_ref[...]
    norm_out[...] = norm
    factor = jnp.minimum(1.0, CLIP_NORM / (norm + 1e-06))[0:1, 0:1]

    def update(n, grad, rows, cols, decay):
        at = (rows, cols)
        master = states[n][at]
        step_grad = factor * grad
        if decay:
            step_grad = step_grad + decay * master
        buffer = MOMENTUM * states[6 + n][at] + step_grad
        new = master - rates[n] * (step_grad + MOMENTUM * buffer)
        news[n][at] = new
        news[6 + n][at] = buffer
        news[12 + n][at] = AVERAGING * states[12 + n][at] + (1.0 - AVERAGING) * new

    every = slice(None)
    width = feed_ref.shape[1]
    expand_rows, expand_cols = states[2].shape
    shrink_rows = states[3].shape[0]
    at = expand_cols // width * expand_rows
    update(0, mine[:, : 3 * inner], every, every, DECAY)
    update(1, feed_ref[at + shrink_rows :, :], every, every, DECAY)
    for g in range(expand_cols // width):
        grad = feed_ref[g * expand_rows : (g + 1) * expand_rows, :]
        update(2, grad, every, slice(g * width, (g + 1) * width), DECAY)
    update(3, feed_ref[at : at + shrink_rows, :], every, every, DECAY)
    small = mine[:, 3 * inner :].T
    update(4, small[0:3], every, every, 0.0)
    update(5, small[3:6], every, every, 0.0)


def update_all(norm, mine, mine_feed, states, rates, inner, moved, steps):
    def like(x):
        return jax.ShapeDtypeStruct(x.shape, x.dtype)

    def whole(x):
        return pl.BlockSpec(x.shape, lambda i: (0, 0), pipeline_mode=pl.Buffered(buffer_count=1))

    def block(x):
        return pl.BlockSpec((x.shape[0] // steps, x.shape[1]), lambda i: (i, 0))

    blocks = [block(x) for x in moved]
    kept = [whole(x) for x in states]
    return pl.pallas_call(
        functools.partial(update_kernel, rates, inner, len(moved)),
        grid=(steps,),
        out_shape=(like(norm),) + tuple(like(x) for x in states) + tuple(like(x) for x in moved),
        in_specs=[whole(norm), whole(mine), whole(mine_feed)] + kept + blocks,
        out_specs=tuple([whole(norm)] + kept + blocks),
        compiler_params=params(),
        name="update",
    )(norm, mine, mine_feed, *states, *moved)


def pack_feed(expand, shrink, output):
    width = shrink.shape[-1]
    groups = expand.shape[-1] // width
    lead = expand.shape[:-2]
    rows = expand.shape[-2]
    cut = expand.reshape(lead + (rows, groups, width))
    cut = jnp.moveaxis(cut, -2, -3).reshape(lead + (groups * rows, width))
    return jnp.concatenate([cut, shrink, output], axis=-2)


def unpack_feed(packed, rows, shrink_rows):
    width = packed.shape[-1]
    lead = packed.shape[:-2]
    groups = (packed.shape[-2] - shrink_rows) // rows
    split = groups * rows
    cut = packed[..., :split, :].reshape(lead + (groups, rows, width))
    expand = jnp.moveaxis(cut, -3, -2).reshape(lead + (rows, groups * width))
    return (
        expand,
        packed[..., split : split + shrink_rows, :],
        packed[..., split + shrink_rows :, :],
    )


def step_size(width, inner, ff):
    return 0.37 * math.sqrt((4 * width * inner + 2 * width * ff) / width)


def lat_pairs(count, along_core):
    pairs = []
    for lat in range(count):
        e, c = lat // 2, lat % 2
        pairs.append((lat, e * 2 + 1 - c if along_core else (1 - e) * 2 + c))
    return pairs


def shards(
    images,
    lats,
    media,
    latents,
    counts,
    cotangent,
    attend_weight,
    output_weight,
    expand_weight,
    shrink_weight,
    layer_gains,
    layer_biases,
    attend_momentum,
    output_momentum,
    expand_momentum,
    shrink_momentum,
    gains_momentum,
    biases_momentum,
    attend_average,
    output_average,
    expand_average,
    shrink_average,
    gains_average,
    biases_average,
):
    devices = images * lats
    depth = images // 2
    fast = devices == BLOCKS and lats == 4 and images % 2 == 0
    samples, lat_dev, width = latents.shape
    rows = samples * lat_dev
    ff = expand_weight.shape[1]
    inner = attend_weight.shape[1] // 3
    patch_dev = media.shape[0]
    frames = patch_dev // PATCH_IMG
    over_core = functools.partial(lax.ppermute, axis_name="lat", perm=lat_pairs(lats, True))
    over_y = functools.partial(lax.ppermute, axis_name="lat", perm=lat_pairs(lats, False))

    attend_rows = attend_weight.shape[0]
    if fast:
        attend, shard_e, shard_s, gains = start(
            attend_weight,
            layer_gains.T,
            layer_biases.T,
            expand_weight,
            shrink_weight,
            output_weight,
            depth,
        )
        attend = attend.reshape(width, attend.shape[2])
    else:

        def everywhere(x):
            return lax.all_gather(x.astype(BF16), AXES, axis=0, tiled=True)

        small = jnp.concatenate([layer_gains, layer_biases], axis=1)
        small = jnp.pad(small, ((0, 0), (0, LANES - small.shape[1])))
        attend = everywhere(jnp.concatenate([attend_weight, small], axis=1))
        feed = pack_feed(
            everywhere(expand_weight).reshape(BLOCKS, width // BLOCKS, ff),
            everywhere(shrink_weight).reshape(BLOCKS, ff // BLOCKS, width),
            everywhere(output_weight).reshape(BLOCKS, inner // BLOCKS, width),
        )
        gains = attend[:, 3 * inner : 3 * inner + 8].astype(F32).T

    sample_ends = jnp.cumsum(counts[0])
    first_frame = lax.axis_index("lat") * frames
    frame_ids = first_frame + jnp.arange(frames, dtype=jnp.int32)
    ids = jnp.sum((frame_ids[:, None] >= sample_ends[None, :]).astype(jnp.int32), axis=1)
    ids = jnp.clip(ids, 0, samples - 1)

    latent_flat = latents.reshape(rows, width)
    cot_flat = cotangent.reshape(rows, width)
    cut = (samples, lat_dev, inner)

    def to_group(own):
        other = over_y(own)
        return [own, over_core(own), other, over_core(other)]

    if fast:
        clip = jnp.arange(samples, dtype=jnp.int32)
        here = ids[None, :] == clip[:, None]
        has = jnp.any(here, axis=1).astype(jnp.int32)
        last = jnp.max(jnp.where(here, jnp.arange(frames, dtype=jnp.int32)[None, :], 0), axis=1)
        same = jnp.concatenate([jnp.zeros((1,), jnp.int32), (ids[1:] == ids[:-1]).astype(jnp.int32)])
        (
            keys,
            values,
            query_all,
            latent_key,
            latent_value,
            out_rows,
            mixed_grad,
            context_grad,
            tile,
            gain_f,
            grad_feed,
        ) = head(
            ids,
            last,
            has,
            same,
            shard_e,
            shard_s,
            media,
            latent_flat,
            cot_flat,
            gains,
            attend,
            samples,
            inner,
            depth,
            3,
            HEAD_PLAN,
            HEAD_LATE,
        )
    else:
        query, latent_key, latent_value = latent_project(latent_flat, gains, attend, inner)
        latent_key = latent_key.reshape(cut)
        latent_value = latent_value.reshape(cut)
        queries = to_group(query.reshape(cut))
        keys, values = media_project(media, gains, attend, inner)
        keep, send, keep_st, send_st = attention_forward(
            ids, queries, keys, values, latent_key, latent_value
        )
        got, got_st = over_core(send), over_core(send_st)
        flat_o, flat_s = (2, rows, inner), (2, rows, LANES)
        own, own_st, away, away_st = join_cores(
            keep.reshape(flat_o),
            keep_st.reshape(flat_s),
            got.reshape(flat_o),
            got_st.reshape(flat_s),
        )
        got, got_st = over_y(away), over_y(away_st)
        out_rows, mixed_grad, context_grad, tile, gain_f, grad_feed = feed_forward(
            own, own_st, got, got_st, latent_flat, cot_flat, gains, feed
        )
    if fast:
        grad_media, latents_grad, grad_attend, mine_feed = back(
            ids,
            last,
            has,
            same,
            grad_feed,
            query_all,
            context_grad.reshape(cut),
            tile,
            keys,
            values,
            media,
            latent_key,
            latent_value,
            gains,
            attend,
            latent_flat,
            mixed_grad,
            gain_f,
            depth,
            2 * LANES,
            BACK_PLAN,
        )
    else:
        grads = to_group(context_grad.reshape(cut))
        tiles = to_group(tile.reshape(samples, lat_dev, LANES))
        grad_media, latent_kv, keep, send, grad_kv, gain_m = attention_backward(
            ids,
            queries,
            grads,
            tiles,
            keys,
            values,
            latent_key,
            latent_value,
            media,
            gains,
            attend,
        )
        got = over_core(send)
        pair = keep.astype(F32) + got.astype(F32)
        got = over_y(pair[1].astype(BF16))
        latents_grad, grad_attend = latent_backward(
            latent_flat,
            mixed_grad,
            pair[0].reshape(rows, inner),
            got.reshape(rows, inner),
            latent_kv.reshape(rows, 2 * inner),
            gains,
            attend,
            grad_kv,
            gain_m,
            gain_f,
        )

        def owners(x):
            return lax.psum_scatter(x.astype(F32), AXES, scatter_dimension=0, tiled=True)

        mine = owners(grad_attend)
        own_expand, own_shrink, own_output = unpack_feed(grad_feed, width // BLOCKS, ff // BLOCKS)
        own_expand = owners(own_expand.reshape(width, ff))
        own_shrink = owners(own_shrink.reshape(ff, width))
        own_output = owners(own_output.reshape(inner, width))
    masters = (
        attend_weight,
        output_weight,
        expand_weight,
        shrink_weight,
        layer_gains,
        layer_biases,
    )
    moments = (
        attend_momentum,
        output_momentum,
        expand_momentum,
        shrink_momentum,
        gains_momentum,
        biases_momentum,
    )
    averages = (
        attend_average,
        output_average,
        expand_average,
        shrink_average,
        gains_average,
        biases_average,
    )
    step_rate = step_size(width, inner, ff)
    if fast:
        rates = tuple(step_rate * scale for scale in RATE_SCALES)
        states = masters + moments + averages
        states = tuple(x.T if x.shape[1] == 3 else x for x in states)
        norm, mine = norm_and_sum(grad_attend, mine_feed, images, lats)
        norm, *news = update_all(
            norm,
            mine,
            mine_feed,
            states,
            rates,
            inner,
            (out_rows, latents_grad, grad_media),
            6,
        )
        out_rows, latents_grad, grad_media = news[18:]
        news = [x.T if x.shape[0] == 3 else x for x in news[:18]]
        grad_norm = norm[0, 0]
        new_masters, new_buffers, new_smoothed = news[:6], news[6:12], news[12:]
    else:
        small = mine[:, 3 * inner :]
        owned = (
            mine[:, : 3 * inner],
            own_output,
            own_expand,
            own_shrink,
            small[:, 0:3],
            small[:, 3:6],
        )
        squares = sum(jnp.sum(piece * piece) for piece in owned)
        squares = lax.psum(squares, AXES)
        grad_norm = jnp.sqrt(squares)
        factor = jnp.minimum(1.0, CLIP_NORM / (grad_norm + 1e-06))
        decay_rates = (DECAY, DECAY, DECAY, DECAY, 0.0, 0.0)
        new_masters = []
        new_buffers = []
        new_smoothed = []
        for master, moment, average, reduced, decay_rate, rate_scale in zip(
            masters, moments, averages, owned, decay_rates, RATE_SCALES
        ):
            step_grad = factor * reduced + decay_rate * master
            buffer = MOMENTUM * moment + step_grad
            master_new = master - step_rate * rate_scale * (step_grad + MOMENTUM * buffer)
            new_masters.append(master_new)
            new_buffers.append(buffer)
            new_smoothed.append(AVERAGING * average + (1.0 - AVERAGING) * master_new)
    return (
        out_rows.reshape(latents.shape),
        grad_media,
        latents_grad.reshape(latents.shape),
        grad_norm,
        *new_masters,
        *new_buffers,
        *new_smoothed,
    )


def solution(mesh):
    rows = P(AXES, None)
    split = P("img", "lat", None)
    return jax.shard_map(
        functools.partial(shards, mesh.shape["img"], mesh.shape["lat"]),
        mesh=mesh,
        in_specs=(rows, split, P("img", None), split) + (rows,) * 18,
        out_specs=(split, rows, split, P()) + (rows,) * 18,
        check_vma=False,
    )
```

```python
import functools
import math

import jax
import jax.numpy as jnp
from jax import lax
from jax.experimental import pallas as pl
from jax.experimental.pallas import tpu as pltpu
from jax.sharding import PartitionSpec as P

HEADS = 8
HDIM = 64
PATCH_IMG = 256
GROUP = 4
TOGETHER = 2
EPS = 1e-05
MOMENTUM = 0.9
DECAY = 0.0001
AVERAGING = 0.6
CLIP_NORM = 1.0
RATE_SCALES = (1.0, 100.0, 1.0, 1.0, 15.0, 1.0)
AXES = ("img", "lat")
LANES = 128
BLOCKS = 32
SCALE = HDIM ** (-0.5)
MASKED = -1e30
F32 = jnp.float32
BF16 = jnp.bfloat16
MESH = pl.DeviceIdType.MESH
START_PLAN = ("b0", "a1", "c0", "b1", "a2", "c1", "b2", "a3", "c2", "b3", "c3")
HEAD_FLIPS = (0,)
BACK_FLIPS = ()
HEAD_PLAN = ((2, ('ea1', 'ez2', 'eb0')), (9, ('ez3',)), (12, ('eb1', 'ea2')), (19, ('ec0', 'eb2', 'ea3', 'sz1')), (24, ('ec1', 'eb3', 'sa0')), (26, ('ec2', 'ec3', 'sa1', 'sz2', 'sb0')))
HEAD_LATE = (
    ("sz3",),
    ("sc0", "sb1", "sa2"),
    (),
    (),
    ("sc1", "sb2", "sa3"),
    ("sc2", "sb3"),
    ("sc3",),
)
BACK_PLAN = ((0, ('a0',)), (1, ('a1',)), (3, ('b0',)), (4, ('a2',)), (7, ('c0', 'b1')), (8, ('a3',)), (11, ('c1', 'b2')), (13, ('c2', 'b3')), (13, ('c3',)))
NORM_PLAN = ("a0", "a1", "b0", "a2", "b1", "c0", "a3", "b2", "c1", "b3", "c2", "c3")
VMEM_LIMIT = 60 * 1024 * 1024


def mm(a, b):
    return jnp.dot(a, b, preferred_element_type=F32)


def mm_tn(a, b):
    return lax.dot_general(a, b, (((0,), (0,)), ((), ())), preferred_element_type=F32)


def mm_nt(a, b):
    return lax.dot_general(a, b, (((1,), (1,)), ((), ())), preferred_element_type=F32)


def any_spec():
    return pl.BlockSpec(memory_space=pl.ANY)


def vmem_spec():
    return pl.BlockSpec(memory_space=pltpu.VMEM)


def params(**more):
    return pltpu.CompilerParams(vmem_limit_bytes=VMEM_LIMIT, **more)


def place():
    img = lax.axis_index("img")
    lat = lax.axis_index("lat")
    return img // 2, img % 2, lat // 2, lat % 2


def flat(a, b, e, c):
    return ((a * 2 + b) * 2 + e) * 2 + c


def device(a, b, e, c):
    return (a * 2 + b, e * 2 + c)


def neighbours(a, b, e, c, colour):
    one = (a, (b + 1 - colour) % 2, (e + colour) % 2, c)
    two = (a, (b + colour) % 2, (e + 1 - colour) % 2, c)
    return [(a, b, e, c), one, two, (a, 1 - b, 1 - e, c)]


def z_order(depth):
    order = [0]
    for k in range(1, depth // 2 + 1):
        order.append(k)
        if depth - k != k:
            order.append(depth - k)
    return order


def greet(depth, a, b, e, c):
    barrier = pltpu.get_barrier_semaphore()
    friends = [device((a + k) % depth, b, e, c) for k in range(1, depth)]
    friends += [device(a, 1 - b, e, c), device(a, b, 1 - e, c), device(a, b, e, 1 - c)]
    for friend in friends:
        pl.semaphore_signal(barrier, inc=1, device_id=friend, device_id_type=MESH)
    pl.semaphore_wait(barrier, len(friends))


def add_into(target, first, second, chunk):
    @pl.loop(0, target.shape[1] // chunk)
    def _(step):
        part = pl.ds(pl.multiple_of(step * chunk, chunk), chunk)
        target[:, part] = first[:, part] + second[:, part]


def normalise(values):
    center = values - jnp.mean(values, axis=-1, keepdims=True)
    spread = jnp.mean(center * center, axis=-1, keepdims=True)
    scale = lax.rsqrt(spread + EPS)
    return center * scale, scale


def norm_back(grad, hat, scale, gain):
    inner = grad * gain
    first = jnp.mean(inner, axis=-1, keepdims=True)
    second = jnp.mean(inner * hat, axis=-1, keepdims=True)
    return scale * (inner - first - hat * second)


def media_kernel(m_ref, gb_ref, wk_ref, wv_ref, k_ref, v_ref):
    hat, _ = normalise(m_ref[...].astype(F32))
    normed = (hat * gb_ref[0:1, :] + gb_ref[3:4, :]).astype(BF16)
    k_ref[...] = mm(normed, wk_ref[...]).astype(BF16)
    v_ref[...] = mm(normed, wv_ref[...]).astype(BF16)


def media_project(media, gains, attend, inner):
    rows, width = media.shape
    out = jax.ShapeDtypeStruct((rows, inner), BF16)
    block = pl.BlockSpec((PATCH_IMG, inner), lambda i: (i, 0))
    return pl.pallas_call(
        media_kernel,
        grid=(rows // PATCH_IMG,),
        out_shape=(out, out),
        in_specs=[
            pl.BlockSpec((PATCH_IMG, width), lambda i: (i, 0)),
            pl.BlockSpec(gains.shape, lambda i: (0, 0)),
            pl.BlockSpec((width, inner), lambda i: (0, 1)),
            pl.BlockSpec((width, inner), lambda i: (0, 2)),
        ],
        out_specs=(block, block),
        compiler_params=params(),
        cost_estimate=pl.CostEstimate(
            flops=4 * rows * width * inner, bytes_accessed=4 * rows * width, transcendentals=0
        ),
        name="media_project",
    )(media, gains, attend, attend)


def latent_kernel(l_ref, gb_ref, w_ref, q_ref, k_ref, v_ref):
    inner = q_ref.shape[1]
    hat, _ = normalise(l_ref[...])
    normed = (hat * gb_ref[1:2, :] + gb_ref[4:5, :]).astype(BF16)
    q_ref[...] = mm(normed, w_ref[:, :inner]).astype(BF16)
    k_ref[...] = mm(normed, w_ref[:, inner : 2 * inner]).astype(BF16)
    v_ref[...] = mm(normed, w_ref[:, 2 * inner : 3 * inner]).astype(BF16)


def latent_project(latents, gains, attend, inner):
    out = jax.ShapeDtypeStruct((latents.shape[0], inner), BF16)
    return pl.pallas_call(
        latent_kernel,
        out_shape=(out, out, out),
        in_specs=[vmem_spec()] * 3,
        out_specs=(vmem_spec(),) * 3,
        compiler_params=params(),
        name="latent_project",
    )(latents, gains, attend)


def head_mask(kind):
    rows = lax.broadcasted_iota(jnp.int32, (GROUP * HDIM, GROUP * HDIM), 0) // HDIM
    cols = lax.broadcasted_iota(jnp.int32, (GROUP * HDIM, GROUP * HDIM), 1) // HDIM
    return (rows == cols).astype(F32).astype(kind)


def spread_heads(queries, group, mask):
    width = GROUP * HDIM
    part = queries[:, group * width : (group + 1) * width]
    return jnp.concatenate([part] * GROUP, axis=0) * mask


def take_heads(full, mask):
    total = None
    for h in range(GROUP):
        part = slice(h * HDIM, (h + 1) * HDIM)
        term = full[part, :] * mask[part, :]
        total = term if total is None else total + term
    return total


def pack_columns(columns, first=0):
    rows = columns[0].shape[0]
    lane = lax.broadcasted_iota(jnp.int32, (rows, LANES), 1)
    tile = jnp.zeros((rows, LANES), F32)
    for h, column in enumerate(columns):
        tile = jnp.where(lane == first + h, column, tile)
    return tile


def expand_columns(tile, width):
    rows = tile.shape[0]
    head = lax.broadcasted_iota(jnp.int32, (rows, width), 1) // HDIM
    out = jnp.zeros((rows, width), F32)
    for h in range(width // HDIM):
        out = jnp.where(head == h, tile[:, h : h + 1], out)
    return out


def forward_kernel(
    ids, q0, q1, q2, q3, k_ref, v_ref, kl_ref, vl_ref, keep, send, keep_st, send_st, acc, tops, sums
):
    step = pl.program_id(0)
    clips = acc.shape[0]
    inner = acc.shape[2]
    groups = inner // (GROUP * HDIM)
    width = GROUP * HDIM
    mask = head_mask(F32)
    mask_half = mask.astype(BF16)

    def clip_queries(clip):
        parts = [q[clip] for q in (q0, q1, q2, q3)]
        return jnp.concatenate(parts, axis=0) * BF16(SCALE)

    def attend(clip, keys, values, fresh):
        queries = clip_queries(clip)
        new_tops, new_sums = [], []
        for g in range(groups):
            cols = slice(g * width, (g + 1) * width)
            scores = mm_nt(spread_heads(queries, g, mask_half), keys[:, cols])
            top = jnp.max(scores, axis=-1, keepdims=True)
            if not fresh:
                old_tile = tops[clip]
                old_top = jnp.concatenate(
                    [old_tile[:, g * GROUP + h : g * GROUP + h + 1] for h in range(GROUP)], axis=0
                )
                top = jnp.maximum(top, old_top)
            probs = jnp.exp(scores - top)
            total = jnp.sum(probs, axis=-1, keepdims=True)
            part = take_heads(mm(probs.astype(BF16), values[:, cols]), mask)
            if not fresh:
                old_tile = sums[clip]
                old_sum = jnp.concatenate(
                    [old_tile[:, g * GROUP + h : g * GROUP + h + 1] for h in range(GROUP)], axis=0
                )
                shrink = jnp.exp(old_top - top)
                total = total + old_sum * shrink
                part = part + acc[clip, :, cols] * take_heads(shrink, mask)
            acc[clip, :, cols] = part
            for h in range(GROUP):
                new_tops.append(top[h * HDIM : (h + 1) * HDIM])
                new_sums.append(total[h * HDIM : (h + 1) * HDIM])
        tops[clip] = pack_columns(new_tops)
        sums[clip] = pack_columns(new_sums)

    @pl.when(step == 0)
    def _():
        @pl.loop(0, clips)
        def _(clip):
            attend(clip, kl_ref[clip], vl_ref[clip], True)

    attend(ids[step], k_ref[...], v_ref[...], False)

    @pl.when(step == pl.num_programs(0) - 1)
    def _():
        rows = keep.shape[2]
        lane = lax.broadcasted_iota(jnp.int32, (HDIM, LANES), 1)

        @pl.loop(0, clips)
        def _(clip):
            total = jnp.where(lane < HEADS, sums[clip], 1.0)
            stat = tops[clip] + jnp.log(total)
            out = (acc[clip] / expand_columns(total, inner)).astype(BF16)
            for r in range(4):
                part = slice(r * rows, (r + 1) * rows)
                where_o, where_s = (send, send_st) if r % 2 else (keep, keep_st)
                where_o[r // 2, clip] = out[part]
                where_s[r // 2, clip] = stat[part]


def attention_forward(ids, queries, keys, values, latent_keys, latent_values):
    clips, rows, inner = queries[0].shape
    frames = keys.shape[0] // PATCH_IMG
    out = jax.ShapeDtypeStruct((2, clips, rows, inner), BF16)
    stat = jax.ShapeDtypeStruct((2, clips, rows, LANES), F32)
    block = pl.BlockSpec((PATCH_IMG, inner), lambda i, ids: (i, 0))

    def whole(shape):
        return pl.BlockSpec(shape, lambda i, ids: (0,) * len(shape))

    return pl.pallas_call(
        forward_kernel,
        grid_spec=pltpu.PrefetchScalarGridSpec(
            num_scalar_prefetch=1,
            grid=(frames,),
            in_specs=[whole((clips, rows, inner))] * 4
            + [block, block]
            + [whole((clips, rows, inner))] * 2,
            out_specs=(whole(out.shape), whole(out.shape), whole(stat.shape), whole(stat.shape)),
            scratch_shapes=[
                pltpu.VMEM((clips, 4 * rows, inner), F32),
                pltpu.VMEM((clips, 4 * rows, LANES), F32),
                pltpu.VMEM((clips, 4 * rows, LANES), F32),
            ],
        ),
        out_shape=(out, out, stat, stat),
        compiler_params=params(),
        name="attention_forward",
    )(ids, *queries, keys, values, latent_keys, latent_values)


def join_partials(first, first_stat, second, second_stat):
    width = first.shape[-1]
    top = jnp.maximum(first_stat, second_stat)
    total = jnp.exp(first_stat - top) + jnp.exp(second_stat - top)
    stat = top + jnp.log(total)
    out = first.astype(F32) * expand_columns(jnp.exp(first_stat - stat), width)
    out = out + second.astype(F32) * expand_columns(jnp.exp(second_stat - stat), width)
    return out, stat


def join_kernel(keep, keep_st, got, got_st, own, own_st, away, away_st):
    out, stat = join_partials(keep[0], keep_st[0], got[0], got_st[0])
    own[...] = out
    own_st[...] = stat
    out, stat = join_partials(keep[1], keep_st[1], got[1], got_st[1])
    away[...] = out.astype(BF16)
    away_st[...] = stat


def join_cores(keep, keep_st, got, got_st):
    _, rows, inner = keep.shape
    stat = jax.ShapeDtypeStruct((rows, LANES), F32)
    return pl.pallas_call(
        join_kernel,
        out_shape=(
            jax.ShapeDtypeStruct((rows, inner), F32),
            stat,
            jax.ShapeDtypeStruct((rows, inner), BF16),
            stat,
        ),
        in_specs=[vmem_spec()] * 4,
        out_specs=(vmem_spec(),) * 4,
        compiler_params=params(),
        name="join_cores",
    )(keep, keep_st, got, got_st)


class Gather:
    def __init__(self, depth, x_ref, o_ref, local_sem, send_sem, recv_sem, flips=()):
        self.depth = depth
        self.refs = x_ref, o_ref
        self.sems = local_sem, send_sem, recv_sem
        self.at = place()
        c = self.at[3]
        self.homes = [neighbours(*self.at, 1 if k in flips else c) for k in range(depth)]
        self.order = z_order(depth)

    def row(self, k, j):
        a, _, _, c = self.at
        _, b, e, _ = self.homes[k][j % 4]
        return flat((a - k) % self.depth, b, e, c if j < 4 else 1 - c)

    def copy(self, k, j):
        x_ref, o_ref = self.refs
        a, b, e, c = self.at
        base = {1: 0, 2: 0, 3: 1}.get(j, j - 4)
        if j == 0:
            target, row, src = ((a + k) % self.depth, b, e, c), flat(a, b, e, c), x_ref
        else:
            target = self.homes[k][min(j, 2)] if j < 4 else (a, b, e, 1 - c)
            row = self.row(k, base)
            src = x_ref if (k, base) == (0, 0) else o_ref.at[row]
        slot = k * 8 + j
        return pltpu.make_async_remote_copy(
            src_ref=src,
            dst_ref=o_ref.at[row],
            send_sem=self.sems[1].at[slot],
            recv_sem=self.sems[2].at[slot],
            device_id=device(*target),
            device_id_type=MESH,
        )

    def arrive(self, k, j):
        x_ref, o_ref = self.refs
        a, b, e, c = self.at
        slot = k * 8 + j
        pltpu.make_async_remote_copy(
            src_ref=x_ref,
            dst_ref=o_ref.at[self.row(k, j)],
            send_sem=self.sems[1].at[slot],
            recv_sem=self.sems[2].at[slot],
            device_id=device(a, b, e, 1 - c),
            device_id_type=MESH,
        ).wait_recv()

    def own(self):
        x_ref, o_ref = self.refs
        return pltpu.make_async_copy(x_ref, o_ref.at[flat(*self.at)], self.sems[0])

    def far(self, k):
        self.copy(k, 0).start()

    def begin(self):
        self.far(self.order[1])
        self.first(0)

    def settle(self, k=None):
        for k in self.order if k is None else [k]:
            for j in range(4, 8):
                self.arrive(k, j)
            if k == 0:
                self.own().wait()

    def first(self, k):
        if k:
            self.arrive(k, 0)
        for j in (1, 2, 4):
            self.copy(k, j).start()

    def second(self, k):
        self.arrive(k, 1)
        self.copy(k, 3).start()
        self.copy(k, 5).start()
        self.arrive(k, 2)
        self.copy(k, 6).start()

    def third(self, k):
        self.arrive(k, 3)
        self.copy(k, 7).start()

    def run(self, names):
        acts = {"z": self.far, "a": self.first, "b": self.second, "c": self.third}
        for name in names:
            acts[name[0]](self.order[int(name[1:])])

    def finish(self):
        for k in range(self.depth):
            for j in range(8):
                if k or j:
                    self.copy(k, j).wait_send()


def start_kernel(
    depth,
    w_ref,
    g_ref,
    b_ref,
    expand_ref,
    shrink_ref,
    output_ref,
    all_ref,
    shard_e,
    shard_s,
    gains_ref,
    shard,
    small,
    local_sem,
    send_sem,
    recv_sem,
    small_sem,
):
    rows, cols = w_ref.shape
    gather = Gather(depth, shard, all_ref, local_sem, send_sem, recv_sem)
    shard[:, :cols] = w_ref[...].astype(BF16)
    zeros = jnp.zeros((LANES - 6, rows), F32)
    lines = jnp.concatenate([g_ref[...], b_ref[...], zeros], axis=0)
    shard[:, cols:] = lines.T.astype(BF16)
    greet(depth, *gather.at)
    gather.own().start()
    gather.begin()
    gather.run(("z2", "z3"))
    width = output_ref.shape[1]
    groups = expand_ref.shape[1] // width
    for n in range(groups):
        shard_e[n * rows : (n + 1) * rows, :] = expand_ref[:, n * width : (n + 1) * width].astype(BF16)
    shard_e[groups * rows :, :] = output_ref[...].astype(BF16)
    shard_s[...] = shrink_ref[...].astype(BF16)
    gather.run(START_PLAN)
    gather.settle()
    load = pltpu.make_async_copy(all_ref.at[:, :, pl.ds(cols, LANES)], small, small_sem)
    load.start()
    load.wait()
    lines = small[...].reshape(depth * 8 * rows, LANES).astype(F32).T
    gains_ref[...] = lines[:8]
    gather.finish()


def start(weight, gains, biases, expand, shrink, output, depth):
    rows, cols = weight.shape
    count = depth * 8
    width = output.shape[1]
    rows_e = expand.shape[1] // width * rows + output.shape[0]
    return pl.pallas_call(
        functools.partial(start_kernel, depth),
        out_shape=(
            jax.ShapeDtypeStruct((count, rows, cols + LANES), BF16),
            jax.ShapeDtypeStruct((rows_e, width), BF16),
            jax.ShapeDtypeStruct(shrink.shape, BF16),
            jax.ShapeDtypeStruct((8, count * rows), F32),
        ),
        in_specs=[vmem_spec()] * 6,
        out_specs=(any_spec(), vmem_spec(), vmem_spec(), vmem_spec()),
        scratch_shapes=[
            pltpu.VMEM((rows, cols + LANES), BF16),
            pltpu.VMEM((count, rows, LANES), BF16),
            pltpu.SemaphoreType.DMA,
            pltpu.SemaphoreType.DMA((count,)),
            pltpu.SemaphoreType.DMA((count,)),
            pltpu.SemaphoreType.DMA,
        ],
        compiler_params=params(collective_id=1, has_side_effects=True),
        name="start",
    )(weight, gains, biases, expand, shrink, output)


def latent_mask(rows, inner):
    row = lax.broadcasted_iota(jnp.int32, (HEADS * rows, inner), 0) // rows
    col = lax.broadcasted_iota(jnp.int32, (HEADS * rows, inner), 1) // HDIM
    return (row == col).astype(F32)


def latent_attention(queries, keys, values, mask):
    rows = keys.shape[0]
    count = queries.shape[0]
    half = mask.astype(BF16)
    wide_k = jnp.concatenate([keys] * HEADS, axis=0) * half
    wide_v = jnp.concatenate([values] * HEADS, axis=0) * half
    scores = mm_nt(wide_k, queries).reshape(HEADS, rows, count)
    top = jnp.max(scores, axis=1, keepdims=True)
    probs = jnp.exp(scores - top)
    total = jnp.sum(probs, axis=1)
    out = mm_tn(probs.reshape(HEADS * rows, count).astype(BF16), wide_v)
    zeros = jnp.zeros((LANES - HEADS, count), F32)

    def tile(x):
        return jnp.concatenate([x, zeros], axis=0).T

    return out, tile(top.reshape(HEADS, count)), tile(total)


def remote_copy(src, dst, sems, slot, target):
    return pltpu.make_async_remote_copy(
        src_ref=src,
        dst_ref=dst,
        send_sem=sems[0].at[slot],
        recv_sem=sems[1].at[slot],
        device_id=device(*target),
        device_id_type=MESH,
    )


def feed_kernel(
    own,
    own_st,
    got,
    got_st,
    lat_ref,
    cot_ref,
    gb_ref,
    w_ref,
    out_ref,
    mixed_grad,
    context_grad,
    tile_ref,
    gain_ref,
    gw_ref,
    expand_v,
    shrink_v,
    output_v,
    grad_e,
    grad_s,
    grad_o,
    normed_v,
    normed_t,
    hat_v,
    acc_g,
    load_sem,
    store_sem,
):
    groups = expand_v.shape[0]
    width = expand_v.shape[3]
    blocks = expand_v.shape[1]
    shrink_rows = shrink_v.shape[1]
    per_group = blocks // groups
    expand_rows = expand_v.shape[2]
    shrink_at = groups * expand_rows
    output_at = shrink_at + shrink_rows
    output_rows = output_v.shape[1]
    half = width // 2
    inner = own.shape[1]

    def load_expand(g):
        return pltpu.make_async_copy(
            w_ref.at[:, pl.ds(g * expand_rows, expand_rows), :], expand_v.at[g], load_sem.at[g]
        )

    def load_shrink(g):
        part = pl.ds(g * per_group, per_group)
        return pltpu.make_async_copy(
            w_ref.at[part, pl.ds(shrink_at, shrink_rows), :],
            shrink_v.at[part],
            load_sem.at[groups + g],
        )

    load_output = pltpu.make_async_copy(
        w_ref.at[:, pl.ds(output_at, output_rows), :], output_v, load_sem.at[2 * groups]
    )
    load_output.start()
    for g in range(groups):
        load_expand(g).start()
        load_shrink(g).start()

    context, stat = join_partials(own[...], own_st[...], got[...], got_st[...])
    context_half = context.astype(BF16)
    load_output.wait()
    weight_o = output_v[...].reshape(inner, width)
    mixed = lat_ref[...] + mm(context_half, weight_o)
    hat, scale = normalise(mixed)
    hat_v[...] = hat
    normed = (hat * gb_ref[2:3, :] + gb_ref[5:6, :]).astype(BF16)
    normed_v[...] = normed
    normed_t[...] = normed.astype(F32).T.astype(BF16)
    out_ref[...] = mixed
    acc_g[...] = jnp.zeros_like(acc_g)

    def store_e(s, slot):
        return pltpu.make_async_copy(
            grad_e.at[slot],
            gw_ref.at[:, pl.ds((s // 2) * expand_rows, expand_rows), pl.ds((s % 2) * half, half)],
            store_sem.at[slot],
        )

    def store_s(s, slot):
        rows = half // shrink_rows
        return pltpu.make_async_copy(
            grad_s.at[slot],
            gw_ref.at[pl.ds(s * rows, rows), pl.ds(shrink_at, shrink_rows), :],
            store_sem.at[2 + slot],
        )

    cot = cot_ref[...]
    steps = 2 * groups
    for s in range(steps):
        g, slot = s // 2, s % 2
        if slot == 0:
            load_expand(g).wait()
            load_shrink(g).wait()
        cols = slice(slot * half, (slot + 1) * half)
        w_e = expand_v[g, :, :, cols].reshape(blocks * expand_rows, half)
        first = s * half // shrink_rows
        w_s = shrink_v[first : first + half // shrink_rows].reshape(half, width)
        pre = mm(normed_v[...], w_e)
        cdf = 0.5 * (1.0 + lax.erf(pre * (0.5**0.5)))
        hidden = (pre * cdf).astype(BF16)
        out_ref[...] += mm(hidden, w_s)
        grad_hidden = mm_nt(cot, w_s)
        pdf = jnp.exp(-0.5 * pre * pre) * (1.0 / math.sqrt(2.0 * math.pi))
        grad_pre = (grad_hidden * (cdf + pre * pdf)).astype(BF16)
        if s >= 2:
            store_e(s - 2, slot).wait()
            store_s(s - 2, slot).wait()
        grad_s[slot] = mm_tn(hidden, cot).astype(BF16).reshape(half // shrink_rows, shrink_rows, width)
        grad_e[slot] = (
            mm(normed_t[...], grad_pre).astype(BF16).reshape(blocks, expand_rows, half)
        )
        store_e(s, slot).start()
        store_s(s, slot).start()
        acc_g[...] += mm_nt(grad_pre, w_e)

    grad_normed = acc_g[...]
    hat = hat_v[...]
    rows = gain_ref.shape[0]
    gain_ref[...] = jnp.concatenate(
        [
            jnp.sum(grad_normed * hat, axis=0, keepdims=True),
            jnp.sum(grad_normed, axis=0, keepdims=True),
            jnp.zeros((rows - 2, width), F32),
        ],
        axis=0,
    )
    total = cot.astype(F32) + norm_back(grad_normed, hat, scale, gb_ref[2:3, :])
    mixed_grad[...] = total
    attended = total.astype(BF16)
    grad_o[...] = mm_tn(context_half, attended).astype(BF16).reshape(grad_o.shape)
    store_o = pltpu.make_async_copy(
        grad_o, gw_ref.at[:, pl.ds(output_at, output_rows), :], store_sem.at[4]
    )
    store_o.start()
    grad_c = mm_nt(attended, weight_o).astype(BF16)
    context_grad[...] = grad_c
    product = grad_c.astype(F32) * context
    head = lax.broadcasted_iota(jnp.int32, product.shape, 1) // HDIM
    deltas = [
        jnp.sum(jnp.where(head == h, product, 0.0), axis=-1, keepdims=True) for h in range(HEADS)
    ]
    lane = lax.broadcasted_iota(jnp.int32, stat.shape, 1)
    tile_ref[...] = jnp.where(lane < HEADS, stat, pack_columns(deltas, HEADS))
    for s in range(steps - 2, steps):
        store_e(s, s % 2).wait()
        store_s(s, s % 2).wait()
    store_o.wait()


def feed_forward(own, own_st, got, got_st, latents, cotangent, gains, weights):
    rows, width = latents.shape
    inner = own.shape[1]
    blocks = weights.shape[0]
    ff = 4 * width
    groups = ff // width
    expand_rows = width // blocks
    shrink_rows = ff // blocks
    output_rows = inner // blocks
    half = width // 2
    flops = 2 * rows * (6 * width * ff + 3 * width * inner)
    return pl.pallas_call(
        feed_kernel,
        out_shape=(
            jax.ShapeDtypeStruct((rows, width), F32),
            jax.ShapeDtypeStruct((rows, width), F32),
            jax.ShapeDtypeStruct((rows, inner), BF16),
            jax.ShapeDtypeStruct((rows, LANES), F32),
            jax.ShapeDtypeStruct((8, width), F32),
            jax.ShapeDtypeStruct(weights.shape, BF16),
        ),
        in_specs=[vmem_spec()] * 7 + [any_spec()],
        out_specs=(vmem_spec(),) * 5 + (any_spec(),),
        scratch_shapes=[
            pltpu.VMEM((groups, blocks, expand_rows, width), BF16),
            pltpu.VMEM((blocks, shrink_rows, width), BF16),
            pltpu.VMEM((blocks, output_rows, width), BF16),
            pltpu.VMEM((2, blocks, expand_rows, half), BF16),
            pltpu.VMEM((2, half // shrink_rows, shrink_rows, width), BF16),
            pltpu.VMEM((blocks, output_rows, width), BF16),
            pltpu.VMEM((rows, width), BF16),
            pltpu.VMEM((width, rows), BF16),
            pltpu.VMEM((rows, width), F32),
            pltpu.VMEM((rows, width), F32),
            pltpu.SemaphoreType.DMA((2 * groups + 1,)),
            pltpu.SemaphoreType.DMA((5,)),
        ],
        compiler_params=params(),
        cost_estimate=pl.CostEstimate(
            flops=flops, bytes_accessed=4 * weights.size, transcendentals=2 * rows * ff
        ),
        name="feed_forward",
    )(own, own_st, got, got_st, latents, cotangent, gains, weights)


def backward_kernel(
    ids,
    q0,
    q1,
    q2,
    q3,
    g0,
    g1,
    g2,
    g3,
    t0,
    t1,
    t2,
    t3,
    k_ref,
    v_ref,
    kl_ref,
    vl_ref,
    m_ref,
    gb_ref,
    wk_ref,
    wv_ref,
    media_grad,
    latent_kv,
    keep,
    send,
    weight_grad,
    gain_ref,
    acc,
):
    step = pl.program_id(0)
    clips = acc.shape[0]
    inner = acc.shape[2]
    groups = inner // (GROUP * HDIM)
    width = GROUP * HDIM
    mask = head_mask(F32)
    mask_half = mask.astype(BF16)

    def attend(clip, keys, values, fresh):
        queries = jnp.concatenate([q[clip] for q in (q0, q1, q2, q3)], axis=0) * BF16(SCALE)
        grads = jnp.concatenate([g[clip] for g in (g0, g1, g2, g3)], axis=0)
        stats = jnp.concatenate([t[clip] for t in (t0, t1, t2, t3)], axis=0).T
        key_parts, value_parts = [], []
        for g in range(groups):
            cols = slice(g * width, (g + 1) * width)

            def line(first):
                at = first + g * GROUP
                return jnp.concatenate([stats[at + h : at + h + 1, :] for h in range(GROUP)], axis=1)

            wide_q = spread_heads(queries, g, mask_half)
            wide_g = spread_heads(grads, g, mask_half)
            probs = jnp.exp(mm_nt(keys[:, cols], wide_q) - line(0))
            grad_probs = mm_nt(values[:, cols], wide_g)
            grad_scores = (probs * (grad_probs - line(HEADS))).astype(BF16)
            key_parts.append(mm(grad_scores, wide_q))
            value_parts.append(mm(probs.astype(BF16), wide_g))
            part = take_heads(mm_tn(grad_scores, keys[:, cols]), mask)
            if fresh:
                acc[clip, :, cols] = part
            else:
                acc[clip, :, cols] += part
        return jnp.concatenate(key_parts + value_parts, axis=1).astype(BF16)

    @pl.when(step == 0)
    def _():
        gain_ref[...] = jnp.zeros_like(gain_ref)
        weight_grad[...] = jnp.zeros_like(weight_grad)

        @pl.loop(0, clips)
        def _(clip):
            latent_kv[clip] = attend(clip, kl_ref[clip], vl_ref[clip], True)

    grad_kv = attend(ids[step], k_ref[...], v_ref[...], False)
    hat, scale = normalise(m_ref[...].astype(F32))
    gain = gb_ref[0:1, :]
    normed = (hat * gain + gb_ref[3:4, :]).astype(BF16)
    weight_grad[...] += mm_tn(normed, grad_kv)
    grad = mm_nt(grad_kv[:, :inner], wk_ref[...]) + mm_nt(grad_kv[:, inner:], wv_ref[...])
    gain_ref[0:1, :] += jnp.sum(grad * hat, axis=0, keepdims=True)
    gain_ref[1:2, :] += jnp.sum(grad, axis=0, keepdims=True)
    media_grad[...] = norm_back(grad, hat, scale, gain).astype(BF16)

    @pl.when(step == pl.num_programs(0) - 1)
    def _():
        rows = keep.shape[2]

        @pl.loop(0, clips)
        def _(clip):
            out = (acc[clip] * SCALE).astype(BF16)
            for r in range(4):
                part = slice(r * rows, (r + 1) * rows)
                where_o = send if r % 2 else keep
                where_o[r // 2, clip] = out[part]


def attention_backward(
    ids, queries, grads, tiles, keys, values, latent_keys, latent_values, media, gains, attend
):
    clips, rows, inner = queries[0].shape
    width = media.shape[1]
    frames = keys.shape[0] // PATCH_IMG
    block = pl.BlockSpec((PATCH_IMG, inner), lambda i, ids: (i, 0))
    wide = pl.BlockSpec((PATCH_IMG, width), lambda i, ids: (i, 0))

    def whole(shape):
        return pl.BlockSpec(shape, lambda i, ids: (0,) * len(shape))

    def column(n):
        return pl.BlockSpec((width, inner), lambda i, ids: (0, n))

    query = whole((clips, rows, inner))
    pair = (2, clips, rows, inner)
    return pl.pallas_call(
        backward_kernel,
        grid_spec=pltpu.PrefetchScalarGridSpec(
            num_scalar_prefetch=1,
            grid=(frames,),
            in_specs=[query] * 8
            + [whole((clips, rows, LANES))] * 4
            + [block, block, query, query, wide, whole(gains.shape), column(1), column(2)],
            out_specs=(
                wide,
                whole((clips, rows, 2 * inner)),
                whole(pair),
                whole(pair),
                whole((width, 2 * inner)),
                whole((8, width)),
            ),
            scratch_shapes=[pltpu.VMEM((clips, 4 * rows, inner), F32)],
        ),
        out_shape=(
            jax.ShapeDtypeStruct(media.shape, BF16),
            jax.ShapeDtypeStruct((clips, rows, 2 * inner), BF16),
            jax.ShapeDtypeStruct(pair, BF16),
            jax.ShapeDtypeStruct(pair, BF16),
            jax.ShapeDtypeStruct((width, 2 * inner), F32),
            jax.ShapeDtypeStruct((8, width), F32),
        ),
        compiler_params=params(),
        name="attention_backward",
    )(
        ids,
        *queries,
        *grads,
        *tiles,
        keys,
        values,
        latent_keys,
        latent_values,
        media,
        gains,
        attend,
        attend,
    )


def last_kernel(
    lat_ref, mixed_grad, first, second, kv_ref, gb_ref, w_ref, gw_ref, gm_ref, gf_ref, out_ref, pack_ref
):
    inner = first.shape[1]
    width = lat_ref.shape[1]
    hat, scale = normalise(lat_ref[...])
    gain = gb_ref[1:2, :]
    normed = (hat * gain + gb_ref[4:5, :]).astype(BF16)
    grad_q = (first[...].astype(F32) + second[...].astype(F32)).astype(BF16)
    grad_kv = kv_ref[...]
    grad = mm_nt(grad_q, w_ref[:, :inner]) + mm_nt(grad_kv, w_ref[:, inner : 3 * inner])
    pack_ref[:, :inner] = mm_tn(normed, grad_q).astype(BF16)
    pack_ref[:, inner : 3 * inner] = (gw_ref[...] + mm_tn(normed, grad_kv)).astype(BF16)
    lines = jnp.concatenate(
        [
            gm_ref[0:1, :],
            jnp.sum(grad * hat, axis=0, keepdims=True),
            gf_ref[0:1, :],
            gm_ref[1:2, :],
            jnp.sum(grad, axis=0, keepdims=True),
            gf_ref[1:2, :],
            jnp.zeros((LANES - 6, width), F32),
        ],
        axis=0,
    )
    pack_ref[:, 3 * inner :] = lines.T.astype(BF16)
    out_ref[...] = mixed_grad[...] + norm_back(grad, hat, scale, gain)


def latent_backward(latents, mixed_grad, first, second, grad_kv, gains, attend, grad_w, gain_m, gain_f):
    return pl.pallas_call(
        last_kernel,
        out_shape=(
            jax.ShapeDtypeStruct(latents.shape, F32),
            jax.ShapeDtypeStruct(attend.shape, BF16),
        ),
        in_specs=[vmem_spec()] * 10,
        out_specs=(vmem_spec(), vmem_spec()),
        compiler_params=params(),
        name="latent_backward",
    )(latents, mixed_grad, first, second, grad_kv, gains, attend, grad_w, gain_m, gain_f)


class Scatter:
    def __init__(self, depth, chunk, g_ref, buffers, load_sem, sems, flips=()):
        self.depth = depth
        self.chunk = chunk
        self.g_ref = g_ref
        self.own, self.from_c, self.from_two, self.from_one, self.from_z = buffers
        self.load_sem = load_sem
        self.sems = sems
        self.at = place()
        a, b, e, c = self.at
        self.flips = flips
        self.homes = [neighbours(*self.at, 1 if k in flips else c) for k in range(depth)]
        self.twin = (a, b, e, 1 - c)
        self.order = z_order(depth)[::-1]

    def row(self, k, j, core):
        _, b, e, _ = self.homes[k][j]
        return flat((self.at[0] + k) % self.depth, b, e, core)

    def load(self, k, j):
        slot = k * 4 + j
        src = self.g_ref.at[self.row(k, j, self.at[3])]
        return pltpu.make_async_copy(src, self.own.at[slot], self.load_sem.at[slot])

    def to_twin(self, k, j):
        there = j if k in self.flips else (0, 2, 1, 3)[j]
        src = self.g_ref.at[self.row(k, there, 1 - self.at[3])]
        return remote_copy(src, self.from_c.at[k * 4 + j], self.sems, k * 8 + j, self.twin)

    def to_two(self, k, j):
        spot = self.from_two.at[k * 2 + j - 2]
        return remote_copy(self.own.at[k * 4 + j], spot, self.sems, k * 8 + 2 + j, self.homes[k][2])

    def to_one(self, k):
        return remote_copy(
            self.own.at[k * 4 + 1], self.from_one.at[k], self.sems, k * 8 + 6, self.homes[k][1]
        )

    def to_far(self, k):
        a, b, e, c = self.at
        target = ((a + k) % self.depth, b, e, c)
        return remote_copy(
            self.own.at[k * 4], self.from_z.at[k - 1], self.sems, k * 8 + 7, target
        )

    def add(self, slot, spot):
        mine = self.own.at[slot]
        add_into(mine, mine, spot, self.chunk)

    def begin(self):
        for k in self.order:
            for j in (3, 2, 1, 0):
                self.load(k, j).start()
                self.to_twin(k, j).start()

    def first(self, k):
        for j in (3, 2, 1, 0):
            self.load(k, j).wait()
            self.to_twin(k, j).wait_recv()
            self.add(k * 4 + j, self.from_c.at[k * 4 + j])
            if j >= 2:
                self.to_two(k, j).start()

    def second(self, k):
        for j in (3, 2):
            self.to_two(k, j).wait_recv()
            self.add(k * 4 + j - 2, self.from_two.at[k * 2 + j - 2])
            if j == 3:
                self.to_one(k).start()

    def third(self, k):
        self.to_one(k).wait_recv()
        self.add(k * 4, self.from_one.at[k])
        if k:
            self.to_far(k).start()

    def run(self, names):
        acts = {"a": self.first, "b": self.second, "c": self.third}
        for name in names:
            acts[name[0]](self.order[int(name[1:])])

    def finish(self, o_ref):
        for k in range(1, self.depth):
            self.to_far(k).wait_recv()

        @pl.loop(0, o_ref.shape[1] // self.chunk)
        def _(step):
            part = pl.ds(pl.multiple_of(step * self.chunk, self.chunk), self.chunk)
            total = self.own[0, :, part].astype(F32)
            for k in range(1, self.depth):
                total = total + self.from_z[k - 1, :, part].astype(F32)
            o_ref[:, part] = total

        for k in range(self.depth):
            for j in range(4):
                self.to_twin(k, j).wait_send()
            self.to_two(k, 3).wait_send()
            self.to_two(k, 2).wait_send()
            self.to_one(k).wait_send()
            if k:
                self.to_far(k).wait_send()


def scatter_buffers(depth, rows, cols):
    def slots(n):
        return pltpu.VMEM((n, rows, cols), BF16)

    return [slots(depth * 4), slots(depth * 4), slots(depth * 2), slots(depth), slots(depth - 1)]


def scatter_sems(depth):
    return [
        pltpu.SemaphoreType.DMA((depth * 4,)),
        pltpu.SemaphoreType.DMA((depth * 8,)),
        pltpu.SemaphoreType.DMA((depth * 8,)),
    ]


def latent_attention_back(queries, grads, stats, keys, values, mask):
    rows = keys.shape[0]
    count = queries.shape[0]
    half = mask.astype(BF16)
    wide_k = jnp.concatenate([keys] * HEADS, axis=0) * half
    wide_v = jnp.concatenate([values] * HEADS, axis=0) * half
    cut = (HEADS, rows, count)
    scores = mm_nt(wide_k, queries).reshape(cut)
    probs = jnp.exp(scores - stats[:HEADS][:, None, :])
    grad_probs = mm_nt(wide_v, grads).reshape(cut)
    grad_scores = probs * (grad_probs - stats[HEADS : 2 * HEADS][:, None, :])
    grad_scores = grad_scores.reshape(HEADS * rows, count).astype(BF16)
    probs = probs.reshape(HEADS * rows, count).astype(BF16)

    def fold(full):
        full = full * mask
        total = full[:rows]
        for h in range(1, HEADS):
            total = total + full[h * rows : (h + 1) * rows]
        return total

    grad_kv = [fold(mm(grad_scores, queries)), fold(mm(probs, grads))]
    return mm_tn(grad_scores, wide_k), jnp.concatenate(grad_kv, axis=1).astype(BF16)


def to_lines(tile):
    return tile.T[: 2 * HEADS]


def from_lines(lines):
    zeros = jnp.zeros((LANES - lines.shape[0], lines.shape[1]), F32)
    return jnp.concatenate([lines, zeros], axis=0).T


def back_kernel(
    depth,
    frames,
    chunk,
    plan,
    ids,
    last,
    has,
    same,
    g_ref,
    q_ref,
    context_grad,
    tile_ref,
    k_ref,
    v_ref,
    m_ref,
    kl_ref,
    vl_ref,
    gb_ref,
    w_ref,
    lat_ref,
    mixed_ref,
    gain_f,
    media_grad,
    latents_grad,
    pack_ref,
    mine_ref,
    own,
    from_c,
    from_two,
    from_one,
    from_z,
    load_sem,
    send_sem,
    recv_sem,
    all_g,
    lines,
    tiles,
    weight_acc,
    gain_acc,
    outs,
    latent_kv,
    keep,
    send,
    core_q,
    away,
    y_q,
    link_send,
    link_recv,
    mixed_sem,
):
    step = pl.program_id(0)
    a, b, e, c = place()
    twin, other = (a, b, e, 1 - c), (a, b, 1 - e, c)
    links = link_send, link_recv
    buffers = own, from_c, from_two, from_one, from_z
    scatter = Scatter(depth, chunk, g_ref, buffers, load_sem, (send_sem, recv_sem), BACK_FLIPS)
    clips, rows, inner = kl_ref.shape
    total_rows = clips * rows
    groups = inner // (GROUP * HDIM)
    width = GROUP * HDIM
    mask = head_mask(F32)
    mask_half = mask.astype(BF16)
    grad_copies = [
        remote_copy(all_g.at[0], all_g.at[2], links, 0, other),
        remote_copy(all_g.at[0], all_g.at[1], links, 1, twin),
        remote_copy(all_g.at[2], all_g.at[3], links, 2, twin),
    ]
    line_copies = [
        remote_copy(lines.at[0], lines.at[2], links, 3, other),
        remote_copy(lines.at[0], lines.at[1], links, 4, twin),
        remote_copy(lines.at[2], lines.at[3], links, 5, twin),
    ]
    core_copy = remote_copy(send, core_q, links, 6, twin)
    y_copy = remote_copy(away, y_q, links, 7, other)

    def clip_queries(clip):
        return jnp.concatenate([q_ref[r, clip] for r in range(4)], axis=0) * BF16(SCALE)

    def clip_grads(clip):
        return jnp.concatenate([all_g[r, clip] for r in range(4)], axis=0)

    def clip_stats(clip):
        return jnp.concatenate([tiles[r, clip] for r in range(4)], axis=0).T

    @pl.when(step == 0)
    def _():
        all_g[0] = context_grad[...]
        lines[0] = to_lines(tile_ref[...])
        greet(depth, a, b, e, c)
        for copies in (grad_copies, line_copies):
            copies[0].start()
            copies[1].start()
        scatter.begin()
        gain_acc[...] = jnp.zeros_like(gain_acc)
        weight_acc[...] = jnp.zeros_like(weight_acc)
        outs[0] = jnp.zeros_like(outs[0])

    for when, names in plan[:-2]:

        @pl.when(step == when)
        def _(names=names):
            scatter.run(names)

    @pl.when(step == 0)
    def _():
        for copies in (grad_copies, line_copies):
            copies[0].wait()
            copies[2].start()
        for copies in (grad_copies, line_copies):
            copies[1].wait()
            copies[2].wait()
        for r in range(4):
            tiles[r] = from_lines(lines[r]).reshape(clips, rows, LANES)

    @pl.when((step >= 1) & (step <= frames))
    def _():
        frame = step - 1
        before = jnp.maximum(frame - 1, 0)
        clip = ids[frame]
        joined = same[frame] == 1
        queries, grads, stats = clip_queries(clip), clip_grads(clip), clip_stats(clip)
        key_parts, value_parts = [], []
        for g in range(groups):
            cols = slice(g * width, (g + 1) * width)

            def line(first):
                at = first + g * GROUP
                return jnp.concatenate([stats[at + h : at + h + 1, :] for h in range(GROUP)], axis=1)

            wide_q = spread_heads(queries, g, mask_half)
            wide_g = spread_heads(grads, g, mask_half)
            keys = k_ref[:, cols]
            probs = jnp.exp(mm_nt(keys, wide_q) - line(0))
            grad_probs = mm_nt(v_ref[:, cols], wide_g)
            grad_scores = (probs * (grad_probs - line(HEADS))).astype(BF16)
            key_parts.append(mm(grad_scores, wide_q))
            value_parts.append(mm(probs.astype(BF16), wide_g))
            part = take_heads(mm_tn(grad_scores, keys), mask)
            outs[frame, :, cols] = part + jnp.where(joined, outs[before, :, cols], 0.0)
        grad_kv = jnp.concatenate(key_parts + value_parts, axis=1).astype(BF16)
        hat, scale = normalise(m_ref[...].astype(F32))
        gain = gb_ref[0:1, :]
        normed = (hat * gain + gb_ref[3:4, :]).astype(BF16)
        weight_acc[...] += mm_tn(normed, grad_kv)
        grad = mm_nt(grad_kv, w_ref[:, inner : 3 * inner])
        gain_acc[0:1, :] += jnp.sum(grad * hat, axis=0, keepdims=True)
        gain_acc[1:2, :] += jnp.sum(grad, axis=0, keepdims=True)
        media_grad[...] = norm_back(grad, hat, scale, gain).astype(BF16)

    @pl.when(step == frames + 1)
    def _():
        wide = latent_mask(rows, inner)

        def one_clip(clip):
            out, grad_kv = latent_attention_back(
                clip_queries(clip),
                clip_grads(clip),
                clip_stats(clip),
                kl_ref[clip],
                vl_ref[clip],
                wide,
            )
            out = (out + jnp.where(has[clip] == 1, outs[last[clip]], 0.0)) * SCALE
            return out, grad_kv

        @pl.loop(0, clips // TOGETHER)
        def _(index):
            some = [index * TOGETHER + n for n in range(TOGETHER)]
            results = [one_clip(clip) for clip in some]
            for clip, (out, grad_kv) in zip(some, results):
                latent_kv[clip] = grad_kv
                for r in range(4):
                    part = slice(r * rows, (r + 1) * rows)
                    if r % 2:
                        send[r // 2, clip] = out[part].astype(BF16)
                    else:
                        keep[r // 2, clip] = out[part]

        core_copy.start()
        hat, scale = normalise(lat_ref[...])
        gain = gb_ref[1:2, :]
        normed = (hat * gain + gb_ref[4:5, :]).astype(BF16)
        core_copy.wait()
        away[...] = (keep[1] + core_q[1].astype(F32)).astype(BF16)
        y_copy.start()
        grad_kv = latent_kv[...].reshape(total_rows, 2 * inner)
        pack_ref[:, inner : 3 * inner] = (weight_acc[...] + mm_tn(normed, grad_kv)).astype(BF16)
        grad = mm_nt(grad_kv, w_ref[:, inner : 3 * inner])
        mixed = weight_acc.at[:total_rows]
        load_mixed = pltpu.make_async_copy(mixed_ref, mixed, mixed_sem)
        load_mixed.start()
        scatter.run(plan[-2][1])
        y_copy.wait()
        grad_q = (keep[0] + core_q[0].astype(F32) + y_q[...].astype(F32)).astype(BF16)
        grad_q = grad_q.reshape(total_rows, inner)
        grad = grad + mm_nt(grad_q, w_ref[:, :inner])
        pack_ref[:, :inner] = mm_tn(normed, grad_q).astype(BF16)
        table = jnp.concatenate(
            [
                gain_acc[0:1, :],
                jnp.sum(grad * hat, axis=0, keepdims=True),
                gain_f[0:1, :],
                gain_acc[1:2, :],
                jnp.sum(grad, axis=0, keepdims=True),
                gain_f[1:2, :],
                jnp.zeros((LANES - 6, grad.shape[1]), F32),
            ],
            axis=0,
        )
        pack_ref[:, 3 * inner :] = table.T.astype(BF16)
        load_mixed.wait()
        latents_grad[...] = mixed[...] + norm_back(grad, hat, scale, gain)
        scatter.run(plan[-1][1])
        scatter.finish(mine_ref)


def back(
    ids,
    last,
    has,
    same,
    grad_feed,
    query_all,
    context_grad,
    tile,
    keys,
    values,
    media,
    latent_key,
    latent_value,
    gains,
    attend,
    latents,
    mixed_grad,
    gain_f,
    depth,
    chunk,
    plan,
):
    clips, rows, inner = latent_key.shape
    frames = media.shape[0] // PATCH_IMG
    width = media.shape[1]
    total = clips * rows
    cut = (clips, rows, inner)
    _, feed_rows, feed_cols = grad_feed.shape
    once = pl.Buffered(buffer_count=1)

    def whole(x):
        return pl.BlockSpec(x.shape, lambda i: (0,) * len(x.shape), pipeline_mode=once)

    def block(columns):
        return pl.BlockSpec((PATCH_IMG, columns), lambda i: (jnp.clip(i - 1, 0, frames - 1), 0))

    smem = pl.BlockSpec(memory_space=pltpu.SMEM)
    outs = (
        jax.ShapeDtypeStruct(media.shape, BF16),
        jax.ShapeDtypeStruct(latents.shape, F32),
        jax.ShapeDtypeStruct(attend.shape, BF16),
        jax.ShapeDtypeStruct((feed_rows, feed_cols), F32),
    )
    return pl.pallas_call(
        functools.partial(back_kernel, depth, frames, chunk, plan),
        grid=(frames + 2,),
        out_shape=outs,
        in_specs=[smem] * 4
        + [any_spec(), whole(query_all), whole(context_grad), whole(tile)]
        + [block(inner), block(inner), block(width)]
        + [whole(x) for x in (latent_key, latent_value, gains, attend, latents)]
        + [any_spec(), whole(gain_f)],
        out_specs=(block(width),) + tuple(whole(x) for x in outs[1:]),
        scratch_shapes=scatter_buffers(depth, feed_rows, feed_cols)
        + scatter_sems(depth)
        + [
            pltpu.VMEM((4,) + cut, BF16),
            pltpu.VMEM((4, 2 * HEADS, total), F32),
            pltpu.VMEM((4, clips, rows, LANES), F32),
            pltpu.VMEM((width, 2 * inner), F32),
            pltpu.VMEM((8, width), F32),
            pltpu.VMEM((frames, 4 * rows, inner), F32),
            pltpu.VMEM((clips, rows, 2 * inner), BF16),
            pltpu.VMEM((2,) + cut, F32),
            pltpu.VMEM((2,) + cut, BF16),
            pltpu.VMEM((2,) + cut, BF16),
            pltpu.VMEM(cut, BF16),
            pltpu.VMEM(cut, BF16),
            pltpu.SemaphoreType.DMA((8,)),
            pltpu.SemaphoreType.DMA((8,)),
            pltpu.SemaphoreType.DMA,
        ],
        compiler_params=params(collective_id=4, has_side_effects=True),
        name="back",
    )(
        ids,
        last,
        has,
        same,
        grad_feed,
        query_all,
        context_grad,
        tile,
        keys,
        values,
        media,
        latent_key,
        latent_value,
        gains,
        attend,
        latents,
        mixed_grad,
        gain_f,
    )


def head_kernel(
    depth,
    frames,
    parts,
    plan,
    late,
    ids,
    last,
    has,
    same,
    shard_e,
    shard_s,
    m_ref,
    lat_ref,
    cot_ref,
    gb_ref,
    wq_ref,
    k_ref,
    v_ref,
    q_ref,
    kl_ref,
    vl_ref,
    out_ref,
    mixed_grad,
    context_grad,
    tile_ref,
    gain_ref,
    gw_ref,
    all_k,
    all_v,
    all_q,
    outs,
    tops,
    sums,
    keep,
    keep_st,
    send,
    send_st,
    core_o,
    send_li,
    core_li,
    away,
    y_o,
    away_li,
    y_li,
    weights_e,
    weights_s,
    grad_s,
    grad_o,
    normed_v,
    normed_t,
    hat_v,
    local_sem,
    send_e,
    recv_e,
    send_s,
    recv_s,
    link_send,
    link_recv,
    out_sem,
    store_sem,
):
    step = pl.program_id(0)
    a, b, e, c = place()
    twin, other = (a, b, e, 1 - c), (a, b, 1 - e, c)
    links = link_send, link_recv
    gather_e = Gather(depth, shard_e, weights_e, local_sem.at[0], send_e, recv_e, HEAD_FLIPS)
    gather_s = Gather(depth, shard_s, weights_s, local_sem.at[1], send_s, recv_s, HEAD_FLIPS)
    clips, rows, inner = kl_ref.shape
    total_rows = clips * rows
    groups = inner // (GROUP * HDIM)
    width = GROUP * HDIM
    slabs = PATCH_IMG // all_k.shape[1]
    mask = head_mask(F32)
    mask_half = mask.astype(BF16)
    query_copies = [
        remote_copy(all_q.at[0], all_q.at[2], links, 0, other),
        remote_copy(all_q.at[0], all_q.at[1], links, 1, twin),
        remote_copy(all_q.at[2], all_q.at[3], links, 2, twin),
    ]
    share = clips // parts
    lot = share * rows

    def core_copies(p):
        some = pl.ds(p * share, share)
        return [
            remote_copy(send.at[:, some], core_o.at[:, some], links, 3 + 4 * p, twin),
            remote_copy(send_li.at[p], core_li.at[p], links, 4 + 4 * p, twin),
        ]

    def y_copies(p):
        some = pl.ds(p * lot, lot)
        return [
            remote_copy(away.at[some], y_o.at[some], links, 5 + 4 * p, other),
            remote_copy(away_li.at[p], y_li.at[p], links, 6 + 4 * p, other),
        ]

    def join_part(p):
        some = slice(p * share, (p + 1) * share)
        for copy in core_copies(p):
            copy.wait()
        for n in (1, 0):
            out, stat = join_partials(
                keep[n, some].reshape(lot, inner),
                keep_st[n, some].reshape(lot, LANES),
                core_o[n, some].reshape(lot, inner),
                from_lines(core_li[p, n]),
            )
            if n:
                away[p * lot : (p + 1) * lot] = out.astype(BF16)
                away_li[p] = to_lines(stat)
                for copy in y_copies(p):
                    copy.start()
            else:
                keep[0, some] = out.reshape(share, rows, inner)
                keep_st[0, some] = stat.reshape(share, rows, LANES)

    keep_queries = pltpu.make_async_copy(all_q, q_ref, out_sem)

    def run(names):
        for name in names:
            (gather_e if name[0] == "e" else gather_s).run((name[1:],))

    def clip_queries(clip):
        return jnp.concatenate([all_q[r, clip] for r in range(4)], axis=0) * BF16(SCALE)

    @pl.when(step == 0)
    def _():
        greet(depth, a, b, e, c)
        hat, _ = normalise(lat_ref[...])
        normed = (hat * gb_ref[1:2, :] + gb_ref[4:5, :]).astype(BF16)
        all_q[0] = mm(normed, wq_ref[:, :inner]).astype(BF16).reshape(clips, rows, inner)
        query_copies[0].start()
        query_copies[1].start()
        gather_s.own().start()
        gather_e.own().start()
        gather_e.begin()
        kl_ref[...] = (
            mm(normed, wq_ref[:, inner : 2 * inner]).astype(BF16).reshape(clips, rows, inner)
        )
        vl_ref[...] = (
            mm(normed, wq_ref[:, 2 * inner : 3 * inner]).astype(BF16).reshape(clips, rows, inner)
        )
        outs[0] = jnp.zeros_like(outs[0])
        tops[0] = jnp.zeros_like(tops[0])
        sums[0] = jnp.zeros_like(sums[0])

    @pl.when(step < frames)
    def _():
        hat, _ = normalise(m_ref[...].astype(F32))
        normed = (hat * gb_ref[0:1, :] + gb_ref[3:4, :]).astype(BF16)
        new_k = mm(normed, wq_ref[:, inner : 2 * inner]).astype(BF16)
        new_v = mm(normed, wq_ref[:, 2 * inner : 3 * inner]).astype(BF16)
        k_ref[...] = new_k
        v_ref[...] = new_v
        at = pl.ds(step * slabs, slabs)
        all_k[at] = new_k.reshape(slabs, PATCH_IMG // slabs, inner)
        all_v[at] = new_v.reshape(slabs, PATCH_IMG // slabs, inner)

    for when, names in plan:

        @pl.when(step == when)
        def _(names=names):
            run(names)

    @pl.when(step == frames // 2)
    def _():
        query_copies[0].wait()
        query_copies[2].start()

    @pl.when(step == frames)
    def _():
        query_copies[1].wait()
        query_copies[2].wait()
        keep_queries.start()

    @pl.when((step >= frames) & (step < 2 * frames))
    def _():
        frame = step - frames
        before = jnp.maximum(frame - 1, 0)
        queries = clip_queries(ids[frame])
        joined = same[frame] == 1
        old_tops = jnp.where(joined, tops[before], MASKED)
        old_sums = jnp.where(joined, sums[before], 0.0)
        at = pl.ds(frame * slabs, slabs)
        new_tops, new_sums = [], []
        for g in range(groups):
            cols = slice(g * width, (g + 1) * width)

            def column(tile):
                first = g * GROUP
                return jnp.concatenate(
                    [tile[:, first + h : first + h + 1] for h in range(GROUP)], axis=0
                )

            keys = all_k[at, :, cols].reshape(PATCH_IMG, width)
            values = all_v[at, :, cols].reshape(PATCH_IMG, width)
            scores = mm_nt(spread_heads(queries, g, mask_half), keys)
            old_top = column(old_tops)
            top = jnp.maximum(jnp.max(scores, axis=-1, keepdims=True), old_top)
            probs = jnp.exp(scores - top)
            shrink = jnp.exp(old_top - top)
            total = jnp.sum(probs, axis=-1, keepdims=True) + column(old_sums) * shrink
            part = take_heads(mm(probs.astype(BF16), values), mask)
            old = jnp.where(joined, outs[before, :, cols], 0.0)
            outs[frame, :, cols] = part + old * take_heads(shrink, mask)
            for h in range(GROUP):
                new_tops.append(top[h * HDIM : (h + 1) * HDIM])
                new_sums.append(total[h * HDIM : (h + 1) * HDIM])
        tops[frame] = pack_columns(new_tops)
        sums[frame] = pack_columns(new_sums)

    @pl.when((step >= 2 * frames) & (step < 2 * frames + parts))
    def _():
        wide = latent_mask(rows, inner)
        lane = lax.broadcasted_iota(jnp.int32, (4 * rows, LANES), 1)
        first = (step - 2 * frames) * share

        def one_clip(clip):
            out, top, total = latent_attention(clip_queries(clip), kl_ref[clip], vl_ref[clip], wide)
            at = last[clip]
            there = has[clip] == 1
            far_top = jnp.where(there, tops[at], MASKED)
            far_sum = jnp.where(there, sums[at], 0.0)
            far_out = jnp.where(there, outs[at], 0.0)
            both = jnp.maximum(top, far_top)
            near, far = jnp.exp(top - both), jnp.exp(far_top - both)
            total = jnp.where(lane < HEADS, total * near + far_sum * far, 1.0)
            stat = both + jnp.log(total)
            out = out * expand_columns(near / total, inner)
            return out + far_out * expand_columns(far / total, inner), stat

        @pl.loop(0, share // TOGETHER)
        def _(index):
            some = [first + index * TOGETHER + n for n in range(TOGETHER)]
            results = [one_clip(clip) for clip in some]
            for clip, (out, stat) in zip(some, results):
                for r in range(4):
                    part = slice(r * rows, (r + 1) * rows)
                    if r % 2:
                        send[r // 2, clip] = out[part].astype(BF16)
                        send_st[r // 2, clip] = stat[part]
                    else:
                        keep[r // 2, clip] = out[part]
                        keep_st[r // 2, clip] = stat[part]

    for p in range(parts):

        @pl.when(step == 2 * frames + p)
        def _(p=p):
            for n in range(2):
                some = slice(p * share, (p + 1) * share)
                send_li[p, n] = to_lines(send_st[n, some].reshape(lot, LANES))
            for copy in core_copies(p):
                copy.start()
            if p:
                join_part(p - 1)

    @pl.when(step == 2 * frames + parts)
    def _():
        run(late[0])
        join_part(parts - 1)
        run(late[1])
        gather_e.settle()
        run(late[2])
        for p in range(parts):
            for copy in y_copies(p):
                copy.wait()
        stat_y = jnp.concatenate([from_lines(y_li[p]) for p in range(parts)], axis=0)
        context, stat = join_partials(
            keep[0].reshape(total_rows, inner),
            keep_st[0].reshape(total_rows, LANES),
            y_o[...],
            stat_y,
        )
        feed_part(
            functools.partial(run_late, run, late[3:], gather_s),
            context,
            stat,
            depth,
            a,
            gather_s.order,
            lat_ref,
            cot_ref,
            gb_ref,
            weights_e,
            weights_s,
            out_ref,
            mixed_grad,
            context_grad,
            tile_ref,
            gain_ref,
            gw_ref,
            all_k,
            grad_s,
            grad_o,
            normed_v,
            normed_t,
            hat_v,
            store_sem,
        )
        keep_queries.wait()
        gather_e.finish()
        gather_s.finish()


def run_late(run, late, gather, n):
    run(late[n])
    gather.settle(gather.order[n])


def feed_part(
    ready,
    context,
    stat,
    depth,
    plane,
    order,
    lat_ref,
    cot_ref,
    gb_ref,
    weights_e,
    weights_s,
    out_ref,
    mixed_grad,
    context_grad,
    tile_ref,
    gain_ref,
    gw_ref,
    grad_e,
    grad_s,
    grad_o,
    normed_v,
    normed_t,
    hat_v,
    store_sem,
):
    blocks, shrink_rows, width = weights_s.shape
    per_plane = blocks // depth
    inner = context.shape[1]
    output_rows = inner // blocks
    expand_rows = (weights_e.shape[1] - output_rows) // depth
    shrink_at = depth * expand_rows
    output_at = shrink_at + shrink_rows
    half = width // 2
    half_rows = half // shrink_rows
    context_half = context.astype(BF16)

    def weight_o():
        return weights_e[:, shrink_at : shrink_at + output_rows, :].reshape(inner, width)

    mixed = lat_ref[...] + mm(context_half, weight_o())
    hat, scale = normalise(mixed)
    hat_v[...] = hat
    normed = (hat * gb_ref[2:3, :] + gb_ref[5:6, :]).astype(BF16)
    normed_v[...] = normed
    normed_t[...] = normed.astype(F32).T.astype(BF16)
    out_ref[...] = mixed
    mixed_grad[...] = jnp.zeros_like(mixed_grad)
    cot = cot_ref[...]
    stores = []
    for n, k in enumerate(order):
        ready(n)
        plane_k = (plane - k) % depth
        e_rows = pl.ds(pl.multiple_of(plane_k * expand_rows, expand_rows), expand_rows)
        for slot in range(2):
            cols = slice(slot * half, (slot + 1) * half)
            w_e = weights_e[:, e_rows, cols].reshape(blocks * expand_rows, half)
            s_rows = pl.ds(plane_k * per_plane + slot * half_rows, half_rows)
            w_s = weights_s[s_rows].reshape(half, width)
            pre = mm(normed_v[...], w_e)
            cdf = 0.5 * (1.0 + lax.erf(pre * (0.5**0.5)))
            hidden = (pre * cdf).astype(BF16)
            out_ref[...] += mm(hidden, w_s)
            grad_hidden = mm_nt(cot, w_s)
            pdf = jnp.exp(-0.5 * pre * pre) * (1.0 / math.sqrt(2.0 * math.pi))
            grad_pre = (grad_hidden * (cdf + pre * pdf)).astype(BF16)
            if n:
                for copy in stores[2 * (2 * n + slot) - 4 : 2 * (2 * n + slot) - 2]:
                    copy.wait()
            grad_s[slot] = mm_tn(hidden, cot).astype(BF16).reshape(half_rows, shrink_rows, width)
            e_spot = grad_e.at[pl.ds(slot * blocks, blocks)]
            e_spot[...] = (
                mm(normed_t[...], grad_pre).astype(BF16).reshape(blocks, expand_rows, half)
            )
            stores += [
                pltpu.make_async_copy(
                    e_spot, gw_ref.at[:, e_rows, pl.ds(slot * half, half)], store_sem.at[slot]
                ),
                pltpu.make_async_copy(
                    grad_s.at[slot],
                    gw_ref.at[s_rows, pl.ds(shrink_at, shrink_rows), :],
                    store_sem.at[2 + slot],
                ),
            ]
            stores[-1].start()
            stores[-2].start()
            mixed_grad[...] += mm_nt(grad_pre, w_e)

    grad_normed = mixed_grad[...]
    hat = hat_v[...]
    rows = gain_ref.shape[0]
    gain_ref[...] = jnp.concatenate(
        [
            jnp.sum(grad_normed * hat, axis=0, keepdims=True),
            jnp.sum(grad_normed, axis=0, keepdims=True),
            jnp.zeros((rows - 2, width), F32),
        ],
        axis=0,
    )
    total = cot.astype(F32) + norm_back(grad_normed, hat, scale, gb_ref[2:3, :])
    mixed_grad[...] = total
    attended = total.astype(BF16)
    grad_o[...] = mm_tn(context_half, attended).astype(BF16).reshape(grad_o.shape)
    store_o = pltpu.make_async_copy(
        grad_o, gw_ref.at[:, pl.ds(output_at, output_rows), :], store_sem.at[4]
    )
    store_o.start()
    grad_c = mm_nt(attended, weight_o()).astype(BF16)
    context_grad[...] = grad_c
    product = grad_c.astype(F32) * context
    head = lax.broadcasted_iota(jnp.int32, product.shape, 1) // HDIM
    deltas = [
        jnp.sum(jnp.where(head == h, product, 0.0), axis=-1, keepdims=True) for h in range(HEADS)
    ]
    lane = lax.broadcasted_iota(jnp.int32, stat.shape, 1)
    tile_ref[...] = jnp.where(lane < HEADS, stat, pack_columns(deltas, HEADS))
    for copy in stores[-4:]:
        copy.wait()
    store_o.wait()


def head(
    ids,
    last,
    has,
    same,
    shard_e,
    shard_s,
    media,
    latents,
    cotangent,
    gains,
    attend,
    clips,
    inner,
    depth,
    parts,
    plan,
    late,
):
    rows = latents.shape[0] // clips
    frames = media.shape[0] // PATCH_IMG
    width = media.shape[1]
    total = clips * rows
    cut = (clips, rows, inner)
    count = depth * 8
    expand_rows = (shard_e.shape[0] - inner // count) // depth
    feed_rows = shard_e.shape[0] + shard_s.shape[0]
    slabs = PATCH_IMG // expand_rows * frames
    half_rows = width // 2 // shard_s.shape[0]
    once = pl.Buffered(buffer_count=1)

    def whole(x):
        return pl.BlockSpec(x.shape, lambda i: (0,) * len(x.shape), pipeline_mode=once)

    def block(columns):
        return pl.BlockSpec((PATCH_IMG, columns), lambda i: (jnp.minimum(i, frames - 1), 0))

    smem = pl.BlockSpec(memory_space=pltpu.SMEM)
    kv = jax.ShapeDtypeStruct((media.shape[0], inner), BF16)
    small = jax.ShapeDtypeStruct(cut, BF16)
    outs = (
        small,
        small,
        jax.ShapeDtypeStruct((total, width), F32),
        jax.ShapeDtypeStruct((total, width), F32),
        jax.ShapeDtypeStruct((total, inner), BF16),
        jax.ShapeDtypeStruct((total, LANES), F32),
        jax.ShapeDtypeStruct((8, width), F32),
    )
    lines = (2 * HEADS, total // parts)
    dma = pltpu.SemaphoreType.DMA
    return pl.pallas_call(
        functools.partial(head_kernel, depth, frames, parts, plan, late),
        grid=(2 * frames + parts + 1,),
        out_shape=(kv, kv, jax.ShapeDtypeStruct((4,) + cut, BF16))
        + outs
        + (jax.ShapeDtypeStruct((count, feed_rows, width), BF16),),
        in_specs=[smem] * 4
        + [any_spec(), any_spec(), block(width)]
        + [whole(x) for x in (latents, cotangent, gains, attend)],
        out_specs=(block(inner), block(inner), any_spec())
        + tuple(whole(x) for x in outs)
        + (any_spec(),),
        scratch_shapes=[
            pltpu.VMEM((slabs, expand_rows, inner), BF16),
            pltpu.VMEM((slabs, expand_rows, inner), BF16),
            pltpu.VMEM((4,) + cut, BF16),
            pltpu.VMEM((frames, 4 * rows, inner), F32),
            pltpu.VMEM((frames, 4 * rows, LANES), F32),
            pltpu.VMEM((frames, 4 * rows, LANES), F32),
            pltpu.VMEM((2,) + cut, F32),
            pltpu.VMEM((2, clips, rows, LANES), F32),
            pltpu.VMEM((2,) + cut, BF16),
            pltpu.VMEM((2, clips, rows, LANES), F32),
            pltpu.VMEM((2,) + cut, BF16),
            pltpu.VMEM((parts, 2) + lines, F32),
            pltpu.VMEM((parts, 2) + lines, F32),
            pltpu.VMEM((total, inner), BF16),
            pltpu.VMEM((total, inner), BF16),
            pltpu.VMEM((parts,) + lines, F32),
            pltpu.VMEM((parts,) + lines, F32),
            pltpu.VMEM((count,) + shard_e.shape, BF16),
            pltpu.VMEM((count,) + shard_s.shape, BF16),
            pltpu.VMEM((2, half_rows) + shard_s.shape, BF16),
            pltpu.VMEM((count, inner // count, width), BF16),
            pltpu.VMEM((total, width), BF16),
            pltpu.VMEM((width, total), BF16),
            pltpu.VMEM((total, width), F32),
            dma((2,)),
            dma((count,)),
            dma((count,)),
            dma((count,)),
            dma((count,)),
            dma((3 + 4 * parts,)),
            dma((3 + 4 * parts,)),
            dma,
            dma((5,)),
        ],
        compiler_params=params(collective_id=2, has_side_effects=True),
        name="head",
    )(ids, last, has, same, shard_e, shard_s, media, latents, cotangent, gains, attend)


def norm_kernel(depth, images, lats, chunk, pack_ref, feed_ref, norm_ref, mine_ref, *refs):
    buffers, refs = refs[:5], refs[5:]
    load_sem, send_sem, recv_sem, tile, slots, tile_send, tile_recv = refs
    count = images * lats
    img = lax.axis_index("img")
    lat = lax.axis_index("lat")
    me = img * lats + lat
    scatter = Scatter(depth, chunk, pack_ref, buffers, load_sem, (send_sem, recv_sem))
    barrier = pltpu.get_barrier_semaphore()

    def other(k):
        there = (me + k) % count
        return there // lats, there % lats

    for k in range(1, count):
        pl.semaphore_signal(barrier, inc=1, device_id=other(k), device_id_type=MESH)
    pl.semaphore_wait(barrier, count - 1)
    scatter.begin()
    feed_rows = feed_ref.shape[0]
    squares = jnp.zeros((8, feed_ref.shape[1]), F32)
    for n in range(feed_rows // 8):
        part = feed_ref[n * 8 : (n + 1) * 8, :]
        squares = squares + part * part
    squares = jnp.sum(squares)
    scatter.run(NORM_PLAN)
    scatter.finish(mine_ref)
    own = mine_ref[...]
    tile[...] = jnp.full(tile.shape, squares + jnp.sum(own * own), F32)
    slots[me] = tile[...]

    def exchange(k, spot):
        return pltpu.make_async_remote_copy(
            src_ref=tile,
            dst_ref=slots.at[spot],
            send_sem=tile_send.at[k],
            recv_sem=tile_recv.at[k],
            device_id=other(k),
            device_id_type=MESH,
        )

    for k in range(1, count):
        exchange(k, me).start()
    for k in range(1, count):
        exchange(k, (me - k) % count).wait_recv()
    norm_ref[...] = jnp.sqrt(jnp.sum(slots[...], axis=0))
    for k in range(1, count):
        exchange(k, me).wait_send()


def norm_and_sum(grad_attend, mine_feed, images, lats):
    count = images * lats
    depth = images // 2
    rows = grad_attend.shape[0] // count
    cols = grad_attend.shape[1]
    tile = (8, LANES)
    return pl.pallas_call(
        functools.partial(norm_kernel, depth, images, lats, cols),
        out_shape=(jax.ShapeDtypeStruct(tile, F32), jax.ShapeDtypeStruct((rows, cols), F32)),
        in_specs=[any_spec(), vmem_spec()],
        out_specs=(vmem_spec(), vmem_spec()),
        scratch_shapes=scatter_buffers(depth, rows, cols)
        + scatter_sems(depth)
        + [
            pltpu.VMEM(tile, F32),
            pltpu.VMEM((count,) + tile, F32),
            pltpu.SemaphoreType.DMA((count,)),
            pltpu.SemaphoreType.DMA((count,)),
        ],
        compiler_params=params(collective_id=3, has_side_effects=True),
        name="norm",
    )(grad_attend.reshape(count, rows, cols), mine_feed)


def update_kernel(rates, inner, count, norm_ref, mine, feed_ref, *refs):
    states, refs = refs[:18], refs[18:]
    olds, refs = refs[:count], refs[count:]
    norm_out, news, moved = refs[0], refs[1:19], refs[19:]
    for old, new in zip(olds, moved):
        new[...] = old[...]

    @pl.when(pl.program_id(0) == 0)
    def _():
        update_states(rates, inner, norm_ref, mine, feed_ref, states, norm_out, news)


def update_states(rates, inner, norm_ref, mine, feed_ref, states, norm_out, news):
    norm = norm_ref[...]
    norm_out[...] = norm
    factor = jnp.minimum(1.0, CLIP_NORM / (norm + 1e-06))[0:1, 0:1]

    def update(n, grad, rows, cols, decay):
        at = (rows, cols)
        master = states[n][at]
        step_grad = factor * grad
        if decay:
            step_grad = step_grad + decay * master
        buffer = MOMENTUM * states[6 + n][at] + step_grad
        new = master - rates[n] * (step_grad + MOMENTUM * buffer)
        news[n][at] = new
        news[6 + n][at] = buffer
        news[12 + n][at] = AVERAGING * states[12 + n][at] + (1.0 - AVERAGING) * new

    every = slice(None)
    width = feed_ref.shape[1]
    expand_rows, expand_cols = states[2].shape
    shrink_rows = states[3].shape[0]
    at = expand_cols // width * expand_rows
    update(0, mine[:, : 3 * inner], every, every, DECAY)
    update(1, feed_ref[at + shrink_rows :, :], every, every, DECAY)
    for g in range(expand_cols // width):
        grad = feed_ref[g * expand_rows : (g + 1) * expand_rows, :]
        update(2, grad, every, slice(g * width, (g + 1) * width), DECAY)
    update(3, feed_ref[at : at + shrink_rows, :], every, every, DECAY)
    small = mine[:, 3 * inner :].T
    update(4, small[0:3], every, every, 0.0)
    update(5, small[3:6], every, every, 0.0)


def update_all(norm, mine, mine_feed, states, rates, inner, moved, steps):
    def like(x):
        return jax.ShapeDtypeStruct(x.shape, x.dtype)

    def whole(x):
        return pl.BlockSpec(x.shape, lambda i: (0, 0), pipeline_mode=pl.Buffered(buffer_count=1))

    def block(x):
        return pl.BlockSpec((x.shape[0] // steps, x.shape[1]), lambda i: (i, 0))

    blocks = [block(x) for x in moved]
    kept = [whole(x) for x in states]
    return pl.pallas_call(
        functools.partial(update_kernel, rates, inner, len(moved)),
        grid=(steps,),
        out_shape=(like(norm),) + tuple(like(x) for x in states) + tuple(like(x) for x in moved),
        in_specs=[whole(norm), whole(mine), whole(mine_feed)] + kept + blocks,
        out_specs=tuple([whole(norm)] + kept + blocks),
        compiler_params=params(),
        name="update",
    )(norm, mine, mine_feed, *states, *moved)


def pack_feed(expand, shrink, output):
    width = shrink.shape[-1]
    groups = expand.shape[-1] // width
    lead = expand.shape[:-2]
    rows = expand.shape[-2]
    cut = expand.reshape(lead + (rows, groups, width))
    cut = jnp.moveaxis(cut, -2, -3).reshape(lead + (groups * rows, width))
    return jnp.concatenate([cut, shrink, output], axis=-2)


def unpack_feed(packed, rows, shrink_rows):
    width = packed.shape[-1]
    lead = packed.shape[:-2]
    groups = (packed.shape[-2] - shrink_rows) // rows
    split = groups * rows
    cut = packed[..., :split, :].reshape(lead + (groups, rows, width))
    expand = jnp.moveaxis(cut, -3, -2).reshape(lead + (rows, groups * width))
    return (
        expand,
        packed[..., split : split + shrink_rows, :],
        packed[..., split + shrink_rows :, :],
    )


def step_size(width, inner, ff):
    return 0.37 * math.sqrt((4 * width * inner + 2 * width * ff) / width)


def lat_pairs(count, along_core):
    pairs = []
    for lat in range(count):
        e, c = lat // 2, lat % 2
        pairs.append((lat, e * 2 + 1 - c if along_core else (1 - e) * 2 + c))
    return pairs


def shards(
    images,
    lats,
    media,
    latents,
    counts,
    cotangent,
    attend_weight,
    output_weight,
    expand_weight,
    shrink_weight,
    layer_gains,
    layer_biases,
    attend_momentum,
    output_momentum,
    expand_momentum,
    shrink_momentum,
    gains_momentum,
    biases_momentum,
    attend_average,
    output_average,
    expand_average,
    shrink_average,
    gains_average,
    biases_average,
):
    devices = images * lats
    depth = images // 2
    fast = devices == BLOCKS and lats == 4 and images % 2 == 0
    samples, lat_dev, width = latents.shape
    rows = samples * lat_dev
    ff = expand_weight.shape[1]
    inner = attend_weight.shape[1] // 3
    patch_dev = media.shape[0]
    frames = patch_dev // PATCH_IMG
    over_core = functools.partial(lax.ppermute, axis_name="lat", perm=lat_pairs(lats, True))
    over_y = functools.partial(lax.ppermute, axis_name="lat", perm=lat_pairs(lats, False))

    attend_rows = attend_weight.shape[0]
    if fast:
        attend, shard_e, shard_s, gains = start(
            attend_weight,
            layer_gains.T,
            layer_biases.T,
            expand_weight,
            shrink_weight,
            output_weight,
            depth,
        )
        attend = attend.reshape(width, attend.shape[2])
    else:

        def everywhere(x):
            return lax.all_gather(x.astype(BF16), AXES, axis=0, tiled=True)

        small = jnp.concatenate([layer_gains, layer_biases], axis=1)
        small = jnp.pad(small, ((0, 0), (0, LANES - small.shape[1])))
        attend = everywhere(jnp.concatenate([attend_weight, small], axis=1))
        feed = pack_feed(
            everywhere(expand_weight).reshape(BLOCKS, width // BLOCKS, ff),
            everywhere(shrink_weight).reshape(BLOCKS, ff // BLOCKS, width),
            everywhere(output_weight).reshape(BLOCKS, inner // BLOCKS, width),
        )
        gains = attend[:, 3 * inner : 3 * inner + 8].astype(F32).T

    sample_ends = jnp.cumsum(counts[0])
    first_frame = lax.axis_index("lat") * frames
    frame_ids = first_frame + jnp.arange(frames, dtype=jnp.int32)
    ids = jnp.sum((frame_ids[:, None] >= sample_ends[None, :]).astype(jnp.int32), axis=1)
    ids = jnp.clip(ids, 0, samples - 1)

    latent_flat = latents.reshape(rows, width)
    cot_flat = cotangent.reshape(rows, width)
    cut = (samples, lat_dev, inner)

    def to_group(own):
        other = over_y(own)
        return [own, over_core(own), other, over_core(other)]

    if fast:
        clip = jnp.arange(samples, dtype=jnp.int32)
        here = ids[None, :] == clip[:, None]
        has = jnp.any(here, axis=1).astype(jnp.int32)
        last = jnp.max(jnp.where(here, jnp.arange(frames, dtype=jnp.int32)[None, :], 0), axis=1)
        same = jnp.concatenate([jnp.zeros((1,), jnp.int32), (ids[1:] == ids[:-1]).astype(jnp.int32)])
        (
            keys,
            values,
            query_all,
            latent_key,
            latent_value,
            out_rows,
            mixed_grad,
            context_grad,
            tile,
            gain_f,
            grad_feed,
        ) = head(
            ids,
            last,
            has,
            same,
            shard_e,
            shard_s,
            media,
            latent_flat,
            cot_flat,
            gains,
            attend,
            samples,
            inner,
            depth,
            3,
            HEAD_PLAN,
            HEAD_LATE,
        )
    else:
        query, latent_key, latent_value = latent_project(latent_flat, gains, attend, inner)
        latent_key = latent_key.reshape(cut)
        latent_value = latent_value.reshape(cut)
        queries = to_group(query.reshape(cut))
        keys, values = media_project(media, gains, attend, inner)
        keep, send, keep_st, send_st = attention_forward(
            ids, queries, keys, values, latent_key, latent_value
        )
        got, got_st = over_core(send), over_core(send_st)
        flat_o, flat_s = (2, rows, inner), (2, rows, LANES)
        own, own_st, away, away_st = join_cores(
            keep.reshape(flat_o),
            keep_st.reshape(flat_s),
            got.reshape(flat_o),
            got_st.reshape(flat_s),
        )
        got, got_st = over_y(away), over_y(away_st)
        out_rows, mixed_grad, context_grad, tile, gain_f, grad_feed = feed_forward(
            own, own_st, got, got_st, latent_flat, cot_flat, gains, feed
        )
    if fast:
        grad_media, latents_grad, grad_attend, mine_feed = back(
            ids,
            last,
            has,
            same,
            grad_feed,
            query_all,
            context_grad.reshape(cut),
            tile,
            keys,
            values,
            media,
            latent_key,
            latent_value,
            gains,
            attend,
            latent_flat,
            mixed_grad,
            gain_f,
            depth,
            2 * LANES,
            BACK_PLAN,
        )
    else:
        grads = to_group(context_grad.reshape(cut))
        tiles = to_group(tile.reshape(samples, lat_dev, LANES))
        grad_media, latent_kv, keep, send, grad_kv, gain_m = attention_backward(
            ids,
            queries,
            grads,
            tiles,
            keys,
            values,
            latent_key,
            latent_value,
            media,
            gains,
            attend,
        )
        got = over_core(send)
        pair = keep.astype(F32) + got.astype(F32)
        got = over_y(pair[1].astype(BF16))
        latents_grad, grad_attend = latent_backward(
            latent_flat,
            mixed_grad,
            pair[0].reshape(rows, inner),
            got.reshape(rows, inner),
            latent_kv.reshape(rows, 2 * inner),
            gains,
            attend,
            grad_kv,
            gain_m,
            gain_f,
        )

        def owners(x):
            return lax.psum_scatter(x.astype(F32), AXES, scatter_dimension=0, tiled=True)

        mine = owners(grad_attend)
        own_expand, own_shrink, own_output = unpack_feed(grad_feed, width // BLOCKS, ff // BLOCKS)
        own_expand = owners(own_expand.reshape(width, ff))
        own_shrink = owners(own_shrink.reshape(ff, width))
        own_output = owners(own_output.reshape(inner, width))
    masters = (
        attend_weight,
        output_weight,
        expand_weight,
        shrink_weight,
        layer_gains,
        layer_biases,
    )
    moments = (
        attend_momentum,
        output_momentum,
        expand_momentum,
        shrink_momentum,
        gains_momentum,
        biases_momentum,
    )
    averages = (
        attend_average,
        output_average,
        expand_average,
        shrink_average,
        gains_average,
        biases_average,
    )
    step_rate = step_size(width, inner, ff)
    if fast:
        rates = tuple(step_rate * scale for scale in RATE_SCALES)
        states = masters + moments + averages
        states = tuple(x.T if x.shape[1] == 3 else x for x in states)
        norm, mine = norm_and_sum(grad_attend, mine_feed, images, lats)
        norm, *news = update_all(
            norm,
            mine,
            mine_feed,
            states,
            rates,
            inner,
            (),
            1,
        )
        news = [x.T if x.shape[0] == 3 else x for x in news[:18]]
        grad_norm = norm[0, 0]
        new_masters, new_buffers, new_smoothed = news[:6], news[6:12], news[12:]
    else:
        small = mine[:, 3 * inner :]
        owned = (
            mine[:, : 3 * inner],
            own_output,
            own_expand,
            own_shrink,
            small[:, 0:3],
            small[:, 3:6],
        )
        squares = sum(jnp.sum(piece * piece) for piece in owned)
        squares = lax.psum(squares, AXES)
        grad_norm = jnp.sqrt(squares)
        factor = jnp.minimum(1.0, CLIP_NORM / (grad_norm + 1e-06))
        decay_rates = (DECAY, DECAY, DECAY, DECAY, 0.0, 0.0)
        new_masters = []
        new_buffers = []
        new_smoothed = []
        for master, moment, average, reduced, decay_rate, rate_scale in zip(
            masters, moments, averages, owned, decay_rates, RATE_SCALES
        ):
            step_grad = factor * reduced + decay_rate * master
            buffer = MOMENTUM * moment + step_grad
            master_new = master - step_rate * rate_scale * (step_grad + MOMENTUM * buffer)
            new_masters.append(master_new)
            new_buffers.append(buffer)
            new_smoothed.append(AVERAGING * average + (1.0 - AVERAGING) * master_new)
    return (
        out_rows.reshape(latents.shape),
        grad_media,
        latents_grad.reshape(latents.shape),
        grad_norm,
        *new_masters,
        *new_buffers,
        *new_smoothed,
    )


def solution(mesh):
    rows = P(AXES, None)
    split = P("img", "lat", None)
    return jax.shard_map(
        functools.partial(shards, mesh.shape["img"], mesh.shape["lat"]),
        mesh=mesh,
        in_specs=(rows, split, P("img", None), split) + (rows,) * 18,
        out_specs=(split, rows, split, P()) + (rows,) * 18,
        check_vma=False,
    )
```

```python
import functools
import math

import jax
import jax.numpy as jnp
from jax import lax
from jax.experimental import pallas as pl
from jax.experimental.pallas import tpu as pltpu
from jax.sharding import PartitionSpec as P

HEADS = 8
HDIM = 64
PATCH_IMG = 256
GROUP = 4
TOGETHER = 2
EPS = 1e-05
MOMENTUM = 0.9
DECAY = 0.0001
AVERAGING = 0.6
CLIP_NORM = 1.0
RATE_SCALES = (1.0, 100.0, 1.0, 1.0, 15.0, 1.0)
AXES = ("img", "lat")
LANES = 128
BLOCKS = 32
SCALE = HDIM ** (-0.5)
MASKED = -1e30
F32 = jnp.float32
BF16 = jnp.bfloat16
MESH = pl.DeviceIdType.MESH
START_PLAN = ('b0', 'a1', 'a2', 'b1', 'c0', 'a3', 'b2', 'c1', 'b3', 'c2', 'c3')
HEAD_FLIPS = (0,)
BACK_FLIPS = ()
HEAD_PLAN = ((2, ('ea1', 'ez2', 'eb0')), (9, ('ez3',)), (12, ('eb1', 'ea2')), (19, ('ec0', 'eb2', 'ea3', 'sz1')), (24, ('ec1', 'eb3', 'sa0')), (26, ('ec2', 'ec3', 'sa1', 'sz2', 'sb0')))
HEAD_LATE = (('sz3',), ('sc0', 'sb1', 'sa2'), (), ('sc1',), ('sb2', 'sa3'), ('sc2', 'sb3'), ('sc3',))
BACK_PLAN = ((0, ('a0',)), (1, ('a1',)), (3, ('b0',)), (4, ('a2',)), (7, ('c0', 'b1')), (8, ('a3',)), (10, ('c1',)), (12, ('b2',)), (13, ('c2', 'b3')), (13, ('c3',)))
NORM_PLAN = ("a0", "a1", "b0", "a2", "b1", "c0", "a3", "b2", "c1", "b3", "c2", "c3")
VMEM_LIMIT = 60 * 1024 * 1024


def mm(a, b):
    return jnp.dot(a, b, preferred_element_type=F32)


def mm_tn(a, b):
    return lax.dot_general(a, b, (((0,), (0,)), ((), ())), preferred_element_type=F32)


def mm_nt(a, b):
    return lax.dot_general(a, b, (((1,), (1,)), ((), ())), preferred_element_type=F32)


def any_spec():
    return pl.BlockSpec(memory_space=pl.ANY)


def vmem_spec():
    return pl.BlockSpec(memory_space=pltpu.VMEM)


def params(**more):
    return pltpu.CompilerParams(vmem_limit_bytes=VMEM_LIMIT, **more)


def place():
    img = lax.axis_index("img")
    lat = lax.axis_index("lat")
    return img // 2, img % 2, lat // 2, lat % 2


def flat(a, b, e, c):
    return ((a * 2 + b) * 2 + e) * 2 + c


def device(a, b, e, c):
    return (a * 2 + b, e * 2 + c)


def neighbours(a, b, e, c, colour):
    one = (a, (b + 1 - colour) % 2, (e + colour) % 2, c)
    two = (a, (b + colour) % 2, (e + 1 - colour) % 2, c)
    return [(a, b, e, c), one, two, (a, 1 - b, 1 - e, c)]


def z_order(depth):
    order = [0]
    for k in range(1, depth // 2 + 1):
        order.append(k)
        if depth - k != k:
            order.append(depth - k)
    return order


def greet(depth, a, b, e, c):
    barrier = pltpu.get_barrier_semaphore()
    friends = [device((a + k) % depth, b, e, c) for k in range(1, depth)]
    friends += [device(a, 1 - b, e, c), device(a, b, 1 - e, c), device(a, b, e, 1 - c)]
    for friend in friends:
        pl.semaphore_signal(barrier, inc=1, device_id=friend, device_id_type=MESH)
    pl.semaphore_wait(barrier, len(friends))


def add_into(target, first, second, chunk):
    @pl.loop(0, target.shape[1] // chunk)
    def _(step):
        part = pl.ds(pl.multiple_of(step * chunk, chunk), chunk)
        target[:, part] = first[:, part] + second[:, part]


def normalise(values):
    center = values - jnp.mean(values, axis=-1, keepdims=True)
    spread = jnp.mean(center * center, axis=-1, keepdims=True)
    scale = lax.rsqrt(spread + EPS)
    return center * scale, scale


def norm_back(grad, hat, scale, gain):
    inner = grad * gain
    first = jnp.mean(inner, axis=-1, keepdims=True)
    second = jnp.mean(inner * hat, axis=-1, keepdims=True)
    return scale * (inner - first - hat * second)


def media_kernel(m_ref, gb_ref, wk_ref, wv_ref, k_ref, v_ref):
    hat, _ = normalise(m_ref[...].astype(F32))
    normed = (hat * gb_ref[0:1, :] + gb_ref[3:4, :]).astype(BF16)
    k_ref[...] = mm(normed, wk_ref[...]).astype(BF16)
    v_ref[...] = mm(normed, wv_ref[...]).astype(BF16)


def media_project(media, gains, attend, inner):
    rows, width = media.shape
    out = jax.ShapeDtypeStruct((rows, inner), BF16)
    block = pl.BlockSpec((PATCH_IMG, inner), lambda i: (i, 0))
    return pl.pallas_call(
        media_kernel,
        grid=(rows // PATCH_IMG,),
        out_shape=(out, out),
        in_specs=[
            pl.BlockSpec((PATCH_IMG, width), lambda i: (i, 0)),
            pl.BlockSpec(gains.shape, lambda i: (0, 0)),
            pl.BlockSpec((width, inner), lambda i: (0, 1)),
            pl.BlockSpec((width, inner), lambda i: (0, 2)),
        ],
        out_specs=(block, block),
        compiler_params=params(),
        cost_estimate=pl.CostEstimate(
            flops=4 * rows * width * inner, bytes_accessed=4 * rows * width, transcendentals=0
        ),
        name="media_project",
    )(media, gains, attend, attend)


def latent_kernel(l_ref, gb_ref, w_ref, q_ref, k_ref, v_ref):
    inner = q_ref.shape[1]
    hat, _ = normalise(l_ref[...])
    normed = (hat * gb_ref[1:2, :] + gb_ref[4:5, :]).astype(BF16)
    q_ref[...] = mm(normed, w_ref[:, :inner]).astype(BF16)
    k_ref[...] = mm(normed, w_ref[:, inner : 2 * inner]).astype(BF16)
    v_ref[...] = mm(normed, w_ref[:, 2 * inner : 3 * inner]).astype(BF16)


def latent_project(latents, gains, attend, inner):
    out = jax.ShapeDtypeStruct((latents.shape[0], inner), BF16)
    return pl.pallas_call(
        latent_kernel,
        out_shape=(out, out, out),
        in_specs=[vmem_spec()] * 3,
        out_specs=(vmem_spec(),) * 3,
        compiler_params=params(),
        name="latent_project",
    )(latents, gains, attend)


def head_mask(kind):
    rows = lax.broadcasted_iota(jnp.int32, (GROUP * HDIM, GROUP * HDIM), 0) // HDIM
    cols = lax.broadcasted_iota(jnp.int32, (GROUP * HDIM, GROUP * HDIM), 1) // HDIM
    return (rows == cols).astype(F32).astype(kind)


def spread_heads(queries, group, mask):
    width = GROUP * HDIM
    part = queries[:, group * width : (group + 1) * width]
    return jnp.concatenate([part] * GROUP, axis=0) * mask


def take_heads(full, mask):
    total = None
    for h in range(GROUP):
        part = slice(h * HDIM, (h + 1) * HDIM)
        term = full[part, :] * mask[part, :]
        total = term if total is None else total + term
    return total


def pack_columns(columns, first=0):
    rows = columns[0].shape[0]
    lane = lax.broadcasted_iota(jnp.int32, (rows, LANES), 1)
    tile = jnp.zeros((rows, LANES), F32)
    for h, column in enumerate(columns):
        tile = jnp.where(lane == first + h, column, tile)
    return tile


def expand_columns(tile, width):
    rows = tile.shape[0]
    head = lax.broadcasted_iota(jnp.int32, (rows, width), 1) // HDIM
    out = jnp.zeros((rows, width), F32)
    for h in range(width // HDIM):
        out = jnp.where(head == h, tile[:, h : h + 1], out)
    return out


def forward_kernel(
    ids, q0, q1, q2, q3, k_ref, v_ref, kl_ref, vl_ref, keep, send, keep_st, send_st, acc, tops, sums
):
    step = pl.program_id(0)
    clips = acc.shape[0]
    inner = acc.shape[2]
    groups = inner // (GROUP * HDIM)
    width = GROUP * HDIM
    mask = head_mask(F32)
    mask_half = mask.astype(BF16)

    def clip_queries(clip):
        parts = [q[clip] for q in (q0, q1, q2, q3)]
        return jnp.concatenate(parts, axis=0) * BF16(SCALE)

    def attend(clip, keys, values, fresh):
        queries = clip_queries(clip)
        new_tops, new_sums = [], []
        for g in range(groups):
            cols = slice(g * width, (g + 1) * width)
            scores = mm_nt(spread_heads(queries, g, mask_half), keys[:, cols])
            top = jnp.max(scores, axis=-1, keepdims=True)
            if not fresh:
                old_tile = tops[clip]
                old_top = jnp.concatenate(
                    [old_tile[:, g * GROUP + h : g * GROUP + h + 1] for h in range(GROUP)], axis=0
                )
                top = jnp.maximum(top, old_top)
            probs = jnp.exp(scores - top)
            total = jnp.sum(probs, axis=-1, keepdims=True)
            part = take_heads(mm(probs.astype(BF16), values[:, cols]), mask)
            if not fresh:
                old_tile = sums[clip]
                old_sum = jnp.concatenate(
                    [old_tile[:, g * GROUP + h : g * GROUP + h + 1] for h in range(GROUP)], axis=0
                )
                shrink = jnp.exp(old_top - top)
                total = total + old_sum * shrink
                part = part + acc[clip, :, cols] * take_heads(shrink, mask)
            acc[clip, :, cols] = part
            for h in range(GROUP):
                new_tops.append(top[h * HDIM : (h + 1) * HDIM])
                new_sums.append(total[h * HDIM : (h + 1) * HDIM])
        tops[clip] = pack_columns(new_tops)
        sums[clip] = pack_columns(new_sums)

    @pl.when(step == 0)
    def _():
        @pl.loop(0, clips)
        def _(clip):
            attend(clip, kl_ref[clip], vl_ref[clip], True)

    attend(ids[step], k_ref[...], v_ref[...], False)

    @pl.when(step == pl.num_programs(0) - 1)
    def _():
        rows = keep.shape[2]
        lane = lax.broadcasted_iota(jnp.int32, (HDIM, LANES), 1)

        @pl.loop(0, clips)
        def _(clip):
            total = jnp.where(lane < HEADS, sums[clip], 1.0)
            stat = tops[clip] + jnp.log(total)
            out = (acc[clip] / expand_columns(total, inner)).astype(BF16)
            for r in range(4):
                part = slice(r * rows, (r + 1) * rows)
                where_o, where_s = (send, send_st) if r % 2 else (keep, keep_st)
                where_o[r // 2, clip] = out[part]
                where_s[r // 2, clip] = stat[part]


def attention_forward(ids, queries, keys, values, latent_keys, latent_values):
    clips, rows, inner = queries[0].shape
    frames = keys.shape[0] // PATCH_IMG
    out = jax.ShapeDtypeStruct((2, clips, rows, inner), BF16)
    stat = jax.ShapeDtypeStruct((2, clips, rows, LANES), F32)
    block = pl.BlockSpec((PATCH_IMG, inner), lambda i, ids: (i, 0))

    def whole(shape):
        return pl.BlockSpec(shape, lambda i, ids: (0,) * len(shape))

    return pl.pallas_call(
        forward_kernel,
        grid_spec=pltpu.PrefetchScalarGridSpec(
            num_scalar_prefetch=1,
            grid=(frames,),
            in_specs=[whole((clips, rows, inner))] * 4
            + [block, block]
            + [whole((clips, rows, inner))] * 2,
            out_specs=(whole(out.shape), whole(out.shape), whole(stat.shape), whole(stat.shape)),
            scratch_shapes=[
                pltpu.VMEM((clips, 4 * rows, inner), F32),
                pltpu.VMEM((clips, 4 * rows, LANES), F32),
                pltpu.VMEM((clips, 4 * rows, LANES), F32),
            ],
        ),
        out_shape=(out, out, stat, stat),
        compiler_params=params(),
        name="attention_forward",
    )(ids, *queries, keys, values, latent_keys, latent_values)


def join_partials(first, first_stat, second, second_stat):
    width = first.shape[-1]
    top = jnp.maximum(first_stat, second_stat)
    total = jnp.exp(first_stat - top) + jnp.exp(second_stat - top)
    stat = top + jnp.log(total)
    out = first.astype(F32) * expand_columns(jnp.exp(first_stat - stat), width)
    out = out + second.astype(F32) * expand_columns(jnp.exp(second_stat - stat), width)
    return out, stat


def join_kernel(keep, keep_st, got, got_st, own, own_st, away, away_st):
    out, stat = join_partials(keep[0], keep_st[0], got[0], got_st[0])
    own[...] = out
    own_st[...] = stat
    out, stat = join_partials(keep[1], keep_st[1], got[1], got_st[1])
    away[...] = out.astype(BF16)
    away_st[...] = stat


def join_cores(keep, keep_st, got, got_st):
    _, rows, inner = keep.shape
    stat = jax.ShapeDtypeStruct((rows, LANES), F32)
    return pl.pallas_call(
        join_kernel,
        out_shape=(
            jax.ShapeDtypeStruct((rows, inner), F32),
            stat,
            jax.ShapeDtypeStruct((rows, inner), BF16),
            stat,
        ),
        in_specs=[vmem_spec()] * 4,
        out_specs=(vmem_spec(),) * 4,
        compiler_params=params(),
        name="join_cores",
    )(keep, keep_st, got, got_st)


class Gather:
    def __init__(self, depth, x_ref, o_ref, local_sem, send_sem, recv_sem, flips=()):
        self.depth = depth
        self.refs = x_ref, o_ref
        self.sems = local_sem, send_sem, recv_sem
        self.at = place()
        c = self.at[3]
        self.homes = [neighbours(*self.at, 1 if k in flips else c) for k in range(depth)]
        self.order = z_order(depth)

    def row(self, k, j):
        a, _, _, c = self.at
        _, b, e, _ = self.homes[k][j % 4]
        return flat((a - k) % self.depth, b, e, c if j < 4 else 1 - c)

    def copy(self, k, j):
        x_ref, o_ref = self.refs
        a, b, e, c = self.at
        base = {1: 0, 2: 0, 3: 1}.get(j, j - 4)
        if j == 0:
            target, row, src = ((a + k) % self.depth, b, e, c), flat(a, b, e, c), x_ref
        else:
            target = self.homes[k][min(j, 2)] if j < 4 else (a, b, e, 1 - c)
            row = self.row(k, base)
            src = x_ref if (k, base) == (0, 0) else o_ref.at[row]
        slot = k * 8 + j
        return pltpu.make_async_remote_copy(
            src_ref=src,
            dst_ref=o_ref.at[row],
            send_sem=self.sems[1].at[slot],
            recv_sem=self.sems[2].at[slot],
            device_id=device(*target),
            device_id_type=MESH,
        )

    def arrive(self, k, j):
        x_ref, o_ref = self.refs
        a, b, e, c = self.at
        slot = k * 8 + j
        pltpu.make_async_remote_copy(
            src_ref=x_ref,
            dst_ref=o_ref.at[self.row(k, j)],
            send_sem=self.sems[1].at[slot],
            recv_sem=self.sems[2].at[slot],
            device_id=device(a, b, e, 1 - c),
            device_id_type=MESH,
        ).wait_recv()

    def own(self):
        x_ref, o_ref = self.refs
        return pltpu.make_async_copy(x_ref, o_ref.at[flat(*self.at)], self.sems[0])

    def far(self, k):
        self.copy(k, 0).start()

    def begin(self):
        self.far(self.order[1])
        self.first(0)

    def settle(self, k=None):
        for k in self.order if k is None else [k]:
            for j in range(4, 8):
                self.arrive(k, j)
            if k == 0:
                self.own().wait()

    def first(self, k):
        if k:
            self.arrive(k, 0)
        for j in (1, 2, 4):
            self.copy(k, j).start()

    def second(self, k):
        self.arrive(k, 1)
        self.copy(k, 3).start()
        self.copy(k, 5).start()
        self.arrive(k, 2)
        self.copy(k, 6).start()

    def third(self, k):
        self.arrive(k, 3)
        self.copy(k, 7).start()

    def run(self, names):
        acts = {"z": self.far, "a": self.first, "b": self.second, "c": self.third}
        for name in names:
            acts[name[0]](self.order[int(name[1:])])

    def finish(self):
        for k in range(self.depth):
            for j in range(8):
                if k or j:
                    self.copy(k, j).wait_send()


def start_kernel(
    depth,
    w_ref,
    g_ref,
    b_ref,
    expand_ref,
    shrink_ref,
    output_ref,
    all_ref,
    shard_e,
    shard_s,
    gains_ref,
    shard,
    small,
    local_sem,
    send_sem,
    recv_sem,
    small_sem,
):
    rows, cols = w_ref.shape
    gather = Gather(depth, shard, all_ref, local_sem, send_sem, recv_sem)
    shard[:, :cols] = w_ref[...].astype(BF16)
    zeros = jnp.zeros((LANES - 6, rows), F32)
    lines = jnp.concatenate([g_ref[...], b_ref[...], zeros], axis=0)
    shard[:, cols:] = lines.T.astype(BF16)
    greet(depth, *gather.at)
    gather.own().start()
    gather.begin()
    gather.run(("z2", "z3"))
    width = output_ref.shape[1]
    groups = expand_ref.shape[1] // width
    for n in range(groups):
        shard_e[n * rows : (n + 1) * rows, :] = expand_ref[:, n * width : (n + 1) * width].astype(BF16)
    shard_e[groups * rows :, :] = output_ref[...].astype(BF16)
    shard_s[...] = shrink_ref[...].astype(BF16)
    gather.run(START_PLAN)
    gather.settle()
    load = pltpu.make_async_copy(all_ref.at[:, :, pl.ds(cols, LANES)], small, small_sem)
    load.start()
    load.wait()
    lines = small[...].reshape(depth * 8 * rows, LANES).astype(F32).T
    gains_ref[...] = lines[:8]
    gather.finish()


def start(weight, gains, biases, expand, shrink, output, depth):
    rows, cols = weight.shape
    count = depth * 8
    width = output.shape[1]
    rows_e = expand.shape[1] // width * rows + output.shape[0]
    return pl.pallas_call(
        functools.partial(start_kernel, depth),
        out_shape=(
            jax.ShapeDtypeStruct((count, rows, cols + LANES), BF16),
            jax.ShapeDtypeStruct((rows_e, width), BF16),
            jax.ShapeDtypeStruct(shrink.shape, BF16),
            jax.ShapeDtypeStruct((8, count * rows), F32),
        ),
        in_specs=[vmem_spec()] * 6,
        out_specs=(any_spec(), vmem_spec(), vmem_spec(), vmem_spec()),
        scratch_shapes=[
            pltpu.VMEM((rows, cols + LANES), BF16),
            pltpu.VMEM((count, rows, LANES), BF16),
            pltpu.SemaphoreType.DMA,
            pltpu.SemaphoreType.DMA((count,)),
            pltpu.SemaphoreType.DMA((count,)),
            pltpu.SemaphoreType.DMA,
        ],
        compiler_params=params(collective_id=1, has_side_effects=True),
        name="start",
    )(weight, gains, biases, expand, shrink, output)


def latent_mask(rows, inner):
    row = lax.broadcasted_iota(jnp.int32, (HEADS * rows, inner), 0) // rows
    col = lax.broadcasted_iota(jnp.int32, (HEADS * rows, inner), 1) // HDIM
    return (row == col).astype(F32)


def latent_attention(queries, keys, values, mask):
    rows = keys.shape[0]
    count = queries.shape[0]
    half = mask.astype(BF16)
    wide_k = jnp.concatenate([keys] * HEADS, axis=0) * half
    wide_v = jnp.concatenate([values] * HEADS, axis=0) * half
    scores = mm_nt(wide_k, queries).reshape(HEADS, rows, count)
    top = jnp.max(scores, axis=1, keepdims=True)
    probs = jnp.exp(scores - top)
    total = jnp.sum(probs, axis=1)
    out = mm_tn(probs.reshape(HEADS * rows, count).astype(BF16), wide_v)
    zeros = jnp.zeros((LANES - HEADS, count), F32)

    def tile(x):
        return jnp.concatenate([x, zeros], axis=0).T

    return out, tile(top.reshape(HEADS, count)), tile(total)


def remote_copy(src, dst, sems, slot, target):
    return pltpu.make_async_remote_copy(
        src_ref=src,
        dst_ref=dst,
        send_sem=sems[0].at[slot],
        recv_sem=sems[1].at[slot],
        device_id=device(*target),
        device_id_type=MESH,
    )


def feed_kernel(
    own,
    own_st,
    got,
    got_st,
    lat_ref,
    cot_ref,
    gb_ref,
    w_ref,
    out_ref,
    mixed_grad,
    context_grad,
    tile_ref,
    gain_ref,
    gw_ref,
    expand_v,
    shrink_v,
    output_v,
    grad_e,
    grad_s,
    grad_o,
    normed_v,
    normed_t,
    hat_v,
    acc_g,
    load_sem,
    store_sem,
):
    groups = expand_v.shape[0]
    width = expand_v.shape[3]
    blocks = expand_v.shape[1]
    shrink_rows = shrink_v.shape[1]
    per_group = blocks // groups
    expand_rows = expand_v.shape[2]
    shrink_at = groups * expand_rows
    output_at = shrink_at + shrink_rows
    output_rows = output_v.shape[1]
    half = width // 2
    inner = own.shape[1]

    def load_expand(g):
        return pltpu.make_async_copy(
            w_ref.at[:, pl.ds(g * expand_rows, expand_rows), :], expand_v.at[g], load_sem.at[g]
        )

    def load_shrink(g):
        part = pl.ds(g * per_group, per_group)
        return pltpu.make_async_copy(
            w_ref.at[part, pl.ds(shrink_at, shrink_rows), :],
            shrink_v.at[part],
            load_sem.at[groups + g],
        )

    load_output = pltpu.make_async_copy(
        w_ref.at[:, pl.ds(output_at, output_rows), :], output_v, load_sem.at[2 * groups]
    )
    load_output.start()
    for g in range(groups):
        load_expand(g).start()
        load_shrink(g).start()

    context, stat = join_partials(own[...], own_st[...], got[...], got_st[...])
    context_half = context.astype(BF16)
    load_output.wait()
    weight_o = output_v[...].reshape(inner, width)
    mixed = lat_ref[...] + mm(context_half, weight_o)
    hat, scale = normalise(mixed)
    hat_v[...] = hat
    normed = (hat * gb_ref[2:3, :] + gb_ref[5:6, :]).astype(BF16)
    normed_v[...] = normed
    normed_t[...] = normed.astype(F32).T.astype(BF16)
    out_ref[...] = mixed
    acc_g[...] = jnp.zeros_like(acc_g)

    def store_e(s, slot):
        return pltpu.make_async_copy(
            grad_e.at[slot],
            gw_ref.at[:, pl.ds((s // 2) * expand_rows, expand_rows), pl.ds((s % 2) * half, half)],
            store_sem.at[slot],
        )

    def store_s(s, slot):
        rows = half // shrink_rows
        return pltpu.make_async_copy(
            grad_s.at[slot],
            gw_ref.at[pl.ds(s * rows, rows), pl.ds(shrink_at, shrink_rows), :],
            store_sem.at[2 + slot],
        )

    cot = cot_ref[...]
    steps = 2 * groups
    for s in range(steps):
        g, slot = s // 2, s % 2
        if slot == 0:
            load_expand(g).wait()
            load_shrink(g).wait()
        cols = slice(slot * half, (slot + 1) * half)
        w_e = expand_v[g, :, :, cols].reshape(blocks * expand_rows, half)
        first = s * half // shrink_rows
        w_s = shrink_v[first : first + half // shrink_rows].reshape(half, width)
        pre = mm(normed_v[...], w_e)
        cdf = 0.5 * (1.0 + lax.erf(pre * (0.5**0.5)))
        hidden = (pre * cdf).astype(BF16)
        out_ref[...] += mm(hidden, w_s)
        grad_hidden = mm_nt(cot, w_s)
        pdf = jnp.exp(-0.5 * pre * pre) * (1.0 / math.sqrt(2.0 * math.pi))
        grad_pre = (grad_hidden * (cdf + pre * pdf)).astype(BF16)
        if s >= 2:
            store_e(s - 2, slot).wait()
            store_s(s - 2, slot).wait()
        grad_s[slot] = mm_tn(hidden, cot).astype(BF16).reshape(half // shrink_rows, shrink_rows, width)
        grad_e[slot] = (
            mm(normed_t[...], grad_pre).astype(BF16).reshape(blocks, expand_rows, half)
        )
        store_e(s, slot).start()
        store_s(s, slot).start()
        acc_g[...] += mm_nt(grad_pre, w_e)

    grad_normed = acc_g[...]
    hat = hat_v[...]
    rows = gain_ref.shape[0]
    gain_ref[...] = jnp.concatenate(
        [
            jnp.sum(grad_normed * hat, axis=0, keepdims=True),
            jnp.sum(grad_normed, axis=0, keepdims=True),
            jnp.zeros((rows - 2, width), F32),
        ],
        axis=0,
    )
    total = cot.astype(F32) + norm_back(grad_normed, hat, scale, gb_ref[2:3, :])
    mixed_grad[...] = total
    attended = total.astype(BF16)
    grad_o[...] = mm_tn(context_half, attended).astype(BF16).reshape(grad_o.shape)
    store_o = pltpu.make_async_copy(
        grad_o, gw_ref.at[:, pl.ds(output_at, output_rows), :], store_sem.at[4]
    )
    store_o.start()
    grad_c = mm_nt(attended, weight_o).astype(BF16)
    context_grad[...] = grad_c
    product = grad_c.astype(F32) * context
    head = lax.broadcasted_iota(jnp.int32, product.shape, 1) // HDIM
    deltas = [
        jnp.sum(jnp.where(head == h, product, 0.0), axis=-1, keepdims=True) for h in range(HEADS)
    ]
    lane = lax.broadcasted_iota(jnp.int32, stat.shape, 1)
    tile_ref[...] = jnp.where(lane < HEADS, stat, pack_columns(deltas, HEADS))
    for s in range(steps - 2, steps):
        store_e(s, s % 2).wait()
        store_s(s, s % 2).wait()
    store_o.wait()


def feed_forward(own, own_st, got, got_st, latents, cotangent, gains, weights):
    rows, width = latents.shape
    inner = own.shape[1]
    blocks = weights.shape[0]
    ff = 4 * width
    groups = ff // width
    expand_rows = width // blocks
    shrink_rows = ff // blocks
    output_rows = inner // blocks
    half = width // 2
    flops = 2 * rows * (6 * width * ff + 3 * width * inner)
    return pl.pallas_call(
        feed_kernel,
        out_shape=(
            jax.ShapeDtypeStruct((rows, width), F32),
            jax.ShapeDtypeStruct((rows, width), F32),
            jax.ShapeDtypeStruct((rows, inner), BF16),
            jax.ShapeDtypeStruct((rows, LANES), F32),
            jax.ShapeDtypeStruct((8, width), F32),
            jax.ShapeDtypeStruct(weights.shape, BF16),
        ),
        in_specs=[vmem_spec()] * 7 + [any_spec()],
        out_specs=(vmem_spec(),) * 5 + (any_spec(),),
        scratch_shapes=[
            pltpu.VMEM((groups, blocks, expand_rows, width), BF16),
            pltpu.VMEM((blocks, shrink_rows, width), BF16),
            pltpu.VMEM((blocks, output_rows, width), BF16),
            pltpu.VMEM((2, blocks, expand_rows, half), BF16),
            pltpu.VMEM((2, half // shrink_rows, shrink_rows, width), BF16),
            pltpu.VMEM((blocks, output_rows, width), BF16),
            pltpu.VMEM((rows, width), BF16),
            pltpu.VMEM((width, rows), BF16),
            pltpu.VMEM((rows, width), F32),
            pltpu.VMEM((rows, width), F32),
            pltpu.SemaphoreType.DMA((2 * groups + 1,)),
            pltpu.SemaphoreType.DMA((5,)),
        ],
        compiler_params=params(),
        cost_estimate=pl.CostEstimate(
            flops=flops, bytes_accessed=4 * weights.size, transcendentals=2 * rows * ff
        ),
        name="feed_forward",
    )(own, own_st, got, got_st, latents, cotangent, gains, weights)


def backward_kernel(
    ids,
    q0,
    q1,
    q2,
    q3,
    g0,
    g1,
    g2,
    g3,
    t0,
    t1,
    t2,
    t3,
    k_ref,
    v_ref,
    kl_ref,
    vl_ref,
    m_ref,
    gb_ref,
    wk_ref,
    wv_ref,
    media_grad,
    latent_kv,
    keep,
    send,
    weight_grad,
    gain_ref,
    acc,
):
    step = pl.program_id(0)
    clips = acc.shape[0]
    inner = acc.shape[2]
    groups = inner // (GROUP * HDIM)
    width = GROUP * HDIM
    mask = head_mask(F32)
    mask_half = mask.astype(BF16)

    def attend(clip, keys, values, fresh):
        queries = jnp.concatenate([q[clip] for q in (q0, q1, q2, q3)], axis=0) * BF16(SCALE)
        grads = jnp.concatenate([g[clip] for g in (g0, g1, g2, g3)], axis=0)
        stats = jnp.concatenate([t[clip] for t in (t0, t1, t2, t3)], axis=0).T
        key_parts, value_parts = [], []
        for g in range(groups):
            cols = slice(g * width, (g + 1) * width)

            def line(first):
                at = first + g * GROUP
                return jnp.concatenate([stats[at + h : at + h + 1, :] for h in range(GROUP)], axis=1)

            wide_q = spread_heads(queries, g, mask_half)
            wide_g = spread_heads(grads, g, mask_half)
            probs = jnp.exp(mm_nt(keys[:, cols], wide_q) - line(0))
            grad_probs = mm_nt(values[:, cols], wide_g)
            grad_scores = (probs * (grad_probs - line(HEADS))).astype(BF16)
            key_parts.append(mm(grad_scores, wide_q))
            value_parts.append(mm(probs.astype(BF16), wide_g))
            part = take_heads(mm_tn(grad_scores, keys[:, cols]), mask)
            if fresh:
                acc[clip, :, cols] = part
            else:
                acc[clip, :, cols] += part
        return jnp.concatenate(key_parts + value_parts, axis=1).astype(BF16)

    @pl.when(step == 0)
    def _():
        gain_ref[...] = jnp.zeros_like(gain_ref)
        weight_grad[...] = jnp.zeros_like(weight_grad)

        @pl.loop(0, clips)
        def _(clip):
            latent_kv[clip] = attend(clip, kl_ref[clip], vl_ref[clip], True)

    grad_kv = attend(ids[step], k_ref[...], v_ref[...], False)
    hat, scale = normalise(m_ref[...].astype(F32))
    gain = gb_ref[0:1, :]
    normed = (hat * gain + gb_ref[3:4, :]).astype(BF16)
    weight_grad[...] += mm_tn(normed, grad_kv)
    grad = mm_nt(grad_kv[:, :inner], wk_ref[...]) + mm_nt(grad_kv[:, inner:], wv_ref[...])
    gain_ref[0:1, :] += jnp.sum(grad * hat, axis=0, keepdims=True)
    gain_ref[1:2, :] += jnp.sum(grad, axis=0, keepdims=True)
    media_grad[...] = norm_back(grad, hat, scale, gain).astype(BF16)

    @pl.when(step == pl.num_programs(0) - 1)
    def _():
        rows = keep.shape[2]

        @pl.loop(0, clips)
        def _(clip):
            out = (acc[clip] * SCALE).astype(BF16)
            for r in range(4):
                part = slice(r * rows, (r + 1) * rows)
                where_o = send if r % 2 else keep
                where_o[r // 2, clip] = out[part]


def attention_backward(
    ids, queries, grads, tiles, keys, values, latent_keys, latent_values, media, gains, attend
):
    clips, rows, inner = queries[0].shape
    width = media.shape[1]
    frames = keys.shape[0] // PATCH_IMG
    block = pl.BlockSpec((PATCH_IMG, inner), lambda i, ids: (i, 0))
    wide = pl.BlockSpec((PATCH_IMG, width), lambda i, ids: (i, 0))

    def whole(shape):
        return pl.BlockSpec(shape, lambda i, ids: (0,) * len(shape))

    def column(n):
        return pl.BlockSpec((width, inner), lambda i, ids: (0, n))

    query = whole((clips, rows, inner))
    pair = (2, clips, rows, inner)
    return pl.pallas_call(
        backward_kernel,
        grid_spec=pltpu.PrefetchScalarGridSpec(
            num_scalar_prefetch=1,
            grid=(frames,),
            in_specs=[query] * 8
            + [whole((clips, rows, LANES))] * 4
            + [block, block, query, query, wide, whole(gains.shape), column(1), column(2)],
            out_specs=(
                wide,
                whole((clips, rows, 2 * inner)),
                whole(pair),
                whole(pair),
                whole((width, 2 * inner)),
                whole((8, width)),
            ),
            scratch_shapes=[pltpu.VMEM((clips, 4 * rows, inner), F32)],
        ),
        out_shape=(
            jax.ShapeDtypeStruct(media.shape, BF16),
            jax.ShapeDtypeStruct((clips, rows, 2 * inner), BF16),
            jax.ShapeDtypeStruct(pair, BF16),
            jax.ShapeDtypeStruct(pair, BF16),
            jax.ShapeDtypeStruct((width, 2 * inner), F32),
            jax.ShapeDtypeStruct((8, width), F32),
        ),
        compiler_params=params(),
        name="attention_backward",
    )(
        ids,
        *queries,
        *grads,
        *tiles,
        keys,
        values,
        latent_keys,
        latent_values,
        media,
        gains,
        attend,
        attend,
    )


def last_kernel(
    lat_ref, mixed_grad, first, second, kv_ref, gb_ref, w_ref, gw_ref, gm_ref, gf_ref, out_ref, pack_ref
):
    inner = first.shape[1]
    width = lat_ref.shape[1]
    hat, scale = normalise(lat_ref[...])
    gain = gb_ref[1:2, :]
    normed = (hat * gain + gb_ref[4:5, :]).astype(BF16)
    grad_q = (first[...].astype(F32) + second[...].astype(F32)).astype(BF16)
    grad_kv = kv_ref[...]
    grad = mm_nt(grad_q, w_ref[:, :inner]) + mm_nt(grad_kv, w_ref[:, inner : 3 * inner])
    pack_ref[:, :inner] = mm_tn(normed, grad_q).astype(BF16)
    pack_ref[:, inner : 3 * inner] = (gw_ref[...] + mm_tn(normed, grad_kv)).astype(BF16)
    lines = jnp.concatenate(
        [
            gm_ref[0:1, :],
            jnp.sum(grad * hat, axis=0, keepdims=True),
            gf_ref[0:1, :],
            gm_ref[1:2, :],
            jnp.sum(grad, axis=0, keepdims=True),
            gf_ref[1:2, :],
            jnp.zeros((LANES - 6, width), F32),
        ],
        axis=0,
    )
    pack_ref[:, 3 * inner :] = lines.T.astype(BF16)
    out_ref[...] = mixed_grad[...] + norm_back(grad, hat, scale, gain)


def latent_backward(latents, mixed_grad, first, second, grad_kv, gains, attend, grad_w, gain_m, gain_f):
    return pl.pallas_call(
        last_kernel,
        out_shape=(
            jax.ShapeDtypeStruct(latents.shape, F32),
            jax.ShapeDtypeStruct(attend.shape, BF16),
        ),
        in_specs=[vmem_spec()] * 10,
        out_specs=(vmem_spec(), vmem_spec()),
        compiler_params=params(),
        name="latent_backward",
    )(latents, mixed_grad, first, second, grad_kv, gains, attend, grad_w, gain_m, gain_f)


class Scatter:
    def __init__(self, depth, chunk, g_ref, buffers, load_sem, sems, flips=()):
        self.depth = depth
        self.chunk = chunk
        self.g_ref = g_ref
        self.own, self.from_c, self.from_two, self.from_one, self.from_z = buffers
        self.load_sem = load_sem
        self.sems = sems
        self.at = place()
        a, b, e, c = self.at
        self.flips = flips
        self.homes = [neighbours(*self.at, 1 if k in flips else c) for k in range(depth)]
        self.twin = (a, b, e, 1 - c)
        self.order = z_order(depth)[::-1]

    def row(self, k, j, core):
        _, b, e, _ = self.homes[k][j]
        return flat((self.at[0] + k) % self.depth, b, e, core)

    def load(self, k, j):
        slot = k * 4 + j
        src = self.g_ref.at[self.row(k, j, self.at[3])]
        return pltpu.make_async_copy(src, self.own.at[slot], self.load_sem.at[slot])

    def to_twin(self, k, j):
        there = j if k in self.flips else (0, 2, 1, 3)[j]
        src = self.g_ref.at[self.row(k, there, 1 - self.at[3])]
        return remote_copy(src, self.from_c.at[k * 4 + j], self.sems, k * 8 + j, self.twin)

    def to_two(self, k, j):
        spot = self.from_two.at[k * 2 + j - 2]
        return remote_copy(self.own.at[k * 4 + j], spot, self.sems, k * 8 + 2 + j, self.homes[k][2])

    def to_one(self, k):
        return remote_copy(
            self.own.at[k * 4 + 1], self.from_one.at[k], self.sems, k * 8 + 6, self.homes[k][1]
        )

    def to_far(self, k):
        a, b, e, c = self.at
        target = ((a + k) % self.depth, b, e, c)
        return remote_copy(
            self.own.at[k * 4], self.from_z.at[k - 1], self.sems, k * 8 + 7, target
        )

    def add(self, slot, spot):
        mine = self.own.at[slot]
        add_into(mine, mine, spot, self.chunk)

    def begin(self):
        for k in self.order:
            for j in (3, 2, 1, 0):
                self.load(k, j).start()
                self.to_twin(k, j).start()

    def first(self, k):
        for j in (3, 2, 1, 0):
            self.load(k, j).wait()
            self.to_twin(k, j).wait_recv()
            self.add(k * 4 + j, self.from_c.at[k * 4 + j])
            if j >= 2:
                self.to_two(k, j).start()

    def second(self, k):
        for j in (3, 2):
            self.to_two(k, j).wait_recv()
            self.add(k * 4 + j - 2, self.from_two.at[k * 2 + j - 2])
            if j == 3:
                self.to_one(k).start()

    def third(self, k):
        self.to_one(k).wait_recv()
        self.add(k * 4, self.from_one.at[k])
        if k:
            self.to_far(k).start()

    def run(self, names):
        acts = {"a": self.first, "b": self.second, "c": self.third}
        for name in names:
            acts[name[0]](self.order[int(name[1:])])

    def finish(self, o_ref):
        for k in range(1, self.depth):
            self.to_far(k).wait_recv()

        @pl.loop(0, o_ref.shape[1] // self.chunk)
        def _(step):
            part = pl.ds(pl.multiple_of(step * self.chunk, self.chunk), self.chunk)
            total = self.own[0, :, part].astype(F32)
            for k in range(1, self.depth):
                total = total + self.from_z[k - 1, :, part].astype(F32)
            o_ref[:, part] = total

        for k in range(self.depth):
            for j in range(4):
                self.to_twin(k, j).wait_send()
            self.to_two(k, 3).wait_send()
            self.to_two(k, 2).wait_send()
            self.to_one(k).wait_send()
            if k:
                self.to_far(k).wait_send()


def scatter_buffers(depth, rows, cols):
    def slots(n):
        return pltpu.VMEM((n, rows, cols), BF16)

    return [slots(depth * 4), slots(depth * 4), slots(depth * 2), slots(depth), slots(depth - 1)]


def scatter_sems(depth):
    return [
        pltpu.SemaphoreType.DMA((depth * 4,)),
        pltpu.SemaphoreType.DMA((depth * 8,)),
        pltpu.SemaphoreType.DMA((depth * 8,)),
    ]


def latent_attention_back(queries, grads, stats, keys, values, mask):
    rows = keys.shape[0]
    count = queries.shape[0]
    half = mask.astype(BF16)
    wide_k = jnp.concatenate([keys] * HEADS, axis=0) * half
    wide_v = jnp.concatenate([values] * HEADS, axis=0) * half
    cut = (HEADS, rows, count)
    scores = mm_nt(wide_k, queries).reshape(cut)
    probs = jnp.exp(scores - stats[:HEADS][:, None, :])
    grad_probs = mm_nt(wide_v, grads).reshape(cut)
    grad_scores = probs * (grad_probs - stats[HEADS : 2 * HEADS][:, None, :])
    grad_scores = grad_scores.reshape(HEADS * rows, count).astype(BF16)
    probs = probs.reshape(HEADS * rows, count).astype(BF16)

    def fold(full):
        full = full * mask
        total = full[:rows]
        for h in range(1, HEADS):
            total = total + full[h * rows : (h + 1) * rows]
        return total

    grad_kv = [fold(mm(grad_scores, queries)), fold(mm(probs, grads))]
    return mm_tn(grad_scores, wide_k), jnp.concatenate(grad_kv, axis=1).astype(BF16)


def to_lines(tile):
    return tile.T[: 2 * HEADS]


def from_lines(lines):
    zeros = jnp.zeros((LANES - lines.shape[0], lines.shape[1]), F32)
    return jnp.concatenate([lines, zeros], axis=0).T


def back_kernel(
    depth,
    frames,
    chunk,
    plan,
    ids,
    last,
    has,
    same,
    g_ref,
    q_ref,
    context_grad,
    tile_ref,
    k_ref,
    v_ref,
    m_ref,
    kl_ref,
    vl_ref,
    gb_ref,
    w_ref,
    lat_ref,
    mixed_ref,
    gain_f,
    media_grad,
    latents_grad,
    pack_ref,
    mine_ref,
    own,
    from_c,
    from_two,
    from_one,
    from_z,
    load_sem,
    send_sem,
    recv_sem,
    all_g,
    lines,
    tiles,
    weight_acc,
    gain_acc,
    outs,
    latent_kv,
    keep,
    send,
    core_q,
    away,
    y_q,
    link_send,
    link_recv,
    mixed_sem,
):
    step = pl.program_id(0)
    a, b, e, c = place()
    twin, other = (a, b, e, 1 - c), (a, b, 1 - e, c)
    links = link_send, link_recv
    buffers = own, from_c, from_two, from_one, from_z
    scatter = Scatter(depth, chunk, g_ref, buffers, load_sem, (send_sem, recv_sem), BACK_FLIPS)
    clips, rows, inner = kl_ref.shape
    total_rows = clips * rows
    groups = inner // (GROUP * HDIM)
    width = GROUP * HDIM
    mask = head_mask(F32)
    mask_half = mask.astype(BF16)
    grad_copies = [
        remote_copy(all_g.at[0], all_g.at[2], links, 0, other),
        remote_copy(all_g.at[0], all_g.at[1], links, 1, twin),
        remote_copy(all_g.at[2], all_g.at[3], links, 2, twin),
    ]
    line_copies = [
        remote_copy(lines.at[0], lines.at[2], links, 3, other),
        remote_copy(lines.at[0], lines.at[1], links, 4, twin),
        remote_copy(lines.at[2], lines.at[3], links, 5, twin),
    ]
    core_copy = remote_copy(send, core_q, links, 6, twin)
    y_copy = remote_copy(away, y_q, links, 7, other)

    def clip_queries(clip):
        return jnp.concatenate([q_ref[r, clip] for r in range(4)], axis=0) * BF16(SCALE)

    def clip_grads(clip):
        return jnp.concatenate([all_g[r, clip] for r in range(4)], axis=0)

    def clip_stats(clip):
        return jnp.concatenate([tiles[r, clip] for r in range(4)], axis=0).T

    @pl.when(step == 0)
    def _():
        all_g[0] = context_grad[...]
        lines[0] = to_lines(tile_ref[...])
        greet(depth, a, b, e, c)
        for copies in (grad_copies, line_copies):
            copies[0].start()
            copies[1].start()
        scatter.begin()
        gain_acc[...] = jnp.zeros_like(gain_acc)
        weight_acc[...] = jnp.zeros_like(weight_acc)
        outs[0] = jnp.zeros_like(outs[0])

    for when, names in plan[:-2]:

        @pl.when(step == when)
        def _(names=names):
            scatter.run(names)

    @pl.when(step == 0)
    def _():
        for copies in (grad_copies, line_copies):
            copies[0].wait()
            copies[2].start()
        for copies in (grad_copies, line_copies):
            copies[1].wait()
            copies[2].wait()
        for r in range(4):
            tiles[r] = from_lines(lines[r]).reshape(clips, rows, LANES)

    @pl.when((step >= 1) & (step <= frames))
    def _():
        frame = step - 1
        before = jnp.maximum(frame - 1, 0)
        clip = ids[frame]
        joined = same[frame] == 1
        queries, grads, stats = clip_queries(clip), clip_grads(clip), clip_stats(clip)
        key_parts, value_parts = [], []
        for g in range(groups):
            cols = slice(g * width, (g + 1) * width)

            def line(first):
                at = first + g * GROUP
                return jnp.concatenate([stats[at + h : at + h + 1, :] for h in range(GROUP)], axis=1)

            wide_q = spread_heads(queries, g, mask_half)
            wide_g = spread_heads(grads, g, mask_half)
            keys = k_ref[:, cols]
            probs = jnp.exp(mm_nt(keys, wide_q) - line(0))
            grad_probs = mm_nt(v_ref[:, cols], wide_g)
            grad_scores = (probs * (grad_probs - line(HEADS))).astype(BF16)
            key_parts.append(mm(grad_scores, wide_q))
            value_parts.append(mm(probs.astype(BF16), wide_g))
            part = take_heads(mm_tn(grad_scores, keys), mask)
            outs[frame, :, cols] = part + jnp.where(joined, outs[before, :, cols], 0.0)
        grad_kv = jnp.concatenate(key_parts + value_parts, axis=1).astype(BF16)
        hat, scale = normalise(m_ref[...].astype(F32))
        gain = gb_ref[0:1, :]
        normed = (hat * gain + gb_ref[3:4, :]).astype(BF16)
        weight_acc[...] += mm_tn(normed, grad_kv)
        grad = mm_nt(grad_kv, w_ref[:, inner : 3 * inner])
        gain_acc[0:1, :] += jnp.sum(grad * hat, axis=0, keepdims=True)
        gain_acc[1:2, :] += jnp.sum(grad, axis=0, keepdims=True)
        media_grad[...] = norm_back(grad, hat, scale, gain).astype(BF16)

    @pl.when(step == frames + 1)
    def _():
        wide = latent_mask(rows, inner)

        def one_clip(clip):
            out, grad_kv = latent_attention_back(
                clip_queries(clip),
                clip_grads(clip),
                clip_stats(clip),
                kl_ref[clip],
                vl_ref[clip],
                wide,
            )
            out = (out + jnp.where(has[clip] == 1, outs[last[clip]], 0.0)) * SCALE
            return out, grad_kv

        @pl.loop(0, clips // TOGETHER)
        def _(index):
            some = [index * TOGETHER + n for n in range(TOGETHER)]
            results = [one_clip(clip) for clip in some]
            for clip, (out, grad_kv) in zip(some, results):
                latent_kv[clip] = grad_kv
                for r in range(4):
                    part = slice(r * rows, (r + 1) * rows)
                    if r % 2:
                        send[r // 2, clip] = out[part].astype(BF16)
                    else:
                        keep[r // 2, clip] = out[part]

        core_copy.start()
        hat, scale = normalise(lat_ref[...])
        gain = gb_ref[1:2, :]
        normed = (hat * gain + gb_ref[4:5, :]).astype(BF16)
        core_copy.wait()
        away[...] = (keep[1] + core_q[1].astype(F32)).astype(BF16)
        y_copy.start()
        grad_kv = latent_kv[...].reshape(total_rows, 2 * inner)
        pack_ref[:, inner : 3 * inner] = (weight_acc[...] + mm_tn(normed, grad_kv)).astype(BF16)
        grad = mm_nt(grad_kv, w_ref[:, inner : 3 * inner])
        mixed = weight_acc.at[:total_rows]
        load_mixed = pltpu.make_async_copy(mixed_ref, mixed, mixed_sem)
        load_mixed.start()
        scatter.run(plan[-2][1])
        y_copy.wait()
        grad_q = (keep[0] + core_q[0].astype(F32) + y_q[...].astype(F32)).astype(BF16)
        grad_q = grad_q.reshape(total_rows, inner)
        grad = grad + mm_nt(grad_q, w_ref[:, :inner])
        pack_ref[:, :inner] = mm_tn(normed, grad_q).astype(BF16)
        table = jnp.concatenate(
            [
                gain_acc[0:1, :],
                jnp.sum(grad * hat, axis=0, keepdims=True),
                gain_f[0:1, :],
                gain_acc[1:2, :],
                jnp.sum(grad, axis=0, keepdims=True),
                gain_f[1:2, :],
                jnp.zeros((LANES - 6, grad.shape[1]), F32),
            ],
            axis=0,
        )
        pack_ref[:, 3 * inner :] = table.T.astype(BF16)
        load_mixed.wait()
        latents_grad[...] = mixed[...] + norm_back(grad, hat, scale, gain)
        scatter.run(plan[-1][1])
        scatter.finish(mine_ref)


def back(
    ids,
    last,
    has,
    same,
    grad_feed,
    query_all,
    context_grad,
    tile,
    keys,
    values,
    media,
    latent_key,
    latent_value,
    gains,
    attend,
    latents,
    mixed_grad,
    gain_f,
    depth,
    chunk,
    plan,
):
    clips, rows, inner = latent_key.shape
    frames = media.shape[0] // PATCH_IMG
    width = media.shape[1]
    total = clips * rows
    cut = (clips, rows, inner)
    _, feed_rows, feed_cols = grad_feed.shape
    once = pl.Buffered(buffer_count=1)

    def whole(x):
        return pl.BlockSpec(x.shape, lambda i: (0,) * len(x.shape), pipeline_mode=once)

    def block(columns):
        return pl.BlockSpec((PATCH_IMG, columns), lambda i: (jnp.clip(i - 1, 0, frames - 1), 0))

    smem = pl.BlockSpec(memory_space=pltpu.SMEM)
    outs = (
        jax.ShapeDtypeStruct(media.shape, BF16),
        jax.ShapeDtypeStruct(latents.shape, F32),
        jax.ShapeDtypeStruct(attend.shape, BF16),
        jax.ShapeDtypeStruct((feed_rows, feed_cols), F32),
    )
    return pl.pallas_call(
        functools.partial(back_kernel, depth, frames, chunk, plan),
        grid=(frames + 2,),
        out_shape=outs,
        in_specs=[smem] * 4
        + [any_spec(), whole(query_all), whole(context_grad), whole(tile)]
        + [block(inner), block(inner), block(width)]
        + [whole(x) for x in (latent_key, latent_value, gains, attend, latents)]
        + [any_spec(), whole(gain_f)],
        out_specs=(block(width),) + tuple(whole(x) for x in outs[1:]),
        scratch_shapes=scatter_buffers(depth, feed_rows, feed_cols)
        + scatter_sems(depth)
        + [
            pltpu.VMEM((4,) + cut, BF16),
            pltpu.VMEM((4, 2 * HEADS, total), F32),
            pltpu.VMEM((4, clips, rows, LANES), F32),
            pltpu.VMEM((width, 2 * inner), F32),
            pltpu.VMEM((8, width), F32),
            pltpu.VMEM((frames, 4 * rows, inner), F32),
            pltpu.VMEM((clips, rows, 2 * inner), BF16),
            pltpu.VMEM((2,) + cut, F32),
            pltpu.VMEM((2,) + cut, BF16),
            pltpu.VMEM((2,) + cut, BF16),
            pltpu.VMEM(cut, BF16),
            pltpu.VMEM(cut, BF16),
            pltpu.SemaphoreType.DMA((8,)),
            pltpu.SemaphoreType.DMA((8,)),
            pltpu.SemaphoreType.DMA,
        ],
        compiler_params=params(collective_id=4, has_side_effects=True),
        name="back",
    )(
        ids,
        last,
        has,
        same,
        grad_feed,
        query_all,
        context_grad,
        tile,
        keys,
        values,
        media,
        latent_key,
        latent_value,
        gains,
        attend,
        latents,
        mixed_grad,
        gain_f,
    )


def head_kernel(
    depth,
    frames,
    parts,
    plan,
    late,
    ids,
    last,
    has,
    same,
    shard_e,
    shard_s,
    m_ref,
    lat_ref,
    cot_ref,
    gb_ref,
    wq_ref,
    k_ref,
    v_ref,
    q_ref,
    kl_ref,
    vl_ref,
    out_ref,
    mixed_grad,
    context_grad,
    tile_ref,
    gain_ref,
    gw_ref,
    all_k,
    all_v,
    all_q,
    outs,
    tops,
    sums,
    keep,
    keep_st,
    send,
    send_st,
    core_o,
    send_li,
    core_li,
    away,
    y_o,
    away_li,
    y_li,
    weights_e,
    weights_s,
    grad_s,
    grad_o,
    normed_v,
    normed_t,
    hat_v,
    local_sem,
    send_e,
    recv_e,
    send_s,
    recv_s,
    link_send,
    link_recv,
    out_sem,
    store_sem,
):
    step = pl.program_id(0)
    a, b, e, c = place()
    twin, other = (a, b, e, 1 - c), (a, b, 1 - e, c)
    links = link_send, link_recv
    gather_e = Gather(depth, shard_e, weights_e, local_sem.at[0], send_e, recv_e, HEAD_FLIPS)
    gather_s = Gather(depth, shard_s, weights_s, local_sem.at[1], send_s, recv_s, HEAD_FLIPS)
    clips, rows, inner = kl_ref.shape
    total_rows = clips * rows
    groups = inner // (GROUP * HDIM)
    width = GROUP * HDIM
    slabs = PATCH_IMG // all_k.shape[1]
    mask = head_mask(F32)
    mask_half = mask.astype(BF16)
    query_copies = [
        remote_copy(all_q.at[0], all_q.at[2], links, 0, other),
        remote_copy(all_q.at[0], all_q.at[1], links, 1, twin),
        remote_copy(all_q.at[2], all_q.at[3], links, 2, twin),
    ]
    share = clips // parts
    lot = share * rows

    def core_copies(p):
        some = pl.ds(p * share, share)
        return [
            remote_copy(send.at[:, some], core_o.at[:, some], links, 3 + 4 * p, twin),
            remote_copy(send_li.at[p], core_li.at[p], links, 4 + 4 * p, twin),
        ]

    def y_copies(p):
        some = pl.ds(p * lot, lot)
        return [
            remote_copy(away.at[some], y_o.at[some], links, 5 + 4 * p, other),
            remote_copy(away_li.at[p], y_li.at[p], links, 6 + 4 * p, other),
        ]

    def join_part(p):
        some = slice(p * share, (p + 1) * share)
        for copy in core_copies(p):
            copy.wait()
        for n in (1, 0):
            out, stat = join_partials(
                keep[n, some].reshape(lot, inner),
                keep_st[n, some].reshape(lot, LANES),
                core_o[n, some].reshape(lot, inner),
                from_lines(core_li[p, n]),
            )
            if n:
                away[p * lot : (p + 1) * lot] = out.astype(BF16)
                away_li[p] = to_lines(stat)
                for copy in y_copies(p):
                    copy.start()
            else:
                keep[0, some] = out.reshape(share, rows, inner)
                keep_st[0, some] = stat.reshape(share, rows, LANES)

    keep_queries = pltpu.make_async_copy(all_q, q_ref, out_sem)

    def run(names):
        for name in names:
            (gather_e if name[0] == "e" else gather_s).run((name[1:],))

    def clip_queries(clip):
        return jnp.concatenate([all_q[r, clip] for r in range(4)], axis=0) * BF16(SCALE)

    @pl.when(step == 0)
    def _():
        greet(depth, a, b, e, c)
        hat, _ = normalise(lat_ref[...])
        normed = (hat * gb_ref[1:2, :] + gb_ref[4:5, :]).astype(BF16)
        all_q[0] = mm(normed, wq_ref[:, :inner]).astype(BF16).reshape(clips, rows, inner)
        query_copies[0].start()
        query_copies[1].start()
        gather_s.own().start()
        gather_e.own().start()
        gather_e.begin()
        kl_ref[...] = (
            mm(normed, wq_ref[:, inner : 2 * inner]).astype(BF16).reshape(clips, rows, inner)
        )
        vl_ref[...] = (
            mm(normed, wq_ref[:, 2 * inner : 3 * inner]).astype(BF16).reshape(clips, rows, inner)
        )
        outs[0] = jnp.zeros_like(outs[0])
        tops[0] = jnp.zeros_like(tops[0])
        sums[0] = jnp.zeros_like(sums[0])

    @pl.when(step < frames)
    def _():
        hat, _ = normalise(m_ref[...].astype(F32))
        normed = (hat * gb_ref[0:1, :] + gb_ref[3:4, :]).astype(BF16)
        new_k = mm(normed, wq_ref[:, inner : 2 * inner]).astype(BF16)
        new_v = mm(normed, wq_ref[:, 2 * inner : 3 * inner]).astype(BF16)
        k_ref[...] = new_k
        v_ref[...] = new_v
        at = pl.ds(step * slabs, slabs)
        all_k[at] = new_k.reshape(slabs, PATCH_IMG // slabs, inner)
        all_v[at] = new_v.reshape(slabs, PATCH_IMG // slabs, inner)

    for when, names in plan:

        @pl.when(step == when)
        def _(names=names):
            run(names)

    @pl.when(step == frames // 2)
    def _():
        query_copies[0].wait()
        query_copies[2].start()

    @pl.when(step == frames)
    def _():
        query_copies[1].wait()
        query_copies[2].wait()
        keep_queries.start()

    @pl.when((step >= frames) & (step < 2 * frames))
    def _():
        frame = step - frames
        before = jnp.maximum(frame - 1, 0)
        queries = clip_queries(ids[frame])
        joined = same[frame] == 1
        old_tops = jnp.where(joined, tops[before], MASKED)
        old_sums = jnp.where(joined, sums[before], 0.0)
        at = pl.ds(frame * slabs, slabs)
        new_tops, new_sums = [], []
        for g in range(groups):
            cols = slice(g * width, (g + 1) * width)

            def column(tile):
                first = g * GROUP
                return jnp.concatenate(
                    [tile[:, first + h : first + h + 1] for h in range(GROUP)], axis=0
                )

            keys = all_k[at, :, cols].reshape(PATCH_IMG, width)
            values = all_v[at, :, cols].reshape(PATCH_IMG, width)
            scores = mm_nt(spread_heads(queries, g, mask_half), keys)
            old_top = column(old_tops)
            top = jnp.maximum(jnp.max(scores, axis=-1, keepdims=True), old_top)
            probs = jnp.exp(scores - top)
            shrink = jnp.exp(old_top - top)
            total = jnp.sum(probs, axis=-1, keepdims=True) + column(old_sums) * shrink
            part = take_heads(mm(probs.astype(BF16), values), mask)
            old = jnp.where(joined, outs[before, :, cols], 0.0)
            outs[frame, :, cols] = part + old * take_heads(shrink, mask)
            for h in range(GROUP):
                new_tops.append(top[h * HDIM : (h + 1) * HDIM])
                new_sums.append(total[h * HDIM : (h + 1) * HDIM])
        tops[frame] = pack_columns(new_tops)
        sums[frame] = pack_columns(new_sums)

    @pl.when((step >= 2 * frames) & (step < 2 * frames + parts))
    def _():
        wide = latent_mask(rows, inner)
        lane = lax.broadcasted_iota(jnp.int32, (4 * rows, LANES), 1)
        first = (step - 2 * frames) * share

        def one_clip(clip):
            out, top, total = latent_attention(clip_queries(clip), kl_ref[clip], vl_ref[clip], wide)
            at = last[clip]
            there = has[clip] == 1
            far_top = jnp.where(there, tops[at], MASKED)
            far_sum = jnp.where(there, sums[at], 0.0)
            far_out = jnp.where(there, outs[at], 0.0)
            both = jnp.maximum(top, far_top)
            near, far = jnp.exp(top - both), jnp.exp(far_top - both)
            total = jnp.where(lane < HEADS, total * near + far_sum * far, 1.0)
            stat = both + jnp.log(total)
            out = out * expand_columns(near / total, inner)
            return out + far_out * expand_columns(far / total, inner), stat

        @pl.loop(0, share // TOGETHER)
        def _(index):
            some = [first + index * TOGETHER + n for n in range(TOGETHER)]
            results = [one_clip(clip) for clip in some]
            for clip, (out, stat) in zip(some, results):
                for r in range(4):
                    part = slice(r * rows, (r + 1) * rows)
                    if r % 2:
                        send[r // 2, clip] = out[part].astype(BF16)
                        send_st[r // 2, clip] = stat[part]
                    else:
                        keep[r // 2, clip] = out[part]
                        keep_st[r // 2, clip] = stat[part]

    for p in range(parts):

        @pl.when(step == 2 * frames + p)
        def _(p=p):
            for n in range(2):
                some = slice(p * share, (p + 1) * share)
                send_li[p, n] = to_lines(send_st[n, some].reshape(lot, LANES))
            for copy in core_copies(p):
                copy.start()
            if p:
                join_part(p - 1)

    @pl.when(step == 2 * frames + parts)
    def _():
        run(late[0])
        join_part(parts - 1)
        run(late[1])
        gather_e.settle()
        run(late[2])
        for p in range(parts):
            for copy in y_copies(p):
                copy.wait()
        stat_y = jnp.concatenate([from_lines(y_li[p]) for p in range(parts)], axis=0)
        context, stat = join_partials(
            keep[0].reshape(total_rows, inner),
            keep_st[0].reshape(total_rows, LANES),
            y_o[...],
            stat_y,
        )
        feed_part(
            functools.partial(run_late, run, late[3:], gather_s),
            context,
            stat,
            depth,
            a,
            gather_s.order,
            lat_ref,
            cot_ref,
            gb_ref,
            weights_e,
            weights_s,
            out_ref,
            mixed_grad,
            context_grad,
            tile_ref,
            gain_ref,
            gw_ref,
            all_k,
            grad_s,
            grad_o,
            normed_v,
            normed_t,
            hat_v,
            store_sem,
        )
        keep_queries.wait()
        gather_e.finish()
        gather_s.finish()


def run_late(run, late, gather, n):
    run(late[n])
    gather.settle(gather.order[n])


def feed_part(
    ready,
    context,
    stat,
    depth,
    plane,
    order,
    lat_ref,
    cot_ref,
    gb_ref,
    weights_e,
    weights_s,
    out_ref,
    mixed_grad,
    context_grad,
    tile_ref,
    gain_ref,
    gw_ref,
    grad_e,
    grad_s,
    grad_o,
    normed_v,
    normed_t,
    hat_v,
    store_sem,
):
    blocks, shrink_rows, width = weights_s.shape
    per_plane = blocks // depth
    inner = context.shape[1]
    output_rows = inner // blocks
    expand_rows = (weights_e.shape[1] - output_rows) // depth
    shrink_at = depth * expand_rows
    output_at = shrink_at + shrink_rows
    half = width // 2
    half_rows = half // shrink_rows
    context_half = context.astype(BF16)

    def weight_o():
        return weights_e[:, shrink_at : shrink_at + output_rows, :].reshape(inner, width)

    mixed = lat_ref[...] + mm(context_half, weight_o())
    hat, scale = normalise(mixed)
    hat_v[...] = hat
    normed = (hat * gb_ref[2:3, :] + gb_ref[5:6, :]).astype(BF16)
    normed_v[...] = normed
    normed_t[...] = normed.astype(F32).T.astype(BF16)
    out_ref[...] = mixed
    mixed_grad[...] = jnp.zeros_like(mixed_grad)
    cot = cot_ref[...]
    stores = []
    for n, k in enumerate(order):
        ready(n)
        plane_k = (plane - k) % depth
        e_rows = pl.ds(pl.multiple_of(plane_k * expand_rows, expand_rows), expand_rows)
        for slot in range(2):
            cols = slice(slot * half, (slot + 1) * half)
            w_e = weights_e[:, e_rows, cols].reshape(blocks * expand_rows, half)
            s_rows = pl.ds(plane_k * per_plane + slot * half_rows, half_rows)
            w_s = weights_s[s_rows].reshape(half, width)
            pre = mm(normed_v[...], w_e)
            cdf = 0.5 * (1.0 + lax.erf(pre * (0.5**0.5)))
            hidden = (pre * cdf).astype(BF16)
            out_ref[...] += mm(hidden, w_s)
            grad_hidden = mm_nt(cot, w_s)
            pdf = jnp.exp(-0.5 * pre * pre) * (1.0 / math.sqrt(2.0 * math.pi))
            grad_pre = (grad_hidden * (cdf + pre * pdf)).astype(BF16)
            if n:
                for copy in stores[2 * (2 * n + slot) - 4 : 2 * (2 * n + slot) - 2]:
                    copy.wait()
            grad_s[slot] = mm_tn(hidden, cot).astype(BF16).reshape(half_rows, shrink_rows, width)
            e_spot = grad_e.at[pl.ds(slot * blocks, blocks)]
            e_spot[...] = (
                mm(normed_t[...], grad_pre).astype(BF16).reshape(blocks, expand_rows, half)
            )
            stores += [
                pltpu.make_async_copy(
                    e_spot, gw_ref.at[:, e_rows, pl.ds(slot * half, half)], store_sem.at[slot]
                ),
                pltpu.make_async_copy(
                    grad_s.at[slot],
                    gw_ref.at[s_rows, pl.ds(shrink_at, shrink_rows), :],
                    store_sem.at[2 + slot],
                ),
            ]
            stores[-1].start()
            stores[-2].start()
            mixed_grad[...] += mm_nt(grad_pre, w_e)

    grad_normed = mixed_grad[...]
    hat = hat_v[...]
    rows = gain_ref.shape[0]
    gain_ref[...] = jnp.concatenate(
        [
            jnp.sum(grad_normed * hat, axis=0, keepdims=True),
            jnp.sum(grad_normed, axis=0, keepdims=True),
            jnp.zeros((rows - 2, width), F32),
        ],
        axis=0,
    )
    total = cot.astype(F32) + norm_back(grad_normed, hat, scale, gb_ref[2:3, :])
    mixed_grad[...] = total
    attended = total.astype(BF16)
    grad_o[...] = mm_tn(context_half, attended).astype(BF16).reshape(grad_o.shape)
    store_o = pltpu.make_async_copy(
        grad_o, gw_ref.at[:, pl.ds(output_at, output_rows), :], store_sem.at[4]
    )
    store_o.start()
    grad_c = mm_nt(attended, weight_o()).astype(BF16)
    context_grad[...] = grad_c
    product = grad_c.astype(F32) * context
    head = lax.broadcasted_iota(jnp.int32, product.shape, 1) // HDIM
    deltas = [
        jnp.sum(jnp.where(head == h, product, 0.0), axis=-1, keepdims=True) for h in range(HEADS)
    ]
    lane = lax.broadcasted_iota(jnp.int32, stat.shape, 1)
    tile_ref[...] = jnp.where(lane < HEADS, stat, pack_columns(deltas, HEADS))
    for copy in stores[-4:]:
        copy.wait()
    store_o.wait()


def head(
    ids,
    last,
    has,
    same,
    shard_e,
    shard_s,
    media,
    latents,
    cotangent,
    gains,
    attend,
    clips,
    inner,
    depth,
    parts,
    plan,
    late,
):
    rows = latents.shape[0] // clips
    frames = media.shape[0] // PATCH_IMG
    width = media.shape[1]
    total = clips * rows
    cut = (clips, rows, inner)
    count = depth * 8
    expand_rows = (shard_e.shape[0] - inner // count) // depth
    feed_rows = shard_e.shape[0] + shard_s.shape[0]
    slabs = PATCH_IMG // expand_rows * frames
    half_rows = width // 2 // shard_s.shape[0]
    once = pl.Buffered(buffer_count=1)

    def whole(x):
        return pl.BlockSpec(x.shape, lambda i: (0,) * len(x.shape), pipeline_mode=once)

    def block(columns):
        return pl.BlockSpec((PATCH_IMG, columns), lambda i: (jnp.minimum(i, frames - 1), 0))

    smem = pl.BlockSpec(memory_space=pltpu.SMEM)
    kv = jax.ShapeDtypeStruct((media.shape[0], inner), BF16)
    small = jax.ShapeDtypeStruct(cut, BF16)
    outs = (
        small,
        small,
        jax.ShapeDtypeStruct((total, width), F32),
        jax.ShapeDtypeStruct((total, width), F32),
        jax.ShapeDtypeStruct((total, inner), BF16),
        jax.ShapeDtypeStruct((total, LANES), F32),
        jax.ShapeDtypeStruct((8, width), F32),
    )
    lines = (2 * HEADS, total // parts)
    dma = pltpu.SemaphoreType.DMA
    return pl.pallas_call(
        functools.partial(head_kernel, depth, frames, parts, plan, late),
        grid=(2 * frames + parts + 1,),
        out_shape=(kv, kv, jax.ShapeDtypeStruct((4,) + cut, BF16))
        + outs
        + (jax.ShapeDtypeStruct((count, feed_rows, width), BF16),),
        in_specs=[smem] * 4
        + [any_spec(), any_spec(), block(width)]
        + [whole(x) for x in (latents, cotangent, gains, attend)],
        out_specs=(block(inner), block(inner), any_spec())
        + tuple(whole(x) for x in outs)
        + (any_spec(),),
        scratch_shapes=[
            pltpu.VMEM((slabs, expand_rows, inner), BF16),
            pltpu.VMEM((slabs, expand_rows, inner), BF16),
            pltpu.VMEM((4,) + cut, BF16),
            pltpu.VMEM((frames, 4 * rows, inner), F32),
            pltpu.VMEM((frames, 4 * rows, LANES), F32),
            pltpu.VMEM((frames, 4 * rows, LANES), F32),
            pltpu.VMEM((2,) + cut, F32),
            pltpu.VMEM((2, clips, rows, LANES), F32),
            pltpu.VMEM((2,) + cut, BF16),
            pltpu.VMEM((2, clips, rows, LANES), F32),
            pltpu.VMEM((2,) + cut, BF16),
            pltpu.VMEM((parts, 2) + lines, F32),
            pltpu.VMEM((parts, 2) + lines, F32),
            pltpu.VMEM((total, inner), BF16),
            pltpu.VMEM((total, inner), BF16),
            pltpu.VMEM((parts,) + lines, F32),
            pltpu.VMEM((parts,) + lines, F32),
            pltpu.VMEM((count,) + shard_e.shape, BF16),
            pltpu.VMEM((count,) + shard_s.shape, BF16),
            pltpu.VMEM((2, half_rows) + shard_s.shape, BF16),
            pltpu.VMEM((count, inner // count, width), BF16),
            pltpu.VMEM((total, width), BF16),
            pltpu.VMEM((width, total), BF16),
            pltpu.VMEM((total, width), F32),
            dma((2,)),
            dma((count,)),
            dma((count,)),
            dma((count,)),
            dma((count,)),
            dma((3 + 4 * parts,)),
            dma((3 + 4 * parts,)),
            dma,
            dma((5,)),
        ],
        compiler_params=params(collective_id=2, has_side_effects=True),
        name="head",
    )(ids, last, has, same, shard_e, shard_s, media, latents, cotangent, gains, attend)


def norm_kernel(depth, images, lats, chunk, pack_ref, feed_ref, norm_ref, mine_ref, *refs):
    buffers, refs = refs[:5], refs[5:]
    load_sem, send_sem, recv_sem, tile, slots, tile_send, tile_recv = refs
    count = images * lats
    img = lax.axis_index("img")
    lat = lax.axis_index("lat")
    me = img * lats + lat
    scatter = Scatter(depth, chunk, pack_ref, buffers, load_sem, (send_sem, recv_sem))
    barrier = pltpu.get_barrier_semaphore()

    def other(k):
        there = (me + k) % count
        return there // lats, there % lats

    for k in range(1, count):
        pl.semaphore_signal(barrier, inc=1, device_id=other(k), device_id_type=MESH)
    pl.semaphore_wait(barrier, count - 1)
    scatter.begin()
    feed_rows = feed_ref.shape[0]
    squares = jnp.zeros((8, feed_ref.shape[1]), F32)
    for n in range(feed_rows // 8):
        part = feed_ref[n * 8 : (n + 1) * 8, :]
        squares = squares + part * part
    squares = jnp.sum(squares)
    scatter.run(NORM_PLAN)
    scatter.finish(mine_ref)
    own = mine_ref[...]
    tile[...] = jnp.full(tile.shape, squares + jnp.sum(own * own), F32)
    slots[me] = tile[...]

    def exchange(k, spot):
        return pltpu.make_async_remote_copy(
            src_ref=tile,
            dst_ref=slots.at[spot],
            send_sem=tile_send.at[k],
            recv_sem=tile_recv.at[k],
            device_id=other(k),
            device_id_type=MESH,
        )

    for k in range(1, count):
        exchange(k, me).start()
    for k in range(1, count):
        exchange(k, (me - k) % count).wait_recv()
    norm_ref[...] = jnp.sqrt(jnp.sum(slots[...], axis=0))
    for k in range(1, count):
        exchange(k, me).wait_send()


def norm_and_sum(grad_attend, mine_feed, images, lats):
    count = images * lats
    depth = images // 2
    rows = grad_attend.shape[0] // count
    cols = grad_attend.shape[1]
    tile = (8, LANES)
    return pl.pallas_call(
        functools.partial(norm_kernel, depth, images, lats, cols),
        out_shape=(jax.ShapeDtypeStruct(tile, F32), jax.ShapeDtypeStruct((rows, cols), F32)),
        in_specs=[any_spec(), vmem_spec()],
        out_specs=(vmem_spec(), vmem_spec()),
        scratch_shapes=scatter_buffers(depth, rows, cols)
        + scatter_sems(depth)
        + [
            pltpu.VMEM(tile, F32),
            pltpu.VMEM((count,) + tile, F32),
            pltpu.SemaphoreType.DMA((count,)),
            pltpu.SemaphoreType.DMA((count,)),
        ],
        compiler_params=params(collective_id=3, has_side_effects=True),
        name="norm",
    )(grad_attend.reshape(count, rows, cols), mine_feed)


def update_kernel(rates, inner, count, norm_ref, mine, feed_ref, *refs):
    states, refs = refs[:18], refs[18:]
    olds, refs = refs[:count], refs[count:]
    norm_out, news, moved = refs[0], refs[1:19], refs[19:]
    for old, new in zip(olds, moved):
        new[...] = old[...]

    @pl.when(pl.program_id(0) == 0)
    def _():
        update_states(rates, inner, norm_ref, mine, feed_ref, states, norm_out, news)


def update_states(rates, inner, norm_ref, mine, feed_ref, states, norm_out, news):
    norm = norm_ref[...]
    norm_out[...] = norm
    factor = jnp.minimum(1.0, CLIP_NORM / (norm + 1e-06))[0:1, 0:1]

    def update(n, grad, rows, cols, decay):
        at = (rows, cols)
        master = states[n][at]
        step_grad = factor * grad
        if decay:
            step_grad = step_grad + decay * master
        buffer = MOMENTUM * states[6 + n][at] + step_grad
        new = master - rates[n] * (step_grad + MOMENTUM * buffer)
        news[n][at] = new
        news[6 + n][at] = buffer
        news[12 + n][at] = AVERAGING * states[12 + n][at] + (1.0 - AVERAGING) * new

    every = slice(None)
    width = feed_ref.shape[1]
    expand_rows, expand_cols = states[2].shape
    shrink_rows = states[3].shape[0]
    at = expand_cols // width * expand_rows
    update(0, mine[:, : 3 * inner], every, every, DECAY)
    update(1, feed_ref[at + shrink_rows :, :], every, every, DECAY)
    for g in range(expand_cols // width):
        grad = feed_ref[g * expand_rows : (g + 1) * expand_rows, :]
        update(2, grad, every, slice(g * width, (g + 1) * width), DECAY)
    update(3, feed_ref[at : at + shrink_rows, :], every, every, DECAY)
    small = mine[:, 3 * inner :].T
    update(4, small[0:3], every, every, 0.0)
    update(5, small[3:6], every, every, 0.0)


def update_all(norm, mine, mine_feed, states, rates, inner, moved, steps):
    def like(x):
        return jax.ShapeDtypeStruct(x.shape, x.dtype)

    def whole(x):
        return pl.BlockSpec(x.shape, lambda i: (0, 0), pipeline_mode=pl.Buffered(buffer_count=1))

    def block(x):
        return pl.BlockSpec((x.shape[0] // steps, x.shape[1]), lambda i: (i, 0))

    blocks = [block(x) for x in moved]
    kept = [whole(x) for x in states]
    return pl.pallas_call(
        functools.partial(update_kernel, rates, inner, len(moved)),
        grid=(steps,),
        out_shape=(like(norm),) + tuple(like(x) for x in states) + tuple(like(x) for x in moved),
        in_specs=[whole(norm), whole(mine), whole(mine_feed)] + kept + blocks,
        out_specs=tuple([whole(norm)] + kept + blocks),
        compiler_params=params(),
        name="update",
    )(norm, mine, mine_feed, *states, *moved)


def pack_feed(expand, shrink, output):
    width = shrink.shape[-1]
    groups = expand.shape[-1] // width
    lead = expand.shape[:-2]
    rows = expand.shape[-2]
    cut = expand.reshape(lead + (rows, groups, width))
    cut = jnp.moveaxis(cut, -2, -3).reshape(lead + (groups * rows, width))
    return jnp.concatenate([cut, shrink, output], axis=-2)


def unpack_feed(packed, rows, shrink_rows):
    width = packed.shape[-1]
    lead = packed.shape[:-2]
    groups = (packed.shape[-2] - shrink_rows) // rows
    split = groups * rows
    cut = packed[..., :split, :].reshape(lead + (groups, rows, width))
    expand = jnp.moveaxis(cut, -3, -2).reshape(lead + (rows, groups * width))
    return (
        expand,
        packed[..., split : split + shrink_rows, :],
        packed[..., split + shrink_rows :, :],
    )


def step_size(width, inner, ff):
    return 0.37 * math.sqrt((4 * width * inner + 2 * width * ff) / width)


def lat_pairs(count, along_core):
    pairs = []
    for lat in range(count):
        e, c = lat // 2, lat % 2
        pairs.append((lat, e * 2 + 1 - c if along_core else (1 - e) * 2 + c))
    return pairs


def shards(
    images,
    lats,
    media,
    latents,
    counts,
    cotangent,
    attend_weight,
    output_weight,
    expand_weight,
    shrink_weight,
    layer_gains,
    layer_biases,
    attend_momentum,
    output_momentum,
    expand_momentum,
    shrink_momentum,
    gains_momentum,
    biases_momentum,
    attend_average,
    output_average,
    expand_average,
    shrink_average,
    gains_average,
    biases_average,
):
    devices = images * lats
    depth = images // 2
    fast = devices == BLOCKS and lats == 4 and images % 2 == 0
    samples, lat_dev, width = latents.shape
    rows = samples * lat_dev
    ff = expand_weight.shape[1]
    inner = attend_weight.shape[1] // 3
    patch_dev = media.shape[0]
    frames = patch_dev // PATCH_IMG
    over_core = functools.partial(lax.ppermute, axis_name="lat", perm=lat_pairs(lats, True))
    over_y = functools.partial(lax.ppermute, axis_name="lat", perm=lat_pairs(lats, False))

    attend_rows = attend_weight.shape[0]
    if fast:
        attend, shard_e, shard_s, gains = start(
            attend_weight,
            layer_gains.T,
            layer_biases.T,
            expand_weight,
            shrink_weight,
            output_weight,
            depth,
        )
        attend = attend.reshape(width, attend.shape[2])
    else:

        def everywhere(x):
            return lax.all_gather(x.astype(BF16), AXES, axis=0, tiled=True)

        small = jnp.concatenate([layer_gains, layer_biases], axis=1)
        small = jnp.pad(small, ((0, 0), (0, LANES - small.shape[1])))
        attend = everywhere(jnp.concatenate([attend_weight, small], axis=1))
        feed = pack_feed(
            everywhere(expand_weight).reshape(BLOCKS, width // BLOCKS, ff),
            everywhere(shrink_weight).reshape(BLOCKS, ff // BLOCKS, width),
            everywhere(output_weight).reshape(BLOCKS, inner // BLOCKS, width),
        )
        gains = attend[:, 3 * inner : 3 * inner + 8].astype(F32).T

    sample_ends = jnp.cumsum(counts[0])
    first_frame = lax.axis_index("lat") * frames
    frame_ids = first_frame + jnp.arange(frames, dtype=jnp.int32)
    ids = jnp.sum((frame_ids[:, None] >= sample_ends[None, :]).astype(jnp.int32), axis=1)
    ids = jnp.clip(ids, 0, samples - 1)

    latent_flat = latents.reshape(rows, width)
    cot_flat = cotangent.reshape(rows, width)
    cut = (samples, lat_dev, inner)

    def to_group(own):
        other = over_y(own)
        return [own, over_core(own), other, over_core(other)]

    if fast:
        clip = jnp.arange(samples, dtype=jnp.int32)
        here = ids[None, :] == clip[:, None]
        has = jnp.any(here, axis=1).astype(jnp.int32)
        last = jnp.max(jnp.where(here, jnp.arange(frames, dtype=jnp.int32)[None, :], 0), axis=1)
        same = jnp.concatenate([jnp.zeros((1,), jnp.int32), (ids[1:] == ids[:-1]).astype(jnp.int32)])
        (
            keys,
            values,
            query_all,
            latent_key,
            latent_value,
            out_rows,
            mixed_grad,
            context_grad,
            tile,
            gain_f,
            grad_feed,
        ) = head(
            ids,
            last,
            has,
            same,
            shard_e,
            shard_s,
            media,
            latent_flat,
            cot_flat,
            gains,
            attend,
            samples,
            inner,
            depth,
            3,
            HEAD_PLAN,
            HEAD_LATE,
        )
    else:
        query, latent_key, latent_value = latent_project(latent_flat, gains, attend, inner)
        latent_key = latent_key.reshape(cut)
        latent_value = latent_value.reshape(cut)
        queries = to_group(query.reshape(cut))
        keys, values = media_project(media, gains, attend, inner)
        keep, send, keep_st, send_st = attention_forward(
            ids, queries, keys, values, latent_key, latent_value
        )
        got, got_st = over_core(send), over_core(send_st)
        flat_o, flat_s = (2, rows, inner), (2, rows, LANES)
        own, own_st, away, away_st = join_cores(
            keep.reshape(flat_o),
            keep_st.reshape(flat_s),
            got.reshape(flat_o),
            got_st.reshape(flat_s),
        )
        got, got_st = over_y(away), over_y(away_st)
        out_rows, mixed_grad, context_grad, tile, gain_f, grad_feed = feed_forward(
            own, own_st, got, got_st, latent_flat, cot_flat, gains, feed
        )
    if fast:
        grad_media, latents_grad, grad_attend, mine_feed = back(
            ids,
            last,
            has,
            same,
            grad_feed,
            query_all,
            context_grad.reshape(cut),
            tile,
            keys,
            values,
            media,
            latent_key,
            latent_value,
            gains,
            attend,
            latent_flat,
            mixed_grad,
            gain_f,
            depth,
            2 * LANES,
            BACK_PLAN,
        )
    else:
        grads = to_group(context_grad.reshape(cut))
        tiles = to_group(tile.reshape(samples, lat_dev, LANES))
        grad_media, latent_kv, keep, send, grad_kv, gain_m = attention_backward(
            ids,
            queries,
            grads,
            tiles,
            keys,
            values,
            latent_key,
            latent_value,
            media,
            gains,
            attend,
        )
        got = over_core(send)
        pair = keep.astype(F32) + got.astype(F32)
        got = over_y(pair[1].astype(BF16))
        latents_grad, grad_attend = latent_backward(
            latent_flat,
            mixed_grad,
            pair[0].reshape(rows, inner),
            got.reshape(rows, inner),
            latent_kv.reshape(rows, 2 * inner),
            gains,
            attend,
            grad_kv,
            gain_m,
            gain_f,
        )

        def owners(x):
            return lax.psum_scatter(x.astype(F32), AXES, scatter_dimension=0, tiled=True)

        mine = owners(grad_attend)
        own_expand, own_shrink, own_output = unpack_feed(grad_feed, width // BLOCKS, ff // BLOCKS)
        own_expand = owners(own_expand.reshape(width, ff))
        own_shrink = owners(own_shrink.reshape(ff, width))
        own_output = owners(own_output.reshape(inner, width))
    masters = (
        attend_weight,
        output_weight,
        expand_weight,
        shrink_weight,
        layer_gains,
        layer_biases,
    )
    moments = (
        attend_momentum,
        output_momentum,
        expand_momentum,
        shrink_momentum,
        gains_momentum,
        biases_momentum,
    )
    averages = (
        attend_average,
        output_average,
        expand_average,
        shrink_average,
        gains_average,
        biases_average,
    )
    step_rate = step_size(width, inner, ff)
    if fast:
        rates = tuple(step_rate * scale for scale in RATE_SCALES)
        states = masters + moments + averages
        states = tuple(x.T if x.shape[1] == 3 else x for x in states)
        norm, mine = norm_and_sum(grad_attend, mine_feed, images, lats)
        norm, *news = update_all(
            norm,
            mine,
            mine_feed,
            states,
            rates,
            inner,
            (),
            1,
        )
        news = [x.T if x.shape[0] == 3 else x for x in news[:18]]
        grad_norm = norm[0, 0]
        new_masters, new_buffers, new_smoothed = news[:6], news[6:12], news[12:]
    else:
        small = mine[:, 3 * inner :]
        owned = (
            mine[:, : 3 * inner],
            own_output,
            own_expand,
            own_shrink,
            small[:, 0:3],
            small[:, 3:6],
        )
        squares = sum(jnp.sum(piece * piece) for piece in owned)
        squares = lax.psum(squares, AXES)
        grad_norm = jnp.sqrt(squares)
        factor = jnp.minimum(1.0, CLIP_NORM / (grad_norm + 1e-06))
        decay_rates = (DECAY, DECAY, DECAY, DECAY, 0.0, 0.0)
        new_masters = []
        new_buffers = []
        new_smoothed = []
        for master, moment, average, reduced, decay_rate, rate_scale in zip(
            masters, moments, averages, owned, decay_rates, RATE_SCALES
        ):
            step_grad = factor * reduced + decay_rate * master
            buffer = MOMENTUM * moment + step_grad
            master_new = master - step_rate * rate_scale * (step_grad + MOMENTUM * buffer)
            new_masters.append(master_new)
            new_buffers.append(buffer)
            new_smoothed.append(AVERAGING * average + (1.0 - AVERAGING) * master_new)
    return (
        out_rows.reshape(latents.shape),
        grad_media,
        latents_grad.reshape(latents.shape),
        grad_norm,
        *new_masters,
        *new_buffers,
        *new_smoothed,
    )


def solution(mesh):
    rows = P(AXES, None)
    split = P("img", "lat", None)
    return jax.shard_map(
        functools.partial(shards, mesh.shape["img"], mesh.shape["lat"]),
        mesh=mesh,
        in_specs=(rows, split, P("img", None), split) + (rows,) * 18,
        out_specs=(split, rows, split, P()) + (rows,) * 18,
        check_vma=False,
    )
```
